32 devices in a mesh: dp: 16 (over z, x, core), rep: 2 (over y).
Axes of the slice: x: 2, y: 2, z: 4, core: 2. Of those that a mesh axis runs over, the one named last changes fastest.
Arguments:
- tokens: bfloat16 [2, 4096, 2048], P('rep', 'dp'), may hold values from -6 to 6
- attention_gain: float32 [2048], replicated, may hold values from 0.1 to 1.9
- query_weight: bfloat16 [2048, 2048], P('dp'), may hold values from -0.125 to 0.125
- key_weight: bfloat16 [2048, 2048], P('dp'), may hold values from -0.125 to 0.125
- value_weight: bfloat16 [2048, 2048], P('dp'), may hold values from -0.125 to 0.125
- output_weight: bfloat16 [2048, 2048], P('dp'), may hold values from -0.5 to 0.5
- dense_gain: float32 [2048], replicated, may hold values from 0.1 to 1.9
- gate_weight: bfloat16 [8192, 2048], P('dp'), may hold values from -0.125 to 0.125
- up_weight: bfloat16 [8192, 2048], P('dp'), may hold values from -0.125 to 0.125
- down_weight: bfloat16 [8192, 2048], P('dp'), may hold values from -0.0625 to 0.0625
- block_document: int32 [2, 32], P('rep'), may hold values from 0 to 7, never falling along the last dimension, each value on 1 to 16 neighbouring positions
- document_tail: int32 [2, 8], P('rep'), may hold values from 1 to 128
- cotangent: bfloat16 [2, 4096, 2048], P('rep', 'dp'), may hold values from -6 to 6
Outputs:
- layer_out: bfloat16 [2, 4096, 2048], P('rep', 'dp')
- input_grad: float32 [2, 4096, 2048], P('rep', 'dp')
- attention_gain_grad: float32 [2048], replicated
- query_grad: float32 [2048, 2048], P('dp')
- key_grad: float32 [2048, 2048], P('dp')
- value_grad: float32 [2048, 2048], P('dp')
- output_grad: float32 [2048, 2048], P('dp')
- dense_gain_grad: float32 [2048], replicated
- gate_grad: float32 [8192, 2048], P('dp')
- up_grad: float32 [8192, 2048], P('dp')
- down_grad: float32 [8192, 2048], P('dp')
The draws below stay inside these ranges and needn't reach their ends.
Inputs may be any that keep to these rules, and one draw needn't show every extreme that they name: `block_document`: document numbers of a pack start at 0, never fall from block to block, and every document covers 1 to 16 whole blocks; each number of 0 to 7 appears.
All inputs are finite; a program needn't handle non-finite values.
Results may differ from the reference program's by a relative error of at most 0.02.
Values may be sent and summed in bfloat16 or wider, within the bound.
A program may use at most 576 MiB of HBM per device.

```python
import math
import jax
import jax.numpy as jnp
import numpy as np
from jax import lax

D = 2048
HEADS = 32
HEAD_DIM = 64
FF = 8192
BLOCK = 128
DOC_MOST = 16
PACKS = 2
PACK_TOK = 4096
PACK_BLK = 32
DOCS = 8


def with_ends(array, own_key, least, largest):
    longest = array.shape.index(max(array.shape))
    spots = []
    for shift in (0, 1):
        where = [jax.random.randint(jax.random.fold_in(own_key, axis), (), 0, length) for axis, length in enumerate(array.shape)]
        where[longest] = (where[longest] + shift) % array.shape[longest]
        spots.append(tuple(where))
    return array.at[spots[0]].set(least).at[spots[1]].set(largest)


def level_of(own_key, shape, pieces, smallest, high):
    def one(dim, parts):
        heights = jax.random.uniform(jax.random.fold_in(jax.random.fold_in(own_key, 6), dim), (parts,), jnp.float32, smallest / len(pieces), high / len(pieces))
        return jnp.repeat(jnp.exp(heights), shape[dim] // parts).reshape((-1,) + (1,) * (len(shape) - dim - 1))

    factor_of = one(*pieces[0])
    for cut in pieces[1:]:
        factor_of = factor_of * one(*cut)
    return factor_of


def split_up(number_of, total, most, slope):
    portions = [(1 << 20) // math.isqrt(grade ** slope) + 1 for grade in range(2, number_of + 1)]
    surplus, given = total - most - (number_of - 1), [1] * (number_of - 1)
    while surplus > 0:
        free = [i for i in range(number_of - 1) if given[i] < most]
        whole, left = sum([portions[i] for i in free]), surplus
        for i in free:
            more = min(most - given[i], max(1, left * portions[i] // whole), surplus)
            given[i] = given[i] + more
            surplus = surplus - more
    return np.array([most] + given)


def ragged_sizes(own_key, number_of, total, most, slope):
    if number_of == 2:
        one = jax.random.randint(own_key, (), max(1, total - most), min(most, total - 1) + 1)
        return jnp.stack([one, total - one])
    tallies = jnp.asarray(split_up(number_of, total, most, slope), jnp.int32)
    twos = (number_of - 1) // 2
    source_of, sink = tallies[1:1 + 2 * twos:2], tallies[2:2 + 2 * twos:2]
    room = jnp.minimum(source_of - 1, most - sink)
    moved = jax.random.randint(jax.random.fold_in(own_key, 1), (twos,), 0, 1 << 20) % (room + 1)
    tallies = tallies.at[1:1 + 2 * twos:2].set(source_of - moved).at[2:2 + 2 * twos:2].set(sink + moved)
    return tallies[jax.random.permutation(jax.random.fold_in(own_key, 2), number_of)]


def gaussian(rng, extent, spread, limit, shards=(), kind=jnp.bfloat16):
    drawn = jax.random.normal(rng, extent, jnp.float32) * spread
    if len(shards) > 0:
        drawn = level_of(rng, extent, shards, -0.22, 0.18) * drawn
    return jnp.clip(drawn, min=-limit, max=limit).astype(kind)


def setup_inputs(seed: int = 0) -> dict:
    key_of = jax.random.split(jax.random.key(seed), 14)
    tokens = gaussian(key_of[0], (PACKS, PACK_TOK, D), 1.0, 6.0, ((0, 2), (1, 16)))
    attention_gain = jnp.clip(1.0 + 0.18 * jax.random.normal(key_of[1], (D,), jnp.float32), 0.1, 1.9)
    query_weight = gaussian(key_of[2], (D, D), D ** -0.5, 0.125, ((0, 16),))
    key_weight = gaussian(key_of[3], (D, D), D ** -0.5, 0.125, ((0, 16),))
    value_weight = gaussian(key_of[4], (D, D), D ** -0.5, 0.125, ((0, 16),))
    output_weight = gaussian(key_of[5], (D, D), (D // 16) ** -0.5, 0.5, ((0, 16),))
    dense_gain = jnp.clip(1.0 + 0.18 * jax.random.normal(key_of[6], (D,), jnp.float32), 0.1, 1.9)
    gate_weight = gaussian(key_of[7], (FF, D), D ** -0.5, 0.125, ((0, 16),))
    up_weight = gaussian(key_of[8], (FF, D), D ** -0.5, 0.125, ((0, 16),))
    down_weight = gaussian(key_of[9], (FF, D), FF ** -0.5, 0.0625, ((0, 16),))
    block_document = jax.vmap(lambda own: jnp.searchsorted(jnp.cumsum(ragged_sizes(own, DOCS, PACK_BLK, DOC_MOST, 2)), jnp.arange(PACK_BLK), side="right"))(jax.random.split(key_of[10], PACKS)).reshape((PACKS, PACK_BLK)).astype(jnp.int32)
    document_tail = with_ends(jax.random.randint(key_of[11], (PACKS, DOCS), 1, BLOCK + 1), jax.random.fold_in(key_of[11], 1), 1, BLOCK).astype(jnp.int32)
    cotangent = gaussian(key_of[12], (PACKS, PACK_TOK, D), 1.0, 6.0, ((0, 2), (1, 16)))
    return {"tokens": tokens, "attention_gain": attention_gain, "query_weight": query_weight, "key_weight": key_weight, "value_weight": value_weight, "output_weight": output_weight, "dense_gain": dense_gain, "gate_weight": gate_weight, "up_weight": up_weight, "down_weight": down_weight, "block_document": block_document, "document_tail": document_tail, "cotangent": cotangent}


EPSILON = 1e-05
ROPE_BASE = 130000.0
MASKED_SCORE = -1e+30
PRECISE = lax.Precision.HIGHEST

@jax.custom_vjp
def low(v):
    return lax.optimization_barrier(v.astype(jnp.bfloat16)).astype(jnp.float32)

@jax.custom_vjp
def low_back(v):
    return v

def low_keep(v):
    return (low(v), None)

def low_pass(kept, grad):
    return (grad,)

def back_keep(v):
    return (v, None)

def back_low(kept, grad):
    return (low(grad),)
low.defvjp(low_keep, low_pass)
low_back.defvjp(back_keep, back_low)

def document_layout(block_document, document_tail):
    pack_blocks = block_document.shape[0]
    doc_count = document_tail.shape[0]
    doc_ids = jnp.arange(doc_count, dtype=jnp.int32)
    member = (block_document[None, :] == doc_ids[:, None]).astype(jnp.int32)
    counts = lax.optimization_barrier(jnp.sum(member, axis=1)).astype(jnp.int32)
    first_block = (jnp.cumsum(counts) - counts).astype(jnp.int32)
    token_doc = jnp.repeat(block_document, BLOCK, total_repeat_length=pack_blocks * BLOCK)
    chosen = (token_doc[:, None] == doc_ids[None, :]).astype(jnp.int32)
    doc_start = lax.optimization_barrier(jnp.sum(chosen * first_block[None, :], axis=1)).astype(jnp.int32) * BLOCK
    length = lax.optimization_barrier(jnp.sum(chosen * ((counts - 1) * BLOCK + document_tail)[None, :], axis=1)).astype(jnp.int32)
    position = jnp.arange(pack_blocks * BLOCK, dtype=jnp.int32) - doc_start
    return (token_doc, position, position < length)

def rope_tables(position):
    half_dim = HEAD_DIM // 2
    frequency = ROPE_BASE ** (-(jnp.arange(half_dim, dtype=jnp.float32) * (2.0 / HEAD_DIM)))
    angles = position.astype(jnp.float32)[:, None] * frequency[None, :]
    cosine = jnp.cos(angles)
    sine = jnp.sin(angles)
    return (jnp.concatenate([cosine, cosine], 1), jnp.concatenate([sine, sine], 1))

def rotate(values, cosine, sine):
    half_dim = values.shape[-1] // 2
    turned = jnp.concatenate([-values[..., half_dim:], values[..., :half_dim]], -1)
    return values * cosine[:, None, :] + turned * sine[:, None, :]

def rms(values, norm_gain):
    return values * lax.rsqrt(lax.optimization_barrier(jnp.mean(values * values, axis=-1, keepdims=True)) + EPSILON) * norm_gain

def project(left, weight):
    return jnp.dot(left, weight.T, precision=PRECISE)

def head_attention(query, key, value, token_doc, valid):
    block_rows = min(512, PACK_TOK)
    window = min(PACK_TOK, DOC_MOST * BLOCK + block_rows)
    score_scale = 1.0 / math.sqrt(HEAD_DIM)

    def block_fn(first_row):
        key_start = jnp.maximum(first_row + block_rows - window, 0).astype(jnp.int32)
        query_rows = lax.dynamic_slice_in_dim(query, first_row, block_rows, 0)
        key_rows = lax.dynamic_slice_in_dim(key, key_start, window, 0)
        value_rows = lax.dynamic_slice_in_dim(value, key_start, window, 0)
        query_doc = lax.dynamic_slice_in_dim(token_doc, first_row, block_rows, 0)
        key_doc = lax.dynamic_slice_in_dim(token_doc, key_start, window, 0)
        key_valid = lax.dynamic_slice_in_dim(valid, key_start, window, 0)
        query_index = first_row + jnp.arange(block_rows, dtype=jnp.int32)
        key_index = key_start + jnp.arange(window, dtype=jnp.int32)
        allowed = (query_doc[:, None] == key_doc[None, :]) & (key_index[None, :] <= query_index[:, None]) & key_valid[None, :]
        raw_scores = low_back(jnp.dot(query_rows, key_rows.T, precision=PRECISE))
        scores = jnp.where(allowed, raw_scores * score_scale, MASKED_SCORE)
        row_max = lax.optimization_barrier(jnp.max(scores, axis=1, keepdims=True))
        weights = jnp.exp(scores - row_max)
        weights_low = low(weights / lax.optimization_barrier(jnp.sum(weights, axis=1, keepdims=True)))
        return jnp.dot(weights_low, value_rows, precision=PRECISE)
    starts = jnp.arange(PACK_TOK // block_rows, dtype=jnp.int32) * block_rows
    blocks = lax.map(jax.checkpoint(block_fn), starts)
    return blocks.reshape(PACK_TOK, HEAD_DIM)

def pack_layer(hidden_in, attention_gain, query_weight, key_weight, value_weight, output_weight, dense_gain, gate_weight, up_weight, down_weight, token_doc, position, valid):
    cosine, sine = rope_tables(position)
    head_shape = (PACK_TOK, HEADS, HEAD_DIM)
    normed = low(rms(hidden_in, attention_gain))
    query = low(rotate(low_back(project(normed, query_weight)).reshape(head_shape), cosine, sine))
    key = low(rotate(low_back(project(normed, key_weight)).reshape(head_shape), cosine, sine))
    value = low(low_back(project(normed, value_weight))).reshape(head_shape)

    def one_head(operands):
        return head_attention(operands[0], operands[1], operands[2], token_doc, valid)
    heads = lax.map(one_head, (query.transpose(1, 0, 2), key.transpose(1, 0, 2), value.transpose(1, 0, 2)))
    attended = low(low_back(heads.transpose(1, 0, 2).reshape(PACK_TOK, D)))
    mixed = hidden_in + low_back(jnp.dot(attended, output_weight, precision=PRECISE))
    normed_two = low(rms(mixed, dense_gain))
    gate = low_back(project(normed_two, gate_weight))
    up_part = low_back(project(normed_two, up_weight))
    hidden = low(jax.nn.silu(gate) * up_part)
    return mixed + low_back(jnp.dot(hidden, down_weight, precision=PRECISE))

def reference(tokens, attention_gain, query_weight, key_weight, value_weight, output_weight, dense_gain, gate_weight, up_weight, down_weight, block_document, document_tail, cotangent):
    token_doc, position, valid = jax.vmap(document_layout)(block_document, document_tail)
    params = (attention_gain.astype(jnp.float32), query_weight.astype(jnp.float32), key_weight.astype(jnp.float32), value_weight.astype(jnp.float32), output_weight.astype(jnp.float32), dense_gain.astype(jnp.float32), gate_weight.astype(jnp.float32), up_weight.astype(jnp.float32), down_weight.astype(jnp.float32))

    def layer(hidden_all, *weights):

        def one_pack(operands):
            return pack_layer(operands[0], *weights, operands[1], operands[2], operands[3])
        return lax.map(jax.checkpoint(one_pack), (hidden_all, token_doc, position, valid))
    layer_out, pullback = jax.vjp(layer, tokens.astype(jnp.float32), *params)
    gradients = pullback(cotangent.astype(jnp.float32))
    return (layer_out.astype(jnp.bfloat16), gradients[0], gradients[1], gradients[2], gradients[3], gradients[4], gradients[5], gradients[6], gradients[7], gradients[8], gradients[9])
```

```python
import functools
import math

import jax
import jax.numpy as jnp
from jax import lax
from jax.experimental import pallas as pl
from jax.experimental.pallas import tpu as pltpu
from jax.sharding import PartitionSpec as P

HEAD_DIM = 64
HALF = HEAD_DIM // 2
BLOCK = 128
CHUNK = 512
FF_TILE = 256
EPSILON = 1e-05
ROPE_BASE = 130000.0
MASKED_SCORE = -1e30
MESH = pl.DeviceIdType.MESH
MIB = 2**20
LOW = jnp.bfloat16
F32 = jnp.float32


def dot_nn(a, b):
    return lax.dot_general(a, b, (((1,), (0,)), ((), ())), preferred_element_type=F32)


def dot_nt(a, b):
    return lax.dot_general(a, b, (((1,), (1,)), ((), ())), preferred_element_type=F32)


def dot_tn(a, b):
    return lax.dot_general(a, b, (((0,), (0,)), ((), ())), preferred_element_type=F32)


def grid_of(chips):
    depth = 4 if chips % 8 == 0 else 2
    return depth, chips // depth


def chip_at(place, chips):
    depth, width = grid_of(chips)
    place = lax.rem(place + chips, chips)
    later = place - depth
    row, column = later // (width - 1), later % (width - 1)
    odd = row % 2
    far = (depth - 1 - row) * width + 1 + column + odd * (width - 2 - 2 * column)
    return jnp.where(place < depth, place * width, far)


def place_of(chip, chips):
    depth, width = grid_of(chips)
    z, x = chip // width, chip % width
    row = depth - 1 - z
    odd = row % 2
    column = x - 1 + odd * (width - 2 * x)
    return jnp.where(x == 0, z, depth + row * (width - 1) + column)


class Ring:
    def __init__(self):
        self.chips = lax.axis_size("dp") // 2
        me = lax.axis_index("dp")
        self.core = me % 2
        self.chip = me // 2
        self.partner = self.chip * 2 + 1 - self.core
        self.place = place_of(self.chip, self.chips)
        self.next = (self.device(1), self.device(-1))
        self.back = (self.next[1], self.next[0])

    def chip_far(self, steps):
        return chip_at(self.place + steps, self.chips)

    def device(self, steps):
        return self.chip_far(steps) * 2 + self.core

    def greet(self, others):
        barrier = pltpu.get_barrier_semaphore()
        for other in others:
            pl.semaphore_signal(barrier, inc=1, device_id={"dp": other}, device_id_type=MESH)
        pl.semaphore_wait(barrier, len(others))


def remote(src, dst, send_sem, recv_sem, device):
    return pltpu.make_async_remote_copy(
        src_ref=src,
        dst_ref=dst,
        send_sem=send_sem,
        recv_sem=recv_sem,
        device_id={"dp": device},
        device_id_type=MESH,
    )


def half_rows(direction, rows):
    return pl.ds(direction * (rows // 2), rows // 2)


def gather_project_kernel(
    normed, weights, cosine, sine, qkv, gathered,
    partner_weights, x_buf, staged,
    ag_send, ag_recv, w_send, w_recv, q_send, q_recv, local_sem,
):
    ring = Ring()
    n = ring.chips
    rows = normed.shape[0]
    r = qkv.shape[2]
    ring.greet((ring.next[0], ring.next[1], ring.partner))
    swap = remote(weights, partner_weights, w_send, w_recv, ring.partner)
    swap.start()
    keep = pltpu.make_async_copy(normed, gathered.at[ring.chip], local_sem.at[2])
    keep.start()

    def hop(t, d):
        chip = ring.chip_far((1 - t) if d == 0 else (t - 1))
        return chip, half_rows(d, rows)

    def send(t, d, first):
        chip, part = hop(t, d)
        src = normed.at[part] if first else gathered.at[chip, part]
        return remote(src, gathered.at[chip, part], ag_send.at[d, t - 1], ag_recv.at[d, t - 1], ring.next[d])

    for d in (0, 1):
        send(1, d, True).start()

    def project_block(t, from_input):
        x = normed[...] if from_input else x_buf[...]
        places = [ring.chip_far(-t), ring.chip_far(t)]
        cos = jnp.concatenate([cosine[places[d], half_rows(d, rows), :] for d in (0, 1)], 0)
        sin = jnp.concatenate([sine[places[d], half_rows(d, rows), :] for d in (0, 1)], 0)

        def heads(w):
            part = [dot_nt(x, w[i * r : (i + 1) * r, :]) for i in range(5)]
            return (
                (part[0] * cos + part[1] * sin).astype(LOW),
                (part[2] * cos + part[3] * sin).astype(LOW),
                part[4].astype(LOW),
            )

        starts = [
            pl.multiple_of((places[d] * 2 + ring.core) * rows + d * (rows // 2), rows // 2)
            for d in (0, 1)
        ]
        for i, value in enumerate(heads(weights)):
            for d in (0, 1):
                qkv[i, pl.ds(starts[d], rows // 2), :] = value[d * (rows // 2) : (d + 1) * (rows // 2)]
        if from_input:
            swap.wait()
        for i, value in enumerate(heads(partner_weights)):
            staged[t, i] = value
        for d in (0, 1):
            remote(
                staged.at[t, :, half_rows(d, rows)],
                qkv.at[:, pl.ds(starts[d], rows // 2)],
                q_send.at[d, t],
                q_recv.at[d, t],
                ring.partner,
            ).start()

    project_block(0, True)

    def step(t, carry):
        for d in (0, 1):
            send(t, d, False).wait_recv()

        @pl.when(t < n - 1)
        def _():
            for d in (0, 1):
                send(t + 1, d, False).start()

        loads = []
        for d in (0, 1):
            chip, part = hop(t + 1, d)
            loads.append(pltpu.make_async_copy(gathered.at[chip, part], x_buf.at[part], local_sem.at[d]))
        for load in loads:
            load.start()
        for load in loads:
            load.wait()
        project_block(t, False)
        return carry

    lax.fori_loop(1, n, step, 0)

    def finish(t, carry):
        for d in (0, 1):
            send(t, d, False).wait_send()
        return carry

    lax.fori_loop(1, n, finish, 0)

    def finish_heads(t, carry):
        for d in (0, 1):
            done = remote(
                staged.at[t, :, half_rows(d, rows)],
                qkv.at[:, half_rows(d, rows)],
                q_send.at[d, t],
                q_recv.at[d, t],
                ring.partner,
            )
            done.wait_send()
            done.wait_recv()
        return carry

    lax.fori_loop(0, n, finish_heads, 0)
    keep.wait()


def gather_project(normed, weights, cosine, sine):
    rows, features = normed.shape
    r = weights.shape[0] // 5
    devices = lax.axis_size("dp")
    n = devices // 2
    vmem = pl.BlockSpec(memory_space=pltpu.VMEM)
    dma = pltpu.SemaphoreType.DMA
    return pl.pallas_call(
        gather_project_kernel,
        out_shape=(
            jax.ShapeDtypeStruct((3, devices * rows, r), LOW),
            jax.ShapeDtypeStruct((n, rows, features), LOW),
        ),
        in_specs=[vmem] * 4,
        out_specs=(vmem, pl.BlockSpec(memory_space=pl.ANY)),
        scratch_shapes=[
            pltpu.VMEM(weights.shape, LOW),
            pltpu.VMEM((rows, features), LOW),
            pltpu.VMEM((n, 3, rows, r), LOW),
            dma((2, n)), dma((2, n)), dma, dma, dma((2, n)), dma((2, n)), dma((3,)),
        ],
        compiler_params=pltpu.CompilerParams(
            collective_id=1, has_side_effects=True, vmem_limit_bytes=40 * MIB
        ),
        cost_estimate=pl.CostEstimate(
            flops=4 * n * rows * features * 5 * r, bytes_accessed=320 * MIB, transcendentals=0
        ),
        name="gather_project",
    )(normed, weights, cosine, sine)


def split_heads(u):
    heads = u.shape[1] // HEAD_DIM
    if heads == 1:
        return u
    lane = lax.broadcasted_iota(jnp.int32, u.shape, 1) // HEAD_DIM
    zero = jnp.zeros_like(u)
    return jnp.concatenate([jnp.where(lane == h, u, zero) for h in range(heads)], 0)


def join_heads(u):
    heads = u.shape[0] // HEAD_DIM
    return jnp.concatenate(
        [u[h * HEAD_DIM : (h + 1) * HEAD_DIM, h * BLOCK : (h + 1) * BLOCK] for h in range(heads)], 0
    )


def transpose_blocks(source, target):
    def one(b, carry):
        at = pl.multiple_of(b * BLOCK, BLOCK)
        target[:, pl.ds(at, BLOCK)] = source[pl.ds(at, BLOCK), :].astype(F32).T.astype(LOW)
        return carry

    lax.fori_loop(0, source.shape[0] // BLOCK, one, 0)


def window_of(b, first, tail, columns):
    start = pl.multiple_of(jnp.maximum(b - (CHUNK // BLOCK - 1), 0) * BLOCK, BLOCK)
    whole = (b - first) // (CHUNK // BLOCK)
    lowest = (first + whole * (CHUNK // BLOCK)) * BLOCK
    key_index = start + lax.broadcasted_iota(jnp.int32, (CHUNK, columns), 0)
    query_index = b * BLOCK + lax.broadcasted_iota(jnp.int32, (CHUNK, columns), 1) % BLOCK
    allowed = (
        (key_index >= lowest)
        & (key_index <= query_index)
        & (key_index < b * BLOCK + tail)
    )
    return start, whole, allowed


def attend_kernel(first_ref, tail_ref, qkv, attended, log_total, value_t):
    tokens, r = qkv.shape[1:]
    columns = (r // HEAD_DIM) * BLOCK
    scale = 1.0 / math.sqrt(HEAD_DIM)
    transpose_blocks(qkv.at[2], value_t)

    def block(b, carry):
        at = pl.multiple_of(b * BLOCK, BLOCK)
        query = split_heads(qkv[0, pl.ds(at, BLOCK), :])
        start, whole, allowed = window_of(b, first_ref[b], tail_ref[b], columns)
        scores = dot_nt(qkv[1, pl.ds(start, CHUNK), :], query) * scale
        scores = jnp.where(allowed, scores, MASKED_SCORE)
        top = jnp.max(scores, axis=0, keepdims=True)
        weights = jnp.exp(scores - top)
        total = jnp.sum(weights, axis=0, keepdims=True)
        out = dot_nn(value_t[:, pl.ds(start, CHUNK)], weights.astype(LOW))

        def more(i, state):
            top, total, out = state
            start = pl.multiple_of(first_ref[b] * BLOCK + i * CHUNK, BLOCK)
            scores = dot_nt(qkv[1, pl.ds(start, CHUNK), :], query) * scale
            higher = jnp.maximum(top, jnp.max(scores, axis=0, keepdims=True))
            shrink = jnp.exp(top - higher)
            weights = jnp.exp(scores - higher)
            total = total * shrink + jnp.sum(weights, axis=0, keepdims=True)
            out = out * shrink + dot_nn(value_t[:, pl.ds(start, CHUNK)], weights.astype(LOW))
            return higher, total, out

        top, total, out = lax.fori_loop(0, whole, more, (top, total, out))
        log_total[pl.ds(b, 1), :] = top + jnp.log(total)
        attended[pl.ds(at, BLOCK), :] = join_heads(out / total).T.astype(LOW)
        return carry

    lax.fori_loop(0, tokens // BLOCK, block, 0)


def attend(first, tail, qkv):
    tokens, r = qkv.shape[1:]
    smem = pl.BlockSpec(memory_space=pltpu.SMEM)
    vmem = pl.BlockSpec(memory_space=pltpu.VMEM)
    return pl.pallas_call(
        attend_kernel,
        out_shape=(
            jax.ShapeDtypeStruct((tokens, r), LOW),
            jax.ShapeDtypeStruct((tokens // BLOCK, (r // HEAD_DIM) * BLOCK), F32),
        ),
        in_specs=[smem, smem, vmem],
        out_specs=(vmem, vmem),
        scratch_shapes=[pltpu.VMEM((r, tokens), LOW)],
        compiler_params=pltpu.CompilerParams(vmem_limit_bytes=40 * MIB),
        cost_estimate=pl.CostEstimate(
            flops=4 * tokens * 1024 * r * 8, bytes_accessed=120 * MIB, transcendentals=tokens * 1024
        ),
        name="attend",
    )(first, tail, qkv)


def unrotate(g, cos, sin):
    parts = []
    for h in range(g.shape[0] // HEAD_DIM):
        one = g[h * HEAD_DIM : h * HEAD_DIM + HALF]
        two = g[h * HEAD_DIM + HALF : (h + 1) * HEAD_DIM]
        parts += [one * cos + two * sin, two * cos - one * sin]
    return jnp.concatenate(parts, 0)


def attend_back_kernel(
    first_ref, tail_ref, qkv, grad_out, attended, log_total, cos_t, sin_t, grads,
    key_t, grad_key, grad_value,
):
    tokens, r = qkv.shape[1:]
    heads = r // HEAD_DIM
    columns = heads * BLOCK
    scale = 1.0 / math.sqrt(HEAD_DIM)
    transpose_blocks(qkv.at[1], key_t)
    grad_key[...] = jnp.zeros_like(grad_key)
    grad_value[...] = jnp.zeros_like(grad_value)

    def block(b, carry):
        at = pl.multiple_of(b * BLOCK, BLOCK)
        here = pl.ds(at, BLOCK)
        query = split_heads(qkv[0, here, :])
        grad_rows = grad_out[here, :]
        grad = split_heads(grad_rows)
        product = (grad_rows.astype(F32) * attended[here, :].astype(F32)).T
        delta = jnp.concatenate(
            [
                jnp.sum(product[h * HEAD_DIM : (h + 1) * HEAD_DIM], axis=0, keepdims=True)
                for h in range(heads)
            ],
            1,
        )
        log_row = log_total[pl.ds(b, 1), :]

        def chunk(start, allowed, grad_query):
            span = pl.ds(start, CHUNK)
            scores = dot_nt(qkv[1, span, :], query) * scale
            weights = jnp.exp(scores - log_row)
            if allowed is not None:
                weights = jnp.where(allowed, weights, 0.0)
            grad_weights = dot_nt(qkv[2, span, :], grad)
            grad_scores = (weights * (grad_weights - delta)).astype(LOW)
            grad_value[span, :] += dot_nn(weights.astype(LOW), grad)
            grad_key[span, :] += dot_nn(grad_scores, query)
            return grad_query + dot_nn(key_t[:, span], grad_scores)

        start, whole, allowed = window_of(b, first_ref[b], tail_ref[b], columns)
        grad_query = chunk(start, allowed, jnp.zeros((r, columns), F32))
        grad_query = lax.fori_loop(
            0,
            whole,
            lambda i, g: chunk(pl.multiple_of(first_ref[b] * BLOCK + i * CHUNK, BLOCK), None, g),
            grad_query,
        )
        turned = unrotate(join_heads(grad_query) * scale, cos_t[:, here], sin_t[:, here])
        grads[0, here, :] = turned.T.astype(LOW)
        return carry

    lax.fori_loop(0, tokens // BLOCK, block, 0)

    def close(b, carry):
        here = pl.ds(pl.multiple_of(b * BLOCK, BLOCK), BLOCK)
        turned = unrotate(grad_key[here, :].T * scale, cos_t[:, here], sin_t[:, here])
        grads[1, here, :] = turned.T.astype(LOW)
        grads[2, here, :] = grad_value[here, :].astype(LOW)
        return carry

    lax.fori_loop(0, tokens // BLOCK, close, 0)


def attend_back(first, tail, qkv, grad_out, attended, log_total, cos_t, sin_t):
    tokens, r = qkv.shape[1:]
    smem = pl.BlockSpec(memory_space=pltpu.SMEM)
    vmem = pl.BlockSpec(memory_space=pltpu.VMEM)
    return pl.pallas_call(
        attend_back_kernel,
        out_shape=jax.ShapeDtypeStruct((3, tokens, r), LOW),
        in_specs=[smem, smem] + [vmem] * 6,
        out_specs=vmem,
        scratch_shapes=[
            pltpu.VMEM((r, tokens), LOW),
            pltpu.VMEM((tokens, r), F32),
            pltpu.VMEM((tokens, r), F32),
        ],
        compiler_params=pltpu.CompilerParams(vmem_limit_bytes=40 * MIB),
        cost_estimate=pl.CostEstimate(
            flops=10 * tokens * 1024 * r * 8, bytes_accessed=240 * MIB, transcendentals=tokens * 1024
        ),
        name="attend_back",
    )(first, tail, qkv, grad_out, attended, log_total, cos_t, sin_t)


def dense_kernel(
    normed, cotangents, gate_w, up_w, down_w, gate_p, up_p, down_p,
    out_sum, grad_sum, gathered, weight_grads,
    weights, totals, x_buf, g_buf, sent, landed, cast_buf,
    ag_send, ag_recv, rs_send, rs_recv, credit, local_sem, w_sem, cast_sem,
):
    ring = Ring()
    n = ring.chips
    rows, features = normed.shape
    half = rows // 2
    own = gate_w.shape[0]
    tiles = 2 * own // FF_TILE
    loads = []
    for i, (mine, theirs) in enumerate(((gate_w, gate_p), (up_w, up_p), (down_w, down_p))):
        loads.append(pltpu.make_async_copy(mine, weights.at[i, pl.ds(0, own)], w_sem.at[2 * i]))
        loads.append(pltpu.make_async_copy(theirs, weights.at[i, pl.ds(own, own)], w_sem.at[2 * i + 1]))
    for load in loads:
        load.start()
    ring.greet((ring.next[0], ring.next[1]))

    def hop(t, d):
        return ring.chip_far((1 - t) if d == 0 else (t - 1)), half_rows(d, rows)

    def send(t, d, first):
        chip, part = hop(t, d)
        src = normed.at[part] if first else gathered.at[chip, part]
        return remote(src, gathered.at[chip, part], ag_send.at[d, t - 1], ag_recv.at[d, t - 1], ring.next[d])

    def reduce_copy(t, d, k):
        return remote(
            sent.at[d, k], landed.at[d, k, t % 2], rs_send.at[d, k], rs_recv.at[d, k, t % 2], ring.next[d]
        )

    for d in (0, 1):
        send(1, d, True).start()

    def clear(i, carry):
        for k in range(3):
            totals[k, pl.ds(pl.multiple_of(i * FF_TILE, FF_TILE), FF_TILE), :] = jnp.zeros(
                (FF_TILE, features), F32
            )
        return carry

    lax.fori_loop(0, tiles, clear, 0)
    for load in loads:
        load.wait()

    def step(t, carry):
        @pl.when(t < n)
        def _():
            for d in (0, 1):
                send(t, d, False).wait_recv()

            @pl.when(t < n - 1)
            def _():
                for d in (0, 1):
                    send(t + 1, d, False).start()

        copies = []
        for d in (0, 1):
            chip, part = hop(t + 1, d)
            copies.append(pltpu.make_async_copy(cotangents.at[chip, part], g_buf.at[part], local_sem.at[d]))
            copies[-1].start()

        @pl.when(t < n)
        def _():
            more = []
            for d in (0, 1):
                chip, part = hop(t + 1, d)
                more.append(pltpu.make_async_copy(gathered.at[chip, part], x_buf.at[part], local_sem.at[2 + d]))
                more[-1].start()
            for copy in more:
                copy.wait()

        @pl.when(t == n)
        def _():
            x_buf[...] = normed[...]

        for copy in copies:
            copy.wait()

        out_sum[...] = jnp.zeros_like(out_sum)
        grad_sum[...] = jnp.zeros_like(grad_sum)

        def tile(i, carry):
            span = pl.ds(pl.multiple_of(i * FF_TILE, FF_TILE), FF_TILE)
            x = x_buf[...]
            g = g_buf[...]
            gate = dot_nt(x, weights[0, span, :])
            up = dot_nt(x, weights[1, span, :])
            grad_hidden = dot_nt(g, weights[2, span, :])
            sigma = 1.0 / (1.0 + jnp.exp(-gate))
            silu = gate * sigma
            hidden = (silu * up).astype(LOW)
            grad_gate = (grad_hidden * up * sigma * (1.0 + gate * (1.0 - sigma))).astype(LOW)
            grad_up = (grad_hidden * silu).astype(LOW)
            out_sum[...] += dot_nn(hidden, weights[2, span, :])
            grad_sum[...] += dot_nn(grad_gate, weights[0, span, :])
            grad_sum[...] += dot_nn(grad_up, weights[1, span, :])
            totals[0, span, :] += dot_tn(grad_gate, x)
            totals[1, span, :] += dot_tn(grad_up, x)
            totals[2, span, :] += dot_tn(hidden, g)
            return carry

        lax.fori_loop(0, tiles, tile, 0)
        for d in (0, 1):
            for k, total in enumerate((out_sum, grad_sum)):
                part = pl.ds(d * half, half)

                @pl.when(t >= 2)
                def _():
                    reduce_copy(t - 1, d, k).wait_recv()
                    total[part, :] += landed[d, k, (t - 1) % 2].astype(F32)

                    @pl.when(t <= n - 2)
                    def _():
                        pl.semaphore_signal(
                            credit.at[d, k], inc=1, device_id={"dp": ring.back[d]}, device_id_type=MESH
                        )

                    reduce_copy(t - 1, d, k).wait_send()

                @pl.when(t < n)
                def _():
                    sent[d, k] = total[part, :].astype(LOW)

                    @pl.when(t >= 3)
                    def _():
                        pl.semaphore_wait(credit.at[d, k], 1)

                    reduce_copy(t, d, k).start()

        return carry

    lax.fori_loop(1, n + 1, step, 0)

    def cast_copy(i):
        return pltpu.make_async_copy(
            cast_buf.at[i % 2],
            weight_grads.at[i // tiles, pl.ds(pl.multiple_of((i % tiles) * FF_TILE, FF_TILE), FF_TILE)],
            cast_sem.at[i % 2],
        )

    def store(i, carry):
        @pl.when(i >= 2)
        def _():
            cast_copy(i - 2).wait()

        span = pl.ds(pl.multiple_of((i % tiles) * FF_TILE, FF_TILE), FF_TILE)
        cast_buf[i % 2] = totals[i // tiles, span, :].astype(LOW)
        cast_copy(i).start()
        return carry

    lax.fori_loop(0, 3 * tiles, store, 0)
    cast_copy(3 * tiles - 2).wait()
    cast_copy(3 * tiles - 1).wait()

    def finish(t, carry):
        for d in (0, 1):
            send(t, d, False).wait_send()
        return carry

    lax.fori_loop(1, n, finish, 0)


def dense(normed, cotangents, own_weights, partner_weights):
    rows, features = normed.shape
    n = lax.axis_size("dp") // 2
    own = own_weights[0].shape[0]
    half = rows // 2
    vmem = pl.BlockSpec(memory_space=pltpu.VMEM)
    hbm = pl.BlockSpec(memory_space=pl.ANY)
    dma = pltpu.SemaphoreType.DMA
    return pl.pallas_call(
        dense_kernel,
        out_shape=(
            jax.ShapeDtypeStruct((rows, features), F32),
            jax.ShapeDtypeStruct((rows, features), F32),
            jax.ShapeDtypeStruct((n, rows, features), LOW),
            jax.ShapeDtypeStruct((3, 2 * own, features), LOW),
        ),
        in_specs=[vmem] + [hbm] * 7,
        out_specs=(vmem, vmem, hbm, hbm),
        scratch_shapes=[
            pltpu.VMEM((3, 2 * own, features), LOW),
            pltpu.VMEM((3, 2 * own, features), F32),
            pltpu.VMEM((rows, features), LOW),
            pltpu.VMEM((rows, features), LOW),
            pltpu.VMEM((2, 2, half, features), LOW),
            pltpu.VMEM((2, 2, 2, half, features), LOW),
            pltpu.VMEM((2, FF_TILE, features), LOW),
            dma((2, n)), dma((2, n)), dma((2, 2)), dma((2, 2, 2)),
            pltpu.SemaphoreType.REGULAR((2, 2)),
            dma((4,)), dma((6,)), dma((2,)),
        ],
        compiler_params=pltpu.CompilerParams(
            collective_id=2, has_side_effects=True, vmem_limit_bytes=62 * MIB
        ),
        cost_estimate=pl.CostEstimate(
            flops=2 * 9 * n * rows * features * 2 * own, bytes_accessed=800 * MIB, transcendentals=0
        ),
        name="dense",
    )(normed, cotangents, *own_weights, *partner_weights)


def normed_back_kernel(
    grads, weights, partner_weights, out,
    partner_grads, sent, landed,
    p_send, p_recv, rs_send, rs_recv, credit,
):
    ring = Ring()
    n = ring.chips
    rows, features = out.shape
    half = rows // 2
    r = grads.shape[2]
    ring.greet((ring.next[0], ring.next[1], ring.partner))

    def place(t, d):
        return ring.chip_far(-t if d == 0 else t)

    def swap(t, d):
        start = (place(t, d) * 2 + 1 - ring.core) * rows + d * half
        return remote(
            grads.at[:, pl.ds(pl.multiple_of(start, half), half)],
            partner_grads.at[:, t % n, half_rows(d, rows)],
            p_send.at[d, t % n],
            p_recv.at[d, t % n],
            ring.partner,
        )

    def begin(t, carry):
        for d in (0, 1):
            swap(t, d).start()
        return carry

    lax.fori_loop(1, n + 1, begin, 0)

    def reduce_copy(t, d):
        return remote(sent.at[d], landed.at[d, t % 2], rs_send.at[d], rs_recv.at[d, t % 2], ring.next[d])

    def step(t, carry):
        for d in (0, 1):
            start = (place(t, d) * 2 + ring.core) * rows + d * half
            mine = pl.ds(pl.multiple_of(start, half), half)
            part = pl.ds(d * half, half)
            swap(t, d).wait_recv()
            total = dot_nn(grads[0, mine, :], weights[0])
            for i in (1, 2):
                total += dot_nn(grads[i, mine, :], weights[i])
            for i in range(3):
                total += dot_nn(partner_grads[i, t % n, part, :], partner_weights[i])
            out[part, :] = total

        for d in (0, 1):
            part = pl.ds(d * half, half)

            @pl.when(t >= 2)
            def _():
                reduce_copy(t - 1, d).wait_recv()
                out[part, :] += landed[d, (t - 1) % 2].astype(F32)

                @pl.when(t <= n - 2)
                def _():
                    pl.semaphore_signal(
                        credit.at[d], inc=1, device_id={"dp": ring.back[d]}, device_id_type=MESH
                    )

                reduce_copy(t - 1, d).wait_send()

            @pl.when(t < n)
            def _():
                sent[d] = out[part, :].astype(LOW)

                @pl.when(t >= 3)
                def _():
                    pl.semaphore_wait(credit.at[d], 1)

                reduce_copy(t, d).start()

        return carry

    lax.fori_loop(1, n + 1, step, 0)

    def finish(t, carry):
        for d in (0, 1):
            swap(t, d).wait_send()
        return carry

    lax.fori_loop(1, n + 1, finish, 0)


def normed_back(grads, weights, partner_weights):
    tokens, r = grads.shape[1:]
    features = weights.shape[2]
    devices = lax.axis_size("dp")
    n = devices // 2
    rows = tokens // devices
    half = rows // 2
    vmem = pl.BlockSpec(memory_space=pltpu.VMEM)
    dma = pltpu.SemaphoreType.DMA
    return pl.pallas_call(
        normed_back_kernel,
        out_shape=jax.ShapeDtypeStruct((rows, features), F32),
        in_specs=[vmem] * 3,
        out_specs=vmem,
        scratch_shapes=[
            pltpu.VMEM((3, n, rows, r), LOW),
            pltpu.VMEM((2, half, features), LOW),
            pltpu.VMEM((2, 2, half, features), LOW),
            dma((2, n)), dma((2, n)), dma((2,)), dma((2, 2)),
            pltpu.SemaphoreType.REGULAR((2,)),
        ],
        compiler_params=pltpu.CompilerParams(
            collective_id=3, has_side_effects=True, vmem_limit_bytes=40 * MIB
        ),
        cost_estimate=pl.CostEstimate(
            flops=2 * n * rows * features * 6 * r, bytes_accessed=320 * MIB, transcendentals=0
        ),
        name="normed_back",
    )(grads, weights, partner_weights)


def rms(values, norm_gain):
    return (
        values * lax.rsqrt(jnp.mean(values * values, axis=-1, keepdims=True) + EPSILON) * norm_gain
    )


def rms_back(values, norm_gain, grads):
    _, pullback = jax.vjp(rms, values, norm_gain)
    return pullback(grads)


def turned_rows(weight):
    parts = weight.reshape(-1, 2, HALF, weight.shape[1])
    return jnp.concatenate([-parts[:, 1:], parts[:, :1]], 1).reshape(weight.shape)


def from_partner(value):
    devices = lax.axis_size("dp")
    return lax.ppermute(value, "dp", [(i, i ^ 1) for i in range(devices)])


def pack_sum(value):
    low = value.astype(LOW)
    if lax.axis_size("rep") == 2:
        other = lax.ppermute(low, "rep", [(0, 1), (1, 0)])
        return low.astype(F32) + other.astype(F32)
    return lax.psum(low, "rep").astype(F32)


def body(
    tokens,
    attention_gain,
    query_weight,
    key_weight,
    value_weight,
    output_weight,
    dense_gain,
    gate_weight,
    up_weight,
    down_weight,
    block_document,
    document_tail,
    cotangent,
):
    devices = lax.axis_size("dp")
    chips = devices // 2
    core = lax.axis_index("dp") % 2
    hidden_in = tokens[0].astype(F32)
    tok_dev = hidden_in.shape[0]
    pack_tok = tok_dev * devices

    documents, tails = block_document[0], document_tail[0]
    first = jnp.sum((documents[None, :] < documents[:, None]).astype(jnp.int32), axis=1)
    last = jnp.concatenate([documents[1:] != documents[:-1], jnp.ones((1,), bool)])
    doc_ids = jnp.arange(tails.shape[0], dtype=jnp.int32)
    own_tail = jnp.sum((documents[:, None] == doc_ids[None, :]) * tails[None, :], axis=1)
    tail = jnp.where(last, own_tail, BLOCK).astype(jnp.int32)
    block_index = jnp.arange(documents.shape[0], dtype=jnp.int32)
    inside = jnp.arange(BLOCK, dtype=jnp.int32)
    position = ((block_index - first)[:, None] * BLOCK + inside[None, :]).reshape(-1)
    frequency = ROPE_BASE ** (-(jnp.arange(HALF, dtype=F32) * (2.0 / HEAD_DIM)))
    angles = position.astype(F32)[None, :] * frequency[:, None]
    cos_t, sin_t = jnp.cos(angles), jnp.sin(angles)
    r = query_weight.shape[0]

    def rows_of(table):
        mine = lax.dynamic_index_in_dim(
            table.reshape(HALF, chips, 2, tok_dev), core, axis=2, keepdims=False
        )
        return jnp.tile(mine.transpose(1, 2, 0), (1, 1, r // HALF))

    normed = rms(hidden_in, attention_gain).astype(LOW)
    stacked = jnp.concatenate(
        [
            query_weight,
            turned_rows(query_weight),
            key_weight,
            turned_rows(key_weight),
            value_weight,
        ],
        0,
    )
    qkv, normed_all = gather_project(normed, stacked, rows_of(cos_t), rows_of(sin_t))

    full_output = lax.all_gather(output_weight, "dp", axis=0, tiled=True)
    groups = [list(range(c, devices, 2)) for c in (0, 1)]
    grad_low = cotangent[0]
    cotangents = lax.all_gather(
        grad_low, "dp", axis=0, tiled=True, axis_index_groups=groups
    ).reshape(chips, tok_dev, -1)
    gate_other, up_other, down_other = (
        from_partner(gate_weight),
        from_partner(up_weight),
        from_partner(down_weight),
    )
    qkv_weight = jnp.stack([query_weight, key_weight, value_weight])
    qkv_other = from_partner(qkv_weight)

    attended, log_total = attend(first, tail, qkv)
    attended_here = lax.all_to_all(attended, "dp", split_axis=0, concat_axis=1, tiled=True)
    mixed = hidden_in + dot_nn(attended_here, full_output)
    normed_two = rms(mixed, dense_gain).astype(LOW)

    out_sum, grad_normed_two, _, dense_grads = dense(
        normed_two,
        cotangents,
        (gate_weight, up_weight, down_weight),
        (gate_other, up_other, down_other),
    )
    layer_out = mixed + out_sum
    own_rows = gate_weight.shape[0]
    dense_low = (
        dense_grads[:, :own_rows].astype(F32)
        + from_partner(dense_grads[:, own_rows:]).astype(F32)
    ).astype(LOW)
    dense_total = pack_sum(dense_low)

    grad_mixed_norm, dense_gain_part = rms_back(mixed, dense_gain, grad_normed_two)
    grad_mixed = grad_low.astype(F32) + grad_mixed_norm
    grad_mixed_low = grad_mixed.astype(LOW)
    grad_attended = dot_nt(grad_mixed_low, full_output).astype(LOW)
    grad_heads = lax.all_to_all(grad_attended, "dp", split_axis=1, concat_axis=0, tiled=True)
    output_grad = lax.psum_scatter(
        dot_tn(attended_here, grad_mixed_low).astype(LOW), "dp", scatter_dimension=0, tiled=True
    )
    output_total = pack_sum(output_grad)

    grads = attend_back(first, tail, qkv, grad_heads, attended, log_total, cos_t, sin_t)
    swapped = from_partner(
        lax.dynamic_index_in_dim(
            grads.reshape(3, chips, 2, tok_dev, r), 1 - core, axis=2, keepdims=False
        )
    )
    mine = lax.dynamic_index_in_dim(
        grads.reshape(3, chips, 2, tok_dev, r), core, axis=2, keepdims=False
    )
    both = jnp.stack([mine, swapped]).reshape(2, 3, chips * tok_dev, r)
    normed_rows = normed_all.reshape(chips * tok_dev, -1)
    qkv_parts = lax.dot_general(
        both, normed_rows, (((2,), (0,)), ((), ())), preferred_element_type=F32
    ).astype(LOW)
    qkv_low = (qkv_parts[0].astype(F32) + from_partner(qkv_parts[1]).astype(F32)).astype(LOW)
    qkv_total = pack_sum(qkv_low)

    grad_normed = normed_back(grads, qkv_weight, qkv_other)
    grad_in_norm, attention_gain_part = rms_back(hidden_in, attention_gain, grad_normed)
    input_grad = grad_mixed + grad_in_norm
    gain_totals = lax.psum((attention_gain_part, dense_gain_part), ("dp", "rep"))
    return (
        layer_out[None].astype(LOW),
        input_grad[None],
        gain_totals[0],
        qkv_total[0],
        qkv_total[1],
        qkv_total[2],
        output_total,
        gain_totals[1],
        dense_total[0],
        dense_total[1],
        dense_total[2],
    )


def solution(mesh):
    return jax.shard_map(
        body,
        mesh=mesh,
        in_specs=(
            P("rep", "dp", None),
            P(),
            P("dp", None),
            P("dp", None),
            P("dp", None),
            P("dp", None),
            P(),
            P("dp", None),
            P("dp", None),
            P("dp", None),
            P("rep", None),
            P("rep", None),
            P("rep", "dp", None),
        ),
        out_specs=(
            P("rep", "dp", None),
            P("rep", "dp", None),
            P(),
            P("dp", None),
            P("dp", None),
            P("dp", None),
            P("dp", None),
            P(),
            P("dp", None),
            P("dp", None),
            P("dp", None),
        ),
        check_vma=False,
    )
```

```python
import functools
import math

import jax
import jax.numpy as jnp
from jax import lax
from jax.experimental import pallas as pl
from jax.experimental.pallas import tpu as pltpu
from jax.sharding import PartitionSpec as P

HEAD_DIM = 64
HALF = HEAD_DIM // 2
BLOCK = 128
CHUNK = 512
FF_TILE = 256
EPSILON = 1e-05
ROPE_BASE = 130000.0
MASKED_SCORE = -1e30
MESH = pl.DeviceIdType.MESH
MIB = 2**20
LOW = jnp.bfloat16
F32 = jnp.float32


def dot_nn(a, b):
    return lax.dot_general(a, b, (((1,), (0,)), ((), ())), preferred_element_type=F32)


def dot_nt(a, b):
    return lax.dot_general(a, b, (((1,), (1,)), ((), ())), preferred_element_type=F32)


def dot_tn(a, b):
    return lax.dot_general(a, b, (((0,), (0,)), ((), ())), preferred_element_type=F32)


def grid_of(chips):
    depth = 4 if chips % 8 == 0 else 2
    return depth, chips // depth


def chip_at(place, chips):
    depth, width = grid_of(chips)
    place = lax.rem(place + chips, chips)
    later = place - depth
    row, column = later // (width - 1), later % (width - 1)
    odd = row % 2
    far = (depth - 1 - row) * width + 1 + column + odd * (width - 2 - 2 * column)
    return jnp.where(place < depth, place * width, far)


def place_of(chip, chips):
    depth, width = grid_of(chips)
    z, x = chip // width, chip % width
    row = depth - 1 - z
    odd = row % 2
    column = x - 1 + odd * (width - 2 * x)
    return jnp.where(x == 0, z, depth + row * (width - 1) + column)


def ring_order(chips):
    depth, width = grid_of(chips)
    order = [z * width for z in range(depth)]
    for row in range(depth):
        columns = list(range(1, width))
        order += [(depth - 1 - row) * width + x for x in (columns[::-1] if row % 2 else columns)]
    return order


class Ring:
    def __init__(self):
        self.chips = lax.axis_size("dp") // 2
        me = lax.axis_index("dp")
        self.core = me % 2
        self.chip = me // 2
        self.partner = self.chip * 2 + 1 - self.core
        self.place = place_of(self.chip, self.chips)
        self.next = (self.device(1), self.device(-1))
        self.back = (self.next[1], self.next[0])

    def chip_far(self, steps):
        return chip_at(self.place + steps, self.chips)

    def device(self, steps):
        return self.chip_far(steps) * 2 + self.core

    def greet(self, others):
        barrier = pltpu.get_barrier_semaphore()
        for other in others:
            pl.semaphore_signal(barrier, inc=1, device_id={"dp": other}, device_id_type=MESH)
        pl.semaphore_wait(barrier, len(others))


def remote(src, dst, send_sem, recv_sem, device):
    return pltpu.make_async_remote_copy(
        src_ref=src,
        dst_ref=dst,
        send_sem=send_sem,
        recv_sem=recv_sem,
        device_id={"dp": device},
        device_id_type=MESH,
    )


def half_rows(direction, rows):
    return pl.ds(direction * (rows // 2), rows // 2)


def gather_project_kernel(
    normed, weights, cosine, sine, qkv, gathered,
    partner_weights, x_buf, staged,
    ag_send, ag_recv, w_send, w_recv, q_send, q_recv, local_sem,
):
    ring = Ring()
    n = ring.chips
    rows = normed.shape[0]
    r = qkv.shape[2]
    ring.greet((ring.next[0], ring.next[1], ring.partner))
    swap = remote(weights, partner_weights, w_send, w_recv, ring.partner)
    swap.start()
    keep = pltpu.make_async_copy(normed, gathered.at[ring.chip], local_sem.at[2])
    keep.start()

    def hop(t, d):
        chip = ring.chip_far((1 - t) if d == 0 else (t - 1))
        return chip, half_rows(d, rows)

    def send(t, d, first):
        chip, part = hop(t, d)
        src = normed.at[part] if first else gathered.at[chip, part]
        return remote(src, gathered.at[chip, part], ag_send.at[d, t - 1], ag_recv.at[d, t - 1], ring.next[d])

    for d in (0, 1):
        send(1, d, True).start()

    def project_block(t, from_input):
        x = normed[...] if from_input else x_buf[...]
        places = [ring.chip_far(-t), ring.chip_far(t)]
        cos = jnp.concatenate([cosine[places[d], half_rows(d, rows), :] for d in (0, 1)], 0)
        sin = jnp.concatenate([sine[places[d], half_rows(d, rows), :] for d in (0, 1)], 0)

        def heads(w):
            part = [dot_nt(x, w[i * r : (i + 1) * r, :]) for i in range(5)]
            return (
                (part[0] * cos + part[1] * sin).astype(LOW),
                (part[2] * cos + part[3] * sin).astype(LOW),
                part[4].astype(LOW),
            )

        starts = [
            pl.multiple_of((places[d] * 2 + ring.core) * rows + d * (rows // 2), rows // 2)
            for d in (0, 1)
        ]
        for i, value in enumerate(heads(weights)):
            for d in (0, 1):
                qkv[i, pl.ds(starts[d], rows // 2), :] = value[d * (rows // 2) : (d + 1) * (rows // 2)]
        if from_input:
            swap.wait()
        for i, value in enumerate(heads(partner_weights)):
            staged[t, i] = value
        for d in (0, 1):
            remote(
                staged.at[t, :, half_rows(d, rows)],
                qkv.at[:, pl.ds(starts[d], rows // 2)],
                q_send.at[d, t],
                q_recv.at[d, t],
                ring.partner,
            ).start()

    project_block(0, True)

    def step(t, carry):
        for d in (0, 1):
            send(t, d, False).wait_recv()

        @pl.when(t < n - 1)
        def _():
            for d in (0, 1):
                send(t + 1, d, False).start()

        loads = []
        for d in (0, 1):
            chip, part = hop(t + 1, d)
            loads.append(pltpu.make_async_copy(gathered.at[chip, part], x_buf.at[part], local_sem.at[d]))
        for load in loads:
            load.start()
        for load in loads:
            load.wait()
        project_block(t, False)
        return carry

    lax.fori_loop(1, n, step, 0)

    def finish(t, carry):
        for d in (0, 1):
            send(t, d, False).wait_send()
        return carry

    lax.fori_loop(1, n, finish, 0)

    def finish_heads(t, carry):
        for d in (0, 1):
            done = remote(
                staged.at[t, :, half_rows(d, rows)],
                qkv.at[:, half_rows(d, rows)],
                q_send.at[d, t],
                q_recv.at[d, t],
                ring.partner,
            )
            done.wait_send()
            done.wait_recv()
        return carry

    lax.fori_loop(0, n, finish_heads, 0)
    keep.wait()


def gather_project(normed, weights, cosine, sine):
    rows, features = normed.shape
    r = weights.shape[0] // 5
    devices = lax.axis_size("dp")
    n = devices // 2
    vmem = pl.BlockSpec(memory_space=pltpu.VMEM)
    dma = pltpu.SemaphoreType.DMA
    return pl.pallas_call(
        gather_project_kernel,
        out_shape=(
            jax.ShapeDtypeStruct((3, devices * rows, r), LOW),
            jax.ShapeDtypeStruct((n, rows, features), LOW),
        ),
        in_specs=[vmem] * 4,
        out_specs=(vmem, pl.BlockSpec(memory_space=pl.ANY)),
        scratch_shapes=[
            pltpu.VMEM(weights.shape, LOW),
            pltpu.VMEM((rows, features), LOW),
            pltpu.VMEM((n, 3, rows, r), LOW),
            dma((2, n)), dma((2, n)), dma, dma, dma((2, n)), dma((2, n)), dma((3,)),
        ],
        compiler_params=pltpu.CompilerParams(
            collective_id=1, has_side_effects=True, vmem_limit_bytes=40 * MIB
        ),
        cost_estimate=pl.CostEstimate(
            flops=4 * n * rows * features * 5 * r, bytes_accessed=320 * MIB, transcendentals=0
        ),
        name="gather_project",
    )(normed, weights, cosine, sine)


def split_heads(u):
    heads = u.shape[1] // HEAD_DIM
    if heads == 1:
        return u
    lane = lax.broadcasted_iota(jnp.int32, u.shape, 1) // HEAD_DIM
    zero = jnp.zeros_like(u)
    return jnp.concatenate([jnp.where(lane == h, u, zero) for h in range(heads)], 0)


def join_heads(u):
    heads = u.shape[0] // HEAD_DIM
    return jnp.concatenate(
        [u[h * HEAD_DIM : (h + 1) * HEAD_DIM, h * BLOCK : (h + 1) * BLOCK] for h in range(heads)], 0
    )


def transpose_blocks(source, target):
    def one(b, carry):
        at = pl.multiple_of(b * BLOCK, BLOCK)
        target[:, pl.ds(at, BLOCK)] = source[pl.ds(at, BLOCK), :].astype(F32).T.astype(LOW)
        return carry

    lax.fori_loop(0, source.shape[0] // BLOCK, one, 0)


def window_of(b, first, tail, columns):
    start = pl.multiple_of(jnp.maximum(b - (CHUNK // BLOCK - 1), 0) * BLOCK, BLOCK)
    whole = (b - first) // (CHUNK // BLOCK)
    lowest = (first + whole * (CHUNK // BLOCK)) * BLOCK
    key_index = start + lax.broadcasted_iota(jnp.int32, (CHUNK, columns), 0)
    query_index = b * BLOCK + lax.broadcasted_iota(jnp.int32, (CHUNK, columns), 1) % BLOCK
    allowed = (
        (key_index >= lowest)
        & (key_index <= query_index)
        & (key_index < b * BLOCK + tail)
    )
    return start, whole, allowed


def attend_kernel(first_ref, tail_ref, qkv, attended, log_total, value_t):
    tokens, r = qkv.shape[1:]
    columns = (r // HEAD_DIM) * BLOCK
    scale = 1.0 / math.sqrt(HEAD_DIM)
    transpose_blocks(qkv.at[2], value_t)

    def block(b, carry):
        at = pl.multiple_of(b * BLOCK, BLOCK)
        query = split_heads(qkv[0, pl.ds(at, BLOCK), :])
        start, whole, allowed = window_of(b, first_ref[b], tail_ref[b], columns)
        scores = dot_nt(qkv[1, pl.ds(start, CHUNK), :], query) * scale
        scores = jnp.where(allowed, scores, MASKED_SCORE)
        top = jnp.max(scores, axis=0, keepdims=True)
        weights = jnp.exp(scores - top)
        total = jnp.sum(weights, axis=0, keepdims=True)
        out = dot_nn(value_t[:, pl.ds(start, CHUNK)], weights.astype(LOW))

        def more(i, state):
            top, total, out = state
            start = pl.multiple_of(first_ref[b] * BLOCK + i * CHUNK, BLOCK)
            scores = dot_nt(qkv[1, pl.ds(start, CHUNK), :], query) * scale
            higher = jnp.maximum(top, jnp.max(scores, axis=0, keepdims=True))
            shrink = jnp.exp(top - higher)
            weights = jnp.exp(scores - higher)
            total = total * shrink + jnp.sum(weights, axis=0, keepdims=True)
            out = out * shrink + dot_nn(value_t[:, pl.ds(start, CHUNK)], weights.astype(LOW))
            return higher, total, out

        top, total, out = lax.fori_loop(0, whole, more, (top, total, out))
        log_total[pl.ds(b, 1), :] = top + jnp.log(total)
        attended[pl.ds(at, BLOCK), :] = join_heads(out / total).T.astype(LOW)
        return carry

    lax.fori_loop(0, tokens // BLOCK, block, 0)


def attend(first, tail, qkv):
    tokens, r = qkv.shape[1:]
    smem = pl.BlockSpec(memory_space=pltpu.SMEM)
    vmem = pl.BlockSpec(memory_space=pltpu.VMEM)
    return pl.pallas_call(
        attend_kernel,
        out_shape=(
            jax.ShapeDtypeStruct((tokens, r), LOW),
            jax.ShapeDtypeStruct((tokens // BLOCK, (r // HEAD_DIM) * BLOCK), F32),
        ),
        in_specs=[smem, smem, vmem],
        out_specs=(vmem, vmem),
        scratch_shapes=[pltpu.VMEM((r, tokens), LOW)],
        compiler_params=pltpu.CompilerParams(vmem_limit_bytes=40 * MIB),
        cost_estimate=pl.CostEstimate(
            flops=4 * tokens * 1024 * r * 8, bytes_accessed=120 * MIB, transcendentals=tokens * 1024
        ),
        name="attend",
    )(first, tail, qkv)


def unrotate(g, cos, sin):
    parts = []
    for h in range(g.shape[0] // HEAD_DIM):
        one = g[h * HEAD_DIM : h * HEAD_DIM + HALF]
        two = g[h * HEAD_DIM + HALF : (h + 1) * HEAD_DIM]
        parts += [one * cos + two * sin, two * cos - one * sin]
    return jnp.concatenate(parts, 0)


def attend_back_kernel(
    first_ref, tail_ref, qkv, grad_out, attended, log_total, cos_t, sin_t, grads,
    key_t, grad_key, grad_value,
):
    tokens, r = qkv.shape[1:]
    heads = r // HEAD_DIM
    columns = heads * BLOCK
    scale = 1.0 / math.sqrt(HEAD_DIM)
    transpose_blocks(qkv.at[1], key_t)
    grad_key[...] = jnp.zeros_like(grad_key)
    grad_value[...] = jnp.zeros_like(grad_value)

    def block(b, carry):
        at = pl.multiple_of(b * BLOCK, BLOCK)
        here = pl.ds(at, BLOCK)
        query = split_heads(qkv[0, here, :])
        grad_rows = grad_out[here, :]
        grad = split_heads(grad_rows)
        product = (grad_rows.astype(F32) * attended[here, :].astype(F32)).T
        delta = jnp.concatenate(
            [
                jnp.sum(product[h * HEAD_DIM : (h + 1) * HEAD_DIM], axis=0, keepdims=True)
                for h in range(heads)
            ],
            1,
        )
        log_row = log_total[pl.ds(b, 1), :]

        def chunk(start, allowed, grad_query):
            span = pl.ds(start, CHUNK)
            scores = dot_nt(qkv[1, span, :], query) * scale
            weights = jnp.exp(scores - log_row)
            if allowed is not None:
                weights = jnp.where(allowed, weights, 0.0)
            grad_weights = dot_nt(qkv[2, span, :], grad)
            grad_scores = (weights * (grad_weights - delta)).astype(LOW)
            grad_value[span, :] += dot_nn(weights.astype(LOW), grad)
            grad_key[span, :] += dot_nn(grad_scores, query)
            return grad_query + dot_nn(key_t[:, span], grad_scores)

        start, whole, allowed = window_of(b, first_ref[b], tail_ref[b], columns)
        grad_query = chunk(start, allowed, jnp.zeros((r, columns), F32))
        grad_query = lax.fori_loop(
            0,
            whole,
            lambda i, g: chunk(pl.multiple_of(first_ref[b] * BLOCK + i * CHUNK, BLOCK), None, g),
            grad_query,
        )
        turned = unrotate(join_heads(grad_query) * scale, cos_t[:, here], sin_t[:, here])
        grads[0, here, :] = turned.T.astype(LOW)
        return carry

    lax.fori_loop(0, tokens // BLOCK, block, 0)

    def close(b, carry):
        here = pl.ds(pl.multiple_of(b * BLOCK, BLOCK), BLOCK)
        turned = unrotate(grad_key[here, :].T * scale, cos_t[:, here], sin_t[:, here])
        grads[1, here, :] = turned.T.astype(LOW)
        grads[2, here, :] = grad_value[here, :].astype(LOW)
        return carry

    lax.fori_loop(0, tokens // BLOCK, close, 0)


def attend_back(first, tail, qkv, grad_out, attended, log_total, cos_t, sin_t):
    tokens, r = qkv.shape[1:]
    smem = pl.BlockSpec(memory_space=pltpu.SMEM)
    vmem = pl.BlockSpec(memory_space=pltpu.VMEM)
    return pl.pallas_call(
        attend_back_kernel,
        out_shape=jax.ShapeDtypeStruct((3, tokens, r), LOW),
        in_specs=[smem, smem] + [vmem] * 6,
        out_specs=vmem,
        scratch_shapes=[
            pltpu.VMEM((r, tokens), LOW),
            pltpu.VMEM((tokens, r), F32),
            pltpu.VMEM((tokens, r), F32),
        ],
        compiler_params=pltpu.CompilerParams(vmem_limit_bytes=40 * MIB),
        cost_estimate=pl.CostEstimate(
            flops=10 * tokens * 1024 * r * 8, bytes_accessed=240 * MIB, transcendentals=tokens * 1024
        ),
        name="attend_back",
    )(first, tail, qkv, grad_out, attended, log_total, cos_t, sin_t)


def dense_kernel(
    normed, cotangents, gate_w, up_w, down_w, gate_p, up_p, down_p,
    grad_sum, out_parts, gathered, weight_grads,
    weights, totals, x_buf, g_buf, out_acc, grad_acc, sent, landed, cast_buf, pair_land,
    ag_send, ag_recv, rs_send, rs_recv, credit, local_sem, w_sem, cast_sem, pair_send, pair_recv,
):
    ring = Ring()
    n = ring.chips
    rows, features = normed.shape
    half = rows // 2
    own = gate_w.shape[0]
    tiles = 2 * own // FF_TILE
    loads = []
    for i, (mine, theirs) in enumerate(((gate_w, gate_p), (up_w, up_p), (down_w, down_p))):
        loads.append(pltpu.make_async_copy(mine, weights.at[i, pl.ds(0, own)], w_sem.at[2 * i]))
        loads.append(pltpu.make_async_copy(theirs, weights.at[i, pl.ds(own, own)], w_sem.at[2 * i + 1]))
    for load in loads:
        load.start()
    ring.greet((ring.next[0], ring.next[1], ring.partner))

    def source(t, d):
        return lax.rem(ring.place + (n - t if d == 0 else t), n)

    def send(t, d, first):
        place, part = source(t - 1, d), half_rows(d, rows)
        src = normed.at[part] if first else gathered.at[place, part]
        return remote(src, gathered.at[place, part], ag_send.at[d, t - 1], ag_recv.at[d, t - 1], ring.next[d])

    def reduce_copy(t, d):
        return remote(sent.at[d], landed.at[d, t % 2], rs_send.at[d], rs_recv.at[d, t % 2], ring.next[d])

    for d in (0, 1):
        send(1, d, True).start()

    def clear(i, carry):
        span = pl.ds(pl.multiple_of(i * FF_TILE, FF_TILE), FF_TILE)
        for k in range(3):
            totals[k, span, :] = jnp.zeros((FF_TILE, features), F32)
        return carry

    lax.fori_loop(0, tiles, clear, 0)
    for load in loads:
        load.wait()

    def out_copy(t, d):
        part = half_rows(d, rows)
        return pltpu.make_async_copy(
            cast_buf.at[t % 2, part], out_parts.at[source(t, d), part], cast_sem.at[t % 2, d]
        )

    def step(t, carry):
        copies = []
        for d in (0, 1):
            part = half_rows(d, rows)
            copies.append(
                pltpu.make_async_copy(cotangents.at[source(t, d), part], g_buf.at[part], local_sem.at[d])
            )
            copies[-1].start()

        @pl.when(t > 0)
        def _():
            for d in (0, 1):
                send(t, d, False).wait_recv()

            @pl.when(t < n - 1)
            def _():
                for d in (0, 1):
                    send(t + 1, d, False).start()

            more = []
            for d in (0, 1):
                part = half_rows(d, rows)
                more.append(
                    pltpu.make_async_copy(gathered.at[source(t, d), part], x_buf.at[part], local_sem.at[2 + d])
                )
                more[-1].start()
            for copy in more:
                copy.wait()

        @pl.when(t == 0)
        def _():
            x_buf[...] = normed[...]

        for copy in copies:
            copy.wait()

        out_acc[...] = jnp.zeros_like(out_acc)
        grad_acc[...] = jnp.zeros_like(grad_acc)

        def tile(i, carry):
            span = pl.ds(pl.multiple_of(i * FF_TILE, FF_TILE), FF_TILE)
            x = x_buf[...]
            g = g_buf[...]
            gate = dot_nt(x, weights[0, span, :])
            up = dot_nt(x, weights[1, span, :])
            grad_hidden = dot_nt(g, weights[2, span, :])
            sigma = 1.0 / (1.0 + jnp.exp(-gate))
            silu = gate * sigma
            hidden = (silu * up).astype(LOW)
            grad_gate = (grad_hidden * up * sigma * (1.0 + gate * (1.0 - sigma))).astype(LOW)
            grad_up = (grad_hidden * silu).astype(LOW)
            out_acc[...] += dot_nn(hidden, weights[2, span, :])
            grad_acc[...] += dot_nn(grad_gate, weights[0, span, :])
            grad_acc[...] += dot_nn(grad_up, weights[1, span, :])
            totals[0, span, :] += dot_tn(grad_gate, x)
            totals[1, span, :] += dot_tn(grad_up, x)
            totals[2, span, :] += dot_tn(hidden, g)
            return carry

        lax.fori_loop(0, tiles, tile, 0)

        @pl.when(t >= 2)
        def _():
            for d in (0, 1):
                out_copy(t - 2, d).wait()

        cast_buf[t % 2] = out_acc[...].astype(LOW)
        for d in (0, 1):
            out_copy(t, d).start()

        @pl.when(t == 0)
        def _():
            grad_sum[...] = grad_acc[...]

        @pl.when(t > 0)
        def _():
            for d in (0, 1):
                part = pl.ds(d * half, half)

                @pl.when(t >= 2)
                def _():
                    reduce_copy(t - 1, d).wait_recv()
                    grad_acc[part, :] += landed[d, (t - 1) % 2].astype(F32)

                    @pl.when(t <= n - 2)
                    def _():
                        pl.semaphore_signal(
                            credit.at[d], inc=1, device_id={"dp": ring.back[d]}, device_id_type=MESH
                        )

                    reduce_copy(t - 1, d).wait_send()

                sent[d] = grad_acc[part, :].astype(LOW)

                @pl.when(t >= 3)
                def _():
                    pl.semaphore_wait(credit.at[d], 1)

                reduce_copy(t, d).start()

        return carry

    lax.fori_loop(0, n, step, 0)
    for t in (n - 2, n - 1):
        for d in (0, 1):
            out_copy(t, d).wait()

    own_tiles = 3 * own // FF_TILE

    def tile_of(i, first):
        return i // (own // FF_TILE), pl.ds(
            pl.multiple_of(first + (i % (own // FF_TILE)) * FF_TILE, FF_TILE), FF_TILE
        )

    def pair_copy(i):
        return remote(cast_buf.at[i % 2], pair_land.at[i], pair_send.at[i % 2], pair_recv.at[i], ring.partner)

    def give(i, carry):
        @pl.when(i >= 2)
        def _():
            pair_copy(i - 2).wait_send()

        k, span = tile_of(i, own)
        cast_buf[i % 2] = totals[k, span, :].astype(LOW)
        pair_copy(i).start()
        return carry

    lax.fori_loop(0, own_tiles, give, 0)
    for i in (own_tiles - 2, own_tiles - 1):
        pair_copy(i).wait_send()

    def total_copy(i):
        k, span = tile_of(i, 0)
        return pltpu.make_async_copy(cast_buf.at[i % 2], weight_grads.at[k, span], cast_sem.at[i % 2, 0])

    def take(i, carry):
        @pl.when(i >= 2)
        def _():
            total_copy(i - 2).wait()

        pair_copy(i).wait_recv()
        k, span = tile_of(i, 0)
        cast_buf[i % 2] = (totals[k, span, :] + pair_land[i].astype(F32)).astype(LOW)
        total_copy(i).start()
        return carry

    lax.fori_loop(0, own_tiles, take, 0)

    for d in (0, 1):
        part = pl.ds(d * half, half)
        reduce_copy(n - 1, d).wait_recv()
        grad_sum[part, :] += landed[d, (n - 1) % 2].astype(F32)
        reduce_copy(n - 1, d).wait_send()

    for i in (own_tiles - 2, own_tiles - 1):
        total_copy(i).wait()

    def finish(t, carry):
        for d in (0, 1):
            send(t, d, False).wait_send()
        return carry

    lax.fori_loop(1, n, finish, 0)


def dense(normed, cotangents, own_weights, partner_weights):
    rows, features = normed.shape
    n = lax.axis_size("dp") // 2
    own = own_weights[0].shape[0]
    half = rows // 2
    vmem = pl.BlockSpec(memory_space=pltpu.VMEM)
    hbm = pl.BlockSpec(memory_space=pl.ANY)
    dma = pltpu.SemaphoreType.DMA
    own_tiles = 3 * own // FF_TILE
    return pl.pallas_call(
        dense_kernel,
        out_shape=(
            jax.ShapeDtypeStruct((rows, features), F32),
            jax.ShapeDtypeStruct((n, rows, features), LOW),
            jax.ShapeDtypeStruct((n, rows, features), LOW),
            jax.ShapeDtypeStruct((3, own, features), LOW),
        ),
        in_specs=[vmem] + [hbm] * 7,
        out_specs=(vmem, hbm, hbm, hbm),
        scratch_shapes=[
            pltpu.VMEM((3, 2 * own, features), LOW),
            pltpu.VMEM((3, 2 * own, features), F32),
            pltpu.VMEM((rows, features), LOW),
            pltpu.VMEM((rows, features), LOW),
            pltpu.VMEM((rows, features), F32),
            pltpu.VMEM((rows, features), F32),
            pltpu.VMEM((2, half, features), LOW),
            pltpu.VMEM((2, 2, half, features), LOW),
            pltpu.VMEM((2, FF_TILE, features), LOW),
            pltpu.VMEM((own_tiles, FF_TILE, features), LOW),
            dma((2, n)), dma((2, n)), dma((2,)), dma((2, 2)),
            pltpu.SemaphoreType.REGULAR((2,)),
            dma((4,)), dma((6,)), dma((2, 2)), dma((2,)), dma((own_tiles,)),
        ],
        compiler_params=pltpu.CompilerParams(
            collective_id=2, has_side_effects=True, vmem_limit_bytes=62 * MIB
        ),
        cost_estimate=pl.CostEstimate(
            flops=2 * 9 * n * rows * features * 2 * own, bytes_accessed=500 * MIB, transcendentals=0
        ),
        name="dense",
    )(normed, cotangents, *own_weights, *partner_weights)


def normed_back_kernel(
    grads, weights, partner_weights, hidden_in, gain, grad_mixed, out, gain_part,
    partner_grads, sent, landed,
    p_send, p_recv, rs_send, rs_recv, credit,
):
    ring = Ring()
    n = ring.chips
    rows, features = out.shape
    half = rows // 2
    r = grads.shape[2]
    ring.greet((ring.next[0], ring.next[1], ring.partner))

    def place(t, d):
        return ring.chip_far(-t if d == 0 else t)

    def swap(t, d):
        start = (place(t, d) * 2 + 1 - ring.core) * rows + d * half
        return remote(
            grads.at[:, pl.ds(pl.multiple_of(start, half), half)],
            partner_grads.at[:, t % n, half_rows(d, rows)],
            p_send.at[d, t % n],
            p_recv.at[d, t % n],
            ring.partner,
        )

    def begin(t, carry):
        for d in (0, 1):
            swap(t, d).start()
        return carry

    lax.fori_loop(1, n + 1, begin, 0)

    def reduce_copy(t, d):
        return remote(sent.at[d], landed.at[d, t % 2], rs_send.at[d], rs_recv.at[d, t % 2], ring.next[d])

    def step(t, carry):
        for d in (0, 1):
            start = (place(t, d) * 2 + ring.core) * rows + d * half
            mine = pl.ds(pl.multiple_of(start, half), half)
            part = pl.ds(d * half, half)
            swap(t, d).wait_recv()
            total = dot_nn(grads[0, mine, :], weights[0])
            for i in (1, 2):
                total += dot_nn(grads[i, mine, :], weights[i])
            for i in range(3):
                total += dot_nn(partner_grads[i, t % n, part, :], partner_weights[i])
            out[part, :] = total

        for d in (0, 1):
            part = pl.ds(d * half, half)

            @pl.when(t >= 2)
            def _():
                reduce_copy(t - 1, d).wait_recv()
                out[part, :] += landed[d, (t - 1) % 2].astype(F32)

                @pl.when(t <= n - 2)
                def _():
                    pl.semaphore_signal(
                        credit.at[d], inc=1, device_id={"dp": ring.back[d]}, device_id_type=MESH
                    )

                reduce_copy(t - 1, d).wait_send()

            @pl.when(t < n)
            def _():
                sent[d] = out[part, :].astype(LOW)

                @pl.when(t >= 3)
                def _():
                    pl.semaphore_wait(credit.at[d], 1)

                reduce_copy(t, d).start()

        return carry

    lax.fori_loop(1, n + 1, step, 0)

    def finish(t, carry):
        for d in (0, 1):
            swap(t, d).wait_send()
        return carry

    lax.fori_loop(1, n + 1, finish, 0)

    gain_part[...] = jnp.zeros_like(gain_part)

    def close(i, carry):
        span = pl.ds(pl.multiple_of(i * 16, 16), 16)
        value = hidden_in[span, :].astype(F32)
        grad = out[span, :]
        scale = lax.rsqrt(jnp.mean(value * value, axis=1, keepdims=True) + EPSILON)
        scaled = grad * gain[...]
        shift = jnp.mean(value * scaled, axis=1, keepdims=True)
        out[span, :] = grad_mixed[span, :] + scale * scaled - value * (scale * scale * scale * shift)
        gain_part[...] += jnp.sum(grad * value * scale, axis=0, keepdims=True)
        return carry

    lax.fori_loop(0, rows // 16, close, 0)


def normed_back(grads, weights, partner_weights, hidden_in, gain, grad_mixed):
    tokens, r = grads.shape[1:]
    features = weights.shape[2]
    devices = lax.axis_size("dp")
    n = devices // 2
    rows = tokens // devices
    half = rows // 2
    vmem = pl.BlockSpec(memory_space=pltpu.VMEM)
    dma = pltpu.SemaphoreType.DMA
    return pl.pallas_call(
        normed_back_kernel,
        out_shape=(
            jax.ShapeDtypeStruct((rows, features), F32),
            jax.ShapeDtypeStruct((1, features), F32),
        ),
        in_specs=[vmem] * 6,
        out_specs=(vmem, vmem),
        scratch_shapes=[
            pltpu.VMEM((3, n, rows, r), LOW),
            pltpu.VMEM((2, half, features), LOW),
            pltpu.VMEM((2, 2, half, features), LOW),
            dma((2, n)), dma((2, n)), dma((2,)), dma((2, 2)),
            pltpu.SemaphoreType.REGULAR((2,)),
        ],
        compiler_params=pltpu.CompilerParams(
            collective_id=3, has_side_effects=True, vmem_limit_bytes=40 * MIB
        ),
        cost_estimate=pl.CostEstimate(
            flops=2 * n * rows * features * 6 * r, bytes_accessed=320 * MIB, transcendentals=0
        ),
        name="normed_back",
    )(grads, weights, partner_weights, hidden_in, gain, grad_mixed)


def gain_total_kernel(part, out, landed, send_sem, recv_sem, local_sem):
    columns, packs = lax.axis_size("dp"), lax.axis_size("rep")
    devices = columns * packs
    me = lax.axis_index("rep") * columns + lax.axis_index("dp")
    barrier = pltpu.get_barrier_semaphore()

    def other(k):
        to = lax.rem(me + k, devices)
        return {"dp": to % columns, "rep": to // columns}

    def greet(k, carry):
        pl.semaphore_signal(barrier, inc=1, device_id=other(k), device_id_type=MESH)
        return carry

    lax.fori_loop(1, devices, greet, 0)
    pl.semaphore_wait(barrier, devices - 1)

    def copy(k):
        return pltpu.make_async_remote_copy(
            src_ref=part,
            dst_ref=landed.at[me],
            send_sem=send_sem.at[k],
            recv_sem=recv_sem.at[k],
            device_id=other(k),
            device_id_type=MESH,
        )

    def begin(k, carry):
        copy(k).start()
        return carry

    lax.fori_loop(1, devices, begin, 0)
    keep = pltpu.make_async_copy(part, landed.at[me], local_sem)
    keep.start()
    keep.wait()

    def wait(k, carry):
        copy(k).wait()
        return carry

    lax.fori_loop(1, devices, wait, 0)
    out[...] = lax.fori_loop(1, devices, lambda i, total: total + landed[i], landed[0])


def gain_total(part):
    devices = lax.axis_size("dp") * lax.axis_size("rep")
    vmem = pl.BlockSpec(memory_space=pltpu.VMEM)
    dma = pltpu.SemaphoreType.DMA
    return pl.pallas_call(
        gain_total_kernel,
        out_shape=jax.ShapeDtypeStruct(part.shape, F32),
        in_specs=[vmem],
        out_specs=vmem,
        scratch_shapes=[
            pltpu.VMEM((devices,) + part.shape, F32),
            dma((devices,)), dma((devices,)), dma,
        ],
        compiler_params=pltpu.CompilerParams(collective_id=4, has_side_effects=True),
        name="gain_total",
    )(part)


def rms(values, norm_gain):
    return (
        values * lax.rsqrt(jnp.mean(values * values, axis=-1, keepdims=True) + EPSILON) * norm_gain
    )


def rms_back(values, norm_gain, grads):
    _, pullback = jax.vjp(rms, values, norm_gain)
    return pullback(grads)


def turned_rows(weight):
    parts = weight.reshape(-1, 2, HALF, weight.shape[1])
    return jnp.concatenate([-parts[:, 1:], parts[:, :1]], 1).reshape(weight.shape)


def from_partner(value):
    devices = lax.axis_size("dp")
    return lax.ppermute(value, "dp", [(i, i ^ 1) for i in range(devices)])


def pack_sum(value):
    low = value.astype(LOW)
    if lax.axis_size("rep") == 2:
        other = lax.ppermute(low, "rep", [(0, 1), (1, 0)])
        return low.astype(F32) + other.astype(F32)
    return lax.psum(low, "rep").astype(F32)


def body(
    tokens,
    attention_gain,
    query_weight,
    key_weight,
    value_weight,
    output_weight,
    dense_gain,
    gate_weight,
    up_weight,
    down_weight,
    block_document,
    document_tail,
    cotangent,
):
    devices = lax.axis_size("dp")
    chips = devices // 2
    core = lax.axis_index("dp") % 2
    hidden_in = tokens[0].astype(F32)
    tok_dev = hidden_in.shape[0]
    pack_tok = tok_dev * devices

    documents, tails = block_document[0], document_tail[0]
    first = jnp.sum((documents[None, :] < documents[:, None]).astype(jnp.int32), axis=1)
    last = jnp.concatenate([documents[1:] != documents[:-1], jnp.ones((1,), bool)])
    doc_ids = jnp.arange(tails.shape[0], dtype=jnp.int32)
    own_tail = jnp.sum((documents[:, None] == doc_ids[None, :]) * tails[None, :], axis=1)
    tail = jnp.where(last, own_tail, BLOCK).astype(jnp.int32)
    block_index = jnp.arange(documents.shape[0], dtype=jnp.int32)
    inside = jnp.arange(BLOCK, dtype=jnp.int32)
    position = ((block_index - first)[:, None] * BLOCK + inside[None, :]).reshape(-1)
    frequency = ROPE_BASE ** (-(jnp.arange(HALF, dtype=F32) * (2.0 / HEAD_DIM)))
    angles = position.astype(F32)[None, :] * frequency[:, None]
    cos_t, sin_t = jnp.cos(angles), jnp.sin(angles)
    r = query_weight.shape[0]

    def rows_of(table):
        mine = lax.dynamic_index_in_dim(
            table.reshape(HALF, chips, 2, tok_dev), core, axis=2, keepdims=False
        )
        return jnp.tile(mine.transpose(1, 2, 0), (1, 1, r // HALF))

    normed = rms(hidden_in, attention_gain).astype(LOW)
    stacked = jnp.concatenate(
        [
            query_weight,
            turned_rows(query_weight),
            key_weight,
            turned_rows(key_weight),
            value_weight,
        ],
        0,
    )
    qkv, normed_all = gather_project(normed, stacked, rows_of(cos_t), rows_of(sin_t))

    order = ring_order(chips)
    walk = [2 * chip + k for chip in order for k in (0, 1)]
    lanes = [[2 * chip + k for chip in order] for k in (0, 1)]
    full_output = lax.all_gather(output_weight, "dp", axis=0, tiled=True, axis_index_groups=[walk])
    grad_low = cotangent[0]
    cotangents = lax.all_gather(
        grad_low, "dp", axis=0, tiled=True, axis_index_groups=lanes
    ).reshape(chips, tok_dev, -1)
    gate_other, up_other, down_other = (
        from_partner(gate_weight),
        from_partner(up_weight),
        from_partner(down_weight),
    )
    qkv_weight = jnp.stack([query_weight, key_weight, value_weight])
    qkv_other = from_partner(qkv_weight)

    attended, log_total = attend(first, tail, qkv)
    attended_blocks = lax.all_to_all(
        attended.reshape(devices, tok_dev, r), "dp", split_axis=0, concat_axis=0, tiled=True
    )
    attended_here = jnp.concatenate([attended_blocks[i] for i in walk], 1)
    mixed = hidden_in + dot_nn(attended_here, full_output)
    normed_two = rms(mixed, dense_gain).astype(LOW)

    grad_normed_two, out_parts, _, dense_low = dense(
        normed_two,
        cotangents,
        (gate_weight, up_weight, down_weight),
        (gate_other, up_other, down_other),
    )
    dense_total = pack_sum(dense_low)

    grad_mixed_norm, dense_gain_part = rms_back(mixed, dense_gain, grad_normed_two)
    grad_mixed = grad_low.astype(F32) + grad_mixed_norm
    grad_mixed_low = grad_mixed.astype(LOW)
    grad_attended = dot_nt(grad_mixed_low, full_output).astype(LOW)
    grad_blocks = jnp.stack(
        [grad_attended[:, walk.index(i) * r : (walk.index(i) + 1) * r] for i in range(devices)]
    )
    grad_heads = lax.all_to_all(
        grad_blocks, "dp", split_axis=0, concat_axis=0, tiled=True
    ).reshape(pack_tok, r)
    output_grad = lax.psum_scatter(
        dot_tn(attended_here, grad_mixed_low).astype(LOW),
        "dp",
        scatter_dimension=0,
        tiled=True,
        axis_index_groups=[walk],
    )
    output_total = pack_sum(output_grad)
    out_sum = lax.psum_scatter(
        out_parts.reshape(chips * tok_dev, -1),
        "dp",
        scatter_dimension=0,
        tiled=True,
        axis_index_groups=lanes,
    )
    layer_out = mixed + out_sum.astype(F32)

    grads = attend_back(first, tail, qkv, grad_heads, attended, log_total, cos_t, sin_t)
    by_core = grads.reshape(3, chips, 2, tok_dev, r)
    swapped = from_partner(lax.dynamic_index_in_dim(by_core, 1 - core, axis=2, keepdims=False))
    mine = lax.dynamic_index_in_dim(by_core, core, axis=2, keepdims=False)
    normed_rows = normed_all.reshape(chips * tok_dev, -1)

    def weight_part(value):
        return lax.dot_general(
            value.reshape(3, chips * tok_dev, r),
            normed_rows,
            (((1,), (0,)), ((), ())),
            preferred_element_type=F32,
        )

    qkv_there = from_partner(weight_part(swapped).astype(LOW))
    qkv_low = (weight_part(mine) + qkv_there.astype(F32)).astype(LOW)
    qkv_total = pack_sum(qkv_low)

    input_grad, attention_gain_part = normed_back(
        grads, qkv_weight, qkv_other, tokens[0], attention_gain[None], grad_mixed
    )
    gain_parts = jnp.stack([attention_gain_part[0], dense_gain_part])
    gain_totals = gain_total(gain_parts.reshape(2, -1, 128)).reshape(2, -1)
    return (
        layer_out[None].astype(LOW),
        input_grad[None],
        gain_totals[0],
        qkv_total[0],
        qkv_total[1],
        qkv_total[2],
        output_total,
        gain_totals[1],
        dense_total[0],
        dense_total[1],
        dense_total[2],
    )


def solution(mesh):
    return jax.shard_map(
        body,
        mesh=mesh,
        in_specs=(
            P("rep", "dp", None),
            P(),
            P("dp", None),
            P("dp", None),
            P("dp", None),
            P("dp", None),
            P(),
            P("dp", None),
            P("dp", None),
            P("dp", None),
            P("rep", None),
            P("rep", None),
            P("rep", "dp", None),
        ),
        out_specs=(
            P("rep", "dp", None),
            P("rep", "dp", None),
            P(),
            P("dp", None),
            P("dp", None),
            P("dp", None),
            P("dp", None),
            P(),
            P("dp", None),
            P("dp", None),
            P("dp", None),
        ),
        check_vma=False,
    )
```

```python
import functools
import math

import jax
import jax.numpy as jnp
from jax import lax
from jax.experimental import pallas as pl
from jax.experimental.pallas import tpu as pltpu
from jax.sharding import PartitionSpec as P

HEAD_DIM = 64
HALF = HEAD_DIM // 2
BLOCK = 128
CHUNK = 512
FF_TILE = 256
EPSILON = 1e-05
ROPE_BASE = 130000.0
MASKED_SCORE = -1e30
MESH = pl.DeviceIdType.MESH
MIB = 2**20
LOW = jnp.bfloat16
F32 = jnp.float32


def dot_nn(a, b):
    return lax.dot_general(a, b, (((1,), (0,)), ((), ())), preferred_element_type=F32)


def dot_nt(a, b):
    return lax.dot_general(a, b, (((1,), (1,)), ((), ())), preferred_element_type=F32)


def dot_tn(a, b):
    return lax.dot_general(a, b, (((0,), (0,)), ((), ())), preferred_element_type=F32)


def grid_of(chips):
    depth = 4 if chips % 8 == 0 else 2
    return depth, chips // depth


def chip_at(place, chips):
    depth, width = grid_of(chips)
    place = lax.rem(place + chips, chips)
    later = place - depth
    row, column = later // (width - 1), later % (width - 1)
    odd = row % 2
    far = (depth - 1 - row) * width + 1 + column + odd * (width - 2 - 2 * column)
    return jnp.where(place < depth, place * width, far)


def place_of(chip, chips):
    depth, width = grid_of(chips)
    z, x = chip // width, chip % width
    row = depth - 1 - z
    odd = row % 2
    column = x - 1 + odd * (width - 2 * x)
    return jnp.where(x == 0, z, depth + row * (width - 1) + column)


def ring_order(chips):
    depth, width = grid_of(chips)
    order = [z * width for z in range(depth)]
    for row in range(depth):
        columns = list(range(1, width))
        order += [(depth - 1 - row) * width + x for x in (columns[::-1] if row % 2 else columns)]
    return order


class Ring:
    def __init__(self):
        self.chips = lax.axis_size("dp") // 2
        me = lax.axis_index("dp")
        self.core = me % 2
        self.chip = me // 2
        self.partner = self.chip * 2 + 1 - self.core
        self.place = place_of(self.chip, self.chips)
        self.next = (self.device(1), self.device(-1))
        self.back = (self.next[1], self.next[0])

    def chip_far(self, steps):
        return chip_at(self.place + steps, self.chips)

    def device(self, steps):
        return self.chip_far(steps) * 2 + self.core

    def greet(self, others):
        barrier = pltpu.get_barrier_semaphore()
        for other in others:
            pl.semaphore_signal(barrier, inc=1, device_id={"dp": other}, device_id_type=MESH)
        pl.semaphore_wait(barrier, len(others))


def remote(src, dst, send_sem, recv_sem, device):
    return pltpu.make_async_remote_copy(
        src_ref=src,
        dst_ref=dst,
        send_sem=send_sem,
        recv_sem=recv_sem,
        device_id={"dp": device},
        device_id_type=MESH,
    )


def half_rows(direction, rows):
    return pl.ds(direction * (rows // 2), rows // 2)


def gather_project_kernel(
    normed, weights, cosine, sine, qkv, gathered,
    partner_weights, x_buf, staged,
    ag_send, ag_recv, w_send, w_recv, q_send, q_recv, local_sem,
):
    ring = Ring()
    n = ring.chips
    rows = normed.shape[0]
    r = qkv.shape[2]
    ring.greet((ring.next[0], ring.next[1], ring.partner))
    swap = remote(weights, partner_weights, w_send, w_recv, ring.partner)
    swap.start()
    keep = pltpu.make_async_copy(normed, gathered.at[ring.chip], local_sem.at[2])
    keep.start()

    def hop(t, d):
        chip = ring.chip_far((1 - t) if d == 0 else (t - 1))
        return chip, half_rows(d, rows)

    def send(t, d, first):
        chip, part = hop(t, d)
        src = normed.at[part] if first else gathered.at[chip, part]
        return remote(src, gathered.at[chip, part], ag_send.at[d, t - 1], ag_recv.at[d, t - 1], ring.next[d])

    for d in (0, 1):
        send(1, d, True).start()

    def project_block(t, from_input):
        x = normed[...] if from_input else x_buf[...]
        places = [ring.chip_far(-t), ring.chip_far(t)]
        cos = jnp.concatenate([cosine[places[d], half_rows(d, rows), :] for d in (0, 1)], 0)
        sin = jnp.concatenate([sine[places[d], half_rows(d, rows), :] for d in (0, 1)], 0)

        def heads(w):
            part = [dot_nt(x, w[i * r : (i + 1) * r, :]) for i in range(5)]
            return (
                (part[0] * cos + part[1] * sin).astype(LOW),
                (part[2] * cos + part[3] * sin).astype(LOW),
                part[4].astype(LOW),
            )

        starts = [
            pl.multiple_of((places[d] * 2 + ring.core) * rows + d * (rows // 2), rows // 2)
            for d in (0, 1)
        ]
        for i, value in enumerate(heads(weights)):
            for d in (0, 1):
                qkv[i, pl.ds(starts[d], rows // 2), :] = value[d * (rows // 2) : (d + 1) * (rows // 2)]
        if from_input:
            swap.wait()
        for i, value in enumerate(heads(partner_weights)):
            staged[t, i] = value
        for d in (0, 1):
            remote(
                staged.at[t, :, half_rows(d, rows)],
                qkv.at[:, pl.ds(starts[d], rows // 2)],
                q_send.at[d, t],
                q_recv.at[d, t],
                ring.partner,
            ).start()

    project_block(0, True)

    def step(t, carry):
        for d in (0, 1):
            send(t, d, False).wait_recv()

        @pl.when(t < n - 1)
        def _():
            for d in (0, 1):
                send(t + 1, d, False).start()

        loads = []
        for d in (0, 1):
            chip, part = hop(t + 1, d)
            loads.append(pltpu.make_async_copy(gathered.at[chip, part], x_buf.at[part], local_sem.at[d]))
        for load in loads:
            load.start()
        for load in loads:
            load.wait()
        project_block(t, False)
        return carry

    lax.fori_loop(1, n, step, 0)

    def finish(t, carry):
        for d in (0, 1):
            send(t, d, False).wait_send()
        return carry

    lax.fori_loop(1, n, finish, 0)

    def finish_heads(t, carry):
        for d in (0, 1):
            done = remote(
                staged.at[t, :, half_rows(d, rows)],
                qkv.at[:, half_rows(d, rows)],
                q_send.at[d, t],
                q_recv.at[d, t],
                ring.partner,
            )
            done.wait_send()
            done.wait_recv()
        return carry

    lax.fori_loop(0, n, finish_heads, 0)
    keep.wait()


def gather_project(normed, weights, cosine, sine):
    rows, features = normed.shape
    r = weights.shape[0] // 5
    devices = lax.axis_size("dp")
    n = devices // 2
    vmem = pl.BlockSpec(memory_space=pltpu.VMEM)
    dma = pltpu.SemaphoreType.DMA
    return pl.pallas_call(
        gather_project_kernel,
        out_shape=(
            jax.ShapeDtypeStruct((3, devices * rows, r), LOW),
            jax.ShapeDtypeStruct((n, rows, features), LOW),
        ),
        in_specs=[vmem] * 4,
        out_specs=(vmem, pl.BlockSpec(memory_space=pl.ANY)),
        scratch_shapes=[
            pltpu.VMEM(weights.shape, LOW),
            pltpu.VMEM((rows, features), LOW),
            pltpu.VMEM((n, 3, rows, r), LOW),
            dma((2, n)), dma((2, n)), dma, dma, dma((2, n)), dma((2, n)), dma((3,)),
        ],
        compiler_params=pltpu.CompilerParams(
            collective_id=1, has_side_effects=True, vmem_limit_bytes=40 * MIB
        ),
        cost_estimate=pl.CostEstimate(
            flops=4 * n * rows * features * 5 * r, bytes_accessed=320 * MIB, transcendentals=0
        ),
        name="gather_project",
    )(normed, weights, cosine, sine)


def split_heads(u):
    heads = u.shape[1] // HEAD_DIM
    if heads == 1:
        return u
    lane = lax.broadcasted_iota(jnp.int32, u.shape, 1) // HEAD_DIM
    zero = jnp.zeros_like(u)
    return jnp.concatenate([jnp.where(lane == h, u, zero) for h in range(heads)], 0)


def join_heads(u):
    heads = u.shape[0] // HEAD_DIM
    return jnp.concatenate(
        [u[h * HEAD_DIM : (h + 1) * HEAD_DIM, h * BLOCK : (h + 1) * BLOCK] for h in range(heads)], 0
    )


def transpose_blocks(source, target):
    def one(b, carry):
        at = pl.multiple_of(b * BLOCK, BLOCK)
        target[:, pl.ds(at, BLOCK)] = source[pl.ds(at, BLOCK), :].astype(F32).T.astype(LOW)
        return carry

    lax.fori_loop(0, source.shape[0] // BLOCK, one, 0)


def window_of(b, first, tail, columns):
    start = pl.multiple_of(jnp.maximum(b - (CHUNK // BLOCK - 1), 0) * BLOCK, BLOCK)
    whole = (b - first) // (CHUNK // BLOCK)
    lowest = (first + whole * (CHUNK // BLOCK)) * BLOCK
    key_index = start + lax.broadcasted_iota(jnp.int32, (CHUNK, columns), 0)
    query_index = b * BLOCK + lax.broadcasted_iota(jnp.int32, (CHUNK, columns), 1) % BLOCK
    allowed = (
        (key_index >= lowest)
        & (key_index <= query_index)
        & (key_index < b * BLOCK + tail)
    )
    return start, whole, allowed


def attend_kernel(first_ref, tail_ref, qkv, attended, log_total, value_t):
    tokens, r = qkv.shape[1:]
    columns = (r // HEAD_DIM) * BLOCK
    scale = 1.0 / math.sqrt(HEAD_DIM)
    transpose_blocks(qkv.at[2], value_t)

    def block(b, carry):
        at = pl.multiple_of(b * BLOCK, BLOCK)
        query = split_heads(qkv[0, pl.ds(at, BLOCK), :])
        start, whole, allowed = window_of(b, first_ref[b], tail_ref[b], columns)
        scores = dot_nt(qkv[1, pl.ds(start, CHUNK), :], query) * scale
        scores = jnp.where(allowed, scores, MASKED_SCORE)
        top = jnp.max(scores, axis=0, keepdims=True)
        weights = jnp.exp(scores - top)
        total = jnp.sum(weights, axis=0, keepdims=True)
        out = dot_nn(value_t[:, pl.ds(start, CHUNK)], weights.astype(LOW))

        def more(i, state):
            top, total, out = state
            start = pl.multiple_of(first_ref[b] * BLOCK + i * CHUNK, BLOCK)
            scores = dot_nt(qkv[1, pl.ds(start, CHUNK), :], query) * scale
            higher = jnp.maximum(top, jnp.max(scores, axis=0, keepdims=True))
            shrink = jnp.exp(top - higher)
            weights = jnp.exp(scores - higher)
            total = total * shrink + jnp.sum(weights, axis=0, keepdims=True)
            out = out * shrink + dot_nn(value_t[:, pl.ds(start, CHUNK)], weights.astype(LOW))
            return higher, total, out

        top, total, out = lax.fori_loop(0, whole, more, (top, total, out))
        log_total[pl.ds(b, 1), :] = top + jnp.log(total)
        attended[pl.ds(at, BLOCK), :] = join_heads(out / total).T.astype(LOW)
        return carry

    lax.fori_loop(0, tokens // BLOCK, block, 0)


def attend(first, tail, qkv):
    tokens, r = qkv.shape[1:]
    smem = pl.BlockSpec(memory_space=pltpu.SMEM)
    vmem = pl.BlockSpec(memory_space=pltpu.VMEM)
    return pl.pallas_call(
        attend_kernel,
        out_shape=(
            jax.ShapeDtypeStruct((tokens, r), LOW),
            jax.ShapeDtypeStruct((tokens // BLOCK, (r // HEAD_DIM) * BLOCK), F32),
        ),
        in_specs=[smem, smem, vmem],
        out_specs=(vmem, vmem),
        scratch_shapes=[pltpu.VMEM((r, tokens), LOW)],
        compiler_params=pltpu.CompilerParams(vmem_limit_bytes=40 * MIB),
        cost_estimate=pl.CostEstimate(
            flops=4 * tokens * 1024 * r * 8, bytes_accessed=120 * MIB, transcendentals=tokens * 1024
        ),
        name="attend",
    )(first, tail, qkv)


def unrotate(g, cos, sin):
    parts = []
    for h in range(g.shape[0] // HEAD_DIM):
        one = g[h * HEAD_DIM : h * HEAD_DIM + HALF]
        two = g[h * HEAD_DIM + HALF : (h + 1) * HEAD_DIM]
        parts += [one * cos + two * sin, two * cos - one * sin]
    return jnp.concatenate(parts, 0)


def attend_back_kernel(
    first_ref, tail_ref, qkv, grad_out, attended, log_total, cos_t, sin_t, grads,
    key_t, grad_key, grad_value,
):
    tokens, r = qkv.shape[1:]
    heads = r // HEAD_DIM
    columns = heads * BLOCK
    scale = 1.0 / math.sqrt(HEAD_DIM)
    transpose_blocks(qkv.at[1], key_t)
    grad_key[...] = jnp.zeros_like(grad_key)
    grad_value[...] = jnp.zeros_like(grad_value)

    def block(b, carry):
        at = pl.multiple_of(b * BLOCK, BLOCK)
        here = pl.ds(at, BLOCK)
        query = split_heads(qkv[0, here, :])
        grad_rows = grad_out[here, :]
        grad = split_heads(grad_rows)
        product = (grad_rows.astype(F32) * attended[here, :].astype(F32)).T
        delta = jnp.concatenate(
            [
                jnp.sum(product[h * HEAD_DIM : (h + 1) * HEAD_DIM], axis=0, keepdims=True)
                for h in range(heads)
            ],
            1,
        )
        log_row = log_total[pl.ds(b, 1), :]

        def chunk(start, allowed, grad_query):
            span = pl.ds(start, CHUNK)
            scores = dot_nt(qkv[1, span, :], query) * scale
            weights = jnp.exp(scores - log_row)
            if allowed is not None:
                weights = jnp.where(allowed, weights, 0.0)
            grad_weights = dot_nt(qkv[2, span, :], grad)
            grad_scores = (weights * (grad_weights - delta)).astype(LOW)
            grad_value[span, :] += dot_nn(weights.astype(LOW), grad)
            grad_key[span, :] += dot_nn(grad_scores, query)
            return grad_query + dot_nn(key_t[:, span], grad_scores)

        start, whole, allowed = window_of(b, first_ref[b], tail_ref[b], columns)
        grad_query = chunk(start, allowed, jnp.zeros((r, columns), F32))
        grad_query = lax.fori_loop(
            0,
            whole,
            lambda i, g: chunk(pl.multiple_of(first_ref[b] * BLOCK + i * CHUNK, BLOCK), None, g),
            grad_query,
        )
        turned = unrotate(join_heads(grad_query) * scale, cos_t[:, here], sin_t[:, here])
        grads[0, here, :] = turned.T.astype(LOW)
        return carry

    lax.fori_loop(0, tokens // BLOCK, block, 0)

    def close(b, carry):
        here = pl.ds(pl.multiple_of(b * BLOCK, BLOCK), BLOCK)
        turned = unrotate(grad_key[here, :].T * scale, cos_t[:, here], sin_t[:, here])
        grads[1, here, :] = turned.T.astype(LOW)
        grads[2, here, :] = grad_value[here, :].astype(LOW)
        return carry

    lax.fori_loop(0, tokens // BLOCK, close, 0)


def attend_back(first, tail, qkv, grad_out, attended, log_total, cos_t, sin_t):
    tokens, r = qkv.shape[1:]
    smem = pl.BlockSpec(memory_space=pltpu.SMEM)
    vmem = pl.BlockSpec(memory_space=pltpu.VMEM)
    return pl.pallas_call(
        attend_back_kernel,
        out_shape=jax.ShapeDtypeStruct((3, tokens, r), LOW),
        in_specs=[smem, smem] + [vmem] * 6,
        out_specs=vmem,
        scratch_shapes=[
            pltpu.VMEM((r, tokens), LOW),
            pltpu.VMEM((tokens, r), F32),
            pltpu.VMEM((tokens, r), F32),
        ],
        compiler_params=pltpu.CompilerParams(vmem_limit_bytes=40 * MIB),
        cost_estimate=pl.CostEstimate(
            flops=10 * tokens * 1024 * r * 8, bytes_accessed=240 * MIB, transcendentals=tokens * 1024
        ),
        name="attend_back",
    )(first, tail, qkv, grad_out, attended, log_total, cos_t, sin_t)


def dense_kernel(
    normed, cotangents, gate_w, up_w, down_w, gate_p, up_p, down_p,
    grad_sum, out_parts, gathered, gate_grad, up_grad, down_grad,
    weights, totals, x_buf, g_buf, out_acc, grad_acc, sent, landed, cast_buf, pair_land,
    ag_send, ag_recv, rs_send, rs_recv, credit, local_sem, w_sem, cast_sem, pair_send, pair_recv,
):
    ring = Ring()
    n = ring.chips
    rows, features = normed.shape
    half = rows // 2
    own = gate_w.shape[0]
    tiles = 2 * own // FF_TILE
    loads = []
    for i, (mine, theirs) in enumerate(((gate_w, gate_p), (up_w, up_p), (down_w, down_p))):
        loads.append(pltpu.make_async_copy(mine, weights.at[i, pl.ds(0, own)], w_sem.at[2 * i]))
        loads.append(pltpu.make_async_copy(theirs, weights.at[i, pl.ds(own, own)], w_sem.at[2 * i + 1]))
    for load in loads:
        load.start()
    ring.greet((ring.next[0], ring.next[1], ring.partner))

    def source(t, d):
        return lax.rem(ring.place + (n - t if d == 0 else t), n)

    def send(t, d, first):
        place, part = source(t - 1, d), half_rows(d, rows)
        src = normed.at[part] if first else gathered.at[place, part]
        return remote(src, gathered.at[place, part], ag_send.at[d, t - 1], ag_recv.at[d, t - 1], ring.next[d])

    def reduce_copy(t, d):
        return remote(sent.at[d], landed.at[d, t % 2], rs_send.at[d], rs_recv.at[d, t % 2], ring.next[d])

    for d in (0, 1):
        send(1, d, True).start()

    def clear(i, carry):
        span = pl.ds(pl.multiple_of(i * FF_TILE, FF_TILE), FF_TILE)
        for k in range(3):
            totals[k, span, :] = jnp.zeros((FF_TILE, features), F32)
        return carry

    lax.fori_loop(0, tiles, clear, 0)
    for load in loads:
        load.wait()

    def out_copy(t, d):
        part = half_rows(d, rows)
        return pltpu.make_async_copy(
            cast_buf.at[t % 2, part], out_parts.at[source(t, d), part], cast_sem.at[t % 2, d]
        )

    def step(t, carry):
        copies = []
        for d in (0, 1):
            part = half_rows(d, rows)
            copies.append(
                pltpu.make_async_copy(cotangents.at[source(t, d), part], g_buf.at[part], local_sem.at[d])
            )
            copies[-1].start()

        @pl.when(t > 0)
        def _():
            for d in (0, 1):
                send(t, d, False).wait_recv()

            @pl.when(t < n - 1)
            def _():
                for d in (0, 1):
                    send(t + 1, d, False).start()

            more = []
            for d in (0, 1):
                part = half_rows(d, rows)
                more.append(
                    pltpu.make_async_copy(gathered.at[source(t, d), part], x_buf.at[part], local_sem.at[2 + d])
                )
                more[-1].start()
            for copy in more:
                copy.wait()

        @pl.when(t == 0)
        def _():
            x_buf[...] = normed[...]

        for copy in copies:
            copy.wait()

        out_acc[...] = jnp.zeros_like(out_acc)
        grad_acc[...] = jnp.zeros_like(grad_acc)

        def tile(i, carry):
            span = pl.ds(pl.multiple_of(i * FF_TILE, FF_TILE), FF_TILE)
            x = x_buf[...]
            g = g_buf[...]
            gate = dot_nt(x, weights[0, span, :])
            up = dot_nt(x, weights[1, span, :])
            grad_hidden = dot_nt(g, weights[2, span, :])
            sigma = 1.0 / (1.0 + jnp.exp(-gate))
            silu = gate * sigma
            hidden = (silu * up).astype(LOW)
            grad_gate = (grad_hidden * up * sigma * (1.0 + gate * (1.0 - sigma))).astype(LOW)
            grad_up = (grad_hidden * silu).astype(LOW)
            out_acc[...] += dot_nn(hidden, weights[2, span, :])
            grad_acc[...] += dot_nn(grad_gate, weights[0, span, :])
            grad_acc[...] += dot_nn(grad_up, weights[1, span, :])
            totals[0, span, :] += dot_tn(grad_gate, x)
            totals[1, span, :] += dot_tn(grad_up, x)
            totals[2, span, :] += dot_tn(hidden, g)
            return carry

        lax.fori_loop(0, tiles, tile, 0)

        @pl.when(t >= 2)
        def _():
            for d in (0, 1):
                out_copy(t - 2, d).wait()

        cast_buf[t % 2] = out_acc[...].astype(LOW)
        for d in (0, 1):
            out_copy(t, d).start()

        @pl.when(t == 0)
        def _():
            grad_sum[...] = grad_acc[...]

        @pl.when(t > 0)
        def _():
            for d in (0, 1):
                part = pl.ds(d * half, half)

                @pl.when(t >= 2)
                def _():
                    reduce_copy(t - 1, d).wait_recv()
                    grad_acc[part, :] += landed[d, (t - 1) % 2].astype(F32)

                    @pl.when(t <= n - 2)
                    def _():
                        pl.semaphore_signal(
                            credit.at[d], inc=1, device_id={"dp": ring.back[d]}, device_id_type=MESH
                        )

                    reduce_copy(t - 1, d).wait_send()

                sent[d] = grad_acc[part, :].astype(LOW)

                @pl.when(t >= 3)
                def _():
                    pl.semaphore_wait(credit.at[d], 1)

                reduce_copy(t, d).start()

        return carry

    lax.fori_loop(0, n, step, 0)
    for t in (n - 2, n - 1):
        for d in (0, 1):
            out_copy(t, d).wait()

    own_tiles = 3 * own // FF_TILE

    def tile_of(i, first):
        return i // (own // FF_TILE), pl.ds(
            pl.multiple_of(first + (i % (own // FF_TILE)) * FF_TILE, FF_TILE), FF_TILE
        )

    def pair_copy(i):
        return remote(cast_buf.at[i % 2], pair_land.at[i], pair_send.at[i % 2], pair_recv.at[i], ring.partner)

    def give(i, carry):
        @pl.when(i >= 2)
        def _():
            pair_copy(i - 2).wait_send()

        k, span = tile_of(i, own)
        cast_buf[i % 2] = totals[k, span, :].astype(LOW)
        pair_copy(i).start()
        return carry

    lax.fori_loop(0, own_tiles, give, 0)
    for i in (own_tiles - 2, own_tiles - 1):
        pair_copy(i).wait_send()

    def total_copy(i):
        target = (gate_grad, up_grad, down_grad)[i // (own // FF_TILE)]
        span = pl.ds((i % (own // FF_TILE)) * FF_TILE, FF_TILE)
        return pltpu.make_async_copy(cast_buf.at[i % 2], target.at[span], cast_sem.at[i % 2, 0])

    for i in range(own_tiles):
        if i >= 2:
            total_copy(i - 2).wait()
        pair_copy(i).wait_recv()
        k, span = tile_of(i, 0)
        cast_buf[i % 2] = (totals[k, span, :] + pair_land[i].astype(F32)).astype(LOW)
        total_copy(i).start()

    for d in (0, 1):
        part = pl.ds(d * half, half)
        reduce_copy(n - 1, d).wait_recv()
        grad_sum[part, :] += landed[d, (n - 1) % 2].astype(F32)
        reduce_copy(n - 1, d).wait_send()

    for i in (own_tiles - 2, own_tiles - 1):
        total_copy(i).wait()

    def finish(t, carry):
        for d in (0, 1):
            send(t, d, False).wait_send()
        return carry

    lax.fori_loop(1, n, finish, 0)


def dense(normed, cotangents, own_weights, partner_weights):
    rows, features = normed.shape
    n = lax.axis_size("dp") // 2
    own = own_weights[0].shape[0]
    half = rows // 2
    vmem = pl.BlockSpec(memory_space=pltpu.VMEM)
    hbm = pl.BlockSpec(memory_space=pl.ANY)
    dma = pltpu.SemaphoreType.DMA
    own_tiles = 3 * own // FF_TILE
    return pl.pallas_call(
        dense_kernel,
        out_shape=(
            jax.ShapeDtypeStruct((rows, features), F32),
            jax.ShapeDtypeStruct((n, rows, features), LOW),
            jax.ShapeDtypeStruct((n, rows, features), LOW),
            jax.ShapeDtypeStruct((own, features), LOW),
            jax.ShapeDtypeStruct((own, features), LOW),
            jax.ShapeDtypeStruct((own, features), LOW),
        ),
        in_specs=[vmem] + [hbm] * 7,
        out_specs=(vmem,) + (hbm,) * 5,
        scratch_shapes=[
            pltpu.VMEM((3, 2 * own, features), LOW),
            pltpu.VMEM((3, 2 * own, features), F32),
            pltpu.VMEM((rows, features), LOW),
            pltpu.VMEM((rows, features), LOW),
            pltpu.VMEM((rows, features), F32),
            pltpu.VMEM((rows, features), F32),
            pltpu.VMEM((2, half, features), LOW),
            pltpu.VMEM((2, 2, half, features), LOW),
            pltpu.VMEM((2, FF_TILE, features), LOW),
            pltpu.VMEM((own_tiles, FF_TILE, features), LOW),
            dma((2, n)), dma((2, n)), dma((2,)), dma((2, 2)),
            pltpu.SemaphoreType.REGULAR((2,)),
            dma((4,)), dma((6,)), dma((2, 2)), dma((2,)), dma((own_tiles,)),
        ],
        compiler_params=pltpu.CompilerParams(
            collective_id=2, has_side_effects=True, vmem_limit_bytes=62 * MIB
        ),
        cost_estimate=pl.CostEstimate(
            flops=2 * 9 * n * rows * features * 2 * own, bytes_accessed=500 * MIB, transcendentals=0
        ),
        name="dense",
    )(normed, cotangents, *own_weights, *partner_weights)


def normed_back_kernel(
    grads, weights, partner_weights, hidden_in, gain, grad_mixed, out, gain_part,
    partner_grads, sent, landed,
    p_send, p_recv, rs_send, rs_recv, credit,
):
    ring = Ring()
    n = ring.chips
    rows, features = out.shape
    half = rows // 2
    r = grads.shape[2]
    ring.greet((ring.next[0], ring.next[1], ring.partner))

    def place(t, d):
        return ring.chip_far(-t if d == 0 else t)

    def swap(t, d):
        start = (place(t, d) * 2 + 1 - ring.core) * rows + d * half
        return remote(
            grads.at[:, pl.ds(pl.multiple_of(start, half), half)],
            partner_grads.at[:, t % n, half_rows(d, rows)],
            p_send.at[d, t % n],
            p_recv.at[d, t % n],
            ring.partner,
        )

    def begin(t, carry):
        for d in (0, 1):
            swap(t, d).start()
        return carry

    lax.fori_loop(1, n + 1, begin, 0)

    def reduce_copy(t, d):
        return remote(sent.at[d], landed.at[d, t % 2], rs_send.at[d], rs_recv.at[d, t % 2], ring.next[d])

    def step(t, carry):
        for d in (0, 1):
            start = (place(t, d) * 2 + ring.core) * rows + d * half
            mine = pl.ds(pl.multiple_of(start, half), half)
            part = pl.ds(d * half, half)
            swap(t, d).wait_recv()
            total = dot_nn(grads[0, mine, :], weights[0])
            for i in (1, 2):
                total += dot_nn(grads[i, mine, :], weights[i])
            for i in range(3):
                total += dot_nn(partner_grads[i, t % n, part, :], partner_weights[i])
            out[part, :] = total

        for d in (0, 1):
            part = pl.ds(d * half, half)

            @pl.when(t >= 2)
            def _():
                reduce_copy(t - 1, d).wait_recv()
                out[part, :] += landed[d, (t - 1) % 2].astype(F32)

                @pl.when(t <= n - 2)
                def _():
                    pl.semaphore_signal(
                        credit.at[d], inc=1, device_id={"dp": ring.back[d]}, device_id_type=MESH
                    )

                reduce_copy(t - 1, d).wait_send()

            @pl.when(t < n)
            def _():
                sent[d] = out[part, :].astype(LOW)

                @pl.when(t >= 3)
                def _():
                    pl.semaphore_wait(credit.at[d], 1)

                reduce_copy(t, d).start()

        return carry

    lax.fori_loop(1, n + 1, step, 0)

    def finish(t, carry):
        for d in (0, 1):
            swap(t, d).wait_send()
        return carry

    lax.fori_loop(1, n + 1, finish, 0)

    gain_part[...] = jnp.zeros_like(gain_part)

    def close(i, carry):
        span = pl.ds(pl.multiple_of(i * 16, 16), 16)
        value = hidden_in[span, :].astype(F32)
        grad = out[span, :]
        scale = lax.rsqrt(jnp.mean(value * value, axis=1, keepdims=True) + EPSILON)
        scaled = grad * gain[...]
        shift = jnp.mean(value * scaled, axis=1, keepdims=True)
        out[span, :] = grad_mixed[span, :] + scale * scaled - value * (scale * scale * scale * shift)
        gain_part[...] += jnp.sum(grad * value * scale, axis=0, keepdims=True)
        return carry

    lax.fori_loop(0, rows // 16, close, 0)


def normed_back(grads, weights, partner_weights, hidden_in, gain, grad_mixed):
    tokens, r = grads.shape[1:]
    features = weights.shape[2]
    devices = lax.axis_size("dp")
    n = devices // 2
    rows = tokens // devices
    half = rows // 2
    vmem = pl.BlockSpec(memory_space=pltpu.VMEM)
    dma = pltpu.SemaphoreType.DMA
    return pl.pallas_call(
        normed_back_kernel,
        out_shape=(
            jax.ShapeDtypeStruct((rows, features), F32),
            jax.ShapeDtypeStruct((1, features), F32),
        ),
        in_specs=[vmem] * 6,
        out_specs=(vmem, vmem),
        scratch_shapes=[
            pltpu.VMEM((3, n, rows, r), LOW),
            pltpu.VMEM((2, half, features), LOW),
            pltpu.VMEM((2, 2, half, features), LOW),
            dma((2, n)), dma((2, n)), dma((2,)), dma((2, 2)),
            pltpu.SemaphoreType.REGULAR((2,)),
        ],
        compiler_params=pltpu.CompilerParams(
            collective_id=3, has_side_effects=True, vmem_limit_bytes=40 * MIB
        ),
        cost_estimate=pl.CostEstimate(
            flops=2 * n * rows * features * 6 * r, bytes_accessed=320 * MIB, transcendentals=0
        ),
        name="normed_back",
    )(grads, weights, partner_weights, hidden_in, gain, grad_mixed)


def gain_total_kernel(part, out, landed, send_sem, recv_sem, local_sem):
    columns, packs = lax.axis_size("dp"), lax.axis_size("rep")
    devices = columns * packs
    me = lax.axis_index("rep") * columns + lax.axis_index("dp")
    barrier = pltpu.get_barrier_semaphore()

    def other(k):
        to = lax.rem(me + k, devices)
        return {"dp": to % columns, "rep": to // columns}

    def greet(k, carry):
        pl.semaphore_signal(barrier, inc=1, device_id=other(k), device_id_type=MESH)
        return carry

    lax.fori_loop(1, devices, greet, 0)
    pl.semaphore_wait(barrier, devices - 1)

    def copy(k):
        return pltpu.make_async_remote_copy(
            src_ref=part,
            dst_ref=landed.at[me],
            send_sem=send_sem.at[k],
            recv_sem=recv_sem.at[k],
            device_id=other(k),
            device_id_type=MESH,
        )

    def begin(k, carry):
        copy(k).start()
        return carry

    lax.fori_loop(1, devices, begin, 0)
    keep = pltpu.make_async_copy(part, landed.at[me], local_sem)
    keep.start()
    keep.wait()

    def wait(k, carry):
        copy(k).wait()
        return carry

    lax.fori_loop(1, devices, wait, 0)
    out[...] = lax.fori_loop(1, devices, lambda i, total: total + landed[i], landed[0])


def gain_total(part):
    devices = lax.axis_size("dp") * lax.axis_size("rep")
    vmem = pl.BlockSpec(memory_space=pltpu.VMEM)
    dma = pltpu.SemaphoreType.DMA
    return pl.pallas_call(
        gain_total_kernel,
        out_shape=jax.ShapeDtypeStruct(part.shape, F32),
        in_specs=[vmem],
        out_specs=vmem,
        scratch_shapes=[
            pltpu.VMEM((devices,) + part.shape, F32),
            dma((devices,)), dma((devices,)), dma,
        ],
        compiler_params=pltpu.CompilerParams(collective_id=4, has_side_effects=True),
        name="gain_total",
    )(part)


def rms(values, norm_gain):
    return (
        values * lax.rsqrt(jnp.mean(values * values, axis=-1, keepdims=True) + EPSILON) * norm_gain
    )


def rms_back(values, norm_gain, grads):
    _, pullback = jax.vjp(rms, values, norm_gain)
    return pullback(grads)


def turned_rows(weight):
    parts = weight.reshape(-1, 2, HALF, weight.shape[1])
    return jnp.concatenate([-parts[:, 1:], parts[:, :1]], 1).reshape(weight.shape)


def from_partner(value):
    devices = lax.axis_size("dp")
    return lax.ppermute(value, "dp", [(i, i ^ 1) for i in range(devices)])


def pack_swap(low):
    if lax.axis_size("rep") == 2:
        return lax.ppermute(low, "rep", [(0, 1), (1, 0)])
    return lax.psum(low, "rep")


def pack_add(low, other):
    if lax.axis_size("rep") == 2:
        return low.astype(F32) + other.astype(F32)
    return other.astype(F32)


def together(*values):
    return lax.optimization_barrier(values)


def body(
    tokens,
    attention_gain,
    query_weight,
    key_weight,
    value_weight,
    output_weight,
    dense_gain,
    gate_weight,
    up_weight,
    down_weight,
    block_document,
    document_tail,
    cotangent,
):
    devices = lax.axis_size("dp")
    chips = devices // 2
    core = lax.axis_index("dp") % 2
    hidden_in = tokens[0].astype(F32)
    tok_dev = hidden_in.shape[0]
    pack_tok = tok_dev * devices

    documents, tails = block_document[0], document_tail[0]
    first = jnp.sum((documents[None, :] < documents[:, None]).astype(jnp.int32), axis=1)
    last = jnp.concatenate([documents[1:] != documents[:-1], jnp.ones((1,), bool)])
    doc_ids = jnp.arange(tails.shape[0], dtype=jnp.int32)
    own_tail = jnp.sum((documents[:, None] == doc_ids[None, :]) * tails[None, :], axis=1)
    tail = jnp.where(last, own_tail, BLOCK).astype(jnp.int32)
    block_index = jnp.arange(documents.shape[0], dtype=jnp.int32)
    inside = jnp.arange(BLOCK, dtype=jnp.int32)
    position = ((block_index - first)[:, None] * BLOCK + inside[None, :]).reshape(-1)
    frequency = ROPE_BASE ** (-(jnp.arange(HALF, dtype=F32) * (2.0 / HEAD_DIM)))
    angles = position.astype(F32)[None, :] * frequency[:, None]
    cos_t, sin_t = jnp.cos(angles), jnp.sin(angles)
    r = query_weight.shape[0]

    def rows_of(table):
        mine = lax.dynamic_index_in_dim(
            table.reshape(HALF, chips, 2, tok_dev), core, axis=2, keepdims=False
        )
        return jnp.tile(mine.transpose(1, 2, 0), (1, 1, r // HALF))

    normed = rms(hidden_in, attention_gain).astype(LOW)
    stacked = jnp.concatenate(
        [
            query_weight,
            turned_rows(query_weight),
            key_weight,
            turned_rows(key_weight),
            value_weight,
        ],
        0,
    )
    qkv, normed_all = gather_project(normed, stacked, rows_of(cos_t), rows_of(sin_t))

    order = ring_order(chips)
    walk = [2 * chip + k for chip in order for k in (0, 1)]
    lanes = [[2 * chip + k for chip in order] for k in (0, 1)]
    full_output = lax.all_gather(output_weight, "dp", axis=0, tiled=True, axis_index_groups=[walk])
    grad_low = cotangent[0]
    cotangents = lax.all_gather(
        grad_low, "dp", axis=0, tiled=True, axis_index_groups=lanes
    ).reshape(chips, tok_dev, -1)
    gate_other, up_other, down_other = (
        from_partner(gate_weight),
        from_partner(up_weight),
        from_partner(down_weight),
    )
    qkv_weight = jnp.stack([query_weight, key_weight, value_weight])
    qkv_other = from_partner(qkv_weight)

    attended, log_total = attend(first, tail, qkv)
    attended_blocks = lax.all_to_all(
        attended.reshape(devices, tok_dev, r), "dp", split_axis=0, concat_axis=0, tiled=True
    )
    attended_here = jnp.concatenate([attended_blocks[i] for i in walk], 1)
    mixed = hidden_in + dot_nn(attended_here, full_output)
    normed_two = rms(mixed, dense_gain).astype(LOW)

    grad_normed_two, out_parts, _, gate_low, up_low, down_low = dense(
        normed_two,
        cotangents,
        (gate_weight, up_weight, down_weight),
        (gate_other, up_other, down_other),
    )
    out_sum = lax.psum_scatter(
        out_parts.reshape(chips * tok_dev, -1),
        "dp",
        scatter_dimension=0,
        tiled=True,
        axis_index_groups=lanes,
    )
    gate_there = pack_swap(gate_low)

    grad_mixed_norm, dense_gain_part = rms_back(mixed, dense_gain, grad_normed_two)
    grad_mixed = grad_low.astype(F32) + grad_mixed_norm
    grad_mixed_low = grad_mixed.astype(LOW)
    grad_attended = dot_nt(grad_mixed_low, full_output).astype(LOW)
    grad_blocks = jnp.stack(
        [grad_attended[:, walk.index(i) * r : (walk.index(i) + 1) * r] for i in range(devices)]
    )
    grad_heads = lax.all_to_all(
        grad_blocks, "dp", split_axis=0, concat_axis=0, tiled=True
    ).reshape(pack_tok, r)

    grad_heads, gate_there = together(grad_heads, gate_there)
    up_low, _ = together(up_low, gate_there)
    up_there = pack_swap(up_low)
    grads = attend_back(first, tail, qkv, grad_heads, attended, log_total, cos_t, sin_t)
    by_core = grads.reshape(3, chips, 2, tok_dev, r)
    swapped = from_partner(lax.dynamic_index_in_dim(by_core, 1 - core, axis=2, keepdims=False))
    mine = lax.dynamic_index_in_dim(by_core, core, axis=2, keepdims=False)
    normed_rows = normed_all.reshape(chips * tok_dev, -1)

    def weight_part(value):
        return lax.dot_general(
            value.reshape(3, chips * tok_dev, r),
            normed_rows,
            (((1,), (0,)), ((), ())),
            preferred_element_type=F32,
        )

    qkv_there = from_partner(weight_part(swapped).astype(LOW))
    qkv_low = (weight_part(mine) + qkv_there.astype(F32)).astype(LOW)

    output_part = dot_tn(attended_here, grad_mixed_low).astype(LOW)
    grads, output_part, out_sum, up_there = together(grads, output_part, out_sum, up_there)
    output_grad = lax.psum_scatter(
        output_part, "dp", scatter_dimension=0, tiled=True, axis_index_groups=[walk]
    )
    down_low, _ = together(down_low, up_there)
    down_there = pack_swap(down_low)
    qkv_other_sum = pack_swap(qkv_low)
    input_grad, attention_gain_part = normed_back(
        grads, qkv_weight, qkv_other, tokens[0], attention_gain[None], grad_mixed
    )
    input_grad, out_sum, gate_there, up_there, down_there, qkv_other_sum, output_grad = together(
        input_grad, out_sum, gate_there, up_there, down_there, qkv_other_sum, output_grad
    )
    output_there = pack_swap(output_grad)
    gain_parts = jnp.stack([attention_gain_part[0], dense_gain_part])
    gain_totals = gain_total(gain_parts.reshape(2, -1, 128)).reshape(2, -1)
    layer_out = mixed + out_sum.astype(F32)
    return (
        layer_out[None].astype(LOW),
        input_grad[None],
        gain_totals[0],
        pack_add(qkv_low[0], qkv_other_sum[0]),
        pack_add(qkv_low[1], qkv_other_sum[1]),
        pack_add(qkv_low[2], qkv_other_sum[2]),
        pack_add(output_grad, output_there),
        gain_totals[1],
        pack_add(gate_low, gate_there),
        pack_add(up_low, up_there),
        pack_add(down_low, down_there),
    )


def solution(mesh):
    return jax.shard_map(
        body,
        mesh=mesh,
        in_specs=(
            P("rep", "dp", None),
            P(),
            P("dp", None),
            P("dp", None),
            P("dp", None),
            P("dp", None),
            P(),
            P("dp", None),
            P("dp", None),
            P("dp", None),
            P("rep", None),
            P("rep", None),
            P("rep", "dp", None),
        ),
        out_specs=(
            P("rep", "dp", None),
            P("rep", "dp", None),
            P(),
            P("dp", None),
            P("dp", None),
            P("dp", None),
            P("dp", None),
            P(),
            P("dp", None),
            P("dp", None),
            P("dp", None),
        ),
        check_vma=False,
    )
```

```python
import functools
import math

import jax
import jax.numpy as jnp
from jax import lax
from jax.experimental import pallas as pl
from jax.experimental.pallas import tpu as pltpu
from jax.sharding import PartitionSpec as P

HEAD_DIM = 64
HALF = HEAD_DIM // 2
BLOCK = 128
CHUNK = 512
FF_TILE = 256
EPSILON = 1e-05
ROPE_BASE = 130000.0
MASKED_SCORE = -1e30
MESH = pl.DeviceIdType.MESH
MIB = 2**20
LOW = jnp.bfloat16
F32 = jnp.float32


def dot_nn(a, b):
    return lax.dot_general(a, b, (((1,), (0,)), ((), ())), preferred_element_type=F32)


def dot_nt(a, b):
    return lax.dot_general(a, b, (((1,), (1,)), ((), ())), preferred_element_type=F32)


def dot_tn(a, b):
    return lax.dot_general(a, b, (((0,), (0,)), ((), ())), preferred_element_type=F32)


def grid_of(chips):
    depth = 4 if chips % 8 == 0 else 2
    return depth, chips // depth


def chip_at(place, chips):
    depth, width = grid_of(chips)
    place = lax.rem(place + chips, chips)
    later = place - depth
    row, column = later // (width - 1), later % (width - 1)
    odd = row % 2
    far = (depth - 1 - row) * width + 1 + column + odd * (width - 2 - 2 * column)
    return jnp.where(place < depth, place * width, far)


def place_of(chip, chips):
    depth, width = grid_of(chips)
    z, x = chip // width, chip % width
    row = depth - 1 - z
    odd = row % 2
    column = x - 1 + odd * (width - 2 * x)
    return jnp.where(x == 0, z, depth + row * (width - 1) + column)


def ring_order(chips):
    depth, width = grid_of(chips)
    order = [z * width for z in range(depth)]
    for row in range(depth):
        columns = list(range(1, width))
        order += [(depth - 1 - row) * width + x for x in (columns[::-1] if row % 2 else columns)]
    return order


class Ring:
    def __init__(self):
        self.chips = lax.axis_size("dp") // 2
        me = lax.axis_index("dp")
        self.core = me % 2
        self.chip = me // 2
        self.partner = self.chip * 2 + 1 - self.core
        self.place = place_of(self.chip, self.chips)
        self.next = (self.device(1), self.device(-1))
        self.back = (self.next[1], self.next[0])

    def chip_far(self, steps):
        return chip_at(self.place + steps, self.chips)

    def device(self, steps):
        return self.chip_far(steps) * 2 + self.core

    def greet(self, others):
        barrier = pltpu.get_barrier_semaphore()
        for other in others:
            pl.semaphore_signal(barrier, inc=1, device_id={"dp": other}, device_id_type=MESH)
        pl.semaphore_wait(barrier, len(others))


def remote(src, dst, send_sem, recv_sem, device):
    return pltpu.make_async_remote_copy(
        src_ref=src,
        dst_ref=dst,
        send_sem=send_sem,
        recv_sem=recv_sem,
        device_id={"dp": device},
        device_id_type=MESH,
    )


def half_rows(direction, rows):
    return pl.ds(direction * (rows // 2), rows // 2)


def turned(u):
    parts = []
    for at in range(0, u.shape[1], HEAD_DIM):
        parts += [-u[:, at + HALF : at + HEAD_DIM], u[:, at : at + HALF]]
    return jnp.concatenate(parts, 1)


def gather_project_kernel(
    tokens, gain, query_w, key_w, value_w, output_w, cos_t, sin_t, qkv, gathered, output_all,
    normed, partner_weights, x_buf, staged,
    ag_send, ag_recv, w_send, w_recv, q_send, q_recv, local_sem,
    o_send, o_recv, pair_send, pair_recv, rep_send, rep_recv, far_send, far_recv,
):
    ring = Ring()
    n = ring.chips
    packs, pack = lax.axis_size("rep"), lax.axis_index("rep")
    rows = normed.shape[0]
    half = rows // 2
    r = qkv.shape[2]
    own_weights = (query_w, key_w, value_w)
    barrier = pltpu.get_barrier_semaphore()
    for k in range(1, packs):
        pl.semaphore_signal(
            barrier, inc=1, device_id={"rep": lax.rem(pack + k, packs)}, device_id_type=MESH
        )
    for other in (ring.next[0], ring.next[1], ring.partner):
        pl.semaphore_signal(barrier, inc=1, device_id={"dp": other}, device_id_type=MESH)
    pl.semaphore_wait(barrier, 3 + packs - 1)

    def normalize(i, carry):
        span = pl.ds(pl.multiple_of(i * 32, 32), 32)
        value = tokens[span, :].astype(F32)
        scale = lax.rsqrt(jnp.mean(value * value, axis=1, keepdims=True) + EPSILON)
        normed[span, :] = (value * scale * gain[...]).astype(LOW)
        return carry

    lax.fori_loop(0, rows // 32, normalize, 0)

    def hop(t, d):
        chip = ring.chip_far((1 - t) if d == 0 else (t - 1))
        return chip, half_rows(d, rows)

    def send(t, d, first):
        chip, part = hop(t, d)
        src = normed.at[part] if first else gathered.at[chip, part]
        return remote(src, gathered.at[chip, part], ag_send.at[d, t - 1], ag_recv.at[d, t - 1], ring.next[d])

    out_rows, features = output_w.shape
    share = out_rows // packs
    spot = ring.place * 2 + ring.core

    def share_of(q, d):
        return pl.ds(pl.multiple_of(q * share, share), share), pl.ds(d * (features // 2), features // 2)

    def block_at(t, d, q, core):
        place = lax.rem(ring.place + (n - t if d == 0 else t), n)
        at_rows, columns = share_of(q, d)
        return output_all.at[place * 2 + core, at_rows, columns]

    def o_copy(t, d, first):
        at_rows, columns = share_of(pack, d)
        src = output_w.at[at_rows, columns] if first else block_at(t - 1, d, pack, ring.core)
        return remote(
            src, block_at(t - 1, d, pack, ring.core), o_send.at[d, t], o_recv.at[d, t], ring.next[d]
        )

    def pair_copy(t, d):
        block = block_at(t, d, pack, ring.core)
        return remote(block, block, pair_send.at[d, t], pair_recv.at[d, t], ring.partner)

    def rep_copy(t, d, k):
        block = block_at(t, d, pack, ring.core)
        return pltpu.make_async_remote_copy(
            src_ref=block,
            dst_ref=block,
            send_sem=rep_send.at[k - 1, d, t],
            recv_sem=rep_recv.at[k - 1, d, t],
            device_id={"rep": lax.rem(pack + k, packs)},
            device_id_type=MESH,
        )

    def far_copy(t, d, k):
        block = block_at(t, d, lax.rem(pack + packs - k, packs), ring.core)
        return remote(block, block, far_send.at[k - 1, d, t], far_recv.at[k - 1, d, t], ring.partner)

    def forward_far(t):
        for d in (0, 1):
            for k in range(1, packs):
                rep_copy(t, d, k).wait_recv()
                far_copy(t, d, k).start()

    for d in (0, 1):
        send(1, d, True).start()
    for d in (0, 1):
        o_copy(1, d, True).start()
    own_rows = remote(output_w, output_all.at[spot], local_sem.at[3], local_sem.at[4], ring.partner)
    own_rows.start()
    own_keep = pltpu.make_async_copy(output_w, output_all.at[spot], local_sem.at[5])
    own_keep.start()
    swaps = [
        remote(own_weights[i], partner_weights.at[i], w_send.at[i], w_recv.at[i], ring.partner)
        for i in range(3)
    ]
    for swap in swaps:
        swap.start()
    keep = pltpu.make_async_copy(normed, gathered.at[ring.chip], local_sem.at[2])
    keep.start()

    def project_block(t, from_input):
        x = normed[...] if from_input else x_buf[...]
        places = [ring.chip_far(-t), ring.chip_far(t)]
        starts = [
            pl.multiple_of((places[d] * 2 + ring.core) * rows + d * half, half) for d in (0, 1)
        ]

        def table(source):
            wide = [source[:, pl.ds(starts[d], half)] for d in (0, 1)]
            return jnp.concatenate(
                [jnp.concatenate([w] * (r // HALF), 0).T for w in wide], 0
            )

        cos, sin = table(cos_t), table(sin_t)

        def heads(w):
            query, key, value = [dot_nt(x, w[i][...]) for i in range(3)]
            return (
                (query * cos + turned(query) * sin).astype(LOW),
                (key * cos + turned(key) * sin).astype(LOW),
                value.astype(LOW),
            )

        for i, value in enumerate(heads(own_weights)):
            for d in (0, 1):
                qkv[i, pl.ds(starts[d], half), :] = value[d * half : (d + 1) * half]
        if from_input:
            for swap in swaps:
                swap.wait()
        for i, value in enumerate(heads([partner_weights.at[i] for i in range(3)])):
            staged[t, i] = value
        for d in (0, 1):
            remote(
                staged.at[t, :, half_rows(d, rows)],
                qkv.at[:, pl.ds(starts[d], half)],
                q_send.at[d, t],
                q_recv.at[d, t],
                ring.partner,
            ).start()

    project_block(0, True)

    def step(t, carry):
        for d in (0, 1):
            send(t, d, False).wait_recv()

        @pl.when(t < n - 1)
        def _():
            for d in (0, 1):
                send(t + 1, d, False).start()

        for d in (0, 1):
            o_copy(t, d, False).wait_recv()

        @pl.when(t < n - 1)
        def _():
            for d in (0, 1):
                o_copy(t + 1, d, False).start()

        for d in (0, 1):
            for k in range(1, packs):
                rep_copy(t, d, k).start()
            pair_copy(t, d).start()

        @pl.when(t > 1)
        def _():
            forward_far(t - 1)

        loads = []
        for d in (0, 1):
            chip, part = hop(t + 1, d)
            loads.append(pltpu.make_async_copy(gathered.at[chip, part], x_buf.at[part], local_sem.at[d]))
        for load in loads:
            load.start()
        for load in loads:
            load.wait()
        project_block(t, False)
        return carry

    lax.fori_loop(1, n, step, 0)
    forward_far(n - 1)

    def finish(t, carry):
        for d in (0, 1):
            send(t, d, False).wait_send()
            o_copy(t, d, False).wait_send()
            pair_copy(t, d).wait()
            for k in range(1, packs):
                rep_copy(t, d, k).wait_send()
                far_copy(t, d, k).wait()
        return carry

    lax.fori_loop(1, n, finish, 0)
    own_rows.wait()
    own_keep.wait()

    def finish_heads(t, carry):
        for d in (0, 1):
            done = remote(
                staged.at[t, :, half_rows(d, rows)],
                qkv.at[:, half_rows(d, rows)],
                q_send.at[d, t],
                q_recv.at[d, t],
                ring.partner,
            )
            done.wait_send()
            done.wait_recv()
        return carry

    lax.fori_loop(0, n, finish_heads, 0)
    keep.wait()


def gather_project(tokens, gain, weights, output_weight, cos_t, sin_t):
    rows, features = tokens.shape
    r = weights[0].shape[0]
    devices = lax.axis_size("dp")
    packs = lax.axis_size("rep")
    n = devices // 2
    vmem = pl.BlockSpec(memory_space=pltpu.VMEM)
    dma = pltpu.SemaphoreType.DMA
    return pl.pallas_call(
        gather_project_kernel,
        out_shape=(
            jax.ShapeDtypeStruct((3, devices * rows, r), LOW),
            jax.ShapeDtypeStruct((n, rows, features), LOW),
            jax.ShapeDtypeStruct((devices,) + output_weight.shape, LOW),
        ),
        in_specs=[vmem] * 8,
        out_specs=(vmem, pl.BlockSpec(memory_space=pl.ANY), pl.BlockSpec(memory_space=pl.ANY)),
        scratch_shapes=[
            pltpu.VMEM((rows, features), LOW),
            pltpu.VMEM((3, r, features), LOW),
            pltpu.VMEM((rows, features), LOW),
            pltpu.VMEM((n, 3, rows, r), LOW),
            dma((2, n)), dma((2, n)), dma((3,)), dma((3,)), dma((2, n)), dma((2, n)), dma((6,)),
            dma((2, n)), dma((2, n)), dma((2, n)), dma((2, n)),
            dma((packs - 1, 2, n)), dma((packs - 1, 2, n)),
            dma((packs - 1, 2, n)), dma((packs - 1, 2, n)),
        ],
        compiler_params=pltpu.CompilerParams(
            collective_id=1, has_side_effects=True, vmem_limit_bytes=40 * MIB
        ),
        cost_estimate=pl.CostEstimate(
            flops=4 * n * rows * features * 3 * r, bytes_accessed=320 * MIB, transcendentals=0
        ),
        name="gather_project",
    )(tokens, gain, *weights, output_weight, cos_t, sin_t)


def split_heads(u):
    heads = u.shape[1] // HEAD_DIM
    if heads == 1:
        return u
    lane = lax.broadcasted_iota(jnp.int32, u.shape, 1) // HEAD_DIM
    zero = jnp.zeros_like(u)
    return jnp.concatenate([jnp.where(lane == h, u, zero) for h in range(heads)], 0)


def join_heads(u):
    heads = u.shape[0] // HEAD_DIM
    return jnp.concatenate(
        [u[h * HEAD_DIM : (h + 1) * HEAD_DIM, h * BLOCK : (h + 1) * BLOCK] for h in range(heads)], 0
    )


def transpose_blocks(source, target):
    def one(b, carry):
        at = pl.multiple_of(b * BLOCK, BLOCK)
        target[:, pl.ds(at, BLOCK)] = source[pl.ds(at, BLOCK), :].astype(F32).T.astype(LOW)
        return carry

    lax.fori_loop(0, source.shape[0] // BLOCK, one, 0)


def window_of(b, first, tail, columns):
    start = pl.multiple_of(jnp.maximum(b - (CHUNK // BLOCK - 1), 0) * BLOCK, BLOCK)
    whole = (b - first) // (CHUNK // BLOCK)
    lowest = (first + whole * (CHUNK // BLOCK)) * BLOCK
    key_index = start + lax.broadcasted_iota(jnp.int32, (CHUNK, columns), 0)
    query_index = b * BLOCK + lax.broadcasted_iota(jnp.int32, (CHUNK, columns), 1) % BLOCK
    allowed = (
        (key_index >= lowest)
        & (key_index <= query_index)
        & (key_index < b * BLOCK + tail)
    )
    return start, whole, allowed


def walk_rows(b, tok_dev, chips):
    device = b * BLOCK // tok_dev
    spot = place_of(device // 2, chips) * 2 + device % 2
    return pl.ds(pl.multiple_of(spot * tok_dev + b * BLOCK % tok_dev, BLOCK), BLOCK)


def attend_kernel(chips, first_ref, tail_ref, qkv, attended, log_total, value_t):
    tokens, r = qkv.shape[1:]
    tok_dev = tokens // (2 * chips)
    columns = (r // HEAD_DIM) * BLOCK
    scale = 1.0 / math.sqrt(HEAD_DIM)
    transpose_blocks(qkv.at[2], value_t)

    def block(b, carry):
        at = pl.multiple_of(b * BLOCK, BLOCK)
        query = split_heads(qkv[0, pl.ds(at, BLOCK), :])
        start, whole, allowed = window_of(b, first_ref[b], tail_ref[b], columns)
        scores = dot_nt(qkv[1, pl.ds(start, CHUNK), :], query) * scale
        scores = jnp.where(allowed, scores, MASKED_SCORE)
        top = jnp.max(scores, axis=0, keepdims=True)
        weights = jnp.exp(scores - top)
        total = jnp.sum(weights, axis=0, keepdims=True)
        out = dot_nn(value_t[:, pl.ds(start, CHUNK)], weights.astype(LOW))

        def more(i, state):
            top, total, out = state
            start = pl.multiple_of(first_ref[b] * BLOCK + i * CHUNK, BLOCK)
            scores = dot_nt(qkv[1, pl.ds(start, CHUNK), :], query) * scale
            higher = jnp.maximum(top, jnp.max(scores, axis=0, keepdims=True))
            shrink = jnp.exp(top - higher)
            weights = jnp.exp(scores - higher)
            total = total * shrink + jnp.sum(weights, axis=0, keepdims=True)
            out = out * shrink + dot_nn(value_t[:, pl.ds(start, CHUNK)], weights.astype(LOW))
            return higher, total, out

        top, total, out = lax.fori_loop(0, whole, more, (top, total, out))
        log_total[pl.ds(b, 1), :] = top + jnp.log(total)
        attended[walk_rows(b, tok_dev, chips), :] = join_heads(out / total).T.astype(LOW)
        return carry

    lax.fori_loop(0, tokens // BLOCK, block, 0)


def attend(first, tail, qkv):
    tokens, r = qkv.shape[1:]
    smem = pl.BlockSpec(memory_space=pltpu.SMEM)
    vmem = pl.BlockSpec(memory_space=pltpu.VMEM)
    return pl.pallas_call(
        functools.partial(attend_kernel, lax.axis_size("dp") // 2),
        out_shape=(
            jax.ShapeDtypeStruct((tokens, r), LOW),
            jax.ShapeDtypeStruct((tokens // BLOCK, (r // HEAD_DIM) * BLOCK), F32),
        ),
        in_specs=[smem, smem, vmem],
        out_specs=(vmem, vmem),
        scratch_shapes=[pltpu.VMEM((r, tokens), LOW)],
        compiler_params=pltpu.CompilerParams(vmem_limit_bytes=40 * MIB),
        cost_estimate=pl.CostEstimate(
            flops=4 * tokens * 1024 * r * 8, bytes_accessed=120 * MIB, transcendentals=tokens * 1024
        ),
        name="attend",
    )(first, tail, qkv)


def unrotate(g, cos, sin):
    parts = []
    for h in range(g.shape[0] // HEAD_DIM):
        one = g[h * HEAD_DIM : h * HEAD_DIM + HALF]
        two = g[h * HEAD_DIM + HALF : (h + 1) * HEAD_DIM]
        parts += [one * cos + two * sin, two * cos - one * sin]
    return jnp.concatenate(parts, 0)


def attend_back_kernel(
    chips, first_ref, tail_ref, qkv, grad_out, attended, log_total, cos_t, sin_t, grads,
    key_t, grad_key, grad_value,
):
    tokens, r = qkv.shape[1:]
    tok_dev = tokens // (2 * chips)
    heads = r // HEAD_DIM
    columns = heads * BLOCK
    scale = 1.0 / math.sqrt(HEAD_DIM)
    transpose_blocks(qkv.at[1], key_t)
    grad_key[...] = jnp.zeros_like(grad_key)
    grad_value[...] = jnp.zeros_like(grad_value)

    def block(b, carry):
        at = pl.multiple_of(b * BLOCK, BLOCK)
        here = pl.ds(at, BLOCK)
        query = split_heads(qkv[0, here, :])
        walk = walk_rows(b, tok_dev, chips)
        grad_rows = grad_out[walk, :]
        grad = split_heads(grad_rows)
        product = (grad_rows.astype(F32) * attended[walk, :].astype(F32)).T
        delta = jnp.concatenate(
            [
                jnp.sum(product[h * HEAD_DIM : (h + 1) * HEAD_DIM], axis=0, keepdims=True)
                for h in range(heads)
            ],
            1,
        )
        log_row = log_total[pl.ds(b, 1), :]

        def chunk(start, allowed, grad_query):
            span = pl.ds(start, CHUNK)
            scores = dot_nt(qkv[1, span, :], query) * scale
            weights = jnp.exp(scores - log_row)
            if allowed is not None:
                weights = jnp.where(allowed, weights, 0.0)
            grad_weights = dot_nt(qkv[2, span, :], grad)
            grad_scores = (weights * (grad_weights - delta)).astype(LOW)
            grad_value[span, :] += dot_nn(weights.astype(LOW), grad)
            grad_key[span, :] += dot_nn(grad_scores, query)
            return grad_query + dot_nn(key_t[:, span], grad_scores)

        start, whole, allowed = window_of(b, first_ref[b], tail_ref[b], columns)
        grad_query = chunk(start, allowed, jnp.zeros((r, columns), F32))
        grad_query = lax.fori_loop(
            0,
            whole,
            lambda i, g: chunk(pl.multiple_of(first_ref[b] * BLOCK + i * CHUNK, BLOCK), None, g),
            grad_query,
        )
        turned = unrotate(join_heads(grad_query) * scale, cos_t[:, here], sin_t[:, here])
        grads[0, here, :] = turned.T.astype(LOW)
        return carry

    lax.fori_loop(0, tokens // BLOCK, block, 0)

    def close(b, carry):
        here = pl.ds(pl.multiple_of(b * BLOCK, BLOCK), BLOCK)
        turned = unrotate(grad_key[here, :].T * scale, cos_t[:, here], sin_t[:, here])
        grads[1, here, :] = turned.T.astype(LOW)
        grads[2, here, :] = grad_value[here, :].astype(LOW)
        return carry

    lax.fori_loop(0, tokens // BLOCK, close, 0)


def attend_back(first, tail, qkv, grad_out, attended, log_total, cos_t, sin_t):
    tokens, r = qkv.shape[1:]
    smem = pl.BlockSpec(memory_space=pltpu.SMEM)
    vmem = pl.BlockSpec(memory_space=pltpu.VMEM)
    return pl.pallas_call(
        functools.partial(attend_back_kernel, lax.axis_size("dp") // 2),
        out_shape=jax.ShapeDtypeStruct((3, tokens, r), LOW),
        in_specs=[smem, smem] + [vmem] * 6,
        out_specs=vmem,
        scratch_shapes=[
            pltpu.VMEM((r, tokens), LOW),
            pltpu.VMEM((tokens, r), F32),
            pltpu.VMEM((tokens, r), F32),
        ],
        compiler_params=pltpu.CompilerParams(vmem_limit_bytes=40 * MIB),
        cost_estimate=pl.CostEstimate(
            flops=10 * tokens * 1024 * r * 8, bytes_accessed=240 * MIB, transcendentals=tokens * 1024
        ),
        name="attend_back",
    )(first, tail, qkv, grad_out, attended, log_total, cos_t, sin_t)


def dense_kernel(
    normed, cotangents_a, cotangents_b, gate_w, up_w, down_w, gate_p, up_p, down_p,
    grad_sum, out_parts, gathered, gate_grad, up_grad, down_grad,
    weights, totals, x_buf, g_buf, out_acc, grad_acc, sent, landed, cast_buf, pair_land,
    ag_send, ag_recv, rs_send, rs_recv, credit, local_sem, w_sem, cast_sem, pair_send, pair_recv,
):
    ring = Ring()
    n = ring.chips
    rows, features = normed.shape
    half = rows // 2
    own = gate_w.shape[0]
    tiles = 2 * own // FF_TILE
    loads = []
    for i, (mine, theirs) in enumerate(((gate_w, gate_p), (up_w, up_p), (down_w, down_p))):
        loads.append(pltpu.make_async_copy(mine, weights.at[i, pl.ds(0, own)], w_sem.at[2 * i]))
        loads.append(pltpu.make_async_copy(theirs, weights.at[i, pl.ds(own, own)], w_sem.at[2 * i + 1]))
    for load in loads:
        load.start()
    ring.greet((ring.next[0], ring.next[1], ring.partner))

    def source(t, d):
        return lax.rem(ring.place + (n - t if d == 0 else t), n)

    def send(t, d, first):
        place, part = source(t - 1, d), half_rows(d, rows)
        src = normed.at[part] if first else gathered.at[place, part]
        return remote(src, gathered.at[place, part], ag_send.at[d, t - 1], ag_recv.at[d, t - 1], ring.next[d])

    def reduce_copy(t, d):
        return remote(sent.at[d], landed.at[d, t % 2], rs_send.at[d], rs_recv.at[d, t % 2], ring.next[d])

    for d in (0, 1):
        send(1, d, True).start()

    def clear(i, carry):
        span = pl.ds(pl.multiple_of(i * FF_TILE, FF_TILE), FF_TILE)
        for k in range(3):
            totals[k, span, :] = jnp.zeros((FF_TILE, features), F32)
        return carry

    lax.fori_loop(0, tiles, clear, 0)
    for load in loads:
        load.wait()

    def out_copy(t, d):
        part = half_rows(d, rows)
        return pltpu.make_async_copy(
            cast_buf.at[t % 2, part], out_parts.at[source(t, d), part], cast_sem.at[t % 2, d]
        )

    def step(t, carry):
        copies = []
        for d in (0, 1):
            part = half_rows(d, rows)
            copies.append(
                pltpu.make_async_copy((cotangents_a, cotangents_b)[d].at[source(t, d)], g_buf.at[part], local_sem.at[d])
            )
            copies[-1].start()

        @pl.when(t > 0)
        def _():
            for d in (0, 1):
                send(t, d, False).wait_recv()

            @pl.when(t < n - 1)
            def _():
                for d in (0, 1):
                    send(t + 1, d, False).start()

            more = []
            for d in (0, 1):
                part = half_rows(d, rows)
                more.append(
                    pltpu.make_async_copy(gathered.at[source(t, d), part], x_buf.at[part], local_sem.at[2 + d])
                )
                more[-1].start()
            for copy in more:
                copy.wait()

        @pl.when(t == 0)
        def _():
            x_buf[...] = normed[...]

        for copy in copies:
            copy.wait()

        out_acc[...] = jnp.zeros_like(out_acc)
        grad_acc[...] = jnp.zeros_like(grad_acc)

        def tile(i, carry):
            span = pl.ds(pl.multiple_of(i * FF_TILE, FF_TILE), FF_TILE)
            x = x_buf[...]
            g = g_buf[...]
            gate = dot_nt(x, weights[0, span, :])
            up = dot_nt(x, weights[1, span, :])
            grad_hidden = dot_nt(g, weights[2, span, :])
            sigma = 1.0 / (1.0 + jnp.exp(-gate))
            silu = gate * sigma
            hidden = (silu * up).astype(LOW)
            grad_gate = (grad_hidden * up * sigma * (1.0 + gate * (1.0 - sigma))).astype(LOW)
            grad_up = (grad_hidden * silu).astype(LOW)
            out_acc[...] += dot_nn(hidden, weights[2, span, :])
            grad_acc[...] += dot_nn(grad_gate, weights[0, span, :])
            grad_acc[...] += dot_nn(grad_up, weights[1, span, :])
            totals[0, span, :] += dot_tn(grad_gate, x)
            totals[1, span, :] += dot_tn(grad_up, x)
            totals[2, span, :] += dot_tn(hidden, g)
            return carry

        lax.fori_loop(0, tiles, tile, 0)

        @pl.when(t >= 2)
        def _():
            for d in (0, 1):
                out_copy(t - 2, d).wait()

        cast_buf[t % 2] = out_acc[...].astype(LOW)
        for d in (0, 1):
            out_copy(t, d).start()

        @pl.when(t == 0)
        def _():
            grad_sum[...] = grad_acc[...]

        @pl.when(t > 0)
        def _():
            for d in (0, 1):
                part = pl.ds(d * half, half)

                @pl.when(t >= 2)
                def _():
                    reduce_copy(t - 1, d).wait_recv()
                    grad_acc[part, :] += landed[d, (t - 1) % 2].astype(F32)

                    @pl.when(t <= n - 2)
                    def _():
                        pl.semaphore_signal(
                            credit.at[d], inc=1, device_id={"dp": ring.back[d]}, device_id_type=MESH
                        )

                    reduce_copy(t - 1, d).wait_send()

                sent[d] = grad_acc[part, :].astype(LOW)

                @pl.when(t >= 3)
                def _():
                    pl.semaphore_wait(credit.at[d], 1)

                reduce_copy(t, d).start()

        return carry

    lax.fori_loop(0, n, step, 0)
    for t in (n - 2, n - 1):
        for d in (0, 1):
            out_copy(t, d).wait()

    own_tiles = 3 * own // FF_TILE

    def tile_of(i, first):
        return i // (own // FF_TILE), pl.ds(
            pl.multiple_of(first + (i % (own // FF_TILE)) * FF_TILE, FF_TILE), FF_TILE
        )

    def pair_copy(i):
        return remote(cast_buf.at[i % 2], pair_land.at[i], pair_send.at[i % 2], pair_recv.at[i], ring.partner)

    def give(i, carry):
        @pl.when(i >= 2)
        def _():
            pair_copy(i - 2).wait_send()

        k, span = tile_of(i, own)
        cast_buf[i % 2] = totals[k, span, :].astype(LOW)
        pair_copy(i).start()
        return carry

    lax.fori_loop(0, own_tiles, give, 0)
    for i in (own_tiles - 2, own_tiles - 1):
        pair_copy(i).wait_send()

    def total_copy(i):
        target = (gate_grad, up_grad, down_grad)[i // (own // FF_TILE)]
        span = pl.ds((i % (own // FF_TILE)) * FF_TILE, FF_TILE)
        return pltpu.make_async_copy(cast_buf.at[i % 2], target.at[span], cast_sem.at[i % 2, 0])

    for i in range(own_tiles):
        if i >= 2:
            total_copy(i - 2).wait()
        pair_copy(i).wait_recv()
        k, span = tile_of(i, 0)
        cast_buf[i % 2] = (totals[k, span, :] + pair_land[i].astype(F32)).astype(LOW)
        total_copy(i).start()

    for d in (0, 1):
        part = pl.ds(d * half, half)
        reduce_copy(n - 1, d).wait_recv()
        grad_sum[part, :] += landed[d, (n - 1) % 2].astype(F32)
        reduce_copy(n - 1, d).wait_send()

    for i in (own_tiles - 2, own_tiles - 1):
        total_copy(i).wait()

    def finish(t, carry):
        for d in (0, 1):
            send(t, d, False).wait_send()
        return carry

    lax.fori_loop(1, n, finish, 0)


def dense(normed, cotangents, own_weights, partner_weights):
    rows, features = normed.shape
    n = lax.axis_size("dp") // 2
    own = own_weights[0].shape[0]
    half = rows // 2
    vmem = pl.BlockSpec(memory_space=pltpu.VMEM)
    hbm = pl.BlockSpec(memory_space=pl.ANY)
    dma = pltpu.SemaphoreType.DMA
    own_tiles = 3 * own // FF_TILE
    return pl.pallas_call(
        dense_kernel,
        out_shape=(
            jax.ShapeDtypeStruct((rows, features), F32),
            jax.ShapeDtypeStruct((n, rows, features), LOW),
            jax.ShapeDtypeStruct((n, rows, features), LOW),
            jax.ShapeDtypeStruct((own, features), LOW),
            jax.ShapeDtypeStruct((own, features), LOW),
            jax.ShapeDtypeStruct((own, features), LOW),
        ),
        in_specs=[vmem] + [hbm] * 8,
        out_specs=(vmem,) + (hbm,) * 5,
        scratch_shapes=[
            pltpu.VMEM((3, 2 * own, features), LOW),
            pltpu.VMEM((3, 2 * own, features), F32),
            pltpu.VMEM((rows, features), LOW),
            pltpu.VMEM((rows, features), LOW),
            pltpu.VMEM((rows, features), F32),
            pltpu.VMEM((rows, features), F32),
            pltpu.VMEM((2, half, features), LOW),
            pltpu.VMEM((2, 2, half, features), LOW),
            pltpu.VMEM((2, FF_TILE, features), LOW),
            pltpu.VMEM((own_tiles, FF_TILE, features), LOW),
            dma((2, n)), dma((2, n)), dma((2,)), dma((2, 2)),
            pltpu.SemaphoreType.REGULAR((2,)),
            dma((4,)), dma((6,)), dma((2, 2)), dma((2,)), dma((own_tiles,)),
        ],
        compiler_params=pltpu.CompilerParams(
            collective_id=2, has_side_effects=True, vmem_limit_bytes=62 * MIB
        ),
        cost_estimate=pl.CostEstimate(
            flops=2 * 9 * n * rows * features * 2 * own, bytes_accessed=500 * MIB, transcendentals=0
        ),
        name="dense",
    )(normed, *cotangents, *own_weights, *partner_weights)


def normed_back_kernel(
    grads, weights, partner_weights, hidden_in, gain, grad_mixed, normed_all,
    out, gain_part, query_total, key_total, value_total,
    partner_grads, sent, landed, x_buf, parts, joined, pair_out, pair_land, rep_land,
    p_send, p_recv, rs_send, rs_recv, credit, x_sem, pair_sem, rep_send, rep_recv,
):
    ring = Ring()
    n = ring.chips
    rows, features = out.shape
    half = rows // 2
    r = grads.shape[2]
    packs, pack = lax.axis_size("rep"), lax.axis_index("rep")
    barrier = pltpu.get_barrier_semaphore()
    for k in range(1, packs):
        pl.semaphore_signal(
            barrier, inc=1, device_id={"rep": lax.rem(pack + k, packs)}, device_id_type=MESH
        )
    for other in (ring.next[0], ring.next[1], ring.partner):
        pl.semaphore_signal(barrier, inc=1, device_id={"dp": other}, device_id_type=MESH)
    pl.semaphore_wait(barrier, 3 + packs - 1)

    def place(t, d):
        return ring.chip_far(-t if d == 0 else t)

    def swap(t, d):
        start = (place(t, d) * 2 + 1 - ring.core) * rows + d * half
        return remote(
            grads.at[:, pl.ds(pl.multiple_of(start, half), half)],
            partner_grads.at[:, t % n, half_rows(d, rows)],
            p_send.at[d, t % n],
            p_recv.at[d, t % n],
            ring.partner,
        )

    def begin(t, carry):
        for d in (0, 1):
            swap(t, d).start()
        return carry

    lax.fori_loop(1, n + 1, begin, 0)

    def reduce_copy(t, d):
        return remote(sent.at[d], landed.at[d, t % 2], rs_send.at[d], rs_recv.at[d, t % 2], ring.next[d])

    def mine(t, d):
        start = (place(t, d) * 2 + ring.core) * rows + d * half
        return pl.ds(pl.multiple_of(start, half), half)

    def load(t, d):
        part = half_rows(d, rows)
        return pltpu.make_async_copy(normed_all.at[place(t, d), part], x_buf.at[t % 2, part], x_sem.at[t % 2, d])

    def block_grads(t):
        return jnp.concatenate(
            [jnp.concatenate([grads[i, mine(t, d), :] for d in (0, 1)], 0) for i in range(3)]
            + [partner_grads[i, t % n] for i in range(3)],
            1,
        )

    def weight_parts(t):
        for d in (0, 1):
            load(t, d).wait()
        parts[...] += dot_tn(block_grads(t), x_buf[t % 2])

    def pair_copy():
        return remote(pair_out, pair_land, pair_sem.at[0], pair_sem.at[1], ring.partner)

    def rep_copy(k):
        return pltpu.make_async_remote_copy(
            src_ref=pair_out,
            dst_ref=rep_land.at[k - 1],
            send_sem=rep_send.at[k - 1],
            recv_sem=rep_recv.at[k - 1],
            device_id={"rep": lax.rem(pack + k, packs)},
            device_id_type=MESH,
        )

    parts[...] = jnp.zeros_like(parts)
    for i in range(3):
        joined[pl.ds(i * r, r), :] = weights[i]
        joined[pl.ds((3 + i) * r, r), :] = partner_weights[i]
    middle = n // 2

    def step(t, carry):
        @pl.when(t <= middle)
        def _():
            for d in (0, 1):
                load(2 * t - 1, d).start()
                load(2 * t, d).start()

        @pl.when(t == 1)
        def _():
            for d in (0, 1):
                swap(t, d).wait_recv()

        out[...] = dot_nn(block_grads(t), joined[...])

        for d in (0, 1):
            part = pl.ds(d * half, half)

            @pl.when(t >= 2)
            def _():
                reduce_copy(t - 1, d).wait_recv()
                out[part, :] += landed[d, (t - 1) % 2].astype(F32)

                @pl.when(t <= n - 2)
                def _():
                    pl.semaphore_signal(
                        credit.at[d], inc=1, device_id={"dp": ring.back[d]}, device_id_type=MESH
                    )

                reduce_copy(t - 1, d).wait_send()

            @pl.when(t < n)
            def _():
                sent[d] = out[part, :].astype(LOW)

                @pl.when(t >= 3)
                def _():
                    pl.semaphore_wait(credit.at[d], 1)

                reduce_copy(t, d).start()

        @pl.when(t == 1)
        def _():
            def arrived(k, carry):
                for d in (0, 1):
                    swap(k, d).wait_recv()
                return carry

            lax.fori_loop(2, n + 1, arrived, 0)

        @pl.when(t <= middle)
        def _():
            weight_parts(2 * t - 1)
            weight_parts(2 * t)

        @pl.when(t == middle)
        def _():
            for i in range(3):
                pair_out[i] = parts[pl.ds((3 + i) * r, r), :].astype(LOW)
            pair_copy().start()

        @pl.when(t == middle + 1)
        def _():
            pair_copy().wait()
            for i in range(3):
                pair_out[i] = (parts[pl.ds(i * r, r), :] + pair_land[i].astype(F32)).astype(LOW)
            for k in range(1, packs):
                rep_copy(k).start()
            rep_land[packs - 1] = pair_out[...]

        return carry

    lax.fori_loop(1, n + 1, step, 0)

    gain_part[...] = jnp.zeros_like(gain_part)

    def close(i, carry):
        span = pl.ds(pl.multiple_of(i * 16, 16), 16)
        value = hidden_in[span, :].astype(F32)
        grad = out[span, :]
        scale = lax.rsqrt(jnp.mean(value * value, axis=1, keepdims=True) + EPSILON)
        scaled = grad * gain[...]
        shift = jnp.mean(value * scaled, axis=1, keepdims=True)
        out[span, :] = grad_mixed[span, :] + scale * scaled - value * (scale * scale * scale * shift)
        gain_part[...] += jnp.sum(grad * value * scale, axis=0, keepdims=True)
        return carry

    lax.fori_loop(0, rows // 16, close, 0)

    def finish(t, carry):
        for d in (0, 1):
            swap(t, d).wait_send()
        return carry

    lax.fori_loop(1, n + 1, finish, 0)
    for k in range(1, packs):
        rep_copy(k).wait()
    for i, total in enumerate((query_total, key_total, value_total)):
        value = rep_land[lax.rem(pack + packs - 1, packs), i].astype(F32)
        for q in range(1, packs):
            value += rep_land[lax.rem(pack + 2 * packs - q - 1, packs), i].astype(F32)
        total[...] = value


def normed_back(grads, weights, partner_weights, hidden_in, gain, grad_mixed, normed_all):
    tokens, r = grads.shape[1:]
    features = weights.shape[2]
    devices = lax.axis_size("dp")
    packs = lax.axis_size("rep")
    n = devices // 2
    rows = tokens // devices
    half = rows // 2
    vmem = pl.BlockSpec(memory_space=pltpu.VMEM)
    dma = pltpu.SemaphoreType.DMA
    return pl.pallas_call(
        normed_back_kernel,
        out_shape=(
            jax.ShapeDtypeStruct((rows, features), F32),
            jax.ShapeDtypeStruct((1, features), F32),
        )
        + (jax.ShapeDtypeStruct((r, features), F32),) * 3,
        in_specs=[vmem] * 6 + [pl.BlockSpec(memory_space=pl.ANY)],
        out_specs=(vmem,) * 5,
        scratch_shapes=[
            pltpu.VMEM((3, n, rows, r), LOW),
            pltpu.VMEM((2, half, features), LOW),
            pltpu.VMEM((2, 2, half, features), LOW),
            pltpu.VMEM((2, rows, features), LOW),
            pltpu.VMEM((6 * r, features), F32),
            pltpu.VMEM((6 * r, features), LOW),
            pltpu.VMEM((3, r, features), LOW),
            pltpu.VMEM((3, r, features), LOW),
            pltpu.VMEM((packs, 3, r, features), LOW),
            dma((2, n)), dma((2, n)), dma((2,)), dma((2, 2)),
            pltpu.SemaphoreType.REGULAR((2,)),
            dma((2, 2)), dma((2,)), dma((packs - 1,)), dma((packs - 1,)),
        ],
        compiler_params=pltpu.CompilerParams(
            collective_id=3, has_side_effects=True, vmem_limit_bytes=56 * MIB
        ),
        cost_estimate=pl.CostEstimate(
            flops=2 * n * rows * features * 12 * r, bytes_accessed=320 * MIB, transcendentals=0
        ),
        name="normed_back",
    )(grads, weights, partner_weights, hidden_in, gain, grad_mixed, normed_all)


def gain_total_kernel(part, out, near_land, near_sum, far_land, near_send, near_recv, far_send, far_recv):
    packs = lax.axis_size("rep")
    chips = lax.axis_size("dp") // 2
    mates = 2 * packs
    me, pack = lax.axis_index("dp"), lax.axis_index("rep")
    core, chip = me % 2, me // 2
    mate = pack * 2 + core
    barrier = pltpu.get_barrier_semaphore()

    def near(k):
        to = lax.rem(mate + k, mates)
        return {"dp": chip * 2 + to % 2, "rep": to // 2}

    def far(k):
        return {"dp": lax.rem(chip + k, chips) * 2 + core}

    for k in range(1, mates):
        pl.semaphore_signal(barrier, inc=1, device_id=near(k), device_id_type=MESH)
    for k in range(1, chips):
        pl.semaphore_signal(barrier, inc=1, device_id=far(k), device_id_type=MESH)
    pl.semaphore_wait(barrier, mates + chips - 2)

    def exchange(src, landed, own, send_sem, recv_sem, device, count):
        copies = [
            pltpu.make_async_remote_copy(
                src_ref=src,
                dst_ref=landed.at[own],
                send_sem=send_sem.at[k],
                recv_sem=recv_sem.at[k],
                device_id=device(k),
                device_id_type=MESH,
            )
            for k in range(1, count)
        ]
        for copy in copies:
            copy.start()
        landed[own] = src[...]
        for copy in copies:
            copy.wait()
        total = landed[0]
        for k in range(1, count):
            total += landed[k]
        return total

    near_sum[...] = exchange(part, near_land, mate, near_send, near_recv, near, mates)
    out[...] = exchange(near_sum, far_land, chip, far_send, far_recv, far, chips)


def gain_total(part):
    mates, chips = 2 * lax.axis_size("rep"), lax.axis_size("dp") // 2
    vmem = pl.BlockSpec(memory_space=pltpu.VMEM)
    dma = pltpu.SemaphoreType.DMA
    return pl.pallas_call(
        gain_total_kernel,
        out_shape=jax.ShapeDtypeStruct(part.shape, F32),
        in_specs=[vmem],
        out_specs=vmem,
        scratch_shapes=[
            pltpu.VMEM((mates,) + part.shape, F32),
            pltpu.VMEM(part.shape, F32),
            pltpu.VMEM((chips,) + part.shape, F32),
            dma((mates,)), dma((mates,)), dma((chips,)), dma((chips,)),
        ],
        compiler_params=pltpu.CompilerParams(collective_id=4, has_side_effects=True),
        name="gain_total",
    )(part)


def rms(values, norm_gain):
    return (
        values * lax.rsqrt(jnp.mean(values * values, axis=-1, keepdims=True) + EPSILON) * norm_gain
    )


def rms_back(values, norm_gain, grads):
    _, pullback = jax.vjp(rms, values, norm_gain)
    return pullback(grads)


def from_partner(value):
    devices = lax.axis_size("dp")
    return lax.ppermute(value, "dp", [(i, i ^ 1) for i in range(devices)])


def pack_swap(low):
    if lax.axis_size("rep") == 2:
        return lax.ppermute(low, "rep", [(0, 1), (1, 0)])
    return lax.psum(low, "rep")


def pack_add(low, other):
    if lax.axis_size("rep") == 2:
        return low.astype(F32) + other.astype(F32)
    return other.astype(F32)


def together(*values):
    return lax.optimization_barrier(values)


def body(
    tokens,
    attention_gain,
    query_weight,
    key_weight,
    value_weight,
    output_weight,
    dense_gain,
    gate_weight,
    up_weight,
    down_weight,
    block_document,
    document_tail,
    cotangent,
):
    devices = lax.axis_size("dp")
    chips = devices // 2
    hidden_in = tokens[0].astype(F32)
    tok_dev = hidden_in.shape[0]
    pack_tok = tok_dev * devices

    documents, tails = block_document[0], document_tail[0]
    first = jnp.sum((documents[None, :] < documents[:, None]).astype(jnp.int32), axis=1)
    last = jnp.concatenate([documents[1:] != documents[:-1], jnp.ones((1,), bool)])
    doc_ids = jnp.arange(tails.shape[0], dtype=jnp.int32)
    own_tail = jnp.sum((documents[:, None] == doc_ids[None, :]) * tails[None, :], axis=1)
    tail = jnp.where(last, own_tail, BLOCK).astype(jnp.int32)
    block_index = jnp.arange(documents.shape[0], dtype=jnp.int32)
    inside = jnp.arange(BLOCK, dtype=jnp.int32)
    position = ((block_index - first)[:, None] * BLOCK + inside[None, :]).reshape(-1)
    frequency = ROPE_BASE ** (-(jnp.arange(HALF, dtype=F32) * (2.0 / HEAD_DIM)))
    angles = position.astype(F32)[None, :] * frequency[:, None]
    cos_t, sin_t = jnp.cos(angles), jnp.sin(angles)
    r = query_weight.shape[0]

    qkv, normed_all, full_output = gather_project(
        tokens[0],
        attention_gain[None],
        (query_weight, key_weight, value_weight),
        output_weight,
        cos_t,
        sin_t,
    )

    order = ring_order(chips)
    walk = [2 * chip + k for chip in order for k in (0, 1)]
    lanes = [[2 * chip + k for chip in order] for k in (0, 1)]
    full_output = full_output.reshape(-1, output_weight.shape[1])
    grad_low = cotangent[0]
    first_half, second_half = grad_low[: tok_dev // 2], grad_low[tok_dev // 2 :]
    second_half, _ = together(second_half, qkv)
    cotangents = [
        lax.all_gather(part, "dp", axis=0, axis_index_groups=lanes)
        for part in (first_half, second_half)
    ]
    gate_other, up_other, down_other = (
        from_partner(gate_weight),
        from_partner(up_weight),
        from_partner(down_weight),
    )
    qkv_weight = jnp.stack([query_weight, key_weight, value_weight])
    qkv_other = from_partner(qkv_weight)

    attended, log_total = attend(first, tail, qkv)
    attended_blocks = lax.all_to_all(
        attended.reshape(devices, tok_dev, r),
        "dp",
        split_axis=0,
        concat_axis=0,
        tiled=True,
        axis_index_groups=[walk],
    )
    attended_here = attended_blocks.transpose(1, 0, 2).reshape(tok_dev, -1)
    mixed = hidden_in + dot_nn(attended_here, full_output)
    normed_two = rms(mixed, dense_gain).astype(LOW)

    grad_normed_two, out_parts, _, gate_low, up_low, down_low = dense(
        normed_two,
        cotangents,
        (gate_weight, up_weight, down_weight),
        (gate_other, up_other, down_other),
    )
    out_sum = lax.psum_scatter(
        out_parts.reshape(chips * tok_dev, -1),
        "dp",
        scatter_dimension=0,
        tiled=True,
        axis_index_groups=lanes,
    )
    gate_there = pack_swap(gate_low)

    grad_mixed_norm, dense_gain_part = rms_back(mixed, dense_gain, grad_normed_two)
    grad_mixed = grad_low.astype(F32) + grad_mixed_norm
    grad_mixed_low = grad_mixed.astype(LOW)
    grad_attended = dot_nt(grad_mixed_low, full_output).astype(LOW)
    grad_heads = lax.all_to_all(
        grad_attended.reshape(tok_dev, devices, r).transpose(1, 0, 2),
        "dp",
        split_axis=0,
        concat_axis=0,
        tiled=True,
        axis_index_groups=[walk],
    ).reshape(pack_tok, r)

    packs, pack = lax.axis_size("rep"), lax.axis_index("rep")
    core = lax.axis_index("dp") % 2
    share = r // packs
    by_share = attended_here.reshape(tok_dev, chips, 2, packs, share)

    def output_rows(from_core, from_pack):
        left = lax.dynamic_index_in_dim(by_share, from_core, axis=2, keepdims=False)
        left = lax.dynamic_index_in_dim(left, from_pack, axis=2, keepdims=False)
        return dot_tn(left.reshape(tok_dev, chips * share), grad_mixed_low)

    others = [lax.rem(pack + k, packs) for k in range(1, packs)]
    output_mine = (
        output_rows(core, pack)
        + from_partner(output_rows(1 - core, pack).astype(LOW)).astype(F32)
    ).astype(LOW)
    output_there = [
        lax.ppermute(
            (
                output_rows(core, other)
                + from_partner(output_rows(1 - core, other).astype(LOW)).astype(F32)
            ).astype(LOW),
            "rep",
            [(i, (i + k) % packs) for i in range(packs)],
        )
        for k, other in enumerate(others, 1)
    ]
    grad_heads, gate_there = together(grad_heads, gate_there)
    grads = attend_back(first, tail, qkv, grad_heads, attended, log_total, cos_t, sin_t)
    grads, output_there, out_sum, up_low, down_low = together(
        grads, output_there, out_sum, up_low, down_low
    )
    up_there = pack_swap(up_low)
    down_there = pack_swap(down_low)
    output_grad = lax.psum_scatter(
        sum((there.astype(F32) for there in output_there), output_mine.astype(F32)).astype(LOW),
        "dp",
        scatter_dimension=0,
        tiled=True,
        axis_index_groups=lanes,
    )
    input_grad, attention_gain_part, query_total, key_total, value_total = normed_back(
        grads, qkv_weight, qkv_other, tokens[0], attention_gain[None], grad_mixed, normed_all
    )
    input_grad, out_sum, gate_there, up_there, down_there, output_grad = together(
        input_grad, out_sum, gate_there, up_there, down_there, output_grad
    )
    output_total = lax.all_gather(output_grad, "rep", axis=0, tiled=True)
    if packs == 2:
        output_other = lax.ppermute(output_grad, "rep", [(0, 1), (1, 0)])
        output_total = jnp.where(
            pack == 0,
            jnp.concatenate([output_grad, output_other], 0),
            jnp.concatenate([output_other, output_grad], 0),
        )
    gain_parts = jnp.stack([attention_gain_part[0], dense_gain_part])
    gain_totals = gain_total(gain_parts.reshape(-1, 128)).reshape(2, -1)
    layer_out = mixed + out_sum.astype(F32)
    return (
        layer_out[None].astype(LOW),
        input_grad[None],
        gain_totals[0],
        query_total,
        key_total,
        value_total,
        output_total.astype(F32),
        gain_totals[1],
        pack_add(gate_low, gate_there),
        pack_add(up_low, up_there),
        pack_add(down_low, down_there),
    )


def solution(mesh):
    return jax.shard_map(
        body,
        mesh=mesh,
        in_specs=(
            P("rep", "dp", None),
            P(),
            P("dp", None),
            P("dp", None),
            P("dp", None),
            P("dp", None),
            P(),
            P("dp", None),
            P("dp", None),
            P("dp", None),
            P("rep", None),
            P("rep", None),
            P("rep", "dp", None),
        ),
        out_specs=(
            P("rep", "dp", None),
            P("rep", "dp", None),
            P(),
            P("dp", None),
            P("dp", None),
            P("dp", None),
            P("dp", None),
            P(),
            P("dp", None),
            P("dp", None),
            P("dp", None),
        ),
        check_vma=False,
    )
```

```python
import functools
import math

import jax
import jax.numpy as jnp
from jax import lax
from jax.experimental import pallas as pl
from jax.experimental.pallas import tpu as pltpu
from jax.sharding import PartitionSpec as P

HEAD_DIM = 64
HALF = HEAD_DIM // 2
BLOCK = 128
CHUNK = 512
FF_TILE = 256
EPSILON = 1e-05
ROPE_BASE = 130000.0
MASKED_SCORE = -1e30
MESH = pl.DeviceIdType.MESH
MIB = 2**20
LOW = jnp.bfloat16
F32 = jnp.float32


def dot_nn(a, b):
    return lax.dot_general(a, b, (((1,), (0,)), ((), ())), preferred_element_type=F32)


def dot_nt(a, b):
    return lax.dot_general(a, b, (((1,), (1,)), ((), ())), preferred_element_type=F32)


def dot_tn(a, b):
    return lax.dot_general(a, b, (((0,), (0,)), ((), ())), preferred_element_type=F32)


def grid_of(chips):
    depth = 4 if chips % 8 == 0 else 2
    return depth, chips // depth


def chip_at(place, chips):
    depth, width = grid_of(chips)
    place = lax.rem(place + chips, chips)
    later = place - depth
    row, column = later // (width - 1), later % (width - 1)
    odd = row % 2
    far = (depth - 1 - row) * width + 1 + column + odd * (width - 2 - 2 * column)
    return jnp.where(place < depth, place * width, far)


def place_of(chip, chips):
    depth, width = grid_of(chips)
    z, x = chip // width, chip % width
    row = depth - 1 - z
    odd = row % 2
    column = x - 1 + odd * (width - 2 * x)
    return jnp.where(x == 0, z, depth + row * (width - 1) + column)


def ring_order(chips):
    depth, width = grid_of(chips)
    order = [z * width for z in range(depth)]
    for row in range(depth):
        columns = list(range(1, width))
        order += [(depth - 1 - row) * width + x for x in (columns[::-1] if row % 2 else columns)]
    return order


class Ring:
    def __init__(self):
        self.chips = lax.axis_size("dp") // 2
        me = lax.axis_index("dp")
        self.core = me % 2
        self.chip = me // 2
        self.partner = self.chip * 2 + 1 - self.core
        self.place = place_of(self.chip, self.chips)
        self.next = (self.device(1), self.device(-1))
        self.back = (self.next[1], self.next[0])

    def chip_far(self, steps):
        return chip_at(self.place + steps, self.chips)

    def device(self, steps):
        return self.chip_far(steps) * 2 + self.core

    def greet(self, others):
        barrier = pltpu.get_barrier_semaphore()
        for other in others:
            pl.semaphore_signal(barrier, inc=1, device_id={"dp": other}, device_id_type=MESH)
        pl.semaphore_wait(barrier, len(others))


def remote(src, dst, send_sem, recv_sem, device):
    return pltpu.make_async_remote_copy(
        src_ref=src,
        dst_ref=dst,
        send_sem=send_sem,
        recv_sem=recv_sem,
        device_id={"dp": device},
        device_id_type=MESH,
    )


def half_rows(direction, rows):
    return pl.ds(direction * (rows // 2), rows // 2)


def turned(u):
    parts = []
    for at in range(0, u.shape[1], HEAD_DIM):
        parts += [-u[:, at + HALF : at + HEAD_DIM], u[:, at : at + HALF]]
    return jnp.concatenate(parts, 1)


def gather_project_kernel(
    tokens, gain, query_w, key_w, value_w, output_w, cos_t, sin_t, qkv, gathered, output_all,
    normed, partner_weights, x_buf, staged,
    ag_send, ag_recv, w_send, w_recv, q_send, q_recv, local_sem,
    o_send, o_recv, pair_send, pair_recv, rep_send, rep_recv, far_send, far_recv,
):
    ring = Ring()
    n = ring.chips
    packs, pack = lax.axis_size("rep"), lax.axis_index("rep")
    rows = normed.shape[0]
    half = rows // 2
    r = qkv.shape[2]
    own_weights = (query_w, key_w, value_w)
    barrier = pltpu.get_barrier_semaphore()
    for k in range(1, packs):
        pl.semaphore_signal(
            barrier, inc=1, device_id={"rep": lax.rem(pack + k, packs)}, device_id_type=MESH
        )
    for other in (ring.next[0], ring.next[1], ring.partner):
        pl.semaphore_signal(barrier, inc=1, device_id={"dp": other}, device_id_type=MESH)
    pl.semaphore_wait(barrier, 3 + packs - 1)

    def normalize(i, carry):
        span = pl.ds(pl.multiple_of(i * 32, 32), 32)
        value = tokens[span, :].astype(F32)
        scale = lax.rsqrt(jnp.mean(value * value, axis=1, keepdims=True) + EPSILON)
        normed[span, :] = (value * scale * gain[...]).astype(LOW)
        return carry

    lax.fori_loop(0, rows // 32, normalize, 0)

    def hop(t, d):
        chip = ring.chip_far((1 - t) if d == 0 else (t - 1))
        return chip, half_rows(d, rows)

    def send(t, d, first):
        chip, part = hop(t, d)
        src = normed.at[part] if first else gathered.at[chip, part]
        return remote(src, gathered.at[chip, part], ag_send.at[d, t - 1], ag_recv.at[d, t - 1], ring.next[d])

    out_rows, features = output_w.shape
    share = out_rows // packs
    spot = ring.place * 2 + ring.core

    def share_of(q, d):
        return pl.ds(pl.multiple_of(q * share, share), share), pl.ds(d * (features // 2), features // 2)

    def block_at(t, d, q, core):
        place = lax.rem(ring.place + (n - t if d == 0 else t), n)
        at_rows, columns = share_of(q, d)
        return output_all.at[place * 2 + core, at_rows, columns]

    def o_copy(t, d, first):
        at_rows, columns = share_of(pack, d)
        src = output_w.at[at_rows, columns] if first else block_at(t - 1, d, pack, ring.core)
        return remote(
            src, block_at(t - 1, d, pack, ring.core), o_send.at[d, t], o_recv.at[d, t], ring.next[d]
        )

    def pair_copy(t, d):
        block = block_at(t, d, pack, ring.core)
        return remote(block, block, pair_send.at[d, t], pair_recv.at[d, t], ring.partner)

    def rep_copy(t, d, k):
        block = block_at(t, d, pack, ring.core)
        return pltpu.make_async_remote_copy(
            src_ref=block,
            dst_ref=block,
            send_sem=rep_send.at[k - 1, d, t],
            recv_sem=rep_recv.at[k - 1, d, t],
            device_id={"rep": lax.rem(pack + k, packs)},
            device_id_type=MESH,
        )

    def far_copy(t, d, k):
        block = block_at(t, d, lax.rem(pack + packs - k, packs), ring.core)
        return remote(block, block, far_send.at[k - 1, d, t], far_recv.at[k - 1, d, t], ring.partner)

    def forward_far(t):
        for d in (0, 1):
            for k in range(1, packs):
                rep_copy(t, d, k).wait_recv()
                far_copy(t, d, k).start()

    for d in (0, 1):
        send(1, d, True).start()
    for d in (0, 1):
        o_copy(1, d, True).start()
    own_rows = remote(output_w, output_all.at[spot], local_sem.at[3], local_sem.at[4], ring.partner)
    own_rows.start()
    own_keep = pltpu.make_async_copy(output_w, output_all.at[spot], local_sem.at[5])
    own_keep.start()
    swaps = [
        remote(own_weights[i], partner_weights.at[i], w_send.at[i], w_recv.at[i], ring.partner)
        for i in range(3)
    ]
    for swap in swaps:
        swap.start()
    keep = pltpu.make_async_copy(normed, gathered.at[ring.chip], local_sem.at[2])
    keep.start()

    def project_block(t, from_input):
        x = normed[...] if from_input else x_buf[...]
        places = [ring.chip_far(-t), ring.chip_far(t)]
        starts = [
            pl.multiple_of((places[d] * 2 + ring.core) * rows + d * half, half) for d in (0, 1)
        ]

        def table(source):
            wide = [source[:, pl.ds(starts[d], half)] for d in (0, 1)]
            return jnp.concatenate(
                [jnp.concatenate([w] * (r // HALF), 0).T for w in wide], 0
            )

        cos, sin = table(cos_t), table(sin_t)

        def heads(w):
            query, key, value = [dot_nt(x, w[i][...]) for i in range(3)]
            return (
                (query * cos + turned(query) * sin).astype(LOW),
                (key * cos + turned(key) * sin).astype(LOW),
                value.astype(LOW),
            )

        for i, value in enumerate(heads(own_weights)):
            for d in (0, 1):
                qkv[i, pl.ds(starts[d], half), :] = value[d * half : (d + 1) * half]
        if from_input:
            for swap in swaps:
                swap.wait()
        for i, value in enumerate(heads([partner_weights.at[i] for i in range(3)])):
            staged[t, i] = value
        for d in (0, 1):
            remote(
                staged.at[t, :, half_rows(d, rows)],
                qkv.at[:, pl.ds(starts[d], half)],
                q_send.at[d, t],
                q_recv.at[d, t],
                ring.partner,
            ).start()

    project_block(0, True)

    def step(t, carry):
        for d in (0, 1):
            send(t, d, False).wait_recv()

        @pl.when(t < n - 1)
        def _():
            for d in (0, 1):
                send(t + 1, d, False).start()

        for d in (0, 1):
            o_copy(t, d, False).wait_recv()

        @pl.when(t < n - 1)
        def _():
            for d in (0, 1):
                o_copy(t + 1, d, False).start()

        for d in (0, 1):
            for k in range(1, packs):
                rep_copy(t, d, k).start()
            pair_copy(t, d).start()

        @pl.when(t > 1)
        def _():
            forward_far(t - 1)

        loads = []
        for d in (0, 1):
            chip, part = hop(t + 1, d)
            loads.append(pltpu.make_async_copy(gathered.at[chip, part], x_buf.at[part], local_sem.at[d]))
        for load in loads:
            load.start()
        for load in loads:
            load.wait()
        project_block(t, False)
        return carry

    lax.fori_loop(1, n, step, 0)
    forward_far(n - 1)

    def finish(t, carry):
        for d in (0, 1):
            send(t, d, False).wait_send()
            o_copy(t, d, False).wait_send()
            pair_copy(t, d).wait()
            for k in range(1, packs):
                rep_copy(t, d, k).wait_send()
                far_copy(t, d, k).wait()
        return carry

    lax.fori_loop(1, n, finish, 0)
    own_rows.wait()
    own_keep.wait()

    def finish_heads(t, carry):
        for d in (0, 1):
            done = remote(
                staged.at[t, :, half_rows(d, rows)],
                qkv.at[:, half_rows(d, rows)],
                q_send.at[d, t],
                q_recv.at[d, t],
                ring.partner,
            )
            done.wait_send()
            done.wait_recv()
        return carry

    lax.fori_loop(0, n, finish_heads, 0)
    keep.wait()


def gather_project(tokens, gain, weights, output_weight, cos_t, sin_t):
    rows, features = tokens.shape
    r = weights[0].shape[0]
    devices = lax.axis_size("dp")
    packs = lax.axis_size("rep")
    n = devices // 2
    vmem = pl.BlockSpec(memory_space=pltpu.VMEM)
    dma = pltpu.SemaphoreType.DMA
    return pl.pallas_call(
        gather_project_kernel,
        out_shape=(
            jax.ShapeDtypeStruct((3, devices * rows, r), LOW),
            jax.ShapeDtypeStruct((n, rows, features), LOW),
            jax.ShapeDtypeStruct((devices,) + output_weight.shape, LOW),
        ),
        in_specs=[vmem] * 8,
        out_specs=(vmem, pl.BlockSpec(memory_space=pl.ANY), pl.BlockSpec(memory_space=pl.ANY)),
        scratch_shapes=[
            pltpu.VMEM((rows, features), LOW),
            pltpu.VMEM((3, r, features), LOW),
            pltpu.VMEM((rows, features), LOW),
            pltpu.VMEM((n, 3, rows, r), LOW),
            dma((2, n)), dma((2, n)), dma((3,)), dma((3,)), dma((2, n)), dma((2, n)), dma((6,)),
            dma((2, n)), dma((2, n)), dma((2, n)), dma((2, n)),
            dma((packs - 1, 2, n)), dma((packs - 1, 2, n)),
            dma((packs - 1, 2, n)), dma((packs - 1, 2, n)),
        ],
        compiler_params=pltpu.CompilerParams(
            collective_id=1, has_side_effects=True, vmem_limit_bytes=40 * MIB
        ),
        cost_estimate=pl.CostEstimate(
            flops=4 * n * rows * features * 3 * r, bytes_accessed=320 * MIB, transcendentals=0
        ),
        name="gather_project",
    )(tokens, gain, *weights, output_weight, cos_t, sin_t)


def split_heads(u):
    heads = u.shape[1] // HEAD_DIM
    if heads == 1:
        return u
    lane = lax.broadcasted_iota(jnp.int32, u.shape, 1) // HEAD_DIM
    zero = jnp.zeros_like(u)
    return jnp.concatenate([jnp.where(lane == h, u, zero) for h in range(heads)], 0)


def join_heads(u):
    heads = u.shape[0] // HEAD_DIM
    return jnp.concatenate(
        [u[h * HEAD_DIM : (h + 1) * HEAD_DIM, h * BLOCK : (h + 1) * BLOCK] for h in range(heads)], 0
    )


def transpose_blocks(source, target):
    def one(b, carry):
        at = pl.multiple_of(b * BLOCK, BLOCK)
        target[:, pl.ds(at, BLOCK)] = source[pl.ds(at, BLOCK), :].astype(F32).T.astype(LOW)
        return carry

    lax.fori_loop(0, source.shape[0] // BLOCK, one, 0)


def window_of(b, first, tail, columns):
    start = pl.multiple_of(jnp.maximum(b - (CHUNK // BLOCK - 1), 0) * BLOCK, BLOCK)
    whole = (b - first) // (CHUNK // BLOCK)
    lowest = (first + whole * (CHUNK // BLOCK)) * BLOCK
    key_index = start + lax.broadcasted_iota(jnp.int32, (CHUNK, columns), 0)
    query_index = b * BLOCK + lax.broadcasted_iota(jnp.int32, (CHUNK, columns), 1) % BLOCK
    allowed = (
        (key_index >= lowest)
        & (key_index <= query_index)
        & (key_index < b * BLOCK + tail)
    )
    return start, whole, allowed


def walk_rows(b, tok_dev, chips):
    device = b * BLOCK // tok_dev
    spot = place_of(device // 2, chips) * 2 + device % 2
    return pl.ds(pl.multiple_of(spot * tok_dev + b * BLOCK % tok_dev, BLOCK), BLOCK)


def attend_kernel(chips, first_ref, tail_ref, qkv, attended, log_total, value_t):
    tokens, r = qkv.shape[1:]
    tok_dev = tokens // (2 * chips)
    columns = (r // HEAD_DIM) * BLOCK
    scale = 1.0 / math.sqrt(HEAD_DIM)
    transpose_blocks(qkv.at[2], value_t)

    def block(b, carry):
        at = pl.multiple_of(b * BLOCK, BLOCK)
        query = split_heads(qkv[0, pl.ds(at, BLOCK), :])
        start, whole, allowed = window_of(b, first_ref[b], tail_ref[b], columns)
        scores = dot_nt(qkv[1, pl.ds(start, CHUNK), :], query) * scale
        scores = jnp.where(allowed, scores, MASKED_SCORE)
        top = jnp.max(scores, axis=0, keepdims=True)
        weights = jnp.exp(scores - top)
        total = jnp.sum(weights, axis=0, keepdims=True)
        out = dot_nn(value_t[:, pl.ds(start, CHUNK)], weights.astype(LOW))

        def more(i, state):
            top, total, out = state
            start = pl.multiple_of(first_ref[b] * BLOCK + i * CHUNK, BLOCK)
            scores = dot_nt(qkv[1, pl.ds(start, CHUNK), :], query) * scale
            higher = jnp.maximum(top, jnp.max(scores, axis=0, keepdims=True))
            shrink = jnp.exp(top - higher)
            weights = jnp.exp(scores - higher)
            total = total * shrink + jnp.sum(weights, axis=0, keepdims=True)
            out = out * shrink + dot_nn(value_t[:, pl.ds(start, CHUNK)], weights.astype(LOW))
            return higher, total, out

        top, total, out = lax.fori_loop(0, whole, more, (top, total, out))
        log_total[pl.ds(b, 1), :] = top + jnp.log(total)
        attended[walk_rows(b, tok_dev, chips), :] = join_heads(out / total).T.astype(LOW)
        return carry

    lax.fori_loop(0, tokens // BLOCK, block, 0)


def attend(first, tail, qkv):
    tokens, r = qkv.shape[1:]
    smem = pl.BlockSpec(memory_space=pltpu.SMEM)
    vmem = pl.BlockSpec(memory_space=pltpu.VMEM)
    return pl.pallas_call(
        functools.partial(attend_kernel, lax.axis_size("dp") // 2),
        out_shape=(
            jax.ShapeDtypeStruct((tokens, r), LOW),
            jax.ShapeDtypeStruct((tokens // BLOCK, (r // HEAD_DIM) * BLOCK), F32),
        ),
        in_specs=[smem, smem, vmem],
        out_specs=(vmem, vmem),
        scratch_shapes=[pltpu.VMEM((r, tokens), LOW)],
        compiler_params=pltpu.CompilerParams(vmem_limit_bytes=40 * MIB),
        cost_estimate=pl.CostEstimate(
            flops=4 * tokens * 1024 * r * 8, bytes_accessed=120 * MIB, transcendentals=tokens * 1024
        ),
        name="attend",
    )(first, tail, qkv)


def unrotate(g, cos, sin):
    parts = []
    for h in range(g.shape[0] // HEAD_DIM):
        one = g[h * HEAD_DIM : h * HEAD_DIM + HALF]
        two = g[h * HEAD_DIM + HALF : (h + 1) * HEAD_DIM]
        parts += [one * cos + two * sin, two * cos - one * sin]
    return jnp.concatenate(parts, 0)


def attend_back_kernel(
    chips, first_ref, tail_ref, qkv, grad_out, attended, log_total, cos_t, sin_t, grads,
    key_t, grad_key, grad_value, staged, store_sem,
):
    tokens, r = qkv.shape[1:]
    tok_dev = tokens // (2 * chips)
    heads = r // HEAD_DIM
    columns = heads * BLOCK
    scale = 1.0 / math.sqrt(HEAD_DIM)
    transpose_blocks(qkv.at[1], key_t)
    grad_key[...] = jnp.zeros_like(grad_key)
    grad_value[...] = jnp.zeros_like(grad_value)

    def block(b, carry):
        at = pl.multiple_of(b * BLOCK, BLOCK)
        here = pl.ds(at, BLOCK)
        query = split_heads(qkv[0, here, :])
        walk = walk_rows(b, tok_dev, chips)
        grad_rows = grad_out[walk, :]
        grad = split_heads(grad_rows)
        product = (grad_rows.astype(F32) * attended[walk, :].astype(F32)).T
        delta = jnp.concatenate(
            [
                jnp.sum(product[h * HEAD_DIM : (h + 1) * HEAD_DIM], axis=0, keepdims=True)
                for h in range(heads)
            ],
            1,
        )
        log_row = log_total[pl.ds(b, 1), :]

        def chunk(start, allowed, grad_query):
            span = pl.ds(start, CHUNK)
            scores = dot_nt(qkv[1, span, :], query) * scale
            weights = jnp.exp(scores - log_row)
            if allowed is not None:
                weights = jnp.where(allowed, weights, 0.0)
            grad_weights = dot_nt(qkv[2, span, :], grad)
            grad_scores = (weights * (grad_weights - delta)).astype(LOW)
            grad_value[span, :] += dot_nn(weights.astype(LOW), grad)
            grad_key[span, :] += dot_nn(grad_scores, query)
            return grad_query + dot_nn(key_t[:, span], grad_scores)

        start, whole, allowed = window_of(b, first_ref[b], tail_ref[b], columns)
        grad_query = chunk(start, allowed, jnp.zeros((r, columns), F32))
        grad_query = lax.fori_loop(
            0,
            whole,
            lambda i, g: chunk(pl.multiple_of(first_ref[b] * BLOCK + i * CHUNK, BLOCK), None, g),
            grad_query,
        )
        turned = unrotate(join_heads(grad_query) * scale, cos_t[:, here], sin_t[:, here])
        staged[0, here, :] = turned.T.astype(LOW)
        return carry

    lax.fori_loop(0, tokens // BLOCK, block, 0)
    query_store = pltpu.make_async_copy(staged.at[0], grads.at[0], store_sem.at[0])
    query_store.start()

    def close(b, carry):
        here = pl.ds(pl.multiple_of(b * BLOCK, BLOCK), BLOCK)
        turned = unrotate(grad_key[here, :].T * scale, cos_t[:, here], sin_t[:, here])
        staged[1, here, :] = turned.T.astype(LOW)
        staged[2, here, :] = grad_value[here, :].astype(LOW)
        return carry

    lax.fori_loop(0, tokens // BLOCK, close, 0)
    rest_store = pltpu.make_async_copy(staged.at[pl.ds(1, 2)], grads.at[pl.ds(1, 2)], store_sem.at[1])
    rest_store.start()
    query_store.wait()
    rest_store.wait()


def attend_back(first, tail, qkv, grad_out, attended, log_total, cos_t, sin_t):
    tokens, r = qkv.shape[1:]
    smem = pl.BlockSpec(memory_space=pltpu.SMEM)
    vmem = pl.BlockSpec(memory_space=pltpu.VMEM)
    return pl.pallas_call(
        functools.partial(attend_back_kernel, lax.axis_size("dp") // 2),
        out_shape=jax.ShapeDtypeStruct((3, tokens, r), LOW),
        in_specs=[smem, smem] + [vmem] * 6,
        out_specs=pl.BlockSpec(memory_space=pl.ANY),
        scratch_shapes=[
            pltpu.VMEM((r, tokens), LOW),
            pltpu.VMEM((tokens, r), F32),
            pltpu.VMEM((tokens, r), F32),
            pltpu.VMEM((3, tokens, r), LOW),
            pltpu.SemaphoreType.DMA((2,)),
        ],
        compiler_params=pltpu.CompilerParams(vmem_limit_bytes=40 * MIB),
        cost_estimate=pl.CostEstimate(
            flops=10 * tokens * 1024 * r * 8, bytes_accessed=240 * MIB, transcendentals=tokens * 1024
        ),
        name="attend_back",
    )(first, tail, qkv, grad_out, attended, log_total, cos_t, sin_t)


def dense_kernel(
    normed, cotangents_a, cotangents_b, gate_w, up_w, down_w, gate_p, up_p, down_p,
    grad_sum, out_parts, gathered, gate_grad, up_a, up_b, down_grad,
    weights, totals, x_buf, g_buf, out_acc, grad_acc, sent, landed, cast_buf, pair_land,
    ag_send, ag_recv, rs_send, rs_recv, credit, local_sem, w_sem, cast_sem, pair_send, pair_recv,
):
    ring = Ring()
    n = ring.chips
    rows, features = normed.shape
    half = rows // 2
    early = cotangents_a.shape[1]
    own = gate_w.shape[0]
    tiles = 2 * own // FF_TILE
    loads = []
    for i, (mine, theirs) in enumerate(((gate_w, gate_p), (up_w, up_p), (down_w, down_p))):
        loads.append(pltpu.make_async_copy(mine, weights.at[i, pl.ds(0, own)], w_sem.at[2 * i]))
        loads.append(pltpu.make_async_copy(theirs, weights.at[i, pl.ds(own, own)], w_sem.at[2 * i + 1]))
    for load in loads:
        load.start()
    ring.greet((ring.next[0], ring.next[1], ring.partner))

    def source(t, d):
        return lax.rem(ring.place + (n - t if d == 0 else t), n)

    def send(t, d, first):
        place, part = source(t - 1, d), half_rows(d, rows)
        src = normed.at[part] if first else gathered.at[place, part]
        return remote(src, gathered.at[place, part], ag_send.at[d, t - 1], ag_recv.at[d, t - 1], ring.next[d])

    def reduce_copy(t, d):
        return remote(sent.at[d], landed.at[d, t % 2], rs_send.at[d], rs_recv.at[d, t % 2], ring.next[d])

    for d in (0, 1):
        send(1, d, True).start()

    def clear(i, carry):
        span = pl.ds(pl.multiple_of(i * FF_TILE, FF_TILE), FF_TILE)
        for k in range(3):
            totals[k, span, :] = jnp.zeros((FF_TILE, features), F32)
        return carry

    lax.fori_loop(0, tiles, clear, 0)
    for load in loads:
        load.wait()

    def out_copy(t, d):
        part = half_rows(d, rows)
        return pltpu.make_async_copy(
            cast_buf.at[t % 2, part], out_parts.at[source(t, d), part], cast_sem.at[t % 2, d]
        )

    def step(t, carry):
        copies = [
            pltpu.make_async_copy(cotangents_a.at[source(t, 0)], g_buf.at[pl.ds(0, early)], local_sem.at[0]),
            pltpu.make_async_copy(
                cotangents_b.at[source(t, 0), pl.ds(0, half - early)],
                g_buf.at[pl.ds(early, half - early)],
                local_sem.at[1],
            ),
            pltpu.make_async_copy(
                cotangents_b.at[source(t, 1), pl.ds(half - early, half)],
                g_buf.at[pl.ds(half, half)],
                local_sem.at[4],
            ),
        ]
        for copy in copies:
            copy.start()

        @pl.when(t > 0)
        def _():
            for d in (0, 1):
                send(t, d, False).wait_recv()

            @pl.when(t < n - 1)
            def _():
                for d in (0, 1):
                    send(t + 1, d, False).start()

            more = []
            for d in (0, 1):
                part = half_rows(d, rows)
                more.append(
                    pltpu.make_async_copy(gathered.at[source(t, d), part], x_buf.at[part], local_sem.at[2 + d])
                )
                more[-1].start()
            for copy in more:
                copy.wait()

        @pl.when(t == 0)
        def _():
            x_buf[...] = normed[...]

        for copy in copies:
            copy.wait()

        out_acc[...] = jnp.zeros_like(out_acc)
        grad_acc[...] = jnp.zeros_like(grad_acc)

        def tile(i, carry):
            span = pl.ds(pl.multiple_of(i * FF_TILE, FF_TILE), FF_TILE)
            x = x_buf[...]
            g = g_buf[...]
            gate = dot_nt(x, weights[0, span, :])
            up = dot_nt(x, weights[1, span, :])
            grad_hidden = dot_nt(g, weights[2, span, :])
            sigma = 1.0 / (1.0 + jnp.exp(-gate))
            silu = gate * sigma
            hidden = (silu * up).astype(LOW)
            grad_gate = (grad_hidden * up * sigma * (1.0 + gate * (1.0 - sigma))).astype(LOW)
            grad_up = (grad_hidden * silu).astype(LOW)
            out_acc[...] += dot_nn(hidden, weights[2, span, :])
            grad_acc[...] += dot_nn(grad_gate, weights[0, span, :])
            grad_acc[...] += dot_nn(grad_up, weights[1, span, :])
            totals[0, span, :] += dot_tn(grad_gate, x)
            totals[1, span, :] += dot_tn(grad_up, x)
            totals[2, span, :] += dot_tn(hidden, g)
            return carry

        lax.fori_loop(0, tiles, tile, 0)

        @pl.when(t >= 2)
        def _():
            for d in (0, 1):
                out_copy(t - 2, d).wait()

        cast_buf[t % 2] = out_acc[...].astype(LOW)
        for d in (0, 1):
            out_copy(t, d).start()

        @pl.when(t == 0)
        def _():
            grad_sum[...] = grad_acc[...]

        @pl.when(t > 0)
        def _():
            for d in (0, 1):
                part = pl.ds(d * half, half)

                @pl.when(t >= 2)
                def _():
                    reduce_copy(t - 1, d).wait_recv()
                    grad_acc[part, :] += landed[d, (t - 1) % 2].astype(F32)

                    @pl.when(t <= n - 2)
                    def _():
                        pl.semaphore_signal(
                            credit.at[d], inc=1, device_id={"dp": ring.back[d]}, device_id_type=MESH
                        )

                    reduce_copy(t - 1, d).wait_send()

                sent[d] = grad_acc[part, :].astype(LOW)

                @pl.when(t >= 3)
                def _():
                    pl.semaphore_wait(credit.at[d], 1)

                reduce_copy(t, d).start()

        return carry

    lax.fori_loop(0, n, step, 0)
    for t in (n - 2, n - 1):
        for d in (0, 1):
            out_copy(t, d).wait()

    own_tiles = 3 * own // FF_TILE

    def tile_of(i, first):
        return i // (own // FF_TILE), pl.ds(
            pl.multiple_of(first + (i % (own // FF_TILE)) * FF_TILE, FF_TILE), FF_TILE
        )

    def pair_copy(i):
        return remote(cast_buf.at[i % 2], pair_land.at[i], pair_send.at[i % 2], pair_recv.at[i], ring.partner)

    def give(i, carry):
        @pl.when(i >= 2)
        def _():
            pair_copy(i - 2).wait_send()

        k, span = tile_of(i, own)
        cast_buf[i % 2] = totals[k, span, :].astype(LOW)
        pair_copy(i).start()
        return carry

    lax.fori_loop(0, own_tiles, give, 0)
    for i in (own_tiles - 2, own_tiles - 1):
        pair_copy(i).wait_send()

    pieces = ((gate_grad,), (up_a, up_b), (down_grad,))

    def total_copies(i):
        matrix, low = i // (own // FF_TILE), (i % (own // FF_TILE)) * FF_TILE
        copies, begin = [], 0
        for piece in pieces[matrix]:
            end = begin + piece.shape[0]
            first, last = max(begin, low), min(end, low + FF_TILE)
            if first < last:
                copies.append(
                    pltpu.make_async_copy(
                        cast_buf.at[i % 2, pl.ds(first - low, last - first)],
                        piece.at[pl.ds(first - begin, last - first)],
                        cast_sem.at[i % 2, len(copies)],
                    )
                )
            begin = end
        return copies

    for i in range(own_tiles):
        if i >= 2:
            for copy in total_copies(i - 2):
                copy.wait()
        pair_copy(i).wait_recv()
        k, span = tile_of(i, 0)
        cast_buf[i % 2] = (totals[k, span, :] + pair_land[i].astype(F32)).astype(LOW)
        for copy in total_copies(i):
            copy.start()

    for d in (0, 1):
        part = pl.ds(d * half, half)
        reduce_copy(n - 1, d).wait_recv()
        grad_sum[part, :] += landed[d, (n - 1) % 2].astype(F32)
        reduce_copy(n - 1, d).wait_send()

    for i in (own_tiles - 2, own_tiles - 1):
        for copy in total_copies(i):
            copy.wait()

    def finish(t, carry):
        for d in (0, 1):
            send(t, d, False).wait_send()
        return carry

    lax.fori_loop(1, n, finish, 0)


def dense(normed, cotangents, own_weights, partner_weights):
    rows, features = normed.shape
    n = lax.axis_size("dp") // 2
    own = own_weights[0].shape[0]
    half = rows // 2
    vmem = pl.BlockSpec(memory_space=pltpu.VMEM)
    hbm = pl.BlockSpec(memory_space=pl.ANY)
    dma = pltpu.SemaphoreType.DMA
    own_tiles = 3 * own // FF_TILE
    return pl.pallas_call(
        dense_kernel,
        out_shape=(
            jax.ShapeDtypeStruct((rows, features), F32),
            jax.ShapeDtypeStruct((n, rows, features), LOW),
            jax.ShapeDtypeStruct((n, rows, features), LOW),
            jax.ShapeDtypeStruct((own, features), LOW),
            jax.ShapeDtypeStruct((own // 8, features), LOW),
            jax.ShapeDtypeStruct((own - own // 8, features), LOW),
            jax.ShapeDtypeStruct((own, features), LOW),
        ),
        in_specs=[vmem] + [hbm] * 8,
        out_specs=(vmem,) + (hbm,) * 6,
        scratch_shapes=[
            pltpu.VMEM((3, 2 * own, features), LOW),
            pltpu.VMEM((3, 2 * own, features), F32),
            pltpu.VMEM((rows, features), LOW),
            pltpu.VMEM((rows, features), LOW),
            pltpu.VMEM((rows, features), F32),
            pltpu.VMEM((rows, features), F32),
            pltpu.VMEM((2, half, features), LOW),
            pltpu.VMEM((2, 2, half, features), LOW),
            pltpu.VMEM((2, FF_TILE, features), LOW),
            pltpu.VMEM((own_tiles, FF_TILE, features), LOW),
            dma((2, n)), dma((2, n)), dma((2,)), dma((2, 2)),
            pltpu.SemaphoreType.REGULAR((2,)),
            dma((5,)), dma((6,)), dma((2, 2)), dma((2,)), dma((own_tiles,)),
        ],
        compiler_params=pltpu.CompilerParams(
            collective_id=2, has_side_effects=True, vmem_limit_bytes=62 * MIB
        ),
        cost_estimate=pl.CostEstimate(
            flops=2 * 9 * n * rows * features * 2 * own, bytes_accessed=500 * MIB, transcendentals=0
        ),
        name="dense",
    )(normed, *cotangents, *own_weights, *partner_weights)


def mixed_back_kernel(
    packs, mixed_in, grad_in, cotangent_in, gain, output_all, shares, grad_mixed, gain_part, grad_heads, *rest
):
    sums = rest[:packs]
    mixed, grad_two, cotangent, low, weights, staged, given, taken, sem, w_sem, send_sem, recv_sem, g_sem, t_sem = (
        rest[packs:]
    )
    ring = Ring()
    n = ring.chips
    devices = 2 * n
    rows, features = mixed.shape
    r = grad_heads.shape[1]
    pack = lax.axis_index("rep")
    spot = ring.place * 2 + ring.core
    loads = [
        pltpu.make_async_copy(src, dst, sem.at[i])
        for i, (src, dst) in enumerate(((mixed_in, mixed), (grad_in, grad_two), (cotangent_in, cotangent)))
    ]
    for load in loads:
        load.start()

    def chip_weights(k):
        at = lax.rem(ring.place + k, n) * 2
        return pltpu.make_async_copy(output_all.at[pl.ds(at, 2)], weights.at[pl.ds(2 * k, 2)], w_sem.at[k])

    def fetch(k, carry):
        chip_weights(k).start()
        return carry

    lax.fori_loop(0, n, fetch, 0)
    barrier = pltpu.get_barrier_semaphore()

    def to(k):
        other = lax.rem(spot + k, devices)
        return {"dp": chip_at(other // 2, n) * 2 + other % 2}

    def greet(k, carry):
        pl.semaphore_signal(barrier, inc=1, device_id=to(k), device_id_type=MESH)
        return carry

    lax.fori_loop(1, devices, greet, 0)
    pl.semaphore_wait(barrier, devices - 1)
    for load in loads:
        load.wait()
    gain_part[...] = jnp.zeros_like(gain_part)

    def norm_back(i, carry):
        span = pl.ds(pl.multiple_of(i * 16, 16), 16)
        value, grad = mixed[span, :], grad_two[span, :]
        scale = lax.rsqrt(jnp.mean(value * value, axis=1, keepdims=True) + EPSILON)
        scaled = grad * gain[...]
        shift = jnp.mean(value * scaled, axis=1, keepdims=True)
        total = cotangent[span, :].astype(F32) + scale * scaled - value * (scale * scale * scale * shift)
        grad_mixed[span, :] = total
        low[span, :] = total.astype(LOW)
        gain_part[...] += jnp.sum(grad * value * scale, axis=0, keepdims=True)
        return carry

    lax.fori_loop(0, rows // 16, norm_back, 0)

    def copy(k):
        return remote(
            staged.at[k],
            grad_heads.at[pl.ds(pl.multiple_of(spot * rows, rows), rows)],
            send_sem.at[k],
            recv_sem.at[k],
            to(k)["dp"],
        )

    def project(k, carry):
        chip_weights(k).wait()
        both = dot_nt(low[...], weights[pl.ds(2 * k, 2)].reshape(2 * r, features))
        for core in (0, 1):
            step = lax.rem(2 * k + core - ring.core + devices, devices)
            staged[step] = both[:, core * r : (core + 1) * r].astype(LOW)

            @pl.when(step > 0)
            def _():
                copy(step).start()

        return carry

    lax.fori_loop(0, n, project, 0)
    grad_heads[pl.ds(pl.multiple_of(spot * rows, rows), rows), :] = staged[0]

    def give(k):
        return remote(given.at[k], taken.at[k], g_sem.at[k], t_sem.at[k], ring.partner)

    for k in range(packs):
        given[k] = dot_tn(shares[1 - ring.core, lax.rem(pack + k, packs)], low[...]).astype(LOW)
        give(k).start()
    for k in range(packs):
        own = dot_tn(shares[ring.core, lax.rem(pack + k, packs)], low[...])
        give(k).wait_recv()
        sums[k][...] = (own + taken[k].astype(F32)).astype(LOW)

    def finish(k, carry):
        copy(k).wait_send()
        copy(k).wait_recv()
        return carry

    lax.fori_loop(1, devices, finish, 0)
    for k in range(packs):
        give(k).wait_send()


def mixed_back(mixed, grad_two, cotangent, gain, output_all, shares):
    rows, features = mixed.shape
    devices, r = output_all.shape[:2]
    packs = lax.axis_size("rep")
    n = devices // 2
    total = shares.shape[3]
    vmem = pl.BlockSpec(memory_space=pltpu.VMEM)
    hbm = pl.BlockSpec(memory_space=pl.ANY)
    dma = pltpu.SemaphoreType.DMA
    return pl.pallas_call(
        functools.partial(mixed_back_kernel, packs),
        out_shape=(
            jax.ShapeDtypeStruct((rows, features), F32),
            jax.ShapeDtypeStruct((1, features), F32),
            jax.ShapeDtypeStruct((devices * rows, r), LOW),
        )
        + (jax.ShapeDtypeStruct((total, features), LOW),) * packs,
        in_specs=[hbm] * 3 + [vmem, hbm, vmem],
        out_specs=(vmem,) * (3 + packs),
        scratch_shapes=[
            pltpu.VMEM((rows, features), F32),
            pltpu.VMEM((rows, features), F32),
            pltpu.VMEM((rows, features), LOW),
            pltpu.VMEM((rows, features), LOW),
            pltpu.VMEM((devices, r, features), LOW),
            pltpu.VMEM((devices, rows, r), LOW),
            pltpu.VMEM((packs, total, features), LOW),
            pltpu.VMEM((packs, total, features), LOW),
            dma((3,)), dma((n,)), dma((devices,)), dma((devices,)), dma((packs,)), dma((packs,)),
        ],
        compiler_params=pltpu.CompilerParams(
            collective_id=4, has_side_effects=True, vmem_limit_bytes=56 * MIB
        ),
        cost_estimate=pl.CostEstimate(
            flops=4 * rows * features * features, bytes_accessed=130 * MIB, transcendentals=0
        ),
        name="mixed_back",
    )(mixed, grad_two, cotangent, gain, output_all, shares)


def normed_back_kernel(
    packs, grads_in, joined, hidden_in, gain, grad_mixed, dense_gain_part, normed_all, output_mine, *rest
):
    output_there = rest[: packs - 1]
    (
        out, gains, query_total, key_total, value_total, output_grad,
        grads, partner_grads, sent, landed, x_buf, parts, pair_out, pair_land, rep_land,
        o_sent, o_landed, near_part, near_land, near_sum, far_land,
        in_sem, p_send, p_recv, rs_send, rs_recv, credit, x_sem, pair_sem, rep_send, rep_recv,
        o_send, o_recv, o_credit, near_send, near_recv, far_send, far_recv,
    ) = rest[packs - 1 :]
    ring = Ring()
    n = ring.chips
    rows, features = out.shape
    half = rows // 2
    r = grads.shape[2]
    share = output_grad.shape[0]
    pack = lax.axis_index("rep")
    mates = 2 * packs
    mate = pack * 2 + ring.core
    barrier = pltpu.get_barrier_semaphore()
    load_grads = pltpu.make_async_copy(grads_in, grads, in_sem)
    load_grads.start()

    def near(k):
        to = lax.rem(mate + k, mates)
        return {"dp": ring.chip * 2 + to % 2, "rep": to // 2}

    def far(k):
        return {"dp": lax.rem(ring.chip + k, n) * 2 + ring.core}

    for k in range(1, mates):
        pl.semaphore_signal(barrier, inc=1, device_id=near(k), device_id_type=MESH)
    for k in range(1, n):
        pl.semaphore_signal(barrier, inc=1, device_id=far(k), device_id_type=MESH)
    pl.semaphore_wait(barrier, mates + n - 2)
    load_grads.wait()

    def place(t, d):
        return ring.chip_far(-t if d == 0 else t)

    def swap(t, d):
        start = (place(t, d) * 2 + 1 - ring.core) * rows + d * half
        return remote(
            grads.at[:, pl.ds(pl.multiple_of(start, half), half)],
            partner_grads.at[:, t % n, half_rows(d, rows)],
            p_send.at[d, t % n],
            p_recv.at[d, t % n],
            ring.partner,
        )

    def begin(t, carry):
        for d in (0, 1):
            swap(t, d).start()
        return carry

    lax.fori_loop(1, n + 1, begin, 0)

    def reduce_copy(t, d, u):
        return remote(
            sent.at[d, u],
            landed.at[d, u, t % 2],
            rs_send.at[d, u],
            rs_recv.at[d, u, t % 2],
            ring.next[d],
        )

    def output_copy(t, d):
        return remote(
            o_sent.at[d], o_landed.at[d, t % 2], o_send.at[d], o_recv.at[d, t % 2], ring.next[d]
        )

    def give_credit(sem, d):
        pl.semaphore_signal(sem, inc=1, device_id={"dp": ring.back[d]}, device_id_type=MESH)

    def mine(t, d):
        start = (place(t, d) * 2 + ring.core) * rows + d * half
        return pl.ds(pl.multiple_of(start, half), half)

    def load(t, d):
        part = half_rows(d, rows)
        return pltpu.make_async_copy(normed_all.at[place(t, d), part], x_buf.at[t % 2, part], x_sem.at[t % 2, d])

    def block_grads(t):
        return jnp.concatenate(
            [jnp.concatenate([grads[i, mine(t, d), :] for d in (0, 1)], 0) for i in range(3)]
            + [partner_grads[i, t % n] for i in range(3)],
            1,
        )

    def weight_parts(t):
        for d in (0, 1):
            load(t, d).wait()
        parts[...] += dot_tn(block_grads(t), x_buf[t % 2])

    def pair_copy():
        return remote(pair_out, pair_land, pair_sem.at[0], pair_sem.at[1], ring.partner)

    def rep_copy(k):
        return pltpu.make_async_remote_copy(
            src_ref=pair_out,
            dst_ref=rep_land.at[k - 1],
            send_sem=rep_send.at[k - 1],
            recv_sem=rep_recv.at[k - 1],
            device_id={"rep": lax.rem(pack + k, packs)},
            device_id_type=MESH,
        )

    middle = n // 2

    def output_step(t):
        for d in (0, 1):
            spot = lax.rem(ring.place + (n - t if d == 0 else t), n)
            at = pl.ds(pl.multiple_of(spot * share, share), share)
            columns = pl.ds(d * (features // 2), features // 2)
            total = output_mine[at, columns].astype(F32)
            for there in output_there:
                total += there[at, columns].astype(F32)

            @pl.when(t == 1)
            def _():
                o_sent[d] = total.astype(LOW)
                output_copy(t, d).start()

            @pl.when(t >= 2)
            def _():
                output_copy(t - 1, d).wait_recv()
                more = total + o_landed[d, (t - 1) % 2].astype(F32)

                @pl.when(t <= n - 2)
                def _():
                    give_credit(o_credit.at[d], d)

                output_copy(t - 1, d).wait_send()

                @pl.when(t < n)
                def _():
                    o_sent[d] = more.astype(LOW)

                    @pl.when(t >= 3)
                    def _():
                        pl.semaphore_wait(o_credit.at[d], 1)

                    output_copy(t, d).start()

                @pl.when(t == n)
                def _():
                    output_grad[:, columns] = more.astype(LOW)

    def step(t, carry):
        @pl.when(t <= middle)
        def _():
            for d in (0, 1):
                load(2 * t - 1, d).start()
                load(2 * t, d).start()

        @pl.when(t == 1)
        def _():
            for d in (0, 1):
                swap(t, d).wait_recv()

        block = block_grads(t)
        for u in (0, 1):
            columns = pl.ds(u * (features // 2), features // 2)
            out[:, columns] = dot_nn(block, joined[:, columns])
            for d in (0, 1):
                part = pl.ds(d * half, half), columns

                @pl.when(t >= 2)
                def _():
                    reduce_copy(t - 1, d, u).wait_recv()
                    out[part] += landed[d, u, (t - 1) % 2].astype(F32)

                    @pl.when(t <= n - 2)
                    def _():
                        give_credit(credit.at[d, u], d)

                    reduce_copy(t - 1, d, u).wait_send()

                @pl.when(t < n)
                def _():
                    sent[d, u] = out[part].astype(LOW)

                    @pl.when(t >= 3)
                    def _():
                        pl.semaphore_wait(credit.at[d, u], 1)

                    reduce_copy(t, d, u).start()

        output_step(t)

        @pl.when(t == 1)
        def _():
            parts[...] = jnp.zeros_like(parts)

            def arrived(k, carry):
                for d in (0, 1):
                    swap(k, d).wait_recv()
                return carry

            lax.fori_loop(2, n + 1, arrived, 0)

        @pl.when(t <= middle)
        def _():
            weight_parts(2 * t - 1)
            weight_parts(2 * t)

        @pl.when(t == middle)
        def _():
            for i in range(3):
                pair_out[i] = parts[pl.ds((3 + i) * r, r), :].astype(LOW)
            pair_copy().start()

        @pl.when(t == middle + 1)
        def _():
            pair_copy().wait()
            for i in range(3):
                pair_out[i] = (parts[pl.ds(i * r, r), :] + pair_land[i].astype(F32)).astype(LOW)
            for k in range(1, packs):
                rep_copy(k).start()
            rep_land[packs - 1] = pair_out[...]

        return carry

    lax.fori_loop(1, n + 1, step, 0)

    near_part[0:1, :] = jnp.zeros((1, features), F32)
    near_part[1:2, :] = dense_gain_part[...]

    def close(i, carry):
        span = pl.ds(pl.multiple_of(i * 16, 16), 16)
        value = hidden_in[span, :].astype(F32)
        grad = out[span, :]
        scale = lax.rsqrt(jnp.mean(value * value, axis=1, keepdims=True) + EPSILON)
        scaled = grad * gain[...]
        shift = jnp.mean(value * scaled, axis=1, keepdims=True)
        out[span, :] = grad_mixed[span, :] + scale * scaled - value * (scale * scale * scale * shift)
        near_part[0:1, :] += jnp.sum(grad * value * scale, axis=0, keepdims=True)
        return carry

    lax.fori_loop(0, rows // 16, close, 0)

    def exchange(src, land, own, send_sem, recv_sem, device, count):
        copies = [
            pltpu.make_async_remote_copy(
                src_ref=src,
                dst_ref=land.at[own],
                send_sem=send_sem.at[k],
                recv_sem=recv_sem.at[k],
                device_id=device(k),
                device_id_type=MESH,
            )
            for k in range(1, count)
        ]
        for copy in copies:
            copy.start()
        land[own] = src[...]
        for copy in copies:
            copy.wait()
        total = land[0]
        for k in range(1, count):
            total += land[k]
        return total

    near_sum[...] = exchange(near_part, near_land, mate, near_send, near_recv, near, mates)
    gains[...] = exchange(near_sum, far_land, ring.chip, far_send, far_recv, far, n)

    def finish(t, carry):
        for d in (0, 1):
            swap(t, d).wait_send()
        return carry

    lax.fori_loop(1, n + 1, finish, 0)
    for k in range(1, packs):
        rep_copy(k).wait()
    for i, total in enumerate((query_total, key_total, value_total)):
        value = rep_land[lax.rem(pack + packs - 1, packs), i].astype(F32)
        for q in range(1, packs):
            value += rep_land[lax.rem(pack + 2 * packs - q - 1, packs), i].astype(F32)
        total[...] = value


def normed_back(
    grads, joined, hidden_in, gain, grad_mixed, dense_gain_part, normed_all, output_mine, output_there
):
    tokens, r = grads.shape[1:]
    features = joined.shape[1]
    devices = lax.axis_size("dp")
    packs = lax.axis_size("rep")
    n = devices // 2
    rows = tokens // devices
    half = rows // 2
    share = output_mine.shape[0] // n
    mates = 2 * packs
    vmem = pl.BlockSpec(memory_space=pltpu.VMEM)
    hbm = pl.BlockSpec(memory_space=pl.ANY)
    dma = pltpu.SemaphoreType.DMA
    return pl.pallas_call(
        functools.partial(normed_back_kernel, packs),
        out_shape=(
            jax.ShapeDtypeStruct((rows, features), F32),
            jax.ShapeDtypeStruct((2, features), F32),
        )
        + (jax.ShapeDtypeStruct((r, features), F32),) * 3
        + (jax.ShapeDtypeStruct((share, features), LOW),),
        in_specs=[hbm] + [vmem] * 5 + [hbm] + [vmem] * packs,
        out_specs=(vmem,) * 6,
        scratch_shapes=[
            pltpu.VMEM(grads.shape, LOW),
            pltpu.VMEM((3, n, rows, r), LOW),
            pltpu.VMEM((2, 2, half, features // 2), LOW),
            pltpu.VMEM((2, 2, 2, half, features // 2), LOW),
            pltpu.VMEM((2, rows, features), LOW),
            pltpu.VMEM((6 * r, features), F32),
            pltpu.VMEM((3, r, features), LOW),
            pltpu.VMEM((3, r, features), LOW),
            pltpu.VMEM((packs, 3, r, features), LOW),
            pltpu.VMEM((2, share, features // 2), LOW),
            pltpu.VMEM((2, 2, share, features // 2), LOW),
            pltpu.VMEM((2, features), F32),
            pltpu.VMEM((mates, 2, features), F32),
            pltpu.VMEM((2, features), F32),
            pltpu.VMEM((n, 2, features), F32),
            dma, dma((2, n)), dma((2, n)), dma((2, 2)), dma((2, 2, 2)),
            pltpu.SemaphoreType.REGULAR((2, 2)),
            dma((2, 2)), dma((2,)), dma((packs - 1,)), dma((packs - 1,)),
            dma((2,)), dma((2, 2)), pltpu.SemaphoreType.REGULAR((2,)),
            dma((mates,)), dma((mates,)), dma((n,)), dma((n,)),
        ],
        compiler_params=pltpu.CompilerParams(
            collective_id=3, has_side_effects=True, vmem_limit_bytes=56 * MIB
        ),
        cost_estimate=pl.CostEstimate(
            flops=2 * n * rows * features * 12 * r, bytes_accessed=320 * MIB, transcendentals=0
        ),
        name="normed_back",
    )(
        grads, joined, hidden_in, gain, grad_mixed, dense_gain_part, normed_all, output_mine, *output_there
    )


def rms(values, norm_gain):
    return (
        values * lax.rsqrt(jnp.mean(values * values, axis=-1, keepdims=True) + EPSILON) * norm_gain
    )


def from_partner(value):
    devices = lax.axis_size("dp")
    return lax.ppermute(value, "dp", [(i, i ^ 1) for i in range(devices)])


def pack_swap(low):
    if lax.axis_size("rep") == 2:
        return lax.ppermute(low, "rep", [(0, 1), (1, 0)])
    return lax.psum(low, "rep")


def pack_add(low, other):
    if lax.axis_size("rep") == 2:
        return low.astype(F32) + other.astype(F32)
    return other.astype(F32)


def together(*values):
    return lax.optimization_barrier(values)


def body(
    tokens,
    attention_gain,
    query_weight,
    key_weight,
    value_weight,
    output_weight,
    dense_gain,
    gate_weight,
    up_weight,
    down_weight,
    block_document,
    document_tail,
    cotangent,
):
    devices = lax.axis_size("dp")
    chips = devices // 2
    hidden_in = tokens[0].astype(F32)
    tok_dev = hidden_in.shape[0]
    pack_tok = tok_dev * devices

    documents, tails = block_document[0], document_tail[0]
    first = jnp.sum((documents[None, :] < documents[:, None]).astype(jnp.int32), axis=1)
    last = jnp.concatenate([documents[1:] != documents[:-1], jnp.ones((1,), bool)])
    doc_ids = jnp.arange(tails.shape[0], dtype=jnp.int32)
    own_tail = jnp.sum((documents[:, None] == doc_ids[None, :]) * tails[None, :], axis=1)
    tail = jnp.where(last, own_tail, BLOCK).astype(jnp.int32)
    block_index = jnp.arange(documents.shape[0], dtype=jnp.int32)
    inside = jnp.arange(BLOCK, dtype=jnp.int32)
    position = ((block_index - first)[:, None] * BLOCK + inside[None, :]).reshape(-1)
    frequency = ROPE_BASE ** (-(jnp.arange(HALF, dtype=F32) * (2.0 / HEAD_DIM)))
    angles = position.astype(F32)[None, :] * frequency[:, None]
    cos_t, sin_t = jnp.cos(angles), jnp.sin(angles)
    r = query_weight.shape[0]

    qkv, normed_all, full_output = gather_project(
        tokens[0],
        attention_gain[None],
        (query_weight, key_weight, value_weight),
        output_weight,
        cos_t,
        sin_t,
    )

    order = ring_order(chips)
    walk = [2 * chip + k for chip in order for k in (0, 1)]
    lanes = [[2 * chip + k for chip in order] for k in (0, 1)]
    grad_low = cotangent[0]
    early, late = grad_low[: tok_dev // 4], grad_low[tok_dev // 4 :]
    early = lax.all_gather(early, "dp", axis=0, axis_index_groups=lanes)
    qkv, early, late = together(qkv, early, late)
    cotangents = (early, lax.all_gather(late, "dp", axis=0, axis_index_groups=lanes))
    gate_other, up_other, down_other = (
        from_partner(gate_weight),
        from_partner(up_weight),
        from_partner(down_weight),
    )
    qkv_weight = jnp.concatenate([query_weight, key_weight, value_weight], 0)
    joined = jnp.concatenate([qkv_weight, from_partner(qkv_weight)], 0)

    attended, log_total = attend(first, tail, qkv)
    attended_blocks = lax.all_to_all(
        attended.reshape(devices, tok_dev, r),
        "dp",
        split_axis=0,
        concat_axis=0,
        tiled=True,
        axis_index_groups=[walk],
    )
    attended_here = attended_blocks.transpose(1, 0, 2).reshape(tok_dev, -1)
    mixed = hidden_in + dot_nn(attended_here, full_output.reshape(-1, output_weight.shape[1]))
    normed_two = rms(mixed, dense_gain).astype(LOW)

    packs, pack = lax.axis_size("rep"), lax.axis_index("rep")
    attended_shares = (
        attended_here.reshape(tok_dev, chips, 2, packs, r // packs)
        .transpose(2, 3, 0, 1, 4)
        .reshape(2, packs, tok_dev, -1)
    )
    normed_two, joined, attended_shares = together(normed_two, joined, attended_shares)

    grad_normed_two, out_parts, _, gate_low, up_a, up_b, down_low = dense(
        normed_two,
        cotangents,
        (gate_weight, up_weight, down_weight),
        (gate_other, up_other, down_other),
    )
    out_sum = lax.psum_scatter(
        out_parts.reshape(chips * tok_dev, -1),
        "dp",
        scatter_dimension=0,
        tiled=True,
        axis_index_groups=lanes,
    )
    gate_there = pack_swap(gate_low)

    grad_mixed, dense_gain_part, grad_heads, output_mine, *output_low = mixed_back(
        mixed, grad_normed_two, grad_low, dense_gain[None], full_output, attended_shares
    )
    output_there = [
        lax.ppermute(low, "rep", [(i, (i + k) % packs) for i in range(packs)])
        for k, low in enumerate(output_low, 1)
    ]
    grad_heads, gate_there, output_mine = together(grad_heads, gate_there, output_mine)
    up_a, _ = together(up_a, grad_heads)
    up_a_there = pack_swap(up_a)
    grads = attend_back(first, tail, qkv, grad_heads, attended, log_total, cos_t, sin_t)
    grads, output_there, out_sum, up_a_there, up_b, down_low = together(
        grads, output_there, out_sum, up_a_there, up_b, down_low
    )
    up_b_there = pack_swap(up_b)
    down_there = pack_swap(down_low)
    up_b_there = pack_swap(up_b)
    down_there = pack_swap(down_low)
    output_grad = lax.psum_scatter(
        sum((there.astype(F32) for there in output_there), output_mine.astype(F32)).astype(LOW),
        "dp",
        scatter_dimension=0,
        tiled=True,
        axis_index_groups=lanes,
    )
    input_grad, gain_totals, query_total, key_total, value_total, output_grad = normed_back(
        grads,
        joined,
        tokens[0],
        attention_gain[None],
        grad_mixed,
        dense_gain_part,
        normed_all,
        output_mine,
        output_there,
    )
    input_grad, out_sum, gate_there, up_a_there, up_b_there, down_there = together(
        input_grad, out_sum, gate_there, up_a_there, up_b_there, down_there
    )
    output_total = lax.all_gather(output_grad, "rep", axis=0, tiled=True)
    if packs == 2:
        output_other = lax.ppermute(output_grad, "rep", [(0, 1), (1, 0)])
        output_total = jnp.where(
            pack == 0,
            jnp.concatenate([output_grad, output_other], 0),
            jnp.concatenate([output_other, output_grad], 0),
        )
    layer_out = mixed + out_sum.astype(F32)
    return (
        layer_out[None].astype(LOW),
        input_grad[None],
        gain_totals[0],
        query_total,
        key_total,
        value_total,
        output_total.astype(F32),
        gain_totals[1],
        pack_add(gate_low, gate_there),
        jnp.concatenate([pack_add(up_a, up_a_there), pack_add(up_b, up_b_there)], 0),
        pack_add(down_low, down_there),
    )


def solution(mesh):
    return jax.shard_map(
        body,
        mesh=mesh,
        in_specs=(
            P("rep", "dp", None),
            P(),
            P("dp", None),
            P("dp", None),
            P("dp", None),
            P("dp", None),
            P(),
            P("dp", None),
            P("dp", None),
            P("dp", None),
            P("rep", None),
            P("rep", None),
            P("rep", "dp", None),
        ),
        out_specs=(
            P("rep", "dp", None),
            P("rep", "dp", None),
            P(),
            P("dp", None),
            P("dp", None),
            P("dp", None),
            P("dp", None),
            P(),
            P("dp", None),
            P("dp", None),
            P("dp", None),
        ),
        check_vma=False,
    )
```

```python
import functools
import math

import jax
import jax.numpy as jnp
from jax import lax
from jax.experimental import pallas as pl
from jax.experimental.pallas import tpu as pltpu
from jax.sharding import PartitionSpec as P

HEAD_DIM = 64
HALF = HEAD_DIM // 2
BLOCK = 128
CHUNK = 512
FF_TILE = 256
EPSILON = 1e-05
ROPE_BASE = 130000.0
MASKED_SCORE = -1e30
MESH = pl.DeviceIdType.MESH
MIB = 2**20
LOW = jnp.bfloat16
F32 = jnp.float32


def dot_nn(a, b):
    return lax.dot_general(a, b, (((1,), (0,)), ((), ())), preferred_element_type=F32)


def dot_nt(a, b):
    return lax.dot_general(a, b, (((1,), (1,)), ((), ())), preferred_element_type=F32)


def dot_tn(a, b):
    return lax.dot_general(a, b, (((0,), (0,)), ((), ())), preferred_element_type=F32)


def grid_of(chips):
    depth = 4 if chips % 8 == 0 else 2
    return depth, chips // depth


def chip_at(place, chips):
    depth, width = grid_of(chips)
    place = lax.rem(place + chips, chips)
    later = place - depth
    row, column = later // (width - 1), later % (width - 1)
    odd = row % 2
    far = (depth - 1 - row) * width + 1 + column + odd * (width - 2 - 2 * column)
    return jnp.where(place < depth, place * width, far)


def place_of(chip, chips):
    depth, width = grid_of(chips)
    z, x = chip // width, chip % width
    row = depth - 1 - z
    odd = row % 2
    column = x - 1 + odd * (width - 2 * x)
    return jnp.where(x == 0, z, depth + row * (width - 1) + column)


def ring_order(chips):
    depth, width = grid_of(chips)
    order = [z * width for z in range(depth)]
    for row in range(depth):
        columns = list(range(1, width))
        order += [(depth - 1 - row) * width + x for x in (columns[::-1] if row % 2 else columns)]
    return order


class Ring:
    def __init__(self):
        self.chips = lax.axis_size("dp") // 2
        me = lax.axis_index("dp")
        self.core = me % 2
        self.chip = me // 2
        self.partner = self.chip * 2 + 1 - self.core
        self.place = place_of(self.chip, self.chips)
        self.next = (self.device(1), self.device(-1))
        self.back = (self.next[1], self.next[0])

    def chip_far(self, steps):
        return chip_at(self.place + steps, self.chips)

    def device(self, steps):
        return self.chip_far(steps) * 2 + self.core

    def greet(self, others):
        barrier = pltpu.get_barrier_semaphore()
        for other in others:
            pl.semaphore_signal(barrier, inc=1, device_id={"dp": other}, device_id_type=MESH)
        pl.semaphore_wait(barrier, len(others))


def remote(src, dst, send_sem, recv_sem, device):
    return pltpu.make_async_remote_copy(
        src_ref=src,
        dst_ref=dst,
        send_sem=send_sem,
        recv_sem=recv_sem,
        device_id={"dp": device},
        device_id_type=MESH,
    )


def half_rows(direction, rows):
    return pl.ds(direction * (rows // 2), rows // 2)


def turned(u):
    parts = []
    for at in range(0, u.shape[1], HEAD_DIM):
        parts += [-u[:, at + HALF : at + HEAD_DIM], u[:, at : at + HALF]]
    return jnp.concatenate(parts, 1)


def gather_project_kernel(
    tokens_in, gain, query_w, key_w, value_w, output_w, cos_t, sin_t, qkv, gathered, output_all,
    tokens, own_weights, normed, partner_weights, x_buf, staged,
    in_sem, ag_send, ag_recv, w_send, w_recv, q_send, q_recv, local_sem,
    o_send, o_recv, pair_send, pair_recv, rep_send, rep_recv, far_send, far_recv,
):
    ring = Ring()
    n = ring.chips
    packs, pack = lax.axis_size("rep"), lax.axis_index("rep")
    rows = normed.shape[0]
    half = rows // 2
    r = qkv.shape[2]
    sources = (query_w, key_w, value_w)
    load_tokens = pltpu.make_async_copy(tokens_in, tokens, in_sem.at[3])
    load_tokens.start()
    load_weights = [
        pltpu.make_async_copy(source, own_weights.at[i], in_sem.at[i]) for i, source in enumerate(sources)
    ]
    for load in load_weights:
        load.start()
    barrier = pltpu.get_barrier_semaphore()
    for k in range(1, packs):
        pl.semaphore_signal(
            barrier, inc=1, device_id={"rep": lax.rem(pack + k, packs)}, device_id_type=MESH
        )
    for other in (ring.next[0], ring.next[1], ring.partner):
        pl.semaphore_signal(barrier, inc=1, device_id={"dp": other}, device_id_type=MESH)
    pl.semaphore_wait(barrier, 3 + packs - 1)

    load_tokens.wait()

    def normalize(i, carry):
        span = pl.ds(pl.multiple_of(i * 32, 32), 32)
        value = tokens[span, :].astype(F32)
        scale = lax.rsqrt(jnp.mean(value * value, axis=1, keepdims=True) + EPSILON)
        normed[span, :] = (value * scale * gain[...]).astype(LOW)
        return carry

    lax.fori_loop(0, rows // 32, normalize, 0)

    def hop(t, d):
        chip = ring.chip_far((1 - t) if d == 0 else (t - 1))
        return chip, half_rows(d, rows)

    def send(t, d, first):
        chip, part = hop(t, d)
        src = normed.at[part] if first else gathered.at[chip, part]
        return remote(src, gathered.at[chip, part], ag_send.at[d, t - 1], ag_recv.at[d, t - 1], ring.next[d])

    out_rows, features = output_w.shape
    share = out_rows // packs
    spot = ring.place * 2 + ring.core

    def share_of(q, d):
        return pl.ds(pl.multiple_of(q * share, share), share), pl.ds(d * (features // 2), features // 2)

    def block_at(t, d, q, core):
        place = lax.rem(ring.place + (n - t if d == 0 else t), n)
        at_rows, columns = share_of(q, d)
        return output_all.at[place * 2 + core, at_rows, columns]

    def o_copy(t, d, first):
        at_rows, columns = share_of(pack, d)
        src = output_w.at[at_rows, columns] if first else block_at(t - 1, d, pack, ring.core)
        return remote(
            src, block_at(t - 1, d, pack, ring.core), o_send.at[d, t], o_recv.at[d, t], ring.next[d]
        )

    def pair_copy(t, d):
        block = block_at(t, d, pack, ring.core)
        return remote(block, block, pair_send.at[d, t], pair_recv.at[d, t], ring.partner)

    def rep_copy(t, d, k):
        block = block_at(t, d, pack, ring.core)
        return pltpu.make_async_remote_copy(
            src_ref=block,
            dst_ref=block,
            send_sem=rep_send.at[k - 1, d, t],
            recv_sem=rep_recv.at[k - 1, d, t],
            device_id={"rep": lax.rem(pack + k, packs)},
            device_id_type=MESH,
        )

    def far_copy(t, d, k):
        block = block_at(t, d, lax.rem(pack + packs - k, packs), ring.core)
        return remote(block, block, far_send.at[k - 1, d, t], far_recv.at[k - 1, d, t], ring.partner)

    def forward_far(t):
        for d in (0, 1):
            for k in range(1, packs):
                rep_copy(t, d, k).wait_recv()
                far_copy(t, d, k).start()

    for d in (0, 1):
        send(1, d, True).start()
    for d in (0, 1):
        o_copy(1, d, True).start()
    own_rows = remote(output_w, output_all.at[spot], local_sem.at[3], local_sem.at[4], ring.partner)
    own_rows.start()
    own_keep = pltpu.make_async_copy(output_w, output_all.at[spot], local_sem.at[5])
    own_keep.start()
    swaps = [
        remote(sources[i], partner_weights.at[i], w_send.at[i], w_recv.at[i], ring.partner)
        for i in range(3)
    ]
    for swap in swaps:
        swap.start()
    keep = pltpu.make_async_copy(normed, gathered.at[ring.chip], local_sem.at[2])
    keep.start()

    def project_block(t, from_input):
        x = normed[...] if from_input else x_buf[...]
        places = [ring.chip_far(-t), ring.chip_far(t)]
        starts = [
            pl.multiple_of((places[d] * 2 + ring.core) * rows + d * half, half) for d in (0, 1)
        ]

        def table(source):
            wide = [source[:, pl.ds(starts[d], half)] for d in (0, 1)]
            return jnp.concatenate(
                [jnp.concatenate([w] * (r // HALF), 0).T for w in wide], 0
            )

        cos, sin = table(cos_t), table(sin_t)

        def heads(w):
            query, key, value = [dot_nt(x, w[i][...]) for i in range(3)]
            return (
                (query * cos + turned(query) * sin).astype(LOW),
                (key * cos + turned(key) * sin).astype(LOW),
                value.astype(LOW),
            )

        for i, value in enumerate(heads([own_weights.at[i] for i in range(3)])):
            for d in (0, 1):
                qkv[i, pl.ds(starts[d], half), :] = value[d * half : (d + 1) * half]
        if from_input:
            for swap in swaps:
                swap.wait()
        for i, value in enumerate(heads([partner_weights.at[i] for i in range(3)])):
            staged[t, i] = value
        for d in (0, 1):
            remote(
                staged.at[t, :, half_rows(d, rows)],
                qkv.at[:, pl.ds(starts[d], half)],
                q_send.at[d, t],
                q_recv.at[d, t],
                ring.partner,
            ).start()

    for load in load_weights:
        load.wait()
    project_block(0, True)

    def step(t, carry):
        for d in (0, 1):
            send(t, d, False).wait_recv()

        @pl.when(t < n - 1)
        def _():
            for d in (0, 1):
                send(t + 1, d, False).start()

        for d in (0, 1):
            o_copy(t, d, False).wait_recv()

        @pl.when(t < n - 1)
        def _():
            for d in (0, 1):
                o_copy(t + 1, d, False).start()

        for d in (0, 1):
            for k in range(1, packs):
                rep_copy(t, d, k).start()
            pair_copy(t, d).start()

        @pl.when(t > 1)
        def _():
            forward_far(t - 1)

        loads = []
        for d in (0, 1):
            chip, part = hop(t + 1, d)
            loads.append(pltpu.make_async_copy(gathered.at[chip, part], x_buf.at[part], local_sem.at[d]))
        for load in loads:
            load.start()
        for load in loads:
            load.wait()
        project_block(t, False)
        return carry

    lax.fori_loop(1, n, step, 0)
    forward_far(n - 1)

    def finish(t, carry):
        for d in (0, 1):
            send(t, d, False).wait_send()
            o_copy(t, d, False).wait_send()
            pair_copy(t, d).wait()
            for k in range(1, packs):
                rep_copy(t, d, k).wait_send()
                far_copy(t, d, k).wait()
        return carry

    lax.fori_loop(1, n, finish, 0)
    own_rows.wait()
    own_keep.wait()

    def finish_heads(t, carry):
        for d in (0, 1):
            done = remote(
                staged.at[t, :, half_rows(d, rows)],
                qkv.at[:, half_rows(d, rows)],
                q_send.at[d, t],
                q_recv.at[d, t],
                ring.partner,
            )
            done.wait_send()
            done.wait_recv()
        return carry

    lax.fori_loop(0, n, finish_heads, 0)
    keep.wait()


def gather_project(tokens, gain, weights, output_weight, cos_t, sin_t):
    rows, features = tokens.shape
    r = weights[0].shape[0]
    devices = lax.axis_size("dp")
    packs = lax.axis_size("rep")
    n = devices // 2
    vmem = pl.BlockSpec(memory_space=pltpu.VMEM)
    dma = pltpu.SemaphoreType.DMA
    hbm = pl.BlockSpec(memory_space=pl.ANY)
    return pl.pallas_call(
        gather_project_kernel,
        out_shape=(
            jax.ShapeDtypeStruct((3, devices * rows, r), LOW),
            jax.ShapeDtypeStruct((n, rows, features), LOW),
            jax.ShapeDtypeStruct((devices,) + output_weight.shape, LOW),
        ),
        in_specs=[hbm, vmem] + [hbm] * 4 + [vmem] * 2,
        out_specs=(vmem, pl.BlockSpec(memory_space=pl.ANY), pl.BlockSpec(memory_space=pl.ANY)),
        scratch_shapes=[
            pltpu.VMEM((rows, features), LOW),
            pltpu.VMEM((3, r, features), LOW),
            pltpu.VMEM((rows, features), LOW),
            pltpu.VMEM((3, r, features), LOW),
            pltpu.VMEM((rows, features), LOW),
            pltpu.VMEM((n, 3, rows, r), LOW),
            dma((4,)),
            dma((2, n)), dma((2, n)), dma((3,)), dma((3,)), dma((2, n)), dma((2, n)), dma((6,)),
            dma((2, n)), dma((2, n)), dma((2, n)), dma((2, n)),
            dma((packs - 1, 2, n)), dma((packs - 1, 2, n)),
            dma((packs - 1, 2, n)), dma((packs - 1, 2, n)),
        ],
        compiler_params=pltpu.CompilerParams(
            collective_id=1, has_side_effects=True, vmem_limit_bytes=60 * MIB
        ),
        cost_estimate=pl.CostEstimate(
            flops=4 * n * rows * features * 3 * r, bytes_accessed=320 * MIB, transcendentals=0
        ),
        name="gather_project",
    )(tokens, gain, *weights, output_weight, cos_t, sin_t)


def split_heads(u):
    heads = u.shape[1] // HEAD_DIM
    if heads == 1:
        return u
    lane = lax.broadcasted_iota(jnp.int32, u.shape, 1) // HEAD_DIM
    zero = jnp.zeros_like(u)
    return jnp.concatenate([jnp.where(lane == h, u, zero) for h in range(heads)], 0)


def join_heads(u):
    heads = u.shape[0] // HEAD_DIM
    return jnp.concatenate(
        [u[h * HEAD_DIM : (h + 1) * HEAD_DIM, h * BLOCK : (h + 1) * BLOCK] for h in range(heads)], 0
    )


def transpose_blocks(source, target):
    def one(b, carry):
        at = pl.multiple_of(b * BLOCK, BLOCK)
        target[:, pl.ds(at, BLOCK)] = source[pl.ds(at, BLOCK), :].astype(F32).T.astype(LOW)
        return carry

    lax.fori_loop(0, source.shape[0] // BLOCK, one, 0)


def window_of(b, first, tail, columns):
    start = pl.multiple_of(jnp.maximum(b - (CHUNK // BLOCK - 1), 0) * BLOCK, BLOCK)
    whole = (b - first) // (CHUNK // BLOCK)
    lowest = (first + whole * (CHUNK // BLOCK)) * BLOCK
    key_index = start + lax.broadcasted_iota(jnp.int32, (CHUNK, columns), 0)
    query_index = b * BLOCK + lax.broadcasted_iota(jnp.int32, (CHUNK, columns), 1) % BLOCK
    allowed = (
        (key_index >= lowest)
        & (key_index <= query_index)
        & (key_index < b * BLOCK + tail)
    )
    return start, whole, allowed


def walk_rows(b, tok_dev, chips):
    device = b * BLOCK // tok_dev
    spot = place_of(device // 2, chips) * 2 + device % 2
    return pl.ds(pl.multiple_of(spot * tok_dev + b * BLOCK % tok_dev, BLOCK), BLOCK)


def attend_kernel(chips, first_ref, tail_ref, qkv, attended, log_total, value_t):
    tokens, r = qkv.shape[1:]
    tok_dev = tokens // (2 * chips)
    columns = (r // HEAD_DIM) * BLOCK
    scale = 1.0 / math.sqrt(HEAD_DIM)
    transpose_blocks(qkv.at[2], value_t)

    def block(b, carry):
        at = pl.multiple_of(b * BLOCK, BLOCK)
        query = split_heads(qkv[0, pl.ds(at, BLOCK), :])
        start, whole, allowed = window_of(b, first_ref[b], tail_ref[b], columns)
        scores = dot_nt(qkv[1, pl.ds(start, CHUNK), :], query) * scale
        scores = jnp.where(allowed, scores, MASKED_SCORE)
        top = jnp.max(scores, axis=0, keepdims=True)
        weights = jnp.exp(scores - top)
        total = jnp.sum(weights, axis=0, keepdims=True)
        out = dot_nn(value_t[:, pl.ds(start, CHUNK)], weights.astype(LOW))

        def more(i, state):
            top, total, out = state
            start = pl.multiple_of(first_ref[b] * BLOCK + i * CHUNK, BLOCK)
            scores = dot_nt(qkv[1, pl.ds(start, CHUNK), :], query) * scale
            higher = jnp.maximum(top, jnp.max(scores, axis=0, keepdims=True))
            shrink = jnp.exp(top - higher)
            weights = jnp.exp(scores - higher)
            total = total * shrink + jnp.sum(weights, axis=0, keepdims=True)
            out = out * shrink + dot_nn(value_t[:, pl.ds(start, CHUNK)], weights.astype(LOW))
            return higher, total, out

        top, total, out = lax.fori_loop(0, whole, more, (top, total, out))
        log_total[pl.ds(b, 1), :] = top + jnp.log(total)
        attended[walk_rows(b, tok_dev, chips), :] = join_heads(out / total).T.astype(LOW)
        return carry

    lax.fori_loop(0, tokens // BLOCK, block, 0)


def attend(first, tail, qkv):
    tokens, r = qkv.shape[1:]
    smem = pl.BlockSpec(memory_space=pltpu.SMEM)
    vmem = pl.BlockSpec(memory_space=pltpu.VMEM)
    return pl.pallas_call(
        functools.partial(attend_kernel, lax.axis_size("dp") // 2),
        out_shape=(
            jax.ShapeDtypeStruct((tokens, r), LOW),
            jax.ShapeDtypeStruct((tokens // BLOCK, (r // HEAD_DIM) * BLOCK), F32),
        ),
        in_specs=[smem, smem, vmem],
        out_specs=(vmem, vmem),
        scratch_shapes=[pltpu.VMEM((r, tokens), LOW)],
        compiler_params=pltpu.CompilerParams(vmem_limit_bytes=40 * MIB),
        cost_estimate=pl.CostEstimate(
            flops=4 * tokens * 1024 * r * 8, bytes_accessed=120 * MIB, transcendentals=tokens * 1024
        ),
        name="attend",
    )(first, tail, qkv)


def unrotate(g, cos, sin):
    parts = []
    for h in range(g.shape[0] // HEAD_DIM):
        one = g[h * HEAD_DIM : h * HEAD_DIM + HALF]
        two = g[h * HEAD_DIM + HALF : (h + 1) * HEAD_DIM]
        parts += [one * cos + two * sin, two * cos - one * sin]
    return jnp.concatenate(parts, 0)


def attend_back_kernel(
    chips, first_ref, tail_ref, qkv, grad_out, attended, log_total, cos_t, sin_t, grads,
    key_t, grad_key, grad_value, staged, store_sem,
):
    tokens, r = qkv.shape[1:]
    tok_dev = tokens // (2 * chips)
    heads = r // HEAD_DIM
    columns = heads * BLOCK
    scale = 1.0 / math.sqrt(HEAD_DIM)
    transpose_blocks(qkv.at[1], key_t)
    grad_key[...] = jnp.zeros_like(grad_key)
    grad_value[...] = jnp.zeros_like(grad_value)

    def block(b, carry):
        at = pl.multiple_of(b * BLOCK, BLOCK)
        here = pl.ds(at, BLOCK)
        query = split_heads(qkv[0, here, :])
        walk = walk_rows(b, tok_dev, chips)
        grad_rows = grad_out[walk, :]
        grad = split_heads(grad_rows)
        product = (grad_rows.astype(F32) * attended[walk, :].astype(F32)).T
        delta = jnp.concatenate(
            [
                jnp.sum(product[h * HEAD_DIM : (h + 1) * HEAD_DIM], axis=0, keepdims=True)
                for h in range(heads)
            ],
            1,
        )
        log_row = log_total[pl.ds(b, 1), :]

        def chunk(start, allowed, grad_query):
            span = pl.ds(start, CHUNK)
            scores = dot_nt(qkv[1, span, :], query) * scale
            weights = jnp.exp(scores - log_row)
            if allowed is not None:
                weights = jnp.where(allowed, weights, 0.0)
            grad_weights = dot_nt(qkv[2, span, :], grad)
            grad_scores = (weights * (grad_weights - delta)).astype(LOW)
            grad_value[span, :] += dot_nn(weights.astype(LOW), grad)
            grad_key[span, :] += dot_nn(grad_scores, query)
            return grad_query + dot_nn(key_t[:, span], grad_scores)

        start, whole, allowed = window_of(b, first_ref[b], tail_ref[b], columns)
        grad_query = chunk(start, allowed, jnp.zeros((r, columns), F32))
        grad_query = lax.fori_loop(
            0,
            whole,
            lambda i, g: chunk(pl.multiple_of(first_ref[b] * BLOCK + i * CHUNK, BLOCK), None, g),
            grad_query,
        )
        turned = unrotate(join_heads(grad_query) * scale, cos_t[:, here], sin_t[:, here])
        staged[0, here, :] = turned.T.astype(LOW)
        return carry

    lax.fori_loop(0, tokens // BLOCK, block, 0)
    query_store = pltpu.make_async_copy(staged.at[0], grads.at[0], store_sem.at[0])
    query_store.start()

    def close(b, carry):
        here = pl.ds(pl.multiple_of(b * BLOCK, BLOCK), BLOCK)
        turned = unrotate(grad_key[here, :].T * scale, cos_t[:, here], sin_t[:, here])
        staged[1, here, :] = turned.T.astype(LOW)
        staged[2, here, :] = grad_value[here, :].astype(LOW)
        return carry

    lax.fori_loop(0, tokens // BLOCK, close, 0)
    rest_store = pltpu.make_async_copy(staged.at[pl.ds(1, 2)], grads.at[pl.ds(1, 2)], store_sem.at[1])
    rest_store.start()
    query_store.wait()
    rest_store.wait()


def attend_back(first, tail, qkv, grad_out, attended, log_total, cos_t, sin_t):
    tokens, r = qkv.shape[1:]
    smem = pl.BlockSpec(memory_space=pltpu.SMEM)
    vmem = pl.BlockSpec(memory_space=pltpu.VMEM)
    return pl.pallas_call(
        functools.partial(attend_back_kernel, lax.axis_size("dp") // 2),
        out_shape=jax.ShapeDtypeStruct((3, tokens, r), LOW),
        in_specs=[smem, smem] + [vmem] * 6,
        out_specs=pl.BlockSpec(memory_space=pl.ANY),
        scratch_shapes=[
            pltpu.VMEM((r, tokens), LOW),
            pltpu.VMEM((tokens, r), F32),
            pltpu.VMEM((tokens, r), F32),
            pltpu.VMEM((3, tokens, r), LOW),
            pltpu.SemaphoreType.DMA((2,)),
        ],
        compiler_params=pltpu.CompilerParams(vmem_limit_bytes=40 * MIB),
        cost_estimate=pl.CostEstimate(
            flops=10 * tokens * 1024 * r * 8, bytes_accessed=240 * MIB, transcendentals=tokens * 1024
        ),
        name="attend_back",
    )(first, tail, qkv, grad_out, attended, log_total, cos_t, sin_t)


def mixed_kernel(
    attended, tokens_in, gain, output_all, mixed, normed, blocks,
    tokens, weights, sem, w_sem, send_sem, recv_sem,
):
    ring = Ring()
    n = ring.chips
    devices = 2 * n
    rows, features = mixed.shape
    r = attended.shape[1]
    spot = ring.place * 2 + ring.core
    load = pltpu.make_async_copy(tokens_in, tokens, sem)
    load.start()

    def place_at(j):
        return lax.rem(ring.place + (j % 2) * ((j + 1) // 2) + (1 - j % 2) * (n - j // 2), n)

    def chip_weights(j):
        place = place_at(j)
        return pltpu.make_async_copy(
            output_all.at[pl.ds(place * 2, 2)], weights.at[pl.ds(place * 2, 2)], w_sem.at[j]
        )

    def fetch(j, carry):
        chip_weights(j).start()
        return carry

    lax.fori_loop(0, n, fetch, 0)
    barrier = pltpu.get_barrier_semaphore()

    def to(k):
        other = lax.rem(spot + k, devices)
        return chip_at(other // 2, n) * 2 + other % 2

    def greet(k, carry):
        pl.semaphore_signal(barrier, inc=1, device_id={"dp": to(k)}, device_id_type=MESH)
        return carry

    lax.fori_loop(1, devices, greet, 0)
    pl.semaphore_wait(barrier, devices - 1)

    def rows_of(at):
        return pl.ds(pl.multiple_of(at * rows, rows), rows)

    def copy(k):
        return remote(
            attended.at[rows_of(lax.rem(spot + k, devices))],
            blocks.at[spot],
            send_sem.at[k],
            recv_sem.at[k],
            to(k),
        )

    def begin(k, carry):
        copy(k).start()
        return carry

    lax.fori_loop(1, devices, begin, 0)
    blocks[spot] = attended[rows_of(spot), :]
    load.wait()
    mixed[...] = tokens[...].astype(F32)

    def add(j, carry):
        chip_weights(j).wait()
        place = place_at(j)
        for core in (0, 1):
            k = lax.rem(spot + devices - place * 2 - core, devices)

            @pl.when(k > 0)
            def _():
                copy(k).wait_recv()

        both = jnp.concatenate([blocks[place * 2 + core] for core in (0, 1)], 1)
        mixed[...] += dot_nn(both, weights[pl.ds(place * 2, 2)].reshape(2 * r, features))
        return carry

    lax.fori_loop(0, n, add, 0)

    def normalize(i, carry):
        span = pl.ds(pl.multiple_of(i * 32, 32), 32)
        value = mixed[span, :]
        scale = lax.rsqrt(jnp.mean(value * value, axis=1, keepdims=True) + EPSILON)
        normed[span, :] = (value * scale * gain[...]).astype(LOW)
        return carry

    lax.fori_loop(0, rows // 32, normalize, 0)

    def finish(k, carry):
        copy(k).wait_send()
        return carry

    lax.fori_loop(1, devices, finish, 0)


def mix(attended, tokens, gain, output_all):
    rows, features = tokens.shape
    devices, r = output_all.shape[:2]
    vmem = pl.BlockSpec(memory_space=pltpu.VMEM)
    hbm = pl.BlockSpec(memory_space=pl.ANY)
    dma = pltpu.SemaphoreType.DMA
    return pl.pallas_call(
        mixed_kernel,
        out_shape=(
            jax.ShapeDtypeStruct((rows, features), F32),
            jax.ShapeDtypeStruct((rows, features), LOW),
            jax.ShapeDtypeStruct((devices, rows, r), LOW),
        ),
        in_specs=[vmem, hbm, vmem, hbm],
        out_specs=(vmem,) * 3,
        scratch_shapes=[
            pltpu.VMEM((rows, features), LOW),
            pltpu.VMEM((devices, r, features), LOW),
            dma, dma((devices // 2,)), dma((devices,)), dma((devices,)),
        ],
        compiler_params=pltpu.CompilerParams(
            collective_id=5, has_side_effects=True, vmem_limit_bytes=56 * MIB
        ),
        cost_estimate=pl.CostEstimate(
            flops=2 * rows * features * features, bytes_accessed=100 * MIB, transcendentals=0
        ),
        name="mix",
    )(attended, tokens, gain, output_all)


def dense_kernel(
    normed, cotangents, gate_w, up_w, down_w, gate_p, up_p, down_p,
    grad_sum, out_parts, gathered, gate_grad, up_a, up_b, down_grad,
    weights, totals, x_buf, g_buf, out_acc, grad_acc, sent, landed, cast_buf, pair_land,
    ag_send, ag_recv, rs_send, rs_recv, credit, local_sem, w_sem, cast_sem, pair_send, pair_recv,
):
    ring = Ring()
    n = ring.chips
    rows, features = normed.shape
    half = rows // 2
    own = gate_w.shape[0]
    tiles = 2 * own // FF_TILE
    loads = []
    for i, (mine, theirs) in enumerate(((gate_w, gate_p), (up_w, up_p), (down_w, down_p))):
        loads.append(pltpu.make_async_copy(mine, weights.at[i, pl.ds(0, own)], w_sem.at[2 * i]))
        loads.append(pltpu.make_async_copy(theirs, weights.at[i, pl.ds(own, own)], w_sem.at[2 * i + 1]))
    for load in loads:
        load.start()
    ring.greet((ring.next[0], ring.next[1], ring.partner))

    def source(t, d):
        return lax.rem(ring.place + (n - t if d == 0 else t), n)

    def send(t, d, first):
        place, part = source(t - 1, d), half_rows(d, rows)
        src = normed.at[part] if first else gathered.at[place, part]
        return remote(src, gathered.at[place, part], ag_send.at[d, t - 1], ag_recv.at[d, t - 1], ring.next[d])

    def reduce_copy(t, d):
        return remote(sent.at[d], landed.at[d, t % 2], rs_send.at[d], rs_recv.at[d, t % 2], ring.next[d])

    for d in (0, 1):
        send(1, d, True).start()

    def clear(i, carry):
        span = pl.ds(pl.multiple_of(i * FF_TILE, FF_TILE), FF_TILE)
        for k in range(3):
            totals[k, span, :] = jnp.zeros((FF_TILE, features), F32)
        return carry

    lax.fori_loop(0, tiles, clear, 0)
    for load in loads:
        load.wait()

    def out_copy(t, d):
        part = half_rows(d, rows)
        return pltpu.make_async_copy(
            cast_buf.at[t % 2, part], out_parts.at[source(t, d), part], cast_sem.at[t % 2, d]
        )

    def pass_on(t):
        for d in (0, 1):
            send(t, d, False).wait_recv()

        @pl.when(t < n - 1)
        def _():
            for d in (0, 1):
                send(t + 1, d, False).start()

    def step(t, carry):
        copies = []
        for d in (0, 1):
            part = half_rows(d, rows)
            copies.append(
                pltpu.make_async_copy(cotangents.at[source(t, d), part], g_buf.at[part], local_sem.at[d])
            )
        for copy in copies:
            copy.start()

        @pl.when(t > 1)
        def _():
            pass_on(t)

        @pl.when(t > 0)
        def _():
            more = []
            for d in (0, 1):
                part = half_rows(d, rows)
                more.append(
                    pltpu.make_async_copy(gathered.at[source(t, d), part], x_buf.at[part], local_sem.at[2 + d])
                )
                more[-1].start()
            for copy in more:
                copy.wait()

        @pl.when(t == 0)
        def _():
            x_buf[...] = normed[...]

        for copy in copies:
            copy.wait()

        out_acc[...] = jnp.zeros_like(out_acc)
        grad_acc[...] = jnp.zeros_like(grad_acc)

        def tile(i, carry):
            @pl.when((t == 0) & (i == tiles - 1))
            def _():
                pass_on(1)

            span = pl.ds(pl.multiple_of(i * FF_TILE, FF_TILE), FF_TILE)
            x = x_buf[...]
            g = g_buf[...]
            gate = dot_nt(x, weights[0, span, :])
            up = dot_nt(x, weights[1, span, :])
            grad_hidden = dot_nt(g, weights[2, span, :])
            sigma = 1.0 / (1.0 + jnp.exp(-gate))
            silu = gate * sigma
            hidden = (silu * up).astype(LOW)
            grad_gate = (grad_hidden * up * sigma * (1.0 + gate * (1.0 - sigma))).astype(LOW)
            grad_up = (grad_hidden * silu).astype(LOW)
            out_acc[...] += dot_nn(hidden, weights[2, span, :])
            grad_acc[...] += dot_nn(grad_gate, weights[0, span, :])
            grad_acc[...] += dot_nn(grad_up, weights[1, span, :])
            totals[0, span, :] += dot_tn(grad_gate, x)
            totals[1, span, :] += dot_tn(grad_up, x)
            totals[2, span, :] += dot_tn(hidden, g)
            return carry

        lax.fori_loop(0, tiles, tile, 0)

        @pl.when(t >= 2)
        def _():
            for d in (0, 1):
                out_copy(t - 2, d).wait()

        cast_buf[t % 2] = out_acc[...].astype(LOW)
        for d in (0, 1):
            out_copy(t, d).start()

        @pl.when(t == 0)
        def _():
            grad_sum[...] = grad_acc[...]

        @pl.when(t > 0)
        def _():
            for d in (0, 1):
                part = pl.ds(d * half, half)

                @pl.when(t >= 2)
                def _():
                    reduce_copy(t - 1, d).wait_recv()
                    grad_acc[part, :] += landed[d, (t - 1) % 2].astype(F32)

                    @pl.when(t <= n - 2)
                    def _():
                        pl.semaphore_signal(
                            credit.at[d], inc=1, device_id={"dp": ring.back[d]}, device_id_type=MESH
                        )

                    reduce_copy(t - 1, d).wait_send()

                sent[d] = grad_acc[part, :].astype(LOW)

                @pl.when(t >= 3)
                def _():
                    pl.semaphore_wait(credit.at[d], 1)

                reduce_copy(t, d).start()

        return carry

    lax.fori_loop(0, n, step, 0)
    for t in (n - 2, n - 1):
        for d in (0, 1):
            out_copy(t, d).wait()

    own_tiles = 3 * own // FF_TILE

    def tile_of(i, first):
        return i // (own // FF_TILE), pl.ds(
            pl.multiple_of(first + (i % (own // FF_TILE)) * FF_TILE, FF_TILE), FF_TILE
        )

    def pair_copy(i):
        return remote(cast_buf.at[i % 2], pair_land.at[i], pair_send.at[i % 2], pair_recv.at[i], ring.partner)

    def give(i, carry):
        @pl.when(i >= 2)
        def _():
            pair_copy(i - 2).wait_send()

        k, span = tile_of(i, own)
        cast_buf[i % 2] = totals[k, span, :].astype(LOW)
        pair_copy(i).start()
        return carry

    lax.fori_loop(0, own_tiles, give, 0)
    for i in (own_tiles - 2, own_tiles - 1):
        pair_copy(i).wait_send()

    pieces = ((gate_grad,), (up_a, up_b), (down_grad,))

    def total_copies(i):
        matrix, low = i // (own // FF_TILE), (i % (own // FF_TILE)) * FF_TILE
        copies, begin = [], 0
        for piece in pieces[matrix]:
            end = begin + piece.shape[0]
            first, last = max(begin, low), min(end, low + FF_TILE)
            if first < last:
                copies.append(
                    pltpu.make_async_copy(
                        cast_buf.at[i % 2, pl.ds(first - low, last - first)],
                        piece.at[pl.ds(first - begin, last - first)],
                        cast_sem.at[i % 2, len(copies)],
                    )
                )
            begin = end
        return copies

    for i in range(own_tiles):
        if i >= 2:
            for copy in total_copies(i - 2):
                copy.wait()
        pair_copy(i).wait_recv()
        k, span = tile_of(i, 0)
        cast_buf[i % 2] = (totals[k, span, :] + pair_land[i].astype(F32)).astype(LOW)
        for copy in total_copies(i):
            copy.start()

    for d in (0, 1):
        part = pl.ds(d * half, half)
        reduce_copy(n - 1, d).wait_recv()
        grad_sum[part, :] += landed[d, (n - 1) % 2].astype(F32)
        reduce_copy(n - 1, d).wait_send()

    for i in (own_tiles - 2, own_tiles - 1):
        for copy in total_copies(i):
            copy.wait()

    def finish(t, carry):
        for d in (0, 1):
            send(t, d, False).wait_send()
        return carry

    lax.fori_loop(1, n, finish, 0)


def dense(normed, cotangents, own_weights, partner_weights):
    rows, features = normed.shape
    n = lax.axis_size("dp") // 2
    own = own_weights[0].shape[0]
    half = rows // 2
    vmem = pl.BlockSpec(memory_space=pltpu.VMEM)
    hbm = pl.BlockSpec(memory_space=pl.ANY)
    dma = pltpu.SemaphoreType.DMA
    own_tiles = 3 * own // FF_TILE
    return pl.pallas_call(
        dense_kernel,
        out_shape=(
            jax.ShapeDtypeStruct((rows, features), F32),
            jax.ShapeDtypeStruct((n, rows, features), LOW),
            jax.ShapeDtypeStruct((n, rows, features), LOW),
            jax.ShapeDtypeStruct((own, features), LOW),
            jax.ShapeDtypeStruct((own // 4, features), LOW),
            jax.ShapeDtypeStruct((own - own // 4, features), LOW),
            jax.ShapeDtypeStruct((own, features), LOW),
        ),
        in_specs=[vmem] + [hbm] * 7,
        out_specs=(vmem,) + (hbm,) * 6,
        scratch_shapes=[
            pltpu.VMEM((3, 2 * own, features), LOW),
            pltpu.VMEM((3, 2 * own, features), F32),
            pltpu.VMEM((rows, features), LOW),
            pltpu.VMEM((rows, features), LOW),
            pltpu.VMEM((rows, features), F32),
            pltpu.VMEM((rows, features), F32),
            pltpu.VMEM((2, half, features), LOW),
            pltpu.VMEM((2, 2, half, features), LOW),
            pltpu.VMEM((2, FF_TILE, features), LOW),
            pltpu.VMEM((own_tiles, FF_TILE, features), LOW),
            dma((2, n)), dma((2, n)), dma((2,)), dma((2, 2)),
            pltpu.SemaphoreType.REGULAR((2,)),
            dma((4,)), dma((6,)), dma((2, 2)), dma((2,)), dma((own_tiles,)),
        ],
        compiler_params=pltpu.CompilerParams(
            collective_id=2, has_side_effects=True, vmem_limit_bytes=62 * MIB
        ),
        cost_estimate=pl.CostEstimate(
            flops=2 * 9 * n * rows * features * 2 * own, bytes_accessed=500 * MIB, transcendentals=0
        ),
        name="dense",
    )(normed, cotangents, *own_weights, *partner_weights)


def output_split(r, packs):
    plain = r // 4 if (r - r // 4) // packs % 16 == 0 else 0
    return (r - plain) // packs, plain


def mixed_back_kernel(
    packs, mixed_in, grad_in, cotangent_in, gain, output_all, blocks, grad_mixed, gain_part, grad_heads, *rest
):
    sums = rest[:packs]
    given, taken = rest[packs : 2 * packs], rest[2 * packs : 3 * packs]
    (
        mixed, grad_two, cotangent, low, weights, staged, product,
        sem, w_sem, send_sem, recv_sem, g_sem, t_sem,
    ) = rest[3 * packs :]
    ring = Ring()
    n = ring.chips
    devices = 2 * n
    rows, features = mixed.shape
    r = grad_heads.shape[1]
    pack = lax.axis_index("rep")
    spot = ring.place * 2 + ring.core
    loads = [
        pltpu.make_async_copy(src, dst, sem.at[i])
        for i, (src, dst) in enumerate(((mixed_in, mixed), (grad_in, grad_two), (cotangent_in, cotangent)))
    ]
    for load in loads:
        load.start()

    def chip_weights(k):
        at = lax.rem(ring.place + k, n) * 2
        return pltpu.make_async_copy(output_all.at[pl.ds(at, 2)], weights.at[pl.ds(2 * k, 2)], w_sem.at[k])

    def fetch(k, carry):
        chip_weights(k).start()
        return carry

    lax.fori_loop(0, n, fetch, 0)
    barrier = pltpu.get_barrier_semaphore()

    def to(k):
        other = lax.rem(spot + k, devices)
        return {"dp": chip_at(other // 2, n) * 2 + other % 2}

    def greet(k, carry):
        pl.semaphore_signal(barrier, inc=1, device_id=to(k), device_id_type=MESH)
        return carry

    lax.fori_loop(1, devices, greet, 0)
    pl.semaphore_wait(barrier, devices - 1)
    for load in loads:
        load.wait()
    gain_part[...] = jnp.zeros_like(gain_part)

    def norm_back(i, carry):
        span = pl.ds(pl.multiple_of(i * 16, 16), 16)
        value, grad = mixed[span, :], grad_two[span, :]
        scale = lax.rsqrt(jnp.mean(value * value, axis=1, keepdims=True) + EPSILON)
        scaled = grad * gain[...]
        shift = jnp.mean(value * scaled, axis=1, keepdims=True)
        total = cotangent[span, :].astype(F32) + scale * scaled - value * (scale * scale * scale * shift)
        grad_mixed[span, :] = total
        low[span, :] = total.astype(LOW)
        gain_part[...] += jnp.sum(grad * value * scale, axis=0, keepdims=True)
        return carry

    lax.fori_loop(0, rows // 16, norm_back, 0)

    def copy(k):
        return remote(
            staged.at[k],
            grad_heads.at[pl.ds(pl.multiple_of(spot * rows, rows), rows)],
            send_sem.at[k],
            recv_sem.at[k],
            to(k)["dp"],
        )

    def project(k, carry):
        chip_weights(k).wait()
        both = dot_nt(low[...], weights[pl.ds(2 * k, 2)].reshape(2 * r, features))
        for core in (0, 1):
            step = lax.rem(2 * k + core - ring.core + devices, devices)
            staged[step] = both[:, core * r : (core + 1) * r].astype(LOW)

            @pl.when(step > 0)
            def _():
                copy(step).start()

        return carry

    lax.fori_loop(0, n, project, 0)
    grad_heads[pl.ds(pl.multiple_of(spot * rows, rows), rows), :] = staged[0]

    def give(k):
        return remote(given[k], taken[k], g_sem.at[k], t_sem.at[k], ring.partner)

    share, plain = output_split(r, packs)

    def spots(k, place, first, count):
        width = share + plain if k == 0 else share
        return pl.ds(pl.multiple_of(place * width + first, 16), count)

    def products(place, core, use):
        product[...] = dot_tn(blocks[place * 2 + core], low[...])
        for k in range(packs):
            at = pl.multiple_of(lax.rem(pack + k, packs) * share, share)
            use(k, spots(k, place, 0, share), product[pl.ds(at, share), :])
        if plain:
            use(0, spots(0, place, share, plain), product[pl.ds(r - plain, plain), :])

    def put(k, at, value):
        given[k][at, :] = value.astype(LOW)

    def total(k, at, value):
        sums[k][at, :] = (value + taken[k][at, :].astype(F32)).astype(LOW)

    def for_partner(place, carry):
        products(place, 1 - ring.core, put)
        return carry

    def for_self(place, carry):
        products(place, ring.core, total)
        return carry

    lax.fori_loop(0, n, for_partner, 0)
    for k in range(packs):
        give(k).start()
    for k in range(packs):
        give(k).wait_recv()
    lax.fori_loop(0, n, for_self, 0)

    def finish(k, carry):
        copy(k).wait_send()
        copy(k).wait_recv()
        return carry

    lax.fori_loop(1, devices, finish, 0)
    for k in range(packs):
        give(k).wait_send()


def mixed_back(mixed, grad_two, cotangent, gain, output_all, blocks):
    rows, features = mixed.shape
    devices, r = output_all.shape[:2]
    packs = lax.axis_size("rep")
    n = devices // 2
    share, plain = output_split(r, packs)
    sizes = [n * (share + plain)] + [n * share] * (packs - 1)
    vmem = pl.BlockSpec(memory_space=pltpu.VMEM)
    hbm = pl.BlockSpec(memory_space=pl.ANY)
    dma = pltpu.SemaphoreType.DMA
    return pl.pallas_call(
        functools.partial(mixed_back_kernel, packs),
        out_shape=(
            jax.ShapeDtypeStruct((rows, features), F32),
            jax.ShapeDtypeStruct((1, features), F32),
            jax.ShapeDtypeStruct((devices * rows, r), LOW),
        )
        + tuple(jax.ShapeDtypeStruct((size, features), LOW) for size in sizes),
        in_specs=[hbm] * 3 + [vmem, hbm, vmem],
        out_specs=(vmem,) * (3 + packs),
        scratch_shapes=[pltpu.VMEM((size, features), LOW) for size in sizes + sizes]
        + [
            pltpu.VMEM((rows, features), F32),
            pltpu.VMEM((rows, features), F32),
            pltpu.VMEM((rows, features), LOW),
            pltpu.VMEM((rows, features), LOW),
            pltpu.VMEM((devices, r, features), LOW),
            pltpu.VMEM((devices, rows, r), LOW),
            pltpu.VMEM((r, features), F32),
            dma((3,)), dma((n,)), dma((devices,)), dma((devices,)), dma((packs,)), dma((packs,)),
        ],
        compiler_params=pltpu.CompilerParams(
            collective_id=4, has_side_effects=True, vmem_limit_bytes=56 * MIB
        ),
        cost_estimate=pl.CostEstimate(
            flops=4 * rows * features * features, bytes_accessed=130 * MIB, transcendentals=0
        ),
        name="mixed_back",
    )(mixed, grad_two, cotangent, gain, output_all, blocks)


def normed_back_kernel(
    packs, grads_in, query_w, key_w, value_w, partner_w, hidden_in, gain, grad_mixed, dense_gain_part, normed_all, output_mine, *rest
):
    output_there = rest[: packs - 1]
    (
        out, gains, rep_land, o_packs,
        grads, joined, partner_grads, sent, landed, x_buf, parts, pair_out, pair_land,
        o_sent, o_landed, near_part, near_land, near_sum, far_land,
        in_sem, w_sem, p_send, p_recv, rs_send, rs_recv, credit, x_sem, pair_sem, rep_send, rep_recv,
        o_send, o_recv, o_credit, swap_send, swap_recv, near_send, near_recv, far_send, far_recv,
    ) = rest[packs - 1 :]
    ring = Ring()
    n = ring.chips
    rows, features = out.shape
    half = rows // 2
    r = grads.shape[2]
    share, plain = output_split(r, packs)
    pack = lax.axis_index("rep")
    mates = 2 * packs
    mate = pack * 2 + ring.core
    barrier = pltpu.get_barrier_semaphore()
    load_grads = pltpu.make_async_copy(grads_in, grads, in_sem)
    load_grads.start()
    load_weights = [
        pltpu.make_async_copy(src, joined.at[pl.ds(i * r, src.shape[0])], w_sem.at[i])
        for i, src in enumerate((query_w, key_w, value_w, partner_w))
    ]
    for load in load_weights:
        load.start()

    def near(k):
        to = lax.rem(mate + k, mates)
        return {"dp": ring.chip * 2 + to % 2, "rep": to // 2}

    def far(k):
        return {"dp": lax.rem(ring.chip + k, n) * 2 + ring.core}

    for k in range(1, mates):
        pl.semaphore_signal(barrier, inc=1, device_id=near(k), device_id_type=MESH)
    for k in range(1, n):
        pl.semaphore_signal(barrier, inc=1, device_id=far(k), device_id_type=MESH)
    pl.semaphore_wait(barrier, mates + n - 2)
    load_grads.wait()

    def place(t, d):
        return ring.chip_far(-t if d == 0 else t)

    def swap(t, d):
        start = (place(t, d) * 2 + 1 - ring.core) * rows + d * half
        return remote(
            grads.at[:, pl.ds(pl.multiple_of(start, half), half)],
            partner_grads.at[:, t % n, half_rows(d, rows)],
            p_send.at[d, t % n],
            p_recv.at[d, t % n],
            ring.partner,
        )

    def begin(t, carry):
        for d in (0, 1):
            swap(t, d).start()
        return carry

    lax.fori_loop(1, n + 1, begin, 0)

    def reduce_copy(t, d, u):
        return remote(
            sent.at[d, u, t % 2],
            landed.at[d, u, t % 2],
            rs_send.at[d, u, t % 2],
            rs_recv.at[d, u, t % 2],
            ring.next[d],
        )

    def output_copy(t, d):
        return remote(
            o_sent.at[d, t % 2],
            o_landed.at[d, t % 2],
            o_send.at[d, t % 2],
            o_recv.at[d, t % 2],
            ring.next[d],
        )

    def give_credit(sem, d):
        pl.semaphore_signal(sem, inc=1, device_id={"dp": ring.back[d]}, device_id_type=MESH)

    def mine(t, d):
        start = (place(t, d) * 2 + ring.core) * rows + d * half
        return pl.ds(pl.multiple_of(start, half), half)

    def load_rows(t, d):
        part = half_rows(d, rows)
        return pltpu.make_async_copy(normed_all.at[place(t, d), part], x_buf.at[t % 2, part], x_sem.at[t % 2, d])

    def block_grads(t):
        return jnp.concatenate(
            [jnp.concatenate([grads[i, mine(t, d), :] for d in (0, 1)], 0) for i in range(3)]
            + [partner_grads[i, t % n] for i in range(3)],
            1,
        )

    def weight_parts(t):
        for d in (0, 1):
            load_rows(t, d).wait()
        parts[...] += dot_tn(block_grads(t), x_buf[t % 2])

    def pair_copy():
        return remote(pair_out, pair_land, pair_sem.at[0], pair_sem.at[1], ring.partner)

    def rep_copy(k):
        return pltpu.make_async_remote_copy(
            src_ref=pair_out,
            dst_ref=rep_land.at[k - 1],
            send_sem=rep_send.at[k - 1],
            recv_sem=rep_recv.at[k - 1],
            device_id={"rep": lax.rem(pack + k, packs)},
            device_id_type=MESH,
        )

    middle = n // 2

    def output_step(t):
        for d in (0, 1):
            spot = lax.rem(ring.place + (n - t if d == 0 else t), n)
            columns = pl.ds(d * (features // 2), features // 2)
            own = pl.multiple_of(spot * (share + plain), 16)
            total = output_mine[pl.ds(own, share), columns].astype(F32)
            for there in output_there:
                total += there[pl.ds(pl.multiple_of(spot * share, share), share), columns].astype(F32)
            if plain:
                rest_rows = pl.ds(pl.multiple_of(own + share, 16), plain)
                total = jnp.concatenate([total, output_mine[rest_rows, columns].astype(F32)], 0)

            def pass_on(value):
                @pl.when(t >= 3)
                def _():
                    output_copy(t - 2, d).wait_send()
                    pl.semaphore_wait(o_credit.at[d], 1)

                o_sent[d, t % 2] = value.astype(LOW)
                output_copy(t, d).start()

            @pl.when(t == 1)
            def _():
                pass_on(total)

            @pl.when(t >= 2)
            def _():
                output_copy(t - 1, d).wait_recv()
                more = total + o_landed[d, (t - 1) % 2].astype(F32)

                @pl.when(t <= n - 2)
                def _():
                    give_credit(o_credit.at[d], d)

                @pl.when(t < n)
                def _():
                    pass_on(more)

                @pl.when(t == n)
                def _():
                    o_packs[packs - 1, :, columns] = more.astype(LOW)

    def output_swap(k):
        return pltpu.make_async_remote_copy(
            src_ref=o_packs.at[packs - 1],
            dst_ref=o_packs.at[k - 1],
            send_sem=swap_send.at[k - 1],
            recv_sem=swap_recv.at[k - 1],
            device_id={"rep": lax.rem(pack + k, packs)},
            device_id_type=MESH,
        )

    def step(t, carry):
        @pl.when(t <= middle)
        def _():
            for d in (0, 1):
                load_rows(2 * t - 1, d).start()
                load_rows(2 * t, d).start()

        @pl.when(2 * t - 1 <= n)
        def _():
            output_step(2 * t - 1)

        for u in (0, 1):
            columns = pl.ds(u * (features // 2), features // 2)
            for d in (0, 1):
                part = pl.ds(d * half, half), columns

                @pl.when(t >= 2)
                def _():
                    reduce_copy(t - 1, d, u).wait_recv()
                    out[part] += landed[d, u, (t - 1) % 2].astype(F32)

                    @pl.when(t <= n - 2)
                    def _():
                        give_credit(credit.at[d, u], d)

                @pl.when(t < n)
                def _():
                    @pl.when(t >= 3)
                    def _():
                        reduce_copy(t - 2, d, u).wait_send()
                        pl.semaphore_wait(credit.at[d, u], 1)

                    sent[d, u, t % 2] = out[part].astype(LOW)
                    reduce_copy(t, d, u).start()

        @pl.when(2 * t <= n)
        def _():
            output_step(2 * t)

        @pl.when(2 * t == n)
        def _():
            for k in range(1, packs):
                output_swap(k).start()

        @pl.when(t == 1)
        def _():
            parts[...] = jnp.zeros_like(parts)

            def arrived(k, carry):
                for d in (0, 1):
                    swap(k, d).wait_recv()
                return carry

            lax.fori_loop(2, n + 1, arrived, 0)

        @pl.when(t <= middle)
        def _():
            weight_parts(2 * t - 1)
            weight_parts(2 * t)

        @pl.when(t == middle)
        def _():
            for i in range(3):
                pair_out[i] = parts[pl.ds((3 + i) * r, r), :].astype(LOW)
            pair_copy().start()

        @pl.when(t == middle + 1)
        def _():
            pair_copy().wait()
            for i in range(3):
                pair_out[i] = (parts[pl.ds(i * r, r), :] + pair_land[i].astype(F32)).astype(LOW)
            for k in range(1, packs):
                rep_copy(k).start()
            rep_land[packs - 1] = pair_out[...]

        @pl.when(t < n)
        def _():
            out[...] = dot_nn(block_grads(t + 1), joined[...])

        return carry

    for d in (0, 1):
        swap(1, d).wait_recv()
    for load in load_weights:
        load.wait()
    out[...] = dot_nn(block_grads(1), joined[...])
    lax.fori_loop(1, n + 1, step, 0)
    for t in (n - 2, n - 1):
        for d in (0, 1):
            output_copy(t, d).wait_send()
            for u in (0, 1):
                reduce_copy(t, d, u).wait_send()

    near_part[0:1, :] = jnp.zeros((1, features), F32)
    near_part[1:2, :] = dense_gain_part[...]

    def close(i, carry):
        span = pl.ds(pl.multiple_of(i * 16, 16), 16)
        value = hidden_in[span, :].astype(F32)
        grad = out[span, :]
        scale = lax.rsqrt(jnp.mean(value * value, axis=1, keepdims=True) + EPSILON)
        scaled = grad * gain[...]
        shift = jnp.mean(value * scaled, axis=1, keepdims=True)
        out[span, :] = grad_mixed[span, :] + scale * scaled - value * (scale * scale * scale * shift)
        near_part[0:1, :] += jnp.sum(grad * value * scale, axis=0, keepdims=True)
        return carry

    lax.fori_loop(0, rows // 16, close, 0)

    def exchange(src, land, own, send_sem, recv_sem, device, count):
        copies = [
            pltpu.make_async_remote_copy(
                src_ref=src,
                dst_ref=land.at[own],
                send_sem=send_sem.at[k],
                recv_sem=recv_sem.at[k],
                device_id=device(k),
                device_id_type=MESH,
            )
            for k in range(1, count)
        ]
        for copy in copies:
            copy.start()
        land[own] = src[...]
        for copy in copies:
            copy.wait()
        total = land[0]
        for k in range(1, count):
            total += land[k]
        return total

    near_sum[...] = exchange(near_part, near_land, mate, near_send, near_recv, near, mates)
    gains[...] = exchange(near_sum, far_land, ring.chip, far_send, far_recv, far, n)

    def finish(t, carry):
        for d in (0, 1):
            swap(t, d).wait_send()
        return carry

    lax.fori_loop(1, n + 1, finish, 0)
    for k in range(1, packs):
        rep_copy(k).wait()
        output_swap(k).wait()


def normed_back(
    grads, weights, partner_weights, hidden_in, gain, grad_mixed, dense_gain_part, normed_all, output_mine, output_there
):
    tokens, r = grads.shape[1:]
    features = partner_weights.shape[1]
    devices = lax.axis_size("dp")
    packs = lax.axis_size("rep")
    n = devices // 2
    rows = tokens // devices
    half = rows // 2
    share, plain = output_split(r, packs)
    carried = share + plain
    mates = 2 * packs
    vmem = pl.BlockSpec(memory_space=pltpu.VMEM)
    hbm = pl.BlockSpec(memory_space=pl.ANY)
    dma = pltpu.SemaphoreType.DMA
    return pl.pallas_call(
        functools.partial(normed_back_kernel, packs),
        out_shape=(
            jax.ShapeDtypeStruct((rows, features), F32),
            jax.ShapeDtypeStruct((2, features), F32),
        )
        + (
            jax.ShapeDtypeStruct((packs, 3, r, features), LOW),
            jax.ShapeDtypeStruct((packs, carried, features), LOW),
        ),
        in_specs=[hbm] * 5 + [vmem] * 4 + [hbm] + [vmem] * packs,
        out_specs=(vmem,) * 4,
        scratch_shapes=[
            pltpu.VMEM(grads.shape, LOW),
            pltpu.VMEM((6 * r, features), LOW),
            pltpu.VMEM((3, n, rows, r), LOW),
            pltpu.VMEM((2, 2, 2, half, features // 2), LOW),
            pltpu.VMEM((2, 2, 2, half, features // 2), LOW),
            pltpu.VMEM((2, rows, features), LOW),
            pltpu.VMEM((6 * r, features), F32),
            pltpu.VMEM((3, r, features), LOW),
            pltpu.VMEM((3, r, features), LOW),
            pltpu.VMEM((2, 2, carried, features // 2), LOW),
            pltpu.VMEM((2, 2, carried, features // 2), LOW),
            pltpu.VMEM((2, features), F32),
            pltpu.VMEM((mates, 2, features), F32),
            pltpu.VMEM((2, features), F32),
            pltpu.VMEM((n, 2, features), F32),
            dma, dma((4,)), dma((2, n)), dma((2, n)), dma((2, 2, 2)), dma((2, 2, 2)),
            pltpu.SemaphoreType.REGULAR((2, 2)),
            dma((2, 2)), dma((2,)), dma((packs - 1,)), dma((packs - 1,)),
            dma((2, 2)), dma((2, 2)), pltpu.SemaphoreType.REGULAR((2,)),
            dma((packs - 1,)), dma((packs - 1,)), dma((mates,)), dma((mates,)), dma((n,)), dma((n,)),
        ],
        compiler_params=pltpu.CompilerParams(
            collective_id=3, has_side_effects=True, vmem_limit_bytes=56 * MIB
        ),
        cost_estimate=pl.CostEstimate(
            flops=2 * n * rows * features * 12 * r, bytes_accessed=320 * MIB, transcendentals=0
        ),
        name="normed_back",
    )(
        grads, *weights, partner_weights, hidden_in, gain, grad_mixed, dense_gain_part, normed_all,
        output_mine, *output_there,
    )


def from_partner(value):
    devices = lax.axis_size("dp")
    return lax.ppermute(value, "dp", [(i, i ^ 1) for i in range(devices)])


def pack_swap(low):
    if lax.axis_size("rep") == 2:
        return lax.ppermute(low, "rep", [(0, 1), (1, 0)])
    return lax.psum(low, "rep")


def pack_add(low, other):
    if lax.axis_size("rep") == 2:
        return low.astype(F32) + other.astype(F32)
    return other.astype(F32)


def together(*values):
    return lax.optimization_barrier(values)


def body(
    tokens,
    attention_gain,
    query_weight,
    key_weight,
    value_weight,
    output_weight,
    dense_gain,
    gate_weight,
    up_weight,
    down_weight,
    block_document,
    document_tail,
    cotangent,
):
    devices = lax.axis_size("dp")
    chips = devices // 2
    tok_dev = tokens.shape[1]
    pack_tok = tok_dev * devices

    documents, tails = block_document[0], document_tail[0]
    first = jnp.sum((documents[None, :] < documents[:, None]).astype(jnp.int32), axis=1)
    last = jnp.concatenate([documents[1:] != documents[:-1], jnp.ones((1,), bool)])
    doc_ids = jnp.arange(tails.shape[0], dtype=jnp.int32)
    own_tail = jnp.sum((documents[:, None] == doc_ids[None, :]) * tails[None, :], axis=1)
    tail = jnp.where(last, own_tail, BLOCK).astype(jnp.int32)
    block_index = jnp.arange(documents.shape[0], dtype=jnp.int32)
    inside = jnp.arange(BLOCK, dtype=jnp.int32)
    position = ((block_index - first)[:, None] * BLOCK + inside[None, :]).reshape(-1)
    frequency = ROPE_BASE ** (-(jnp.arange(HALF, dtype=F32) * (2.0 / HEAD_DIM)))
    angles = position.astype(F32)[None, :] * frequency[:, None]
    cos_t, sin_t = jnp.cos(angles), jnp.sin(angles)
    r = query_weight.shape[0]

    qkv, normed_all, full_output = gather_project(
        tokens[0],
        attention_gain[None],
        (query_weight, key_weight, value_weight),
        output_weight,
        cos_t,
        sin_t,
    )

    order = ring_order(chips)
    lanes = [[2 * chip + k for chip in order] for k in (0, 1)]
    grad_low = cotangent[0]
    qkv, grad_late = together(qkv, grad_low)
    cotangents = lax.all_gather(grad_late, "dp", axis=0, axis_index_groups=lanes)
    gate_other, up_other, down_other = (
        from_partner(gate_weight),
        from_partner(up_weight),
        from_partner(down_weight),
    )
    qkv_weight = jnp.concatenate([query_weight, key_weight, value_weight], 0)

    attended, log_total = attend(first, tail, qkv)
    mixed, normed_two, attended_blocks = mix(attended, tokens[0], dense_gain[None], full_output)
    normed_two, qkv_weight = together(normed_two, qkv_weight)
    qkv_other = from_partner(qkv_weight)
    packs, pack = lax.axis_size("rep"), lax.axis_index("rep")

    grad_normed_two, out_parts, _, gate_low, up_a, up_b, down_low = dense(
        normed_two,
        cotangents,
        (gate_weight, up_weight, down_weight),
        (gate_other, up_other, down_other),
    )
    out_sum = lax.psum_scatter(
        out_parts.reshape(chips * tok_dev, -1),
        "dp",
        scatter_dimension=0,
        tiled=True,
        axis_index_groups=lanes,
    )
    gate_there = pack_swap(gate_low)

    grad_mixed, dense_gain_part, grad_heads, output_mine, *output_low = mixed_back(
        mixed, grad_normed_two, grad_low, dense_gain[None], full_output, attended_blocks
    )
    output_there = [
        lax.ppermute(low, "rep", [(i, (i + k) % packs) for i in range(packs)])
        for k, low in enumerate(output_low, 1)
    ]
    grad_heads, gate_there, output_mine = together(grad_heads, gate_there, output_mine)
    up_a, _ = together(up_a, grad_heads)
    up_a_there = pack_swap(up_a)
    grads = attend_back(first, tail, qkv, grad_heads, attended, log_total, cos_t, sin_t)
    grads, output_there, up_a_there, up_b, down_low = together(
        grads, output_there, up_a_there, up_b, down_low
    )
    up_b_there = pack_swap(up_b)
    down_there = pack_swap(down_low)
    input_grad, gain_totals, qkv_packs, output_packs = normed_back(
        grads,
        (query_weight, key_weight, value_weight),
        qkv_other,
        tokens[0],
        attention_gain[None],
        grad_mixed,
        dense_gain_part,
        normed_all,
        output_mine,
        output_there,
    )
    input_grad, out_sum, gate_there, up_a_there, up_b_there, down_there = together(
        input_grad, out_sum, gate_there, up_a_there, up_b_there, down_there
    )
    slots = [lax.rem(pack + 2 * packs - q - 1, packs) for q in range(packs)]
    query_total, key_total, value_total = [
        sum(qkv_packs[slot, i].astype(F32) for slot in (slots if packs > 2 else range(2)))
        for i in range(3)
    ]
    share, plain = output_split(r, packs)
    output_total = jnp.concatenate([output_packs[slot, :share] for slot in slots], 0).astype(F32)
    if plain:
        plain_total = sum(
            output_packs[slot, share:].astype(F32) for slot in (slots if packs > 2 else range(2))
        )
        output_total = jnp.concatenate([output_total, plain_total], 0)
    layer_out = mixed + out_sum.astype(F32)
    return (
        layer_out[None].astype(LOW),
        input_grad[None],
        gain_totals[0],
        query_total,
        key_total,
        value_total,
        output_total,
        gain_totals[1],
        pack_add(gate_low, gate_there),
        jnp.concatenate([pack_add(up_a, up_a_there), pack_add(up_b, up_b_there)], 0),
        pack_add(down_low, down_there),
    )


def solution(mesh):
    return jax.shard_map(
        body,
        mesh=mesh,
        in_specs=(
            P("rep", "dp", None),
            P(),
            P("dp", None),
            P("dp", None),
            P("dp", None),
            P("dp", None),
            P(),
            P("dp", None),
            P("dp", None),
            P("dp", None),
            P("rep", None),
            P("rep", None),
            P("rep", "dp", None),
        ),
        out_specs=(
            P("rep", "dp", None),
            P("rep", "dp", None),
            P(),
            P("dp", None),
            P("dp", None),
            P("dp", None),
            P("dp", None),
            P(),
            P("dp", None),
            P("dp", None),
            P("dp", None),
        ),
        check_vma=False,
    )
```

```python
import functools
import math

import jax
import jax.numpy as jnp
from jax import lax
from jax.experimental import pallas as pl
from jax.experimental.pallas import tpu as pltpu
from jax.sharding import PartitionSpec as P

HEAD_DIM = 64
HALF = HEAD_DIM // 2
BLOCK = 128
CHUNK = 512
FF_TILE = 256
STRIPE = 64
EPSILON = 1e-05
ROPE_BASE = 130000.0
MASKED_SCORE = -1e30
MESH = pl.DeviceIdType.MESH
MIB = 2**20
LOW = jnp.bfloat16
F32 = jnp.float32


def dot_nn(a, b):
    return lax.dot_general(a, b, (((1,), (0,)), ((), ())), preferred_element_type=F32)


def dot_nt(a, b):
    return lax.dot_general(a, b, (((1,), (1,)), ((), ())), preferred_element_type=F32)


def dot_tn(a, b):
    return lax.dot_general(a, b, (((0,), (0,)), ((), ())), preferred_element_type=F32)


def grid_of(chips):
    depth = 4 if chips % 8 == 0 else 2
    return depth, chips // depth


def chip_at(place, chips):
    depth, width = grid_of(chips)
    place = lax.rem(place + chips, chips)
    later = place - depth
    row, column = later // (width - 1), later % (width - 1)
    odd = row % 2
    far = (depth - 1 - row) * width + 1 + column + odd * (width - 2 - 2 * column)
    return jnp.where(place < depth, place * width, far)


def place_of(chip, chips):
    depth, width = grid_of(chips)
    z, x = chip // width, chip % width
    row = depth - 1 - z
    odd = row % 2
    column = x - 1 + odd * (width - 2 * x)
    return jnp.where(x == 0, z, depth + row * (width - 1) + column)


def ring_order(chips):
    depth, width = grid_of(chips)
    order = [z * width for z in range(depth)]
    for row in range(depth):
        columns = list(range(1, width))
        order += [(depth - 1 - row) * width + x for x in (columns[::-1] if row % 2 else columns)]
    return order


class Ring:
    def __init__(self):
        self.chips = lax.axis_size("dp") // 2
        me = lax.axis_index("dp")
        self.core = me % 2
        self.chip = me // 2
        self.partner = self.chip * 2 + 1 - self.core
        self.place = place_of(self.chip, self.chips)
        self.next = (self.device(1), self.device(-1))
        self.back = (self.next[1], self.next[0])

    def chip_far(self, steps):
        return chip_at(self.place + steps, self.chips)

    def device(self, steps):
        return self.chip_far(steps) * 2 + self.core

    def greet(self, others):
        barrier = pltpu.get_barrier_semaphore()
        for other in others:
            pl.semaphore_signal(barrier, inc=1, device_id={"dp": other}, device_id_type=MESH)
        pl.semaphore_wait(barrier, len(others))


def remote(src, dst, send_sem, recv_sem, device):
    return pltpu.make_async_remote_copy(
        src_ref=src,
        dst_ref=dst,
        send_sem=send_sem,
        recv_sem=recv_sem,
        device_id={"dp": device},
        device_id_type=MESH,
    )


def half_rows(direction, rows):
    return pl.ds(direction * (rows // 2), rows // 2)


def turned(u):
    parts = []
    for at in range(0, u.shape[1], HEAD_DIM):
        parts += [-u[:, at + HALF : at + HEAD_DIM], u[:, at : at + HALF]]
    return jnp.concatenate(parts, 1)


def gather_project_kernel(
    tokens_in, gain, query_w, key_w, value_w, output_w, cos_t, sin_t, qkv, gathered, output_all,
    tokens, own_weights, normed, partner_weights, x_buf, staged,
    in_sem, ag_send, ag_recv, w_send, w_recv, q_send, q_recv, local_sem,
    o_send, o_recv, pair_send, pair_recv, rep_send, rep_recv, far_send, far_recv,
):
    ring = Ring()
    n = ring.chips
    packs, pack = lax.axis_size("rep"), lax.axis_index("rep")
    rows = normed.shape[0]
    half = rows // 2
    r = qkv.shape[2]
    sources = (query_w, key_w, value_w)
    load_tokens = pltpu.make_async_copy(tokens_in, tokens, in_sem.at[3])
    load_tokens.start()
    load_weights = [
        pltpu.make_async_copy(source, own_weights.at[i], in_sem.at[i]) for i, source in enumerate(sources)
    ]
    for load in load_weights:
        load.start()
    barrier = pltpu.get_barrier_semaphore()
    for k in range(1, packs):
        pl.semaphore_signal(
            barrier, inc=1, device_id={"rep": lax.rem(pack + k, packs)}, device_id_type=MESH
        )
    for other in (ring.next[0], ring.next[1], ring.partner):
        pl.semaphore_signal(barrier, inc=1, device_id={"dp": other}, device_id_type=MESH)
    pl.semaphore_wait(barrier, 3 + packs - 1)

    load_tokens.wait()

    def normalize(i, carry):
        span = pl.ds(pl.multiple_of(i * 32, 32), 32)
        value = tokens[span, :].astype(F32)
        scale = lax.rsqrt(jnp.mean(value * value, axis=1, keepdims=True) + EPSILON)
        normed[span, :] = (value * scale * gain[...]).astype(LOW)
        return carry

    lax.fori_loop(0, rows // 32, normalize, 0)

    def hop(t, d):
        chip = ring.chip_far((1 - t) if d == 0 else (t - 1))
        return chip, half_rows(d, rows)

    def send(t, d, first):
        chip, part = hop(t, d)
        src = normed.at[part] if first else gathered.at[chip, part]
        return remote(src, gathered.at[chip, part], ag_send.at[d, t - 1], ag_recv.at[d, t - 1], ring.next[d])

    out_rows, features = output_w.shape
    share = out_rows // packs
    spot = ring.place * 2 + ring.core

    def share_of(q, d):
        return pl.ds(pl.multiple_of(q * share, share), share), pl.ds(d * (features // 2), features // 2)

    def block_at(t, d, q, core):
        place = lax.rem(ring.place + (n - t if d == 0 else t), n)
        at_rows, columns = share_of(q, d)
        return output_all.at[place * 2 + core, at_rows, columns]

    def o_copy(t, d, first):
        at_rows, columns = share_of(pack, d)
        src = output_w.at[at_rows, columns] if first else block_at(t - 1, d, pack, ring.core)
        return remote(
            src, block_at(t - 1, d, pack, ring.core), o_send.at[d, t], o_recv.at[d, t], ring.next[d]
        )

    def pair_copy(t, d):
        block = block_at(t, d, pack, ring.core)
        return remote(block, block, pair_send.at[d, t], pair_recv.at[d, t], ring.partner)

    def rep_copy(t, d, k):
        block = block_at(t, d, pack, ring.core)
        return pltpu.make_async_remote_copy(
            src_ref=block,
            dst_ref=block,
            send_sem=rep_send.at[k - 1, d, t],
            recv_sem=rep_recv.at[k - 1, d, t],
            device_id={"rep": lax.rem(pack + k, packs)},
            device_id_type=MESH,
        )

    def far_copy(t, d, k):
        block = block_at(t, d, lax.rem(pack + packs - k, packs), ring.core)
        return remote(block, block, far_send.at[k - 1, d, t], far_recv.at[k - 1, d, t], ring.partner)

    def forward_far(t):
        for d in (0, 1):
            for k in range(1, packs):
                rep_copy(t, d, k).wait_recv()
                far_copy(t, d, k).start()

    for d in (0, 1):
        send(1, d, True).start()
    for d in (0, 1):
        o_copy(1, d, True).start()
    own_rows = remote(output_w, output_all.at[spot], local_sem.at[3], local_sem.at[4], ring.partner)
    own_rows.start()
    own_keep = pltpu.make_async_copy(output_w, output_all.at[spot], local_sem.at[5])
    own_keep.start()
    swaps = [
        remote(sources[i], partner_weights.at[i], w_send.at[i], w_recv.at[i], ring.partner)
        for i in range(3)
    ]
    for swap in swaps:
        swap.start()
    keep = pltpu.make_async_copy(normed, gathered.at[ring.chip], local_sem.at[2])
    keep.start()

    def project_block(t, from_input):
        x = normed[...] if from_input else x_buf[...]
        places = [ring.chip_far(-t), ring.chip_far(t)]
        starts = [
            pl.multiple_of((places[d] * 2 + ring.core) * rows + d * half, half) for d in (0, 1)
        ]

        def table(source):
            wide = [source[:, pl.ds(starts[d], half)] for d in (0, 1)]
            return jnp.concatenate(
                [jnp.concatenate([w] * (r // HALF), 0).T for w in wide], 0
            )

        cos, sin = table(cos_t), table(sin_t)

        def heads(w):
            query, key, value = [dot_nt(x, w[i][...]) for i in range(3)]
            return (
                (query * cos + turned(query) * sin).astype(LOW),
                (key * cos + turned(key) * sin).astype(LOW),
                value.astype(LOW),
            )

        for i, value in enumerate(heads([own_weights.at[i] for i in range(3)])):
            for d in (0, 1):
                qkv[i, pl.ds(starts[d], half), :] = value[d * half : (d + 1) * half]
        if from_input:
            for swap in swaps:
                swap.wait()
        for i, value in enumerate(heads([partner_weights.at[i] for i in range(3)])):
            staged[t, i] = value
        for d in (0, 1):
            remote(
                staged.at[t, :, half_rows(d, rows)],
                qkv.at[:, pl.ds(starts[d], half)],
                q_send.at[d, t],
                q_recv.at[d, t],
                ring.partner,
            ).start()

    for load in load_weights:
        load.wait()
    project_block(0, True)

    def step(t, carry):
        for d in (0, 1):
            send(t, d, False).wait_recv()

        @pl.when(t < n - 1)
        def _():
            for d in (0, 1):
                send(t + 1, d, False).start()

        for d in (0, 1):
            o_copy(t, d, False).wait_recv()

        @pl.when(t < n - 1)
        def _():
            for d in (0, 1):
                o_copy(t + 1, d, False).start()

        for d in (0, 1):
            for k in range(1, packs):
                rep_copy(t, d, k).start()
            pair_copy(t, d).start()

        @pl.when(t > 1)
        def _():
            forward_far(t - 1)

        loads = []
        for d in (0, 1):
            chip, part = hop(t + 1, d)
            loads.append(pltpu.make_async_copy(gathered.at[chip, part], x_buf.at[part], local_sem.at[d]))
        for load in loads:
            load.start()
        for load in loads:
            load.wait()
        project_block(t, False)
        return carry

    lax.fori_loop(1, n, step, 0)
    forward_far(n - 1)

    def finish(t, carry):
        for d in (0, 1):
            send(t, d, False).wait_send()
            o_copy(t, d, False).wait_send()
            pair_copy(t, d).wait()
            for k in range(1, packs):
                rep_copy(t, d, k).wait_send()
                far_copy(t, d, k).wait()
        return carry

    lax.fori_loop(1, n, finish, 0)
    own_rows.wait()
    own_keep.wait()

    def finish_heads(t, carry):
        for d in (0, 1):
            done = remote(
                staged.at[t, :, half_rows(d, rows)],
                qkv.at[:, half_rows(d, rows)],
                q_send.at[d, t],
                q_recv.at[d, t],
                ring.partner,
            )
            done.wait_send()
            done.wait_recv()
        return carry

    lax.fori_loop(0, n, finish_heads, 0)
    keep.wait()


def gather_project(tokens, gain, weights, output_weight, cos_t, sin_t):
    rows, features = tokens.shape
    r = weights[0].shape[0]
    devices = lax.axis_size("dp")
    packs = lax.axis_size("rep")
    n = devices // 2
    vmem = pl.BlockSpec(memory_space=pltpu.VMEM)
    dma = pltpu.SemaphoreType.DMA
    hbm = pl.BlockSpec(memory_space=pl.ANY)
    return pl.pallas_call(
        gather_project_kernel,
        out_shape=(
            jax.ShapeDtypeStruct((3, devices * rows, r), LOW),
            jax.ShapeDtypeStruct((n, rows, features), LOW),
            jax.ShapeDtypeStruct((devices,) + output_weight.shape, LOW),
        ),
        in_specs=[hbm, vmem] + [hbm] * 4 + [vmem] * 2,
        out_specs=(vmem, pl.BlockSpec(memory_space=pl.ANY), pl.BlockSpec(memory_space=pl.ANY)),
        scratch_shapes=[
            pltpu.VMEM((rows, features), LOW),
            pltpu.VMEM((3, r, features), LOW),
            pltpu.VMEM((rows, features), LOW),
            pltpu.VMEM((3, r, features), LOW),
            pltpu.VMEM((rows, features), LOW),
            pltpu.VMEM((n, 3, rows, r), LOW),
            dma((4,)),
            dma((2, n)), dma((2, n)), dma((3,)), dma((3,)), dma((2, n)), dma((2, n)), dma((6,)),
            dma((2, n)), dma((2, n)), dma((2, n)), dma((2, n)),
            dma((packs - 1, 2, n)), dma((packs - 1, 2, n)),
            dma((packs - 1, 2, n)), dma((packs - 1, 2, n)),
        ],
        compiler_params=pltpu.CompilerParams(
            collective_id=1, has_side_effects=True, vmem_limit_bytes=60 * MIB
        ),
        cost_estimate=pl.CostEstimate(
            flops=4 * n * rows * features * 3 * r, bytes_accessed=320 * MIB, transcendentals=0
        ),
        name="gather_project",
    )(tokens, gain, *weights, output_weight, cos_t, sin_t)


def split_heads(u):
    heads = u.shape[1] // HEAD_DIM
    if heads == 1:
        return u
    lane = lax.broadcasted_iota(jnp.int32, u.shape, 1) // HEAD_DIM
    zero = jnp.zeros_like(u)
    return jnp.concatenate([jnp.where(lane == h, u, zero) for h in range(heads)], 0)


def join_heads(u):
    heads = u.shape[0] // HEAD_DIM
    return jnp.concatenate(
        [u[h * HEAD_DIM : (h + 1) * HEAD_DIM, h * BLOCK : (h + 1) * BLOCK] for h in range(heads)], 0
    )


def transpose_blocks(source, target):
    def one(b, carry):
        at = pl.multiple_of(b * BLOCK, BLOCK)
        target[:, pl.ds(at, BLOCK)] = source[pl.ds(at, BLOCK), :].astype(F32).T.astype(LOW)
        return carry

    lax.fori_loop(0, source.shape[0] // BLOCK, one, 0)


def window_of(b, first, tail, columns):
    start = pl.multiple_of(jnp.maximum(b - (CHUNK // BLOCK - 1), 0) * BLOCK, BLOCK)
    whole = (b - first) // (CHUNK // BLOCK)
    lowest = (first + whole * (CHUNK // BLOCK)) * BLOCK
    key_index = start + lax.broadcasted_iota(jnp.int32, (CHUNK, columns), 0)
    query_index = b * BLOCK + lax.broadcasted_iota(jnp.int32, (CHUNK, columns), 1) % BLOCK
    allowed = (
        (key_index >= lowest)
        & (key_index <= query_index)
        & (key_index < b * BLOCK + tail)
    )
    return start, whole, allowed


def walk_rows(b, tok_dev, chips):
    device = b * BLOCK // tok_dev
    spot = place_of(device // 2, chips) * 2 + device % 2
    return pl.ds(pl.multiple_of(spot * tok_dev + b * BLOCK % tok_dev, BLOCK), BLOCK)


def attend_kernel(chips, first_ref, tail_ref, qkv, attended, log_total, value_t):
    tokens, r = qkv.shape[1:]
    tok_dev = tokens // (2 * chips)
    columns = (r // HEAD_DIM) * BLOCK
    scale = 1.0 / math.sqrt(HEAD_DIM)
    transpose_blocks(qkv.at[2], value_t)

    def block(b, carry):
        at = pl.multiple_of(b * BLOCK, BLOCK)
        query = split_heads(qkv[0, pl.ds(at, BLOCK), :])
        start, whole, allowed = window_of(b, first_ref[b], tail_ref[b], columns)
        scores = dot_nt(qkv[1, pl.ds(start, CHUNK), :], query) * scale
        scores = jnp.where(allowed, scores, MASKED_SCORE)
        top = jnp.max(scores, axis=0, keepdims=True)
        weights = jnp.exp(scores - top)
        total = jnp.sum(weights, axis=0, keepdims=True)
        out = dot_nn(value_t[:, pl.ds(start, CHUNK)], weights.astype(LOW))

        def more(i, state):
            top, total, out = state
            start = pl.multiple_of(first_ref[b] * BLOCK + i * CHUNK, BLOCK)
            scores = dot_nt(qkv[1, pl.ds(start, CHUNK), :], query) * scale
            higher = jnp.maximum(top, jnp.max(scores, axis=0, keepdims=True))
            shrink = jnp.exp(top - higher)
            weights = jnp.exp(scores - higher)
            total = total * shrink + jnp.sum(weights, axis=0, keepdims=True)
            out = out * shrink + dot_nn(value_t[:, pl.ds(start, CHUNK)], weights.astype(LOW))
            return higher, total, out

        top, total, out = lax.fori_loop(0, whole, more, (top, total, out))
        log_total[pl.ds(b, 1), :] = top + jnp.log(total)
        attended[walk_rows(b, tok_dev, chips), :] = join_heads(out / total).T.astype(LOW)
        return carry

    lax.fori_loop(0, tokens // BLOCK, block, 0)


def attend(first, tail, qkv):
    tokens, r = qkv.shape[1:]
    smem = pl.BlockSpec(memory_space=pltpu.SMEM)
    vmem = pl.BlockSpec(memory_space=pltpu.VMEM)
    return pl.pallas_call(
        functools.partial(attend_kernel, lax.axis_size("dp") // 2),
        out_shape=(
            jax.ShapeDtypeStruct((tokens, r), LOW),
            jax.ShapeDtypeStruct((tokens // BLOCK, (r // HEAD_DIM) * BLOCK), F32),
        ),
        in_specs=[smem, smem, vmem],
        out_specs=(vmem, vmem),
        scratch_shapes=[pltpu.VMEM((r, tokens), LOW)],
        compiler_params=pltpu.CompilerParams(vmem_limit_bytes=40 * MIB),
        cost_estimate=pl.CostEstimate(
            flops=4 * tokens * 1024 * r * 8, bytes_accessed=120 * MIB, transcendentals=tokens * 1024
        ),
        name="attend",
    )(first, tail, qkv)


def unrotate(g, cos, sin):
    parts = []
    for h in range(g.shape[0] // HEAD_DIM):
        one = g[h * HEAD_DIM : h * HEAD_DIM + HALF]
        two = g[h * HEAD_DIM + HALF : (h + 1) * HEAD_DIM]
        parts += [one * cos + two * sin, two * cos - one * sin]
    return jnp.concatenate(parts, 0)


def attend_back_kernel(
    chips, first_ref, tail_ref, qkv, grad_out, attended, log_total, cos_t, sin_t, grads,
    key_t, grad_key, grad_value, staged, store_sem,
):
    tokens, r = qkv.shape[1:]
    tok_dev = tokens // (2 * chips)
    heads = r // HEAD_DIM
    columns = heads * BLOCK
    scale = 1.0 / math.sqrt(HEAD_DIM)
    transpose_blocks(qkv.at[1], key_t)
    grad_key[...] = jnp.zeros_like(grad_key)
    grad_value[...] = jnp.zeros_like(grad_value)

    def block(b, carry):
        at = pl.multiple_of(b * BLOCK, BLOCK)
        here = pl.ds(at, BLOCK)
        query = split_heads(qkv[0, here, :])
        walk = walk_rows(b, tok_dev, chips)
        grad_rows = grad_out[walk, :]
        grad = split_heads(grad_rows)
        product = (grad_rows.astype(F32) * attended[walk, :].astype(F32)).T
        delta = jnp.concatenate(
            [
                jnp.sum(product[h * HEAD_DIM : (h + 1) * HEAD_DIM], axis=0, keepdims=True)
                for h in range(heads)
            ],
            1,
        )
        log_row = log_total[pl.ds(b, 1), :]

        def chunk(start, allowed, grad_query):
            span = pl.ds(start, CHUNK)
            scores = dot_nt(qkv[1, span, :], query) * scale
            weights = jnp.exp(scores - log_row)
            if allowed is not None:
                weights = jnp.where(allowed, weights, 0.0)
            grad_weights = dot_nt(qkv[2, span, :], grad)
            grad_scores = (weights * (grad_weights - delta)).astype(LOW)
            grad_value[span, :] += dot_nn(weights.astype(LOW), grad)
            grad_key[span, :] += dot_nn(grad_scores, query)
            return grad_query + dot_nn(key_t[:, span], grad_scores)

        start, whole, allowed = window_of(b, first_ref[b], tail_ref[b], columns)
        grad_query = chunk(start, allowed, jnp.zeros((r, columns), F32))
        grad_query = lax.fori_loop(
            0,
            whole,
            lambda i, g: chunk(pl.multiple_of(first_ref[b] * BLOCK + i * CHUNK, BLOCK), None, g),
            grad_query,
        )
        turned = unrotate(join_heads(grad_query) * scale, cos_t[:, here], sin_t[:, here])
        staged[0, here, :] = turned.T.astype(LOW)
        return carry

    lax.fori_loop(0, tokens // BLOCK, block, 0)
    query_store = pltpu.make_async_copy(staged.at[0], grads.at[0], store_sem.at[0])
    query_store.start()

    def close(b, carry):
        here = pl.ds(pl.multiple_of(b * BLOCK, BLOCK), BLOCK)
        turned = unrotate(grad_key[here, :].T * scale, cos_t[:, here], sin_t[:, here])
        staged[1, here, :] = turned.T.astype(LOW)
        staged[2, here, :] = grad_value[here, :].astype(LOW)
        return carry

    lax.fori_loop(0, tokens // BLOCK, close, 0)
    rest_store = pltpu.make_async_copy(staged.at[pl.ds(1, 2)], grads.at[pl.ds(1, 2)], store_sem.at[1])
    rest_store.start()
    query_store.wait()
    rest_store.wait()


def attend_back(first, tail, qkv, grad_out, attended, log_total, cos_t, sin_t):
    tokens, r = qkv.shape[1:]
    smem = pl.BlockSpec(memory_space=pltpu.SMEM)
    vmem = pl.BlockSpec(memory_space=pltpu.VMEM)
    return pl.pallas_call(
        functools.partial(attend_back_kernel, lax.axis_size("dp") // 2),
        out_shape=jax.ShapeDtypeStruct((3, tokens, r), LOW),
        in_specs=[smem, smem] + [vmem] * 6,
        out_specs=pl.BlockSpec(memory_space=pl.ANY),
        scratch_shapes=[
            pltpu.VMEM((r, tokens), LOW),
            pltpu.VMEM((tokens, r), F32),
            pltpu.VMEM((tokens, r), F32),
            pltpu.VMEM((3, tokens, r), LOW),
            pltpu.SemaphoreType.DMA((2,)),
        ],
        compiler_params=pltpu.CompilerParams(vmem_limit_bytes=40 * MIB),
        cost_estimate=pl.CostEstimate(
            flops=10 * tokens * 1024 * r * 8, bytes_accessed=240 * MIB, transcendentals=tokens * 1024
        ),
        name="attend_back",
    )(first, tail, qkv, grad_out, attended, log_total, cos_t, sin_t)


def mixed_kernel(
    attended, tokens_in, gain, output_all, mixed, normed, blocks,
    tokens, weights, sem, w_sem, send_sem, recv_sem,
):
    ring = Ring()
    n = ring.chips
    devices = 2 * n
    rows, features = mixed.shape
    r = attended.shape[1]
    spot = ring.place * 2 + ring.core
    load = pltpu.make_async_copy(tokens_in, tokens, sem)
    load.start()

    def place_at(j):
        return lax.rem(ring.place + (j % 2) * ((j + 1) // 2) + (1 - j % 2) * (n - j // 2), n)

    def chip_weights(j):
        place = place_at(j)
        return pltpu.make_async_copy(
            output_all.at[pl.ds(place * 2, 2)], weights.at[pl.ds(place * 2, 2)], w_sem.at[j]
        )

    def fetch(j, carry):
        chip_weights(j).start()
        return carry

    lax.fori_loop(0, n, fetch, 0)
    barrier = pltpu.get_barrier_semaphore()

    def to(k):
        other = lax.rem(spot + k, devices)
        return chip_at(other // 2, n) * 2 + other % 2

    def greet(k, carry):
        pl.semaphore_signal(barrier, inc=1, device_id={"dp": to(k)}, device_id_type=MESH)
        return carry

    lax.fori_loop(1, devices, greet, 0)
    pl.semaphore_wait(barrier, devices - 1)

    def rows_of(at):
        return pl.ds(pl.multiple_of(at * rows, rows), rows)

    def copy(k):
        return remote(
            attended.at[rows_of(lax.rem(spot + k, devices))],
            blocks.at[spot],
            send_sem.at[k],
            recv_sem.at[k],
            to(k),
        )

    def begin(k, carry):
        copy(k).start()
        return carry

    lax.fori_loop(1, devices, begin, 0)
    blocks[spot] = attended[rows_of(spot), :]
    load.wait()
    mixed[...] = tokens[...].astype(F32)

    def add(j, carry):
        chip_weights(j).wait()
        place = place_at(j)
        for core in (0, 1):
            k = lax.rem(spot + devices - place * 2 - core, devices)

            @pl.when(k > 0)
            def _():
                copy(k).wait_recv()

        both = jnp.concatenate([blocks[place * 2 + core] for core in (0, 1)], 1)
        mixed[...] += dot_nn(both, weights[pl.ds(place * 2, 2)].reshape(2 * r, features))
        return carry

    lax.fori_loop(0, n, add, 0)

    def normalize(i, carry):
        span = pl.ds(pl.multiple_of(i * 32, 32), 32)
        value = mixed[span, :]
        scale = lax.rsqrt(jnp.mean(value * value, axis=1, keepdims=True) + EPSILON)
        normed[span, :] = (value * scale * gain[...]).astype(LOW)
        return carry

    lax.fori_loop(0, rows // 32, normalize, 0)

    def finish(k, carry):
        copy(k).wait_send()
        return carry

    lax.fori_loop(1, devices, finish, 0)


def mix(attended, tokens, gain, output_all):
    rows, features = tokens.shape
    devices, r = output_all.shape[:2]
    vmem = pl.BlockSpec(memory_space=pltpu.VMEM)
    hbm = pl.BlockSpec(memory_space=pl.ANY)
    dma = pltpu.SemaphoreType.DMA
    return pl.pallas_call(
        mixed_kernel,
        out_shape=(
            jax.ShapeDtypeStruct((rows, features), F32),
            jax.ShapeDtypeStruct((rows, features), LOW),
            jax.ShapeDtypeStruct((devices, rows, r), LOW),
        ),
        in_specs=[vmem, hbm, vmem, hbm],
        out_specs=(vmem,) * 3,
        scratch_shapes=[
            pltpu.VMEM((rows, features), LOW),
            pltpu.VMEM((devices, r, features), LOW),
            dma, dma((devices // 2,)), dma((devices,)), dma((devices,)),
        ],
        compiler_params=pltpu.CompilerParams(
            collective_id=5, has_side_effects=True, vmem_limit_bytes=56 * MIB
        ),
        cost_estimate=pl.CostEstimate(
            flops=2 * rows * features * features, bytes_accessed=100 * MIB, transcendentals=0
        ),
        name="mix",
    )(attended, tokens, gain, output_all)


def dense_kernel(
    normed, cotangents, gate_w, up_w, down_w, gate_p, up_p, down_p,
    grad_sum, out_parts, gathered, gate_grad, up_a, up_b, down_grad,
    weights, totals, x_buf, g_buf, out_acc, grad_acc, sent, landed, cast_buf, pair_land,
    ag_send, ag_recv, rs_send, rs_recv, credit, local_sem, w_sem, cast_sem, pair_send, pair_recv,
):
    ring = Ring()
    n = ring.chips
    rows, features = normed.shape
    half = rows // 2
    own = gate_w.shape[0]
    tiles = 2 * own // FF_TILE
    loads = []
    for i, (mine, theirs) in enumerate(((gate_w, gate_p), (up_w, up_p), (down_w, down_p))):
        loads.append(pltpu.make_async_copy(mine, weights.at[i, pl.ds(0, own)], w_sem.at[2 * i]))
        loads.append(pltpu.make_async_copy(theirs, weights.at[i, pl.ds(own, own)], w_sem.at[2 * i + 1]))
    for load in loads:
        load.start()
    ring.greet((ring.next[0], ring.next[1], ring.partner))

    def source(t, d):
        return lax.rem(ring.place + (n - t if d == 0 else t), n)

    def send(t, d, first):
        place, part = source(t - 1, d), half_rows(d, rows)
        src = normed.at[part] if first else gathered.at[place, part]
        return remote(src, gathered.at[place, part], ag_send.at[d, t - 1], ag_recv.at[d, t - 1], ring.next[d])

    def reduce_copy(t, d):
        return remote(sent.at[d], landed.at[d, t % 2], rs_send.at[d], rs_recv.at[d, t % 2], ring.next[d])

    for d in (0, 1):
        send(1, d, True).start()

    def clear(i, carry):
        span = pl.ds(pl.multiple_of(i * FF_TILE, FF_TILE), FF_TILE)
        for k in range(3):
            totals[k, span, :] = jnp.zeros((FF_TILE, features), F32)
        return carry

    lax.fori_loop(0, tiles, clear, 0)
    for load in loads:
        load.wait()

    def out_copy(t, d):
        part = half_rows(d, rows)
        return pltpu.make_async_copy(
            cast_buf.at[t % 2, part], out_parts.at[source(t, d), part], cast_sem.at[t % 2, d]
        )

    def pass_on(t):
        for d in (0, 1):
            send(t, d, False).wait_recv()

        @pl.when(t < n - 1)
        def _():
            for d in (0, 1):
                send(t + 1, d, False).start()

    def step(t, carry):
        copies = []
        for d in (0, 1):
            part = half_rows(d, rows)
            copies.append(
                pltpu.make_async_copy(cotangents.at[source(t, d), part], g_buf.at[part], local_sem.at[d])
            )
        for copy in copies:
            copy.start()

        @pl.when(t > 1)
        def _():
            pass_on(t)

        @pl.when(t > 0)
        def _():
            more = []
            for d in (0, 1):
                part = half_rows(d, rows)
                more.append(
                    pltpu.make_async_copy(gathered.at[source(t, d), part], x_buf.at[part], local_sem.at[2 + d])
                )
                more[-1].start()
            for copy in more:
                copy.wait()

        @pl.when(t == 0)
        def _():
            x_buf[...] = normed[...]

        for copy in copies:
            copy.wait()

        out_acc[...] = jnp.zeros_like(out_acc)
        grad_acc[...] = jnp.zeros_like(grad_acc)

        def tile(i, carry):
            @pl.when((t == 0) & (i == tiles - 1))
            def _():
                pass_on(1)

            span = pl.ds(pl.multiple_of(i * FF_TILE, FF_TILE), FF_TILE)
            x = x_buf[...]
            g = g_buf[...]
            gate = dot_nt(x, weights[0, span, :])
            up = dot_nt(x, weights[1, span, :])
            grad_hidden = dot_nt(g, weights[2, span, :])
            sigma = 1.0 / (1.0 + jnp.exp(-gate))
            silu = gate * sigma
            hidden = (silu * up).astype(LOW)
            grad_gate = (grad_hidden * up * sigma * (1.0 + gate * (1.0 - sigma))).astype(LOW)
            grad_up = (grad_hidden * silu).astype(LOW)
            out_acc[...] += dot_nn(hidden, weights[2, span, :])
            grad_acc[...] += dot_nn(grad_gate, weights[0, span, :])
            grad_acc[...] += dot_nn(grad_up, weights[1, span, :])
            totals[0, span, :] += dot_tn(grad_gate, x)
            totals[1, span, :] += dot_tn(grad_up, x)
            totals[2, span, :] += dot_tn(hidden, g)
            return carry

        lax.fori_loop(0, tiles, tile, 0)

        @pl.when(t >= 2)
        def _():
            for d in (0, 1):
                out_copy(t - 2, d).wait()

        cast_buf[t % 2] = out_acc[...].astype(LOW)
        for d in (0, 1):
            out_copy(t, d).start()

        @pl.when(t == 0)
        def _():
            grad_sum[...] = grad_acc[...]

        @pl.when(t > 0)
        def _():
            for d in (0, 1):
                part = pl.ds(d * half, half)

                @pl.when(t >= 2)
                def _():
                    reduce_copy(t - 1, d).wait_recv()
                    grad_acc[part, :] += landed[d, (t - 1) % 2].astype(F32)

                    @pl.when(t <= n - 2)
                    def _():
                        pl.semaphore_signal(
                            credit.at[d], inc=1, device_id={"dp": ring.back[d]}, device_id_type=MESH
                        )

                    reduce_copy(t - 1, d).wait_send()

                sent[d] = grad_acc[part, :].astype(LOW)

                @pl.when(t >= 3)
                def _():
                    pl.semaphore_wait(credit.at[d], 1)

                reduce_copy(t, d).start()

        return carry

    lax.fori_loop(0, n, step, 0)
    for t in (n - 2, n - 1):
        for d in (0, 1):
            out_copy(t, d).wait()

    own_tiles = 3 * own // FF_TILE

    def tile_of(i, first):
        return i // (own // FF_TILE), pl.ds(
            pl.multiple_of(first + (i % (own // FF_TILE)) * FF_TILE, FF_TILE), FF_TILE
        )

    def pair_copy(i):
        return remote(cast_buf.at[i % 2], pair_land.at[i], pair_send.at[i % 2], pair_recv.at[i], ring.partner)

    def give(i, carry):
        @pl.when(i >= 2)
        def _():
            pair_copy(i - 2).wait_send()

        k, span = tile_of(i, own)
        cast_buf[i % 2] = totals[k, span, :].astype(LOW)
        pair_copy(i).start()
        return carry

    lax.fori_loop(0, own_tiles, give, 0)
    for i in (own_tiles - 2, own_tiles - 1):
        pair_copy(i).wait_send()

    def total_copies(i):
        matrix, low = i // (own // FF_TILE), (i % (own // FF_TILE)) * FF_TILE
        if matrix != 1:
            target = (gate_grad, None, down_grad)[matrix].at[pl.ds(low, FF_TILE)]
            return [pltpu.make_async_copy(cast_buf.at[i % 2], target, cast_sem.at[i % 2, 0])]
        copies = []
        for j in range(FF_TILE // STRIPE):
            for target, first, count in ((up_a, 0, STRIPE // 4), (up_b, STRIPE // 4, 3 * STRIPE // 4)):
                copies.append(
                    pltpu.make_async_copy(
                        cast_buf.at[i % 2, pl.ds(j * STRIPE + first, count)],
                        target.at[pl.ds((low // STRIPE + j) * count, count)],
                        cast_sem.at[i % 2, len(copies)],
                    )
                )
        return copies

    for i in range(own_tiles):
        if i >= 2:
            for copy in total_copies(i - 2):
                copy.wait()
        pair_copy(i).wait_recv()
        k, span = tile_of(i, 0)
        cast_buf[i % 2] = (totals[k, span, :] + pair_land[i].astype(F32)).astype(LOW)
        for copy in total_copies(i):
            copy.start()

    for d in (0, 1):
        part = pl.ds(d * half, half)
        reduce_copy(n - 1, d).wait_recv()
        grad_sum[part, :] += landed[d, (n - 1) % 2].astype(F32)
        reduce_copy(n - 1, d).wait_send()

    for i in (own_tiles - 2, own_tiles - 1):
        for copy in total_copies(i):
            copy.wait()

    def finish(t, carry):
        for d in (0, 1):
            send(t, d, False).wait_send()
        return carry

    lax.fori_loop(1, n, finish, 0)


def dense(normed, cotangents, own_weights, partner_weights):
    rows, features = normed.shape
    n = lax.axis_size("dp") // 2
    own = own_weights[0].shape[0]
    half = rows // 2
    vmem = pl.BlockSpec(memory_space=pltpu.VMEM)
    hbm = pl.BlockSpec(memory_space=pl.ANY)
    dma = pltpu.SemaphoreType.DMA
    own_tiles = 3 * own // FF_TILE
    return pl.pallas_call(
        dense_kernel,
        out_shape=(
            jax.ShapeDtypeStruct((rows, features), F32),
            jax.ShapeDtypeStruct((n, rows, features), LOW),
            jax.ShapeDtypeStruct((n, rows, features), LOW),
            jax.ShapeDtypeStruct((own, features), LOW),
            jax.ShapeDtypeStruct((own // 4, features), LOW),
            jax.ShapeDtypeStruct((own - own // 4, features), LOW),
            jax.ShapeDtypeStruct((own, features), LOW),
        ),
        in_specs=[vmem] + [hbm] * 7,
        out_specs=(vmem,) + (hbm,) * 6,
        scratch_shapes=[
            pltpu.VMEM((3, 2 * own, features), LOW),
            pltpu.VMEM((3, 2 * own, features), F32),
            pltpu.VMEM((rows, features), LOW),
            pltpu.VMEM((rows, features), LOW),
            pltpu.VMEM((rows, features), F32),
            pltpu.VMEM((rows, features), F32),
            pltpu.VMEM((2, half, features), LOW),
            pltpu.VMEM((2, 2, half, features), LOW),
            pltpu.VMEM((2, FF_TILE, features), LOW),
            pltpu.VMEM((own_tiles, FF_TILE, features), LOW),
            dma((2, n)), dma((2, n)), dma((2,)), dma((2, 2)),
            pltpu.SemaphoreType.REGULAR((2,)),
            dma((4,)), dma((6,)), dma((2, 2 * FF_TILE // STRIPE)), dma((2,)), dma((own_tiles,)),
        ],
        compiler_params=pltpu.CompilerParams(
            collective_id=2, has_side_effects=True, vmem_limit_bytes=62 * MIB
        ),
        cost_estimate=pl.CostEstimate(
            flops=2 * 9 * n * rows * features * 2 * own, bytes_accessed=500 * MIB, transcendentals=0
        ),
        name="dense",
    )(normed, cotangents, *own_weights, *partner_weights)


def output_split(r, packs):
    plain = r // 4 if (r - r // 4) // packs % 16 == 0 else 0
    return (r - plain) // packs, plain


def mixed_back_kernel(
    packs, mixed_in, grad_in, cotangent_in, gain, output_all, blocks, grad_mixed, gain_part, grad_heads, *rest
):
    sums = rest[:packs]
    given, taken = rest[packs : 2 * packs], rest[2 * packs : 3 * packs]
    (
        mixed, grad_two, cotangent, low, weights, staged, product,
        sem, w_sem, send_sem, recv_sem, g_sem, t_sem,
    ) = rest[3 * packs :]
    ring = Ring()
    n = ring.chips
    devices = 2 * n
    rows, features = mixed.shape
    r = grad_heads.shape[1]
    pack = lax.axis_index("rep")
    spot = ring.place * 2 + ring.core
    loads = [
        pltpu.make_async_copy(src, dst, sem.at[i])
        for i, (src, dst) in enumerate(((mixed_in, mixed), (grad_in, grad_two), (cotangent_in, cotangent)))
    ]
    for load in loads:
        load.start()

    def chip_weights(k):
        at = lax.rem(ring.place + k, n) * 2
        return pltpu.make_async_copy(output_all.at[pl.ds(at, 2)], weights.at[pl.ds(2 * k, 2)], w_sem.at[k])

    def fetch(k, carry):
        chip_weights(k).start()
        return carry

    lax.fori_loop(0, n, fetch, 0)
    barrier = pltpu.get_barrier_semaphore()

    def to(k):
        other = lax.rem(spot + k, devices)
        return {"dp": chip_at(other // 2, n) * 2 + other % 2}

    def greet(k, carry):
        pl.semaphore_signal(barrier, inc=1, device_id=to(k), device_id_type=MESH)
        return carry

    lax.fori_loop(1, devices, greet, 0)
    pl.semaphore_wait(barrier, devices - 1)
    for load in loads:
        load.wait()
    gain_part[...] = jnp.zeros_like(gain_part)

    def norm_back(i, carry):
        span = pl.ds(pl.multiple_of(i * 16, 16), 16)
        value, grad = mixed[span, :], grad_two[span, :]
        scale = lax.rsqrt(jnp.mean(value * value, axis=1, keepdims=True) + EPSILON)
        scaled = grad * gain[...]
        shift = jnp.mean(value * scaled, axis=1, keepdims=True)
        total = cotangent[span, :].astype(F32) + scale * scaled - value * (scale * scale * scale * shift)
        grad_mixed[span, :] = total
        low[span, :] = total.astype(LOW)
        gain_part[...] += jnp.sum(grad * value * scale, axis=0, keepdims=True)
        return carry

    lax.fori_loop(0, rows // 16, norm_back, 0)

    def copy(k):
        return remote(
            staged.at[k],
            grad_heads.at[pl.ds(pl.multiple_of(spot * rows, rows), rows)],
            send_sem.at[k],
            recv_sem.at[k],
            to(k)["dp"],
        )

    def project(k, carry):
        chip_weights(k).wait()
        both = dot_nt(low[...], weights[pl.ds(2 * k, 2)].reshape(2 * r, features))
        for core in (0, 1):
            step = lax.rem(2 * k + core - ring.core + devices, devices)
            staged[step] = both[:, core * r : (core + 1) * r].astype(LOW)

            @pl.when(step > 0)
            def _():
                copy(step).start()

        return carry

    lax.fori_loop(0, n, project, 0)
    grad_heads[pl.ds(pl.multiple_of(spot * rows, rows), rows), :] = staged[0]

    def give(k):
        return remote(given[k], taken[k], g_sem.at[k], t_sem.at[k], ring.partner)

    share, plain = output_split(r, packs)

    def spots(k, place, first, count):
        width = share + plain if k == 0 else share
        return pl.ds(pl.multiple_of(place * width + first, 16), count)

    def products(place, core, use):
        product[...] = dot_tn(blocks[place * 2 + core], low[...])
        for k in range(packs):
            at = pl.multiple_of(lax.rem(pack + k, packs) * share, share)
            use(k, spots(k, place, 0, share), product[pl.ds(at, share), :])
        if plain:
            use(0, spots(0, place, share, plain), product[pl.ds(r - plain, plain), :])

    def put(k, at, value):
        given[k][at, :] = value.astype(LOW)

    def total(k, at, value):
        sums[k][at, :] = (value + taken[k][at, :].astype(F32)).astype(LOW)

    def for_partner(place, carry):
        products(place, 1 - ring.core, put)
        return carry

    def for_self(place, carry):
        products(place, ring.core, total)
        return carry

    lax.fori_loop(0, n, for_partner, 0)
    for k in range(packs):
        give(k).start()
    for k in range(packs):
        give(k).wait_recv()
    lax.fori_loop(0, n, for_self, 0)

    def finish(k, carry):
        copy(k).wait_send()
        copy(k).wait_recv()
        return carry

    lax.fori_loop(1, devices, finish, 0)
    for k in range(packs):
        give(k).wait_send()


def mixed_back(mixed, grad_two, cotangent, gain, output_all, blocks):
    rows, features = mixed.shape
    devices, r = output_all.shape[:2]
    packs = lax.axis_size("rep")
    n = devices // 2
    share, plain = output_split(r, packs)
    sizes = [n * (share + plain)] + [n * share] * (packs - 1)
    vmem = pl.BlockSpec(memory_space=pltpu.VMEM)
    hbm = pl.BlockSpec(memory_space=pl.ANY)
    dma = pltpu.SemaphoreType.DMA
    return pl.pallas_call(
        functools.partial(mixed_back_kernel, packs),
        out_shape=(
            jax.ShapeDtypeStruct((rows, features), F32),
            jax.ShapeDtypeStruct((1, features), F32),
            jax.ShapeDtypeStruct((devices * rows, r), LOW),
        )
        + tuple(jax.ShapeDtypeStruct((size, features), LOW) for size in sizes),
        in_specs=[hbm] * 3 + [vmem, hbm, vmem],
        out_specs=(vmem,) * (3 + packs),
        scratch_shapes=[pltpu.VMEM((size, features), LOW) for size in sizes + sizes]
        + [
            pltpu.VMEM((rows, features), F32),
            pltpu.VMEM((rows, features), F32),
            pltpu.VMEM((rows, features), LOW),
            pltpu.VMEM((rows, features), LOW),
            pltpu.VMEM((devices, r, features), LOW),
            pltpu.VMEM((devices, rows, r), LOW),
            pltpu.VMEM((r, features), F32),
            dma((3,)), dma((n,)), dma((devices,)), dma((devices,)), dma((packs,)), dma((packs,)),
        ],
        compiler_params=pltpu.CompilerParams(
            collective_id=4, has_side_effects=True, vmem_limit_bytes=56 * MIB
        ),
        cost_estimate=pl.CostEstimate(
            flops=4 * rows * features * features, bytes_accessed=130 * MIB, transcendentals=0
        ),
        name="mixed_back",
    )(mixed, grad_two, cotangent, gain, output_all, blocks)


def normed_back_kernel(
    packs, grads_in, query_w, key_w, value_w, partner_w, hidden_in, gain, grad_mixed, dense_gain_part, normed_all, output_mine, *rest
):
    output_there = rest[: packs - 1]
    (
        out, gains, rep_land, o_packs,
        grads, joined, partner_grads, sent, landed, x_buf, parts, pair_out, pair_land,
        o_sent, o_landed, far_part, far_land, near_part, near_land,
        in_sem, w_sem, p_send, p_recv, rs_send, rs_recv, credit, x_sem, pair_sem, rep_send, rep_recv,
        o_send, o_recv, o_credit, swap_send, swap_recv, near_send, near_recv, far_send, far_recv,
    ) = rest[packs - 1 :]
    ring = Ring()
    n = ring.chips
    rows, features = out.shape
    half = rows // 2
    r = grads.shape[2]
    share, plain = output_split(r, packs)
    pack = lax.axis_index("rep")
    mates = 2 * packs
    mate = pack * 2 + ring.core
    barrier = pltpu.get_barrier_semaphore()
    load_grads = pltpu.make_async_copy(grads_in, grads, in_sem)
    load_grads.start()
    load_weights = [
        pltpu.make_async_copy(src, joined.at[pl.ds(i * r, src.shape[0])], w_sem.at[i])
        for i, src in enumerate((query_w, key_w, value_w, partner_w))
    ]
    for load in load_weights:
        load.start()

    def near(k):
        to = lax.rem(mate + k, mates)
        return {"dp": ring.chip * 2 + to % 2, "rep": to // 2}

    def far(k):
        return {"dp": lax.rem(ring.chip + k, n) * 2 + ring.core}

    for k in range(1, mates):
        pl.semaphore_signal(barrier, inc=1, device_id=near(k), device_id_type=MESH)
    for k in range(1, n):
        pl.semaphore_signal(barrier, inc=1, device_id=far(k), device_id_type=MESH)
    pl.semaphore_wait(barrier, mates + n - 2)
    load_grads.wait()

    def place(t, d):
        return ring.chip_far(-t if d == 0 else t)

    def swap(t, d):
        start = (place(t, d) * 2 + 1 - ring.core) * rows + d * half
        return remote(
            grads.at[:, pl.ds(pl.multiple_of(start, half), half)],
            partner_grads.at[:, t % n, half_rows(d, rows)],
            p_send.at[d, t % n],
            p_recv.at[d, t % n],
            ring.partner,
        )

    def begin(t, carry):
        for d in (0, 1):
            swap(t, d).start()
        return carry

    lax.fori_loop(1, n + 1, begin, 0)

    def reduce_copy(t, d, u):
        return remote(
            sent.at[d, u, t % 2],
            landed.at[d, u, t % 2],
            rs_send.at[d, u, t % 2],
            rs_recv.at[d, u, t % 2],
            ring.next[d],
        )

    def output_copy(t, d):
        return remote(
            o_sent.at[d, t % 2],
            o_landed.at[d, t % 2],
            o_send.at[d, t % 2],
            o_recv.at[d, t % 2],
            ring.next[d],
        )

    def give_credit(sem, d):
        pl.semaphore_signal(sem, inc=1, device_id={"dp": ring.back[d]}, device_id_type=MESH)

    def mine(t, d):
        start = (place(t, d) * 2 + ring.core) * rows + d * half
        return pl.ds(pl.multiple_of(start, half), half)

    def load_rows(t, d):
        part = half_rows(d, rows)
        return pltpu.make_async_copy(normed_all.at[place(t, d), part], x_buf.at[t % 2, part], x_sem.at[t % 2, d])

    def block_grads(t):
        return jnp.concatenate(
            [jnp.concatenate([grads[i, mine(t, d), :] for d in (0, 1)], 0) for i in range(3)]
            + [partner_grads[i, t % n] for i in range(3)],
            1,
        )

    def weight_parts(t):
        for d in (0, 1):
            load_rows(t, d).wait()
        parts[...] += dot_tn(block_grads(t), x_buf[t % 2])

    def pair_copy():
        return remote(pair_out, pair_land, pair_sem.at[0], pair_sem.at[1], ring.partner)

    def rep_copy(k):
        return pltpu.make_async_remote_copy(
            src_ref=pair_out,
            dst_ref=rep_land.at[k - 1],
            send_sem=rep_send.at[k - 1],
            recv_sem=rep_recv.at[k - 1],
            device_id={"rep": lax.rem(pack + k, packs)},
            device_id_type=MESH,
        )

    middle = n // 2

    def output_step(t):
        for d in (0, 1):
            spot = lax.rem(ring.place + (n - t if d == 0 else t), n)
            columns = pl.ds(d * (features // 2), features // 2)
            own = pl.multiple_of(spot * (share + plain), 16)
            total = output_mine[pl.ds(own, share), columns].astype(F32)
            for there in output_there:
                total += there[pl.ds(pl.multiple_of(spot * share, share), share), columns].astype(F32)
            if plain:
                rest_rows = pl.ds(pl.multiple_of(own + share, 16), plain)
                total = jnp.concatenate([total, output_mine[rest_rows, columns].astype(F32)], 0)

            def pass_on(value):
                @pl.when(t >= 3)
                def _():
                    output_copy(t - 2, d).wait_send()
                    pl.semaphore_wait(o_credit.at[d], 1)

                o_sent[d, t % 2] = value.astype(LOW)
                output_copy(t, d).start()

            @pl.when(t == 1)
            def _():
                pass_on(total)

            @pl.when(t >= 2)
            def _():
                output_copy(t - 1, d).wait_recv()
                more = total + o_landed[d, (t - 1) % 2].astype(F32)

                @pl.when(t <= n - 2)
                def _():
                    give_credit(o_credit.at[d], d)

                @pl.when(t < n)
                def _():
                    pass_on(more)

                @pl.when(t == n)
                def _():
                    o_packs[packs - 1, :, columns] = more.astype(LOW)

    def output_swap(k):
        return pltpu.make_async_remote_copy(
            src_ref=o_packs.at[packs - 1],
            dst_ref=o_packs.at[k - 1],
            send_sem=swap_send.at[k - 1],
            recv_sem=swap_recv.at[k - 1],
            device_id={"rep": lax.rem(pack + k, packs)},
            device_id_type=MESH,
        )

    def copies_to(src, land, own, send_sem, recv_sem, device, count):
        return [
            pltpu.make_async_remote_copy(
                src_ref=src,
                dst_ref=land.at[own],
                send_sem=send_sem.at[k],
                recv_sem=recv_sem.at[k],
                device_id=device(k),
                device_id_type=MESH,
            )
            for k in range(1, count)
        ]

    def far_copies():
        return copies_to(far_part, far_land, ring.chip, far_send, far_recv, far, n)

    def near_copies():
        return copies_to(near_part, near_land, mate, near_send, near_recv, near, mates)

    def collect(copies, src, land, own, count):
        land[own] = src[...]
        for copy in copies:
            copy.wait()
        total = land[0]
        for k in range(1, count):
            total += land[k]
        return total

    def first_gain():
        def add(i, total):
            at = pl.ds(pl.multiple_of(i * 64, 64), 64)
            product = joined[at, :].astype(F32) * parts[at, :]
            return total + jnp.sum(product, axis=0, keepdims=True)

        return lax.fori_loop(0, 6 * r // 64, add, jnp.zeros((1, features), F32)) / gain[...]

    def step(t, carry):
        @pl.when(t <= middle)
        def _():
            for d in (0, 1):
                load_rows(2 * t - 1, d).start()
                load_rows(2 * t, d).start()

        for u in (0, 1):
            columns = pl.ds(u * (features // 2), features // 2)
            for d in (0, 1):
                part = pl.ds(d * half, half), columns

                @pl.when(t >= 2)
                def _():
                    reduce_copy(t - 1, d, u).wait_recv()
                    out[part] += landed[d, u, (t - 1) % 2].astype(F32)

                    @pl.when(t <= n - 2)
                    def _():
                        give_credit(credit.at[d, u], d)

                @pl.when(t < n)
                def _():
                    @pl.when(t >= 3)
                    def _():
                        reduce_copy(t - 2, d, u).wait_send()
                        pl.semaphore_wait(credit.at[d, u], 1)

                    sent[d, u, t % 2] = out[part].astype(LOW)
                    reduce_copy(t, d, u).start()

            @pl.when(2 * t - 1 + u <= n)
            def _():
                output_step(2 * t - 1 + u)

        @pl.when(2 * t == n)
        def _():
            for k in range(1, packs):
                output_swap(k).start()

        @pl.when(t == 1)
        def _():
            parts[...] = jnp.zeros_like(parts)

            def arrived(k, carry):
                for d in (0, 1):
                    swap(k, d).wait_recv()
                return carry

            lax.fori_loop(2, n + 1, arrived, 0)

        @pl.when(t <= middle)
        def _():
            weight_parts(2 * t - 1)
            weight_parts(2 * t)

        @pl.when(t == middle)
        def _():
            for i in range(3):
                pair_out[i] = parts[pl.ds((3 + i) * r, r), :].astype(LOW)
            pair_copy().start()
            far_part[0:1, :] = first_gain()
            far_part[1:2, :] = dense_gain_part[...]
            for copy in far_copies():
                copy.start()

        @pl.when(t == middle + 1)
        def _():
            pair_copy().wait()
            for i in range(3):
                pair_out[i] = (parts[pl.ds(i * r, r), :] + pair_land[i].astype(F32)).astype(LOW)
            for k in range(1, packs):
                rep_copy(k).start()
            rep_land[packs - 1] = pair_out[...]

        @pl.when(t == middle + 2)
        def _():
            near_part[...] = collect(far_copies(), far_part, far_land, ring.chip, n)
            for copy in near_copies():
                copy.start()

        @pl.when(t < n)
        def _():
            out[...] = dot_nn(block_grads(t + 1), joined[...])

        return carry

    for d in (0, 1):
        swap(1, d).wait_recv()
    for load in load_weights:
        load.wait()
    out[...] = dot_nn(block_grads(1), joined[...])
    lax.fori_loop(1, n + 1, step, 0)
    for t in (n - 2, n - 1):
        for d in (0, 1):
            output_copy(t, d).wait_send()
            for u in (0, 1):
                reduce_copy(t, d, u).wait_send()

    def close(i, carry):
        span = pl.ds(pl.multiple_of(i * 16, 16), 16)
        value = hidden_in[span, :].astype(F32)
        grad = out[span, :]
        scale = lax.rsqrt(jnp.mean(value * value, axis=1, keepdims=True) + EPSILON)
        scaled = grad * gain[...]
        shift = jnp.mean(value * scaled, axis=1, keepdims=True)
        out[span, :] = grad_mixed[span, :] + scale * scaled - value * (scale * scale * scale * shift)
        return carry

    lax.fori_loop(0, rows // 16, close, 0)

    def finish(t, carry):
        for d in (0, 1):
            swap(t, d).wait_send()
        return carry

    lax.fori_loop(1, n + 1, finish, 0)
    gains[...] = collect(near_copies(), near_part, near_land, mate, mates)
    for k in range(1, packs):
        rep_copy(k).wait()
        output_swap(k).wait()


def normed_back(
    grads, weights, partner_weights, hidden_in, gain, grad_mixed, dense_gain_part, normed_all, output_mine, output_there
):
    tokens, r = grads.shape[1:]
    features = partner_weights.shape[1]
    devices = lax.axis_size("dp")
    packs = lax.axis_size("rep")
    n = devices // 2
    rows = tokens // devices
    half = rows // 2
    share, plain = output_split(r, packs)
    carried = share + plain
    mates = 2 * packs
    vmem = pl.BlockSpec(memory_space=pltpu.VMEM)
    hbm = pl.BlockSpec(memory_space=pl.ANY)
    dma = pltpu.SemaphoreType.DMA
    return pl.pallas_call(
        functools.partial(normed_back_kernel, packs),
        out_shape=(
            jax.ShapeDtypeStruct((rows, features), F32),
            jax.ShapeDtypeStruct((2, features), F32),
        )
        + (
            jax.ShapeDtypeStruct((packs, 3, r, features), LOW),
            jax.ShapeDtypeStruct((packs, carried, features), LOW),
        ),
        in_specs=[hbm] * 5 + [vmem] * 4 + [hbm] + [vmem] * packs,
        out_specs=(vmem,) * 4,
        scratch_shapes=[
            pltpu.VMEM(grads.shape, LOW),
            pltpu.VMEM((6 * r, features), LOW),
            pltpu.VMEM((3, n, rows, r), LOW),
            pltpu.VMEM((2, 2, 2, half, features // 2), LOW),
            pltpu.VMEM((2, 2, 2, half, features // 2), LOW),
            pltpu.VMEM((2, rows, features), LOW),
            pltpu.VMEM((6 * r, features), F32),
            pltpu.VMEM((3, r, features), LOW),
            pltpu.VMEM((3, r, features), LOW),
            pltpu.VMEM((2, 2, carried, features // 2), LOW),
            pltpu.VMEM((2, 2, carried, features // 2), LOW),
            pltpu.VMEM((2, features), F32),
            pltpu.VMEM((n, 2, features), F32),
            pltpu.VMEM((2, features), F32),
            pltpu.VMEM((mates, 2, features), F32),
            dma, dma((4,)), dma((2, n)), dma((2, n)), dma((2, 2, 2)), dma((2, 2, 2)),
            pltpu.SemaphoreType.REGULAR((2, 2)),
            dma((2, 2)), dma((2,)), dma((packs - 1,)), dma((packs - 1,)),
            dma((2, 2)), dma((2, 2)), pltpu.SemaphoreType.REGULAR((2,)),
            dma((packs - 1,)), dma((packs - 1,)), dma((mates,)), dma((mates,)), dma((n,)), dma((n,)),
        ],
        compiler_params=pltpu.CompilerParams(
            collective_id=3, has_side_effects=True, vmem_limit_bytes=56 * MIB
        ),
        cost_estimate=pl.CostEstimate(
            flops=2 * n * rows * features * 12 * r, bytes_accessed=320 * MIB, transcendentals=0
        ),
        name="normed_back",
    )(
        grads, *weights, partner_weights, hidden_in, gain, grad_mixed, dense_gain_part, normed_all,
        output_mine, *output_there,
    )


def last_sums_kernel(packs, *refs):
    gate, up_a, up_b, down, gate_o, up_a_o, up_b_o, down_o, qkv, mixed, out_sum, grad_in, output = refs[:13]
    gate_t, up_t, down_t, query_t, key_t, value_t, layer, grad, output_t = refs[13:]

    def add(low, other):
        if packs == 2:
            return low[...].astype(F32) + other[...].astype(F32)
        return other[...].astype(F32)

    gate_t[...] = add(gate, gate_o)
    down_t[...] = add(down, down_o)
    up_t[...] = jnp.concatenate([add(up_a, up_a_o), add(up_b, up_b_o)], 0)
    pack = lax.axis_index("rep")
    slots = [lax.rem(pack + 2 * packs - q - 1, packs) for q in range(packs)]
    for i, target in enumerate((query_t, key_t, value_t)):
        total = qkv[slots[0], i].astype(F32)
        for slot in slots[1:]:
            total += qkv[slot, i].astype(F32)
        target[...] = total

    @pl.when(pl.program_id(0) == 0)
    def _():
        r = output_t.shape[0]
        share, plain = output_split(r, packs)
        for q, slot in enumerate(slots):
            output_t[q * share : (q + 1) * share, :] = output[slot, :share].astype(F32)
        if plain:
            total = output[slots[0], share:].astype(F32)
            for slot in slots[1:]:
                total += output[slot, share:].astype(F32)
            output_t[r - plain :, :] = total

    layer[...] = (mixed[...] + out_sum[...].astype(F32)).astype(LOW)
    grad[...] = grad_in[...]


def last_sums(lows, others, qkv, mixed, out_sum, grad_in, output):
    own, features = lows[0].shape
    rows, r = mixed.shape[0], qkv.shape[2]
    packs = qkv.shape[0]
    steps = own // STRIPE

    def striped(array):
        return pl.BlockSpec((array.shape[0] // steps, features), lambda i: (i, 0))

    wide = jax.ShapeDtypeStruct((own, features), F32)
    narrow = jax.ShapeDtypeStruct((r, features), F32)
    layer = jax.ShapeDtypeStruct((rows, features), LOW)
    out_shape = (wide,) * 3 + (narrow,) * 3 + (layer, grad_in, narrow)
    return pl.pallas_call(
        functools.partial(last_sums_kernel, packs),
        out_shape=tuple(jax.ShapeDtypeStruct(a.shape, a.dtype) for a in out_shape),
        grid=(steps,),
        in_specs=[striped(a) for a in (*lows, *others)]
        + [pl.BlockSpec((packs, 3, r // steps, features), lambda i: (0, 0, i, 0))]
        + [striped(a) for a in (mixed, out_sum, grad_in)]
        + [pl.BlockSpec(output.shape, lambda i: (0, 0, 0))],
        out_specs=tuple(striped(a) for a in out_shape[:-1])
        + (pl.BlockSpec((r, features), lambda i: (0, 0)),),
        compiler_params=pltpu.CompilerParams(vmem_limit_bytes=62 * MIB),
        cost_estimate=pl.CostEstimate(flops=8 * own * features, bytes_accessed=40 * MIB, transcendentals=0),
        name="last_sums",
    )(*lows, *others, qkv, mixed, out_sum, grad_in, output)


def from_partner(value):
    devices = lax.axis_size("dp")
    return lax.ppermute(value, "dp", [(i, i ^ 1) for i in range(devices)])


def pack_swap(low):
    if lax.axis_size("rep") == 2:
        return lax.ppermute(low, "rep", [(0, 1), (1, 0)])
    return lax.psum(low, "rep")


def together(*values):
    return lax.optimization_barrier(values)


def body(
    tokens,
    attention_gain,
    query_weight,
    key_weight,
    value_weight,
    output_weight,
    dense_gain,
    gate_weight,
    up_weight,
    down_weight,
    block_document,
    document_tail,
    cotangent,
):
    devices = lax.axis_size("dp")
    chips = devices // 2
    tok_dev = tokens.shape[1]
    pack_tok = tok_dev * devices

    documents, tails = block_document[0], document_tail[0]
    first = jnp.sum((documents[None, :] < documents[:, None]).astype(jnp.int32), axis=1)
    last = jnp.concatenate([documents[1:] != documents[:-1], jnp.ones((1,), bool)])
    doc_ids = jnp.arange(tails.shape[0], dtype=jnp.int32)
    own_tail = jnp.sum((documents[:, None] == doc_ids[None, :]) * tails[None, :], axis=1)
    tail = jnp.where(last, own_tail, BLOCK).astype(jnp.int32)
    block_index = jnp.arange(documents.shape[0], dtype=jnp.int32)
    inside = jnp.arange(BLOCK, dtype=jnp.int32)
    frequency = ROPE_BASE ** (-(jnp.arange(HALF, dtype=F32) * (2.0 / HEAD_DIM)))
    start = ((block_index - first) * BLOCK).astype(F32)[None, :] * frequency[:, None]
    within = inside.astype(F32)[None, :] * frequency[:, None]
    cos_a, sin_a = jnp.cos(start)[:, :, None], jnp.sin(start)[:, :, None]
    cos_b, sin_b = jnp.cos(within)[:, None, :], jnp.sin(within)[:, None, :]
    cos_t = (cos_a * cos_b - sin_a * sin_b).reshape(HALF, -1)
    sin_t = (sin_a * cos_b + cos_a * sin_b).reshape(HALF, -1)
    r = query_weight.shape[0]

    qkv, normed_all, full_output = gather_project(
        tokens[0],
        attention_gain[None],
        (query_weight, key_weight, value_weight),
        output_weight,
        cos_t,
        sin_t,
    )

    order = ring_order(chips)
    lanes = [[2 * chip + k for chip in order] for k in (0, 1)]
    grad_low = cotangent[0]
    qkv, grad_late = together(qkv, grad_low)
    cotangents = lax.all_gather(grad_late, "dp", axis=0, axis_index_groups=lanes)
    gate_other, up_other, down_other = (
        from_partner(gate_weight),
        from_partner(up_weight),
        from_partner(down_weight),
    )
    qkv_weight = jnp.concatenate([query_weight, key_weight, value_weight], 0)

    attended, log_total = attend(first, tail, qkv)
    mixed, normed_two, attended_blocks = mix(attended, tokens[0], dense_gain[None], full_output)
    normed_two, qkv_weight = together(normed_two, qkv_weight)
    qkv_other = from_partner(qkv_weight)
    packs, pack = lax.axis_size("rep"), lax.axis_index("rep")

    grad_normed_two, out_parts, _, gate_low, up_a, up_b, down_low = dense(
        normed_two,
        cotangents,
        (gate_weight, up_weight, down_weight),
        (gate_other, up_other, down_other),
    )
    out_sum = lax.psum_scatter(
        out_parts.reshape(chips * tok_dev, -1),
        "dp",
        scatter_dimension=0,
        tiled=True,
        axis_index_groups=lanes,
    )
    gate_there = pack_swap(gate_low)

    grad_mixed, dense_gain_part, grad_heads, output_mine, *output_low = mixed_back(
        mixed, grad_normed_two, grad_low, dense_gain[None], full_output, attended_blocks
    )
    output_there = [
        lax.ppermute(low, "rep", [(i, (i + k) % packs) for i in range(packs)])
        for k, low in enumerate(output_low, 1)
    ]
    grad_heads, gate_there, output_mine = together(grad_heads, gate_there, output_mine)
    up_a, _ = together(up_a, grad_heads)
    up_a_there = pack_swap(up_a)
    grads = attend_back(first, tail, qkv, grad_heads, attended, log_total, cos_t, sin_t)
    grads, output_there, up_a_there, up_b, down_low = together(
        grads, output_there, up_a_there, up_b, down_low
    )
    up_b_there = pack_swap(up_b)
    down_there = pack_swap(down_low)
    input_grad, gain_totals, qkv_packs, output_packs = normed_back(
        grads,
        (query_weight, key_weight, value_weight),
        qkv_other,
        tokens[0],
        attention_gain[None],
        grad_mixed,
        dense_gain_part,
        normed_all,
        output_mine,
        output_there,
    )
    input_grad, out_sum, gate_there, up_a_there, up_b_there, down_there = together(
        input_grad, out_sum, gate_there, up_a_there, up_b_there, down_there
    )
    (
        gate_total, up_total, down_total, query_total, key_total, value_total, layer_out, input_grad, output_total
    ) = last_sums(
        (gate_low, up_a, up_b, down_low),
        (gate_there, up_a_there, up_b_there, down_there),
        qkv_packs,
        mixed,
        out_sum,
        input_grad,
        output_packs,
    )
    return (
        layer_out[None],
        input_grad[None],
        gain_totals[0],
        query_total,
        key_total,
        value_total,
        output_total,
        gain_totals[1],
        gate_total,
        up_total,
        down_total,
    )


def solution(mesh):
    return jax.shard_map(
        body,
        mesh=mesh,
        in_specs=(
            P("rep", "dp", None),
            P(),
            P("dp", None),
            P("dp", None),
            P("dp", None),
            P("dp", None),
            P(),
            P("dp", None),
            P("dp", None),
            P("dp", None),
            P("rep", None),
            P("rep", None),
            P("rep", "dp", None),
        ),
        out_specs=(
            P("rep", "dp", None),
            P("rep", "dp", None),
            P(),
            P("dp", None),
            P("dp", None),
            P("dp", None),
            P("dp", None),
            P(),
            P("dp", None),
            P("dp", None),
            P("dp", None),
        ),
        check_vma=False,
    )
```

```python
import functools
import math

import jax
import jax.numpy as jnp
from jax import lax
from jax.experimental import pallas as pl
from jax.experimental.pallas import tpu as pltpu
from jax.sharding import PartitionSpec as P

HEAD_DIM = 64
HALF = HEAD_DIM // 2
BLOCK = 128
CHUNK = 512
FF_TILE = 256
STRIPE = 128
EPSILON = 1e-05
ROPE_BASE = 130000.0
MASKED_SCORE = -1e30
MESH = pl.DeviceIdType.MESH
MIB = 2**20
LOW = jnp.bfloat16
F32 = jnp.float32


def dot_nn(a, b):
    return lax.dot_general(a, b, (((1,), (0,)), ((), ())), preferred_element_type=F32)


def dot_nt(a, b):
    return lax.dot_general(a, b, (((1,), (1,)), ((), ())), preferred_element_type=F32)


def dot_tn(a, b):
    return lax.dot_general(a, b, (((0,), (0,)), ((), ())), preferred_element_type=F32)


def grid_of(chips):
    depth = 4 if chips % 8 == 0 else 2
    return depth, chips // depth


def chip_at(place, chips):
    depth, width = grid_of(chips)
    place = lax.rem(place + chips, chips)
    later = place - depth
    row, column = later // (width - 1), later % (width - 1)
    odd = row % 2
    far = (depth - 1 - row) * width + 1 + column + odd * (width - 2 - 2 * column)
    return jnp.where(place < depth, place * width, far)


def place_of(chip, chips):
    depth, width = grid_of(chips)
    z, x = chip // width, chip % width
    row = depth - 1 - z
    odd = row % 2
    column = x - 1 + odd * (width - 2 * x)
    return jnp.where(x == 0, z, depth + row * (width - 1) + column)


def ring_order(chips):
    depth, width = grid_of(chips)
    order = [z * width for z in range(depth)]
    for row in range(depth):
        columns = list(range(1, width))
        order += [(depth - 1 - row) * width + x for x in (columns[::-1] if row % 2 else columns)]
    return order


class Ring:
    def __init__(self):
        self.chips = lax.axis_size("dp") // 2
        me = lax.axis_index("dp")
        self.core = me % 2
        self.chip = me // 2
        self.partner = self.chip * 2 + 1 - self.core
        self.place = place_of(self.chip, self.chips)
        self.next = (self.device(1), self.device(-1))
        self.back = (self.next[1], self.next[0])

    def chip_far(self, steps):
        return chip_at(self.place + steps, self.chips)

    def device(self, steps):
        return self.chip_far(steps) * 2 + self.core

    def greet(self, others):
        barrier = pltpu.get_barrier_semaphore()
        for other in others:
            pl.semaphore_signal(barrier, inc=1, device_id={"dp": other}, device_id_type=MESH)
        pl.semaphore_wait(barrier, len(others))


def remote(src, dst, send_sem, recv_sem, device):
    return pltpu.make_async_remote_copy(
        src_ref=src,
        dst_ref=dst,
        send_sem=send_sem,
        recv_sem=recv_sem,
        device_id={"dp": device},
        device_id_type=MESH,
    )


def half_rows(direction, rows):
    return pl.ds(direction * (rows // 2), rows // 2)


def turned(u):
    parts = []
    for at in range(0, u.shape[1], HEAD_DIM):
        parts += [-u[:, at + HALF : at + HEAD_DIM], u[:, at : at + HALF]]
    return jnp.concatenate(parts, 1)


def gather_project_kernel(
    tokens_in, gain, query_w, key_w, value_w, output_w, cos_t, sin_t, qkv, gathered, output_all,
    tokens, own_weights, normed, partner_weights, x_buf, staged,
    in_sem, ag_send, ag_recv, w_send, w_recv, q_send, q_recv, local_sem,
    o_send, o_recv, pair_send, pair_recv, rep_send, rep_recv, far_send, far_recv,
):
    ring = Ring()
    n = ring.chips
    packs, pack = lax.axis_size("rep"), lax.axis_index("rep")
    rows = normed.shape[0]
    half = rows // 2
    r = qkv.shape[2]
    sources = (query_w, key_w, value_w)
    load_tokens = pltpu.make_async_copy(tokens_in, tokens, in_sem.at[3])
    load_tokens.start()
    load_weights = [
        pltpu.make_async_copy(source, own_weights.at[i], in_sem.at[i]) for i, source in enumerate(sources)
    ]
    for load in load_weights:
        load.start()
    barrier = pltpu.get_barrier_semaphore()
    for k in range(1, packs):
        pl.semaphore_signal(
            barrier, inc=1, device_id={"rep": lax.rem(pack + k, packs)}, device_id_type=MESH
        )
    for other in (ring.next[0], ring.next[1], ring.partner):
        pl.semaphore_signal(barrier, inc=1, device_id={"dp": other}, device_id_type=MESH)
    pl.semaphore_wait(barrier, 3 + packs - 1)

    load_tokens.wait()

    def normalize(i, carry):
        span = pl.ds(pl.multiple_of(i * 32, 32), 32)
        value = tokens[span, :].astype(F32)
        scale = lax.rsqrt(jnp.mean(value * value, axis=1, keepdims=True) + EPSILON)
        normed[span, :] = (value * scale * gain[...]).astype(LOW)
        return carry

    lax.fori_loop(0, rows // 32, normalize, 0)

    def hop(t, d):
        chip = ring.chip_far((1 - t) if d == 0 else (t - 1))
        return chip, half_rows(d, rows)

    def send(t, d, first):
        chip, part = hop(t, d)
        src = normed.at[part] if first else gathered.at[chip, part]
        return remote(src, gathered.at[chip, part], ag_send.at[d, t - 1], ag_recv.at[d, t - 1], ring.next[d])

    out_rows, features = output_w.shape
    share = out_rows // packs
    spot = ring.place * 2 + ring.core

    def share_of(q, d):
        return pl.ds(pl.multiple_of(q * share, share), share), pl.ds(d * (features // 2), features // 2)

    def block_at(t, d, q, core):
        place = lax.rem(ring.place + (n - t if d == 0 else t), n)
        at_rows, columns = share_of(q, d)
        return output_all.at[place * 2 + core, at_rows, columns]

    def o_copy(t, d, first):
        at_rows, columns = share_of(pack, d)
        src = output_w.at[at_rows, columns] if first else block_at(t - 1, d, pack, ring.core)
        return remote(
            src, block_at(t - 1, d, pack, ring.core), o_send.at[d, t], o_recv.at[d, t], ring.next[d]
        )

    def pair_copy(t, d):
        block = block_at(t, d, pack, ring.core)
        return remote(block, block, pair_send.at[d, t], pair_recv.at[d, t], ring.partner)

    def rep_copy(t, d, k):
        block = block_at(t, d, pack, ring.core)
        return pltpu.make_async_remote_copy(
            src_ref=block,
            dst_ref=block,
            send_sem=rep_send.at[k - 1, d, t],
            recv_sem=rep_recv.at[k - 1, d, t],
            device_id={"rep": lax.rem(pack + k, packs)},
            device_id_type=MESH,
        )

    def far_copy(t, d, k):
        block = block_at(t, d, lax.rem(pack + packs - k, packs), ring.core)
        return remote(block, block, far_send.at[k - 1, d, t], far_recv.at[k - 1, d, t], ring.partner)

    def forward_far(t):
        for d in (0, 1):
            for k in range(1, packs):
                rep_copy(t, d, k).wait_recv()
                far_copy(t, d, k).start()

    for d in (0, 1):
        send(1, d, True).start()
    for d in (0, 1):
        o_copy(1, d, True).start()
    own_rows = remote(output_w, output_all.at[spot], local_sem.at[3], local_sem.at[4], ring.partner)
    own_rows.start()
    own_keep = pltpu.make_async_copy(output_w, output_all.at[spot], local_sem.at[5])
    own_keep.start()
    swaps = [
        remote(sources[i], partner_weights.at[i], w_send.at[i], w_recv.at[i], ring.partner)
        for i in range(3)
    ]
    for swap in swaps:
        swap.start()
    keep = pltpu.make_async_copy(normed, gathered.at[ring.chip], local_sem.at[2])
    keep.start()

    def project_block(t, from_input):
        x = normed[...] if from_input else x_buf[...]
        places = [ring.chip_far(-t), ring.chip_far(t)]
        starts = [
            pl.multiple_of((places[d] * 2 + ring.core) * rows + d * half, half) for d in (0, 1)
        ]

        def table(source):
            wide = [source[:, pl.ds(starts[d], half)] for d in (0, 1)]
            return jnp.concatenate(
                [jnp.concatenate([w] * (r // HALF), 0).T for w in wide], 0
            )

        cos, sin = table(cos_t), table(sin_t)

        def heads(w):
            query, key, value = [dot_nt(x, w[i][...]) for i in range(3)]
            return (
                (query * cos + turned(query) * sin).astype(LOW),
                (key * cos + turned(key) * sin).astype(LOW),
                value.astype(LOW),
            )

        for i, value in enumerate(heads([own_weights.at[i] for i in range(3)])):
            for d in (0, 1):
                qkv[i, pl.ds(starts[d], half), :] = value[d * half : (d + 1) * half]
        if from_input:
            for swap in swaps:
                swap.wait()
        for i, value in enumerate(heads([partner_weights.at[i] for i in range(3)])):
            staged[t, i] = value
        for d in (0, 1):
            remote(
                staged.at[t, :, half_rows(d, rows)],
                qkv.at[:, pl.ds(starts[d], half)],
                q_send.at[d, t],
                q_recv.at[d, t],
                ring.partner,
            ).start()

    for load in load_weights:
        load.wait()
    project_block(0, True)

    def step(t, carry):
        for d in (0, 1):
            send(t, d, False).wait_recv()

        @pl.when(t < n - 1)
        def _():
            for d in (0, 1):
                send(t + 1, d, False).start()

        for d in (0, 1):
            o_copy(t, d, False).wait_recv()

        @pl.when(t < n - 1)
        def _():
            for d in (0, 1):
                o_copy(t + 1, d, False).start()

        for d in (0, 1):
            for k in range(1, packs):
                rep_copy(t, d, k).start()
            pair_copy(t, d).start()

        @pl.when(t > 1)
        def _():
            forward_far(t - 1)

        loads = []
        for d in (0, 1):
            chip, part = hop(t + 1, d)
            loads.append(pltpu.make_async_copy(gathered.at[chip, part], x_buf.at[part], local_sem.at[d]))
        for load in loads:
            load.start()
        for load in loads:
            load.wait()
        project_block(t, False)
        return carry

    lax.fori_loop(1, n, step, 0)
    forward_far(n - 1)

    def finish(t, carry):
        for d in (0, 1):
            send(t, d, False).wait_send()
            o_copy(t, d, False).wait_send()
            pair_copy(t, d).wait()
            for k in range(1, packs):
                rep_copy(t, d, k).wait_send()
                far_copy(t, d, k).wait()
        return carry

    lax.fori_loop(1, n, finish, 0)
    own_rows.wait()
    own_keep.wait()

    def finish_heads(t, carry):
        for d in (0, 1):
            done = remote(
                staged.at[t, :, half_rows(d, rows)],
                qkv.at[:, half_rows(d, rows)],
                q_send.at[d, t],
                q_recv.at[d, t],
                ring.partner,
            )
            done.wait_send()
            done.wait_recv()
        return carry

    lax.fori_loop(0, n, finish_heads, 0)
    keep.wait()


def gather_project(tokens, gain, weights, output_weight, cos_t, sin_t):
    rows, features = tokens.shape
    r = weights[0].shape[0]
    devices = lax.axis_size("dp")
    packs = lax.axis_size("rep")
    n = devices // 2
    vmem = pl.BlockSpec(memory_space=pltpu.VMEM)
    dma = pltpu.SemaphoreType.DMA
    hbm = pl.BlockSpec(memory_space=pl.ANY)
    return pl.pallas_call(
        gather_project_kernel,
        out_shape=(
            jax.ShapeDtypeStruct((3, devices * rows, r), LOW),
            jax.ShapeDtypeStruct((n, rows, features), LOW),
            jax.ShapeDtypeStruct((devices,) + output_weight.shape, LOW),
        ),
        in_specs=[hbm, vmem] + [hbm] * 4 + [vmem] * 2,
        out_specs=(vmem, pl.BlockSpec(memory_space=pl.ANY), pl.BlockSpec(memory_space=pl.ANY)),
        scratch_shapes=[
            pltpu.VMEM((rows, features), LOW),
            pltpu.VMEM((3, r, features), LOW),
            pltpu.VMEM((rows, features), LOW),
            pltpu.VMEM((3, r, features), LOW),
            pltpu.VMEM((rows, features), LOW),
            pltpu.VMEM((n, 3, rows, r), LOW),
            dma((4,)),
            dma((2, n)), dma((2, n)), dma((3,)), dma((3,)), dma((2, n)), dma((2, n)), dma((6,)),
            dma((2, n)), dma((2, n)), dma((2, n)), dma((2, n)),
            dma((packs - 1, 2, n)), dma((packs - 1, 2, n)),
            dma((packs - 1, 2, n)), dma((packs - 1, 2, n)),
        ],
        compiler_params=pltpu.CompilerParams(
            collective_id=1, has_side_effects=True, vmem_limit_bytes=60 * MIB
        ),
        cost_estimate=pl.CostEstimate(
            flops=4 * n * rows * features * 3 * r, bytes_accessed=320 * MIB, transcendentals=0
        ),
        name="gather_project",
    )(tokens, gain, *weights, output_weight, cos_t, sin_t)


def split_heads(u):
    heads = u.shape[1] // HEAD_DIM
    if heads == 1:
        return u
    lane = lax.broadcasted_iota(jnp.int32, u.shape, 1) // HEAD_DIM
    zero = jnp.zeros_like(u)
    return jnp.concatenate([jnp.where(lane == h, u, zero) for h in range(heads)], 0)


def join_heads(u):
    heads = u.shape[0] // HEAD_DIM
    return jnp.concatenate(
        [u[h * HEAD_DIM : (h + 1) * HEAD_DIM, h * BLOCK : (h + 1) * BLOCK] for h in range(heads)], 0
    )


def transpose_blocks(source, target):
    def one(b, carry):
        at = pl.multiple_of(b * BLOCK, BLOCK)
        target[:, pl.ds(at, BLOCK)] = source[pl.ds(at, BLOCK), :].astype(F32).T.astype(LOW)
        return carry

    lax.fori_loop(0, source.shape[0] // BLOCK, one, 0)


def window_of(b, first, tail, columns):
    start = pl.multiple_of(jnp.maximum(b - (CHUNK // BLOCK - 1), 0) * BLOCK, BLOCK)
    whole = (b - first) // (CHUNK // BLOCK)
    lowest = (first + whole * (CHUNK // BLOCK)) * BLOCK
    key_index = start + lax.broadcasted_iota(jnp.int32, (CHUNK, columns), 0)
    query_index = b * BLOCK + lax.broadcasted_iota(jnp.int32, (CHUNK, columns), 1) % BLOCK
    allowed = (
        (key_index >= lowest)
        & (key_index <= query_index)
        & (key_index < b * BLOCK + tail)
    )
    return start, whole, allowed


def walk_rows(b, tok_dev, chips):
    device = b * BLOCK // tok_dev
    spot = place_of(device // 2, chips) * 2 + device % 2
    return pl.ds(pl.multiple_of(spot * tok_dev + b * BLOCK % tok_dev, BLOCK), BLOCK)


def attend_kernel(chips, first_ref, tail_ref, qkv, attended, log_total, value_t):
    tokens, r = qkv.shape[1:]
    tok_dev = tokens // (2 * chips)
    columns = (r // HEAD_DIM) * BLOCK
    scale = 1.0 / math.sqrt(HEAD_DIM)
    transpose_blocks(qkv.at[2], value_t)

    def block(b, carry):
        at = pl.multiple_of(b * BLOCK, BLOCK)
        query = split_heads(qkv[0, pl.ds(at, BLOCK), :])
        start, whole, allowed = window_of(b, first_ref[b], tail_ref[b], columns)
        scores = dot_nt(qkv[1, pl.ds(start, CHUNK), :], query) * scale
        scores = jnp.where(allowed, scores, MASKED_SCORE)
        top = jnp.max(scores, axis=0, keepdims=True)
        weights = jnp.exp(scores - top)
        total = jnp.sum(weights, axis=0, keepdims=True)
        out = dot_nn(value_t[:, pl.ds(start, CHUNK)], weights.astype(LOW))

        def more(i, state):
            top, total, out = state
            start = pl.multiple_of(first_ref[b] * BLOCK + i * CHUNK, BLOCK)
            scores = dot_nt(qkv[1, pl.ds(start, CHUNK), :], query) * scale
            higher = jnp.maximum(top, jnp.max(scores, axis=0, keepdims=True))
            shrink = jnp.exp(top - higher)
            weights = jnp.exp(scores - higher)
            total = total * shrink + jnp.sum(weights, axis=0, keepdims=True)
            out = out * shrink + dot_nn(value_t[:, pl.ds(start, CHUNK)], weights.astype(LOW))
            return higher, total, out

        top, total, out = lax.fori_loop(0, whole, more, (top, total, out))
        log_total[pl.ds(b, 1), :] = top + jnp.log(total)
        attended[walk_rows(b, tok_dev, chips), :] = join_heads(out / total).T.astype(LOW)
        return carry

    lax.fori_loop(0, tokens // BLOCK, block, 0)


def attend(first, tail, qkv):
    tokens, r = qkv.shape[1:]
    smem = pl.BlockSpec(memory_space=pltpu.SMEM)
    vmem = pl.BlockSpec(memory_space=pltpu.VMEM)
    return pl.pallas_call(
        functools.partial(attend_kernel, lax.axis_size("dp") // 2),
        out_shape=(
            jax.ShapeDtypeStruct((tokens, r), LOW),
            jax.ShapeDtypeStruct((tokens // BLOCK, (r // HEAD_DIM) * BLOCK), F32),
        ),
        in_specs=[smem, smem, vmem],
        out_specs=(vmem, vmem),
        scratch_shapes=[pltpu.VMEM((r, tokens), LOW)],
        compiler_params=pltpu.CompilerParams(vmem_limit_bytes=40 * MIB),
        cost_estimate=pl.CostEstimate(
            flops=4 * tokens * 1024 * r * 8, bytes_accessed=120 * MIB, transcendentals=tokens * 1024
        ),
        name="attend",
    )(first, tail, qkv)


def unrotate(g, cos, sin):
    parts = []
    for h in range(g.shape[0] // HEAD_DIM):
        one = g[h * HEAD_DIM : h * HEAD_DIM + HALF]
        two = g[h * HEAD_DIM + HALF : (h + 1) * HEAD_DIM]
        parts += [one * cos + two * sin, two * cos - one * sin]
    return jnp.concatenate(parts, 0)


def attend_back_kernel(
    chips, first_ref, tail_ref, qkv, grad_out, attended, log_total, cos_t, sin_t, grads,
    key_t, grad_key, grad_value, staged, store_sem,
):
    tokens, r = qkv.shape[1:]
    tok_dev = tokens // (2 * chips)
    heads = r // HEAD_DIM
    columns = heads * BLOCK
    scale = 1.0 / math.sqrt(HEAD_DIM)
    transpose_blocks(qkv.at[1], key_t)
    grad_key[...] = jnp.zeros_like(grad_key)
    grad_value[...] = jnp.zeros_like(grad_value)

    def block(b, carry):
        at = pl.multiple_of(b * BLOCK, BLOCK)
        here = pl.ds(at, BLOCK)
        query = split_heads(qkv[0, here, :])
        walk = walk_rows(b, tok_dev, chips)
        grad_rows = grad_out[walk, :]
        grad = split_heads(grad_rows)
        product = (grad_rows.astype(F32) * attended[walk, :].astype(F32)).T
        delta = jnp.concatenate(
            [
                jnp.sum(product[h * HEAD_DIM : (h + 1) * HEAD_DIM], axis=0, keepdims=True)
                for h in range(heads)
            ],
            1,
        )
        log_row = log_total[pl.ds(b, 1), :]

        def chunk(start, allowed, grad_query):
            span = pl.ds(start, CHUNK)
            scores = dot_nt(qkv[1, span, :], query) * scale
            weights = jnp.exp(scores - log_row)
            if allowed is not None:
                weights = jnp.where(allowed, weights, 0.0)
            grad_weights = dot_nt(qkv[2, span, :], grad)
            grad_scores = (weights * (grad_weights - delta)).astype(LOW)
            grad_value[span, :] += dot_nn(weights.astype(LOW), grad)
            grad_key[span, :] += dot_nn(grad_scores, query)
            return grad_query + dot_nn(key_t[:, span], grad_scores)

        start, whole, allowed = window_of(b, first_ref[b], tail_ref[b], columns)
        grad_query = chunk(start, allowed, jnp.zeros((r, columns), F32))
        grad_query = lax.fori_loop(
            0,
            whole,
            lambda i, g: chunk(pl.multiple_of(first_ref[b] * BLOCK + i * CHUNK, BLOCK), None, g),
            grad_query,
        )
        turned = unrotate(join_heads(grad_query) * scale, cos_t[:, here], sin_t[:, here])
        staged[0, here, :] = turned.T.astype(LOW)
        return carry

    lax.fori_loop(0, tokens // BLOCK, block, 0)
    query_store = pltpu.make_async_copy(staged.at[0], grads.at[0], store_sem.at[0])
    query_store.start()

    def close(b, carry):
        here = pl.ds(pl.multiple_of(b * BLOCK, BLOCK), BLOCK)
        turned = unrotate(grad_key[here, :].T * scale, cos_t[:, here], sin_t[:, here])
        staged[1, here, :] = turned.T.astype(LOW)
        staged[2, here, :] = grad_value[here, :].astype(LOW)
        return carry

    lax.fori_loop(0, tokens // BLOCK, close, 0)
    rest_store = pltpu.make_async_copy(staged.at[pl.ds(1, 2)], grads.at[pl.ds(1, 2)], store_sem.at[1])
    rest_store.start()
    query_store.wait()
    rest_store.wait()


def attend_back(first, tail, qkv, grad_out, attended, log_total, cos_t, sin_t):
    tokens, r = qkv.shape[1:]
    smem = pl.BlockSpec(memory_space=pltpu.SMEM)
    vmem = pl.BlockSpec(memory_space=pltpu.VMEM)
    return pl.pallas_call(
        functools.partial(attend_back_kernel, lax.axis_size("dp") // 2),
        out_shape=jax.ShapeDtypeStruct((3, tokens, r), LOW),
        in_specs=[smem, smem] + [vmem] * 6,
        out_specs=pl.BlockSpec(memory_space=pl.ANY),
        scratch_shapes=[
            pltpu.VMEM((r, tokens), LOW),
            pltpu.VMEM((tokens, r), F32),
            pltpu.VMEM((tokens, r), F32),
            pltpu.VMEM((3, tokens, r), LOW),
            pltpu.SemaphoreType.DMA((2,)),
        ],
        compiler_params=pltpu.CompilerParams(vmem_limit_bytes=40 * MIB),
        cost_estimate=pl.CostEstimate(
            flops=10 * tokens * 1024 * r * 8, bytes_accessed=240 * MIB, transcendentals=tokens * 1024
        ),
        name="attend_back",
    )(first, tail, qkv, grad_out, attended, log_total, cos_t, sin_t)


def mixed_kernel(
    attended, tokens_in, gain, output_all, mixed, normed, blocks,
    tokens, weights, sem, w_sem, send_sem, recv_sem,
):
    ring = Ring()
    n = ring.chips
    devices = 2 * n
    rows, features = mixed.shape
    r = attended.shape[1]
    spot = ring.place * 2 + ring.core
    load = pltpu.make_async_copy(tokens_in, tokens, sem)
    load.start()

    def place_at(j):
        return lax.rem(ring.place + (j % 2) * ((j + 1) // 2) + (1 - j % 2) * (n - j // 2), n)

    def chip_weights(j):
        place = place_at(j)
        return pltpu.make_async_copy(
            output_all.at[pl.ds(place * 2, 2)], weights.at[pl.ds(place * 2, 2)], w_sem.at[j]
        )

    def fetch(j, carry):
        chip_weights(j).start()
        return carry

    lax.fori_loop(0, n, fetch, 0)
    barrier = pltpu.get_barrier_semaphore()

    def to(k):
        other = lax.rem(spot + k, devices)
        return chip_at(other // 2, n) * 2 + other % 2

    def greet(k, carry):
        pl.semaphore_signal(barrier, inc=1, device_id={"dp": to(k)}, device_id_type=MESH)
        return carry

    lax.fori_loop(1, devices, greet, 0)
    pl.semaphore_wait(barrier, devices - 1)

    def rows_of(at):
        return pl.ds(pl.multiple_of(at * rows, rows), rows)

    def copy(k):
        return remote(
            attended.at[rows_of(lax.rem(spot + k, devices))],
            blocks.at[spot],
            send_sem.at[k],
            recv_sem.at[k],
            to(k),
        )

    def begin(k, carry):
        copy(k).start()
        return carry

    lax.fori_loop(1, devices, begin, 0)
    blocks[spot] = attended[rows_of(spot), :]
    load.wait()
    mixed[...] = tokens[...].astype(F32)

    def add(j, carry):
        chip_weights(j).wait()
        place = place_at(j)
        for core in (0, 1):
            k = lax.rem(spot + devices - place * 2 - core, devices)

            @pl.when(k > 0)
            def _():
                copy(k).wait_recv()

        both = jnp.concatenate([blocks[place * 2 + core] for core in (0, 1)], 1)
        mixed[...] += dot_nn(both, weights[pl.ds(place * 2, 2)].reshape(2 * r, features))
        return carry

    lax.fori_loop(0, n, add, 0)

    def normalize(i, carry):
        span = pl.ds(pl.multiple_of(i * 32, 32), 32)
        value = mixed[span, :]
        scale = lax.rsqrt(jnp.mean(value * value, axis=1, keepdims=True) + EPSILON)
        normed[span, :] = (value * scale * gain[...]).astype(LOW)
        return carry

    lax.fori_loop(0, rows // 32, normalize, 0)

    def finish(k, carry):
        copy(k).wait_send()
        return carry

    lax.fori_loop(1, devices, finish, 0)


def mix(attended, tokens, gain, output_all):
    rows, features = tokens.shape
    devices, r = output_all.shape[:2]
    vmem = pl.BlockSpec(memory_space=pltpu.VMEM)
    hbm = pl.BlockSpec(memory_space=pl.ANY)
    dma = pltpu.SemaphoreType.DMA
    return pl.pallas_call(
        mixed_kernel,
        out_shape=(
            jax.ShapeDtypeStruct((rows, features), F32),
            jax.ShapeDtypeStruct((rows, features), LOW),
            jax.ShapeDtypeStruct((devices, rows, r), LOW),
        ),
        in_specs=[vmem, hbm, vmem, hbm],
        out_specs=(vmem,) * 3,
        scratch_shapes=[
            pltpu.VMEM((rows, features), LOW),
            pltpu.VMEM((devices, r, features), LOW),
            dma, dma((devices // 2,)), dma((devices,)), dma((devices,)),
        ],
        compiler_params=pltpu.CompilerParams(
            collective_id=5, has_side_effects=True, vmem_limit_bytes=56 * MIB
        ),
        cost_estimate=pl.CostEstimate(
            flops=2 * rows * features * features, bytes_accessed=100 * MIB, transcendentals=0
        ),
        name="mix",
    )(attended, tokens, gain, output_all)


def dense_kernel(
    normed, cotangents, gate_w, up_w, down_w, gate_p, up_p, down_p,
    grad_sum, out_parts, gathered, gate_grad, up_a, up_b, down_grad,
    weights, totals, x_buf, g_buf, out_acc, grad_acc, sent, landed, cast_buf, pair_land,
    ag_send, ag_recv, rs_send, rs_recv, credit, local_sem, w_sem, cast_sem, pair_send, pair_recv,
):
    ring = Ring()
    n = ring.chips
    rows, features = normed.shape
    half = rows // 2
    own = gate_w.shape[0]
    tiles = 2 * own // FF_TILE
    loads = []
    for i, (mine, theirs) in enumerate(((gate_w, gate_p), (up_w, up_p), (down_w, down_p))):
        loads.append(pltpu.make_async_copy(mine, weights.at[i, pl.ds(0, own)], w_sem.at[2 * i]))
        loads.append(pltpu.make_async_copy(theirs, weights.at[i, pl.ds(own, own)], w_sem.at[2 * i + 1]))
    for load in loads:
        load.start()
    ring.greet((ring.next[0], ring.next[1], ring.partner))

    def source(t, d):
        return lax.rem(ring.place + (n - t if d == 0 else t), n)

    def send(t, d, first):
        place, part = source(t - 1, d), half_rows(d, rows)
        src = normed.at[part] if first else gathered.at[place, part]
        return remote(src, gathered.at[place, part], ag_send.at[d, t - 1], ag_recv.at[d, t - 1], ring.next[d])

    def reduce_copy(t, d):
        return remote(sent.at[d], landed.at[d, t % 2], rs_send.at[d], rs_recv.at[d, t % 2], ring.next[d])

    for d in (0, 1):
        send(1, d, True).start()

    def clear(i, carry):
        span = pl.ds(pl.multiple_of(i * FF_TILE, FF_TILE), FF_TILE)
        for k in range(3):
            totals[k, span, :] = jnp.zeros((FF_TILE, features), F32)
        return carry

    lax.fori_loop(0, tiles, clear, 0)
    for load in loads:
        load.wait()

    def out_copy(t, d):
        part = half_rows(d, rows)
        return pltpu.make_async_copy(
            cast_buf.at[t % 2, part], out_parts.at[source(t, d), part], cast_sem.at[t % 2, d]
        )

    def pass_on(t):
        for d in (0, 1):
            send(t, d, False).wait_recv()

        @pl.when(t < n - 1)
        def _():
            for d in (0, 1):
                send(t + 1, d, False).start()

    def step(t, carry):
        copies = []
        for d in (0, 1):
            part = half_rows(d, rows)
            copies.append(
                pltpu.make_async_copy(cotangents.at[source(t, d), part], g_buf.at[part], local_sem.at[d])
            )
        for copy in copies:
            copy.start()

        @pl.when(t > 1)
        def _():
            pass_on(t)

        @pl.when(t > 0)
        def _():
            more = []
            for d in (0, 1):
                part = half_rows(d, rows)
                more.append(
                    pltpu.make_async_copy(gathered.at[source(t, d), part], x_buf.at[part], local_sem.at[2 + d])
                )
                more[-1].start()
            for copy in more:
                copy.wait()

        @pl.when(t == 0)
        def _():
            x_buf[...] = normed[...]

        for copy in copies:
            copy.wait()

        out_acc[...] = jnp.zeros_like(out_acc)
        grad_acc[...] = jnp.zeros_like(grad_acc)

        def tile(i, carry):
            @pl.when((t == 0) & (i == tiles - 1))
            def _():
                pass_on(1)

            span = pl.ds(pl.multiple_of(i * FF_TILE, FF_TILE), FF_TILE)
            x = x_buf[...]
            g = g_buf[...]
            gate = dot_nt(x, weights[0, span, :])
            up = dot_nt(x, weights[1, span, :])
            grad_hidden = dot_nt(g, weights[2, span, :])
            sigma = 1.0 / (1.0 + jnp.exp(-gate))
            silu = gate * sigma
            hidden = (silu * up).astype(LOW)
            grad_gate = (grad_hidden * up * sigma * (1.0 + gate * (1.0 - sigma))).astype(LOW)
            grad_up = (grad_hidden * silu).astype(LOW)
            out_acc[...] += dot_nn(hidden, weights[2, span, :])
            grad_acc[...] += dot_nn(grad_gate, weights[0, span, :])
            grad_acc[...] += dot_nn(grad_up, weights[1, span, :])
            totals[0, span, :] += dot_tn(grad_gate, x)
            totals[1, span, :] += dot_tn(grad_up, x)
            totals[2, span, :] += dot_tn(hidden, g)
            return carry

        lax.fori_loop(0, tiles, tile, 0)

        @pl.when(t >= 2)
        def _():
            for d in (0, 1):
                out_copy(t - 2, d).wait()

        cast_buf[t % 2] = out_acc[...].astype(LOW)
        for d in (0, 1):
            out_copy(t, d).start()

        @pl.when(t == 0)
        def _():
            grad_sum[...] = grad_acc[...]

        @pl.when(t > 0)
        def _():
            for d in (0, 1):
                part = pl.ds(d * half, half)

                @pl.when(t >= 2)
                def _():
                    reduce_copy(t - 1, d).wait_recv()
                    grad_acc[part, :] += landed[d, (t - 1) % 2].astype(F32)

                    @pl.when(t <= n - 2)
                    def _():
                        pl.semaphore_signal(
                            credit.at[d], inc=1, device_id={"dp": ring.back[d]}, device_id_type=MESH
                        )

                    reduce_copy(t - 1, d).wait_send()

                sent[d] = grad_acc[part, :].astype(LOW)

                @pl.when(t >= 3)
                def _():
                    pl.semaphore_wait(credit.at[d], 1)

                reduce_copy(t, d).start()

        return carry

    lax.fori_loop(0, n, step, 0)
    for t in (n - 2, n - 1):
        for d in (0, 1):
            out_copy(t, d).wait()

    own_tiles = 3 * own // FF_TILE

    def tile_of(i, first):
        return i // (own // FF_TILE), pl.ds(
            pl.multiple_of(first + (i % (own // FF_TILE)) * FF_TILE, FF_TILE), FF_TILE
        )

    def pair_copy(i):
        return remote(cast_buf.at[i % 2], pair_land.at[i], pair_send.at[i % 2], pair_recv.at[i], ring.partner)

    def give(i, carry):
        @pl.when(i >= 2)
        def _():
            pair_copy(i - 2).wait_send()

        k, span = tile_of(i, own)
        cast_buf[i % 2] = totals[k, span, :].astype(LOW)
        pair_copy(i).start()
        return carry

    lax.fori_loop(0, own_tiles, give, 0)
    for i in (own_tiles - 2, own_tiles - 1):
        pair_copy(i).wait_send()

    def total_copies(i):
        matrix, low = i // (own // FF_TILE), (i % (own // FF_TILE)) * FF_TILE
        if matrix != 1:
            target = (gate_grad, None, down_grad)[matrix].at[pl.ds(low, FF_TILE)]
            return [pltpu.make_async_copy(cast_buf.at[i % 2], target, cast_sem.at[i % 2, 0])]
        copies = []
        for j in range(FF_TILE // STRIPE):
            for target, first, count in ((up_a, 0, STRIPE // 4), (up_b, STRIPE // 4, 3 * STRIPE // 4)):
                copies.append(
                    pltpu.make_async_copy(
                        cast_buf.at[i % 2, pl.ds(j * STRIPE + first, count)],
                        target.at[pl.ds((low // STRIPE + j) * count, count)],
                        cast_sem.at[i % 2, len(copies)],
                    )
                )
        return copies

    for i in range(own_tiles):
        if i >= 2:
            for copy in total_copies(i - 2):
                copy.wait()
        pair_copy(i).wait_recv()
        k, span = tile_of(i, 0)
        cast_buf[i % 2] = (totals[k, span, :] + pair_land[i].astype(F32)).astype(LOW)
        for copy in total_copies(i):
            copy.start()

    for d in (0, 1):
        part = pl.ds(d * half, half)
        reduce_copy(n - 1, d).wait_recv()
        grad_sum[part, :] += landed[d, (n - 1) % 2].astype(F32)
        reduce_copy(n - 1, d).wait_send()

    for i in (own_tiles - 2, own_tiles - 1):
        for copy in total_copies(i):
            copy.wait()

    def finish(t, carry):
        for d in (0, 1):
            send(t, d, False).wait_send()
        return carry

    lax.fori_loop(1, n, finish, 0)


def dense(normed, cotangents, own_weights, partner_weights):
    rows, features = normed.shape
    n = lax.axis_size("dp") // 2
    own = own_weights[0].shape[0]
    half = rows // 2
    vmem = pl.BlockSpec(memory_space=pltpu.VMEM)
    hbm = pl.BlockSpec(memory_space=pl.ANY)
    dma = pltpu.SemaphoreType.DMA
    own_tiles = 3 * own // FF_TILE
    return pl.pallas_call(
        dense_kernel,
        out_shape=(
            jax.ShapeDtypeStruct((rows, features), F32),
            jax.ShapeDtypeStruct((n, rows, features), LOW),
            jax.ShapeDtypeStruct((n, rows, features), LOW),
            jax.ShapeDtypeStruct((own, features), LOW),
            jax.ShapeDtypeStruct((own // 4, features), LOW),
            jax.ShapeDtypeStruct((own - own // 4, features), LOW),
            jax.ShapeDtypeStruct((own, features), LOW),
        ),
        in_specs=[vmem] + [hbm] * 7,
        out_specs=(vmem,) + (hbm,) * 6,
        scratch_shapes=[
            pltpu.VMEM((3, 2 * own, features), LOW),
            pltpu.VMEM((3, 2 * own, features), F32),
            pltpu.VMEM((rows, features), LOW),
            pltpu.VMEM((rows, features), LOW),
            pltpu.VMEM((rows, features), F32),
            pltpu.VMEM((rows, features), F32),
            pltpu.VMEM((2, half, features), LOW),
            pltpu.VMEM((2, 2, half, features), LOW),
            pltpu.VMEM((2, FF_TILE, features), LOW),
            pltpu.VMEM((own_tiles, FF_TILE, features), LOW),
            dma((2, n)), dma((2, n)), dma((2,)), dma((2, 2)),
            pltpu.SemaphoreType.REGULAR((2,)),
            dma((4,)), dma((6,)), dma((2, 2 * FF_TILE // STRIPE)), dma((2,)), dma((own_tiles,)),
        ],
        compiler_params=pltpu.CompilerParams(
            collective_id=2, has_side_effects=True, vmem_limit_bytes=62 * MIB
        ),
        cost_estimate=pl.CostEstimate(
            flops=2 * 9 * n * rows * features * 2 * own, bytes_accessed=500 * MIB, transcendentals=0
        ),
        name="dense",
    )(normed, cotangents, *own_weights, *partner_weights)


def output_split(r, packs):
    plain = r // 4 if (r - r // 4) // packs % 16 == 0 else 0
    return (r - plain) // packs, plain


def mixed_back_kernel(
    packs, mixed_in, grad_in, cotangent_in, gain, output_all, blocks, grad_mixed, gain_part, grad_heads, *rest
):
    sums = rest[:packs]
    given, taken = rest[packs : 2 * packs], rest[2 * packs : 3 * packs]
    (
        mixed, grad_two, cotangent, low, weights, staged, product,
        sem, w_sem, send_sem, recv_sem, g_sem, t_sem,
    ) = rest[3 * packs :]
    ring = Ring()
    n = ring.chips
    devices = 2 * n
    rows, features = mixed.shape
    r = grad_heads.shape[1]
    pack = lax.axis_index("rep")
    spot = ring.place * 2 + ring.core
    loads = [
        pltpu.make_async_copy(src, dst, sem.at[i])
        for i, (src, dst) in enumerate(((mixed_in, mixed), (grad_in, grad_two), (cotangent_in, cotangent)))
    ]
    for load in loads:
        load.start()

    def chip_weights(k):
        at = lax.rem(ring.place + k, n) * 2
        return pltpu.make_async_copy(output_all.at[pl.ds(at, 2)], weights.at[pl.ds(2 * k, 2)], w_sem.at[k])

    def fetch(k, carry):
        chip_weights(k).start()
        return carry

    lax.fori_loop(0, n, fetch, 0)
    barrier = pltpu.get_barrier_semaphore()

    def to(k):
        other = lax.rem(spot + k, devices)
        return {"dp": chip_at(other // 2, n) * 2 + other % 2}

    def greet(k, carry):
        pl.semaphore_signal(barrier, inc=1, device_id=to(k), device_id_type=MESH)
        return carry

    lax.fori_loop(1, devices, greet, 0)
    pl.semaphore_wait(barrier, devices - 1)
    for load in loads:
        load.wait()
    gain_part[...] = jnp.zeros_like(gain_part)

    def norm_back(i, carry):
        span = pl.ds(pl.multiple_of(i * 16, 16), 16)
        value, grad = mixed[span, :], grad_two[span, :]
        scale = lax.rsqrt(jnp.mean(value * value, axis=1, keepdims=True) + EPSILON)
        scaled = grad * gain[...]
        shift = jnp.mean(value * scaled, axis=1, keepdims=True)
        total = cotangent[span, :].astype(F32) + scale * scaled - value * (scale * scale * scale * shift)
        grad_mixed[span, :] = total
        low[span, :] = total.astype(LOW)
        gain_part[...] += jnp.sum(grad * value * scale, axis=0, keepdims=True)
        return carry

    lax.fori_loop(0, rows // 16, norm_back, 0)

    def copy(k):
        return remote(
            staged.at[k],
            grad_heads.at[pl.ds(pl.multiple_of(spot * rows, rows), rows)],
            send_sem.at[k],
            recv_sem.at[k],
            to(k)["dp"],
        )

    def project(k, carry):
        chip_weights(k).wait()
        both = dot_nt(low[...], weights[pl.ds(2 * k, 2)].reshape(2 * r, features))
        for core in (0, 1):
            step = lax.rem(2 * k + core - ring.core + devices, devices)
            staged[step] = both[:, core * r : (core + 1) * r].astype(LOW)

            @pl.when(step > 0)
            def _():
                copy(step).start()

        return carry

    lax.fori_loop(0, n, project, 0)
    grad_heads[pl.ds(pl.multiple_of(spot * rows, rows), rows), :] = staged[0]

    def give(k):
        return remote(given[k], taken[k], g_sem.at[k], t_sem.at[k], ring.partner)

    share, plain = output_split(r, packs)

    def spots(k, place, first, count):
        width = share + plain if k == 0 else share
        return pl.ds(pl.multiple_of(place * width + first, 16), count)

    def products(place, core, use):
        product[...] = dot_tn(blocks[place * 2 + core], low[...])
        for k in range(packs):
            at = pl.multiple_of(lax.rem(pack + k, packs) * share, share)
            use(k, spots(k, place, 0, share), product[pl.ds(at, share), :])
        if plain:
            use(0, spots(0, place, share, plain), product[pl.ds(r - plain, plain), :])

    def put(k, at, value):
        given[k][at, :] = value.astype(LOW)

    def total(k, at, value):
        sums[k][at, :] = (value + taken[k][at, :].astype(F32)).astype(LOW)

    def for_partner(place, carry):
        products(place, 1 - ring.core, put)
        return carry

    def for_self(place, carry):
        products(place, ring.core, total)
        return carry

    lax.fori_loop(0, n, for_partner, 0)
    for k in range(packs):
        give(k).start()
    for k in range(packs):
        give(k).wait_recv()
    lax.fori_loop(0, n, for_self, 0)

    def finish(k, carry):
        copy(k).wait_send()
        copy(k).wait_recv()
        return carry

    lax.fori_loop(1, devices, finish, 0)
    for k in range(packs):
        give(k).wait_send()


def mixed_back(mixed, grad_two, cotangent, gain, output_all, blocks):
    rows, features = mixed.shape
    devices, r = output_all.shape[:2]
    packs = lax.axis_size("rep")
    n = devices // 2
    share, plain = output_split(r, packs)
    sizes = [n * (share + plain)] + [n * share] * (packs - 1)
    vmem = pl.BlockSpec(memory_space=pltpu.VMEM)
    hbm = pl.BlockSpec(memory_space=pl.ANY)
    dma = pltpu.SemaphoreType.DMA
    return pl.pallas_call(
        functools.partial(mixed_back_kernel, packs),
        out_shape=(
            jax.ShapeDtypeStruct((rows, features), F32),
            jax.ShapeDtypeStruct((1, features), F32),
            jax.ShapeDtypeStruct((devices * rows, r), LOW),
        )
        + tuple(jax.ShapeDtypeStruct((size, features), LOW) for size in sizes),
        in_specs=[hbm] * 3 + [vmem, hbm, vmem],
        out_specs=(vmem,) * (3 + packs),
        scratch_shapes=[pltpu.VMEM((size, features), LOW) for size in sizes + sizes]
        + [
            pltpu.VMEM((rows, features), F32),
            pltpu.VMEM((rows, features), F32),
            pltpu.VMEM((rows, features), LOW),
            pltpu.VMEM((rows, features), LOW),
            pltpu.VMEM((devices, r, features), LOW),
            pltpu.VMEM((devices, rows, r), LOW),
            pltpu.VMEM((r, features), F32),
            dma((3,)), dma((n,)), dma((devices,)), dma((devices,)), dma((packs,)), dma((packs,)),
        ],
        compiler_params=pltpu.CompilerParams(
            collective_id=4, has_side_effects=True, vmem_limit_bytes=56 * MIB
        ),
        cost_estimate=pl.CostEstimate(
            flops=4 * rows * features * features, bytes_accessed=130 * MIB, transcendentals=0
        ),
        name="mixed_back",
    )(mixed, grad_two, cotangent, gain, output_all, blocks)


def normed_back_kernel(
    packs, grads_in, query_w, key_w, value_w, partner_w, hidden_in, gain, grad_mixed, dense_gain_part, normed_all, output_mine, *rest
):
    output_there = rest[: packs - 1]
    (
        out, gains, rep_land, o_packs,
        grads, joined, partner_grads, sent, landed, x_buf, parts, pair_out, pair_land,
        o_sent, o_landed, far_part, far_land, near_part, near_land,
        in_sem, w_sem, p_send, p_recv, rs_send, rs_recv, credit, x_sem, pair_sem, rep_send, rep_recv,
        o_send, o_recv, o_credit, swap_send, swap_recv, near_send, near_recv, far_send, far_recv,
    ) = rest[packs - 1 :]
    ring = Ring()
    n = ring.chips
    rows, features = out.shape
    half = rows // 2
    r = grads.shape[2]
    share, plain = output_split(r, packs)
    pack = lax.axis_index("rep")
    mates = 2 * packs
    mate = pack * 2 + ring.core
    barrier = pltpu.get_barrier_semaphore()
    load_grads = pltpu.make_async_copy(grads_in, grads, in_sem)
    load_grads.start()
    load_weights = [
        pltpu.make_async_copy(src, joined.at[pl.ds(i * r, src.shape[0])], w_sem.at[i])
        for i, src in enumerate((query_w, key_w, value_w, partner_w))
    ]
    for load in load_weights:
        load.start()

    def near(k):
        to = lax.rem(mate + k, mates)
        return {"dp": ring.chip * 2 + to % 2, "rep": to // 2}

    def far(k):
        return {"dp": lax.rem(ring.chip + k, n) * 2 + ring.core}

    for k in range(1, mates):
        pl.semaphore_signal(barrier, inc=1, device_id=near(k), device_id_type=MESH)
    for k in range(1, n):
        pl.semaphore_signal(barrier, inc=1, device_id=far(k), device_id_type=MESH)
    pl.semaphore_wait(barrier, mates + n - 2)
    load_grads.wait()

    def place(t, d):
        return ring.chip_far(-t if d == 0 else t)

    def swap(t, d):
        start = (place(t, d) * 2 + 1 - ring.core) * rows + d * half
        return remote(
            grads.at[:, pl.ds(pl.multiple_of(start, half), half)],
            partner_grads.at[:, t % n, half_rows(d, rows)],
            p_send.at[d, t % n],
            p_recv.at[d, t % n],
            ring.partner,
        )

    def begin(t, carry):
        for d in (0, 1):
            swap(t, d).start()
        return carry

    lax.fori_loop(1, n + 1, begin, 0)

    def reduce_copy(t, d, u):
        return remote(
            sent.at[d, u, t % 2],
            landed.at[d, u, t % 2],
            rs_send.at[d, u, t % 2],
            rs_recv.at[d, u, t % 2],
            ring.next[d],
        )

    def output_copy(t, d):
        return remote(
            o_sent.at[d, t % 2],
            o_landed.at[d, t % 2],
            o_send.at[d, t % 2],
            o_recv.at[d, t % 2],
            ring.next[d],
        )

    def give_credit(sem, d):
        pl.semaphore_signal(sem, inc=1, device_id={"dp": ring.back[d]}, device_id_type=MESH)

    def mine(t, d):
        start = (place(t, d) * 2 + ring.core) * rows + d * half
        return pl.ds(pl.multiple_of(start, half), half)

    def load_rows(t, d):
        part = half_rows(d, rows)
        return pltpu.make_async_copy(normed_all.at[place(t, d), part], x_buf.at[t % 2, part], x_sem.at[t % 2, d])

    def block_grads(t):
        return jnp.concatenate(
            [jnp.concatenate([grads[i, mine(t, d), :] for d in (0, 1)], 0) for i in range(3)]
            + [partner_grads[i, t % n] for i in range(3)],
            1,
        )

    def weight_parts(t):
        for d in (0, 1):
            load_rows(t, d).wait()
        parts[...] += dot_tn(block_grads(t), x_buf[t % 2])

    def pair_copy():
        return remote(pair_out, pair_land, pair_sem.at[0], pair_sem.at[1], ring.partner)

    def rep_copy(k):
        return pltpu.make_async_remote_copy(
            src_ref=pair_out,
            dst_ref=rep_land.at[k - 1],
            send_sem=rep_send.at[k - 1],
            recv_sem=rep_recv.at[k - 1],
            device_id={"rep": lax.rem(pack + k, packs)},
            device_id_type=MESH,
        )

    middle = n // 2

    def output_step(t):
        for d in (0, 1):
            spot = lax.rem(ring.place + (n - t if d == 0 else t), n)
            columns = pl.ds(d * (features // 2), features // 2)
            own = pl.multiple_of(spot * (share + plain), 16)
            total = output_mine[pl.ds(own, share), columns].astype(F32)
            for there in output_there:
                total += there[pl.ds(pl.multiple_of(spot * share, share), share), columns].astype(F32)
            if plain:
                rest_rows = pl.ds(pl.multiple_of(own + share, 16), plain)
                total = jnp.concatenate([total, output_mine[rest_rows, columns].astype(F32)], 0)

            def pass_on(value):
                @pl.when(t >= 3)
                def _():
                    output_copy(t - 2, d).wait_send()
                    pl.semaphore_wait(o_credit.at[d], 1)

                o_sent[d, t % 2] = value.astype(LOW)
                output_copy(t, d).start()

            @pl.when(t == 1)
            def _():
                pass_on(total)

            @pl.when(t >= 2)
            def _():
                output_copy(t - 1, d).wait_recv()
                more = total + o_landed[d, (t - 1) % 2].astype(F32)

                @pl.when(t <= n - 2)
                def _():
                    give_credit(o_credit.at[d], d)

                @pl.when(t < n)
                def _():
                    pass_on(more)

                @pl.when(t == n)
                def _():
                    o_packs[packs - 1, :, columns] = more.astype(LOW)

    def output_swap(k):
        return pltpu.make_async_remote_copy(
            src_ref=o_packs.at[packs - 1],
            dst_ref=o_packs.at[k - 1],
            send_sem=swap_send.at[k - 1],
            recv_sem=swap_recv.at[k - 1],
            device_id={"rep": lax.rem(pack + k, packs)},
            device_id_type=MESH,
        )

    def copies_to(src, land, own, send_sem, recv_sem, device, count):
        return [
            pltpu.make_async_remote_copy(
                src_ref=src,
                dst_ref=land.at[own],
                send_sem=send_sem.at[k],
                recv_sem=recv_sem.at[k],
                device_id=device(k),
                device_id_type=MESH,
            )
            for k in range(1, count)
        ]

    def far_copies():
        return copies_to(far_part, far_land, ring.chip, far_send, far_recv, far, n)

    def near_copies():
        return copies_to(near_part, near_land, mate, near_send, near_recv, near, mates)

    def collect(copies, src, land, own, count):
        land[own] = src[...]
        for copy in copies:
            copy.wait()
        total = land[0]
        for k in range(1, count):
            total += land[k]
        return total

    def first_gain():
        def add(i, total):
            at = pl.ds(pl.multiple_of(i * 64, 64), 64)
            product = joined[at, :].astype(F32) * parts[at, :]
            return total + jnp.sum(product, axis=0, keepdims=True)

        return lax.fori_loop(0, 6 * r // 64, add, jnp.zeros((1, features), F32)) / gain[...]

    def step(t, carry):
        @pl.when(t <= middle)
        def _():
            for d in (0, 1):
                load_rows(2 * t - 1, d).start()
                load_rows(2 * t, d).start()

        for u in (0, 1):
            columns = pl.ds(u * (features // 2), features // 2)
            for d in (0, 1):
                part = pl.ds(d * half, half), columns

                @pl.when(t >= 2)
                def _():
                    reduce_copy(t - 1, d, u).wait_recv()
                    out[part] += landed[d, u, (t - 1) % 2].astype(F32)

                    @pl.when(t <= n - 2)
                    def _():
                        give_credit(credit.at[d, u], d)

                @pl.when(t < n)
                def _():
                    @pl.when(t >= 3)
                    def _():
                        reduce_copy(t - 2, d, u).wait_send()
                        pl.semaphore_wait(credit.at[d, u], 1)

                    sent[d, u, t % 2] = out[part].astype(LOW)
                    reduce_copy(t, d, u).start()

            @pl.when(2 * t - 1 + u <= n)
            def _():
                output_step(2 * t - 1 + u)

        @pl.when(2 * t == n)
        def _():
            for k in range(1, packs):
                output_swap(k).start()

        @pl.when(t == 1)
        def _():
            parts[...] = jnp.zeros_like(parts)

            def arrived(k, carry):
                for d in (0, 1):
                    swap(k, d).wait_recv()
                return carry

            lax.fori_loop(2, n + 1, arrived, 0)

        @pl.when(t <= middle)
        def _():
            weight_parts(2 * t - 1)
            weight_parts(2 * t)

        @pl.when(t == middle)
        def _():
            for i in range(3):
                pair_out[i] = parts[pl.ds((3 + i) * r, r), :].astype(LOW)
            pair_copy().start()
            far_part[0:1, :] = first_gain()
            far_part[1:2, :] = dense_gain_part[...]
            for copy in far_copies():
                copy.start()

        @pl.when(t == middle + 1)
        def _():
            pair_copy().wait()
            for i in range(3):
                pair_out[i] = (parts[pl.ds(i * r, r), :] + pair_land[i].astype(F32)).astype(LOW)
            for k in range(1, packs):
                rep_copy(k).start()
            rep_land[packs - 1] = pair_out[...]

        @pl.when(t == middle + 2)
        def _():
            near_part[...] = collect(far_copies(), far_part, far_land, ring.chip, n)
            for copy in near_copies():
                copy.start()

        @pl.when(t < n)
        def _():
            out[...] = dot_nn(block_grads(t + 1), joined[...])

        return carry

    for d in (0, 1):
        swap(1, d).wait_recv()
    for load in load_weights:
        load.wait()
    out[...] = dot_nn(block_grads(1), joined[...])
    lax.fori_loop(1, n + 1, step, 0)
    for t in (n - 2, n - 1):
        for d in (0, 1):
            output_copy(t, d).wait_send()
            for u in (0, 1):
                reduce_copy(t, d, u).wait_send()

    def close(i, carry):
        span = pl.ds(pl.multiple_of(i * 16, 16), 16)
        value = hidden_in[span, :].astype(F32)
        grad = out[span, :]
        scale = lax.rsqrt(jnp.mean(value * value, axis=1, keepdims=True) + EPSILON)
        scaled = grad * gain[...]
        shift = jnp.mean(value * scaled, axis=1, keepdims=True)
        out[span, :] = grad_mixed[span, :] + scale * scaled - value * (scale * scale * scale * shift)
        return carry

    lax.fori_loop(0, rows // 16, close, 0)

    def finish(t, carry):
        for d in (0, 1):
            swap(t, d).wait_send()
        return carry

    lax.fori_loop(1, n + 1, finish, 0)
    gains[...] = collect(near_copies(), near_part, near_land, mate, mates)
    for k in range(1, packs):
        rep_copy(k).wait()
        output_swap(k).wait()


def normed_back(
    grads, weights, partner_weights, hidden_in, gain, grad_mixed, dense_gain_part, normed_all, output_mine, output_there
):
    tokens, r = grads.shape[1:]
    features = partner_weights.shape[1]
    devices = lax.axis_size("dp")
    packs = lax.axis_size("rep")
    n = devices // 2
    rows = tokens // devices
    half = rows // 2
    share, plain = output_split(r, packs)
    carried = share + plain
    mates = 2 * packs
    vmem = pl.BlockSpec(memory_space=pltpu.VMEM)
    hbm = pl.BlockSpec(memory_space=pl.ANY)
    dma = pltpu.SemaphoreType.DMA
    return pl.pallas_call(
        functools.partial(normed_back_kernel, packs),
        out_shape=(
            jax.ShapeDtypeStruct((rows, features), F32),
            jax.ShapeDtypeStruct((2, features), F32),
        )
        + (
            jax.ShapeDtypeStruct((packs, 3, r, features), LOW),
            jax.ShapeDtypeStruct((packs, carried, features), LOW),
        ),
        in_specs=[hbm] * 5 + [vmem] * 4 + [hbm] + [vmem] * packs,
        out_specs=(vmem,) * 4,
        scratch_shapes=[
            pltpu.VMEM(grads.shape, LOW),
            pltpu.VMEM((6 * r, features), LOW),
            pltpu.VMEM((3, n, rows, r), LOW),
            pltpu.VMEM((2, 2, 2, half, features // 2), LOW),
            pltpu.VMEM((2, 2, 2, half, features // 2), LOW),
            pltpu.VMEM((2, rows, features), LOW),
            pltpu.VMEM((6 * r, features), F32),
            pltpu.VMEM((3, r, features), LOW),
            pltpu.VMEM((3, r, features), LOW),
            pltpu.VMEM((2, 2, carried, features // 2), LOW),
            pltpu.VMEM((2, 2, carried, features // 2), LOW),
            pltpu.VMEM((2, features), F32),
            pltpu.VMEM((n, 2, features), F32),
            pltpu.VMEM((2, features), F32),
            pltpu.VMEM((mates, 2, features), F32),
            dma, dma((4,)), dma((2, n)), dma((2, n)), dma((2, 2, 2)), dma((2, 2, 2)),
            pltpu.SemaphoreType.REGULAR((2, 2)),
            dma((2, 2)), dma((2,)), dma((packs - 1,)), dma((packs - 1,)),
            dma((2, 2)), dma((2, 2)), pltpu.SemaphoreType.REGULAR((2,)),
            dma((packs - 1,)), dma((packs - 1,)), dma((mates,)), dma((mates,)), dma((n,)), dma((n,)),
        ],
        compiler_params=pltpu.CompilerParams(
            collective_id=3, has_side_effects=True, vmem_limit_bytes=56 * MIB
        ),
        cost_estimate=pl.CostEstimate(
            flops=2 * n * rows * features * 12 * r, bytes_accessed=320 * MIB, transcendentals=0
        ),
        name="normed_back",
    )(
        grads, *weights, partner_weights, hidden_in, gain, grad_mixed, dense_gain_part, normed_all,
        output_mine, *output_there,
    )


def last_sums_kernel(packs, *refs):
    gate, up_a, up_b, down, gate_o, up_a_o, up_b_o, down_o, qkv, mixed, out_sum, grad_in, output, gains = refs[:14]
    gate_t, up_t, down_t, query_t, key_t, value_t, layer, grad, output_t, first_gain, second_gain = refs[14:]

    def add(low, other):
        if packs == 2:
            return low[...].astype(F32) + other[...].astype(F32)
        return other[...].astype(F32)

    gate_t[...] = add(gate, gate_o)
    down_t[...] = add(down, down_o)
    up_t[...] = jnp.concatenate([add(up_a, up_a_o), add(up_b, up_b_o)], 0)
    pack = lax.axis_index("rep")
    slots = [lax.rem(pack + 2 * packs - q - 1, packs) for q in range(packs)]
    for i, target in enumerate((query_t, key_t, value_t)):
        total = qkv[slots[0], i].astype(F32)
        for slot in slots[1:]:
            total += qkv[slot, i].astype(F32)
        target[...] = total

    @pl.when(pl.program_id(0) == 0)
    def _():
        first_gain[...] = gains[0, :]
        second_gain[...] = gains[1, :]
        r = output_t.shape[0]
        share, plain = output_split(r, packs)
        for q, slot in enumerate(slots):
            output_t[q * share : (q + 1) * share, :] = output[slot, :share].astype(F32)
        if plain:
            total = output[slots[0], share:].astype(F32)
            for slot in slots[1:]:
                total += output[slot, share:].astype(F32)
            output_t[r - plain :, :] = total

    layer[...] = (mixed[...] + out_sum[...].astype(F32)).astype(LOW)
    grad[...] = grad_in[...]


def last_sums(lows, others, qkv, mixed, out_sum, grad_in, output, gains):
    own, features = lows[0].shape
    rows, r = mixed.shape[0], qkv.shape[2]
    packs = qkv.shape[0]
    steps = own // STRIPE

    def striped(array):
        return pl.BlockSpec((array.shape[0] // steps, features), lambda i: (i, 0))

    wide = jax.ShapeDtypeStruct((own, features), F32)
    narrow = jax.ShapeDtypeStruct((r, features), F32)
    layer = jax.ShapeDtypeStruct((rows, features), LOW)
    line = jax.ShapeDtypeStruct((features,), F32)
    out_shape = (wide,) * 3 + (narrow,) * 3 + (layer, grad_in, narrow, line, line)
    return pl.pallas_call(
        functools.partial(last_sums_kernel, packs),
        out_shape=tuple(jax.ShapeDtypeStruct(a.shape, a.dtype) for a in out_shape),
        grid=(steps,),
        in_specs=[striped(a) for a in (*lows, *others)]
        + [pl.BlockSpec((packs, 3, r // steps, features), lambda i: (0, 0, i, 0))]
        + [striped(a) for a in (mixed, out_sum, grad_in)]
        + [pl.BlockSpec(output.shape, lambda i: (0, 0, 0)), pl.BlockSpec(gains.shape, lambda i: (0, 0))],
        out_specs=tuple(striped(a) for a in out_shape[:-3])
        + (pl.BlockSpec((r, features), lambda i: (0, 0)),)
        + (pl.BlockSpec((features,), lambda i: (0,)),) * 2,
        compiler_params=pltpu.CompilerParams(vmem_limit_bytes=62 * MIB),
        cost_estimate=pl.CostEstimate(flops=8 * own * features, bytes_accessed=40 * MIB, transcendentals=0),
        name="last_sums",
    )(*lows, *others, qkv, mixed, out_sum, grad_in, output, gains)


def from_partner(value):
    devices = lax.axis_size("dp")
    return lax.ppermute(value, "dp", [(i, i ^ 1) for i in range(devices)])


def pack_swap(low):
    if lax.axis_size("rep") == 2:
        return lax.ppermute(low, "rep", [(0, 1), (1, 0)])
    return lax.psum(low, "rep")


def together(*values):
    return lax.optimization_barrier(values)


def body(
    tokens,
    attention_gain,
    query_weight,
    key_weight,
    value_weight,
    output_weight,
    dense_gain,
    gate_weight,
    up_weight,
    down_weight,
    block_document,
    document_tail,
    cotangent,
):
    devices = lax.axis_size("dp")
    chips = devices // 2
    tok_dev = tokens.shape[1]
    pack_tok = tok_dev * devices

    documents, tails = block_document[0], document_tail[0]
    first = jnp.sum((documents[None, :] < documents[:, None]).astype(jnp.int32), axis=1)
    last = jnp.concatenate([documents[1:] != documents[:-1], jnp.ones((1,), bool)])
    doc_ids = jnp.arange(tails.shape[0], dtype=jnp.int32)
    own_tail = jnp.sum((documents[:, None] == doc_ids[None, :]) * tails[None, :], axis=1)
    tail = jnp.where(last, own_tail, BLOCK).astype(jnp.int32)
    block_index = jnp.arange(documents.shape[0], dtype=jnp.int32)
    inside = jnp.arange(BLOCK, dtype=jnp.int32)
    frequency = ROPE_BASE ** (-(jnp.arange(HALF, dtype=F32) * (2.0 / HEAD_DIM)))
    start = ((block_index - first) * BLOCK).astype(F32)[None, :] * frequency[:, None]
    within = inside.astype(F32)[None, :] * frequency[:, None]
    cos_a, sin_a = jnp.cos(start)[:, :, None], jnp.sin(start)[:, :, None]
    cos_b, sin_b = jnp.cos(within)[:, None, :], jnp.sin(within)[:, None, :]
    cos_t = (cos_a * cos_b - sin_a * sin_b).reshape(HALF, -1)
    sin_t = (sin_a * cos_b + cos_a * sin_b).reshape(HALF, -1)
    r = query_weight.shape[0]

    qkv, normed_all, full_output = gather_project(
        tokens[0],
        attention_gain[None],
        (query_weight, key_weight, value_weight),
        output_weight,
        cos_t,
        sin_t,
    )

    order = ring_order(chips)
    lanes = [[2 * chip + k for chip in order] for k in (0, 1)]
    grad_low = cotangent[0]
    qkv, grad_late = together(qkv, grad_low)
    cotangents = lax.all_gather(grad_late, "dp", axis=0, axis_index_groups=lanes)
    gate_other, up_other, down_other = (
        from_partner(gate_weight),
        from_partner(up_weight),
        from_partner(down_weight),
    )
    qkv_weight = jnp.concatenate([query_weight, key_weight, value_weight], 0)

    attended, log_total = attend(first, tail, qkv)
    mixed, normed_two, attended_blocks = mix(attended, tokens[0], dense_gain[None], full_output)
    normed_two, qkv_weight = together(normed_two, qkv_weight)
    qkv_other = from_partner(qkv_weight)
    packs, pack = lax.axis_size("rep"), lax.axis_index("rep")

    grad_normed_two, out_parts, _, gate_low, up_a, up_b, down_low = dense(
        normed_two,
        cotangents,
        (gate_weight, up_weight, down_weight),
        (gate_other, up_other, down_other),
    )
    out_sum = lax.psum_scatter(
        out_parts.reshape(chips * tok_dev, -1),
        "dp",
        scatter_dimension=0,
        tiled=True,
        axis_index_groups=lanes,
    )
    gate_there = pack_swap(gate_low)

    grad_mixed, dense_gain_part, grad_heads, output_mine, *output_low = mixed_back(
        mixed, grad_normed_two, grad_low, dense_gain[None], full_output, attended_blocks
    )
    output_there = [
        lax.ppermute(low, "rep", [(i, (i + k) % packs) for i in range(packs)])
        for k, low in enumerate(output_low, 1)
    ]
    grad_heads, gate_there, output_mine = together(grad_heads, gate_there, output_mine)
    up_a, _ = together(up_a, grad_heads)
    up_a_there = pack_swap(up_a)
    grads = attend_back(first, tail, qkv, grad_heads, attended, log_total, cos_t, sin_t)
    grads, output_there, up_a_there, up_b, down_low = together(
        grads, output_there, up_a_there, up_b, down_low
    )
    up_b_there = pack_swap(up_b)
    down_there = pack_swap(down_low)
    input_grad, gain_totals, qkv_packs, output_packs = normed_back(
        grads,
        (query_weight, key_weight, value_weight),
        qkv_other,
        tokens[0],
        attention_gain[None],
        grad_mixed,
        dense_gain_part,
        normed_all,
        output_mine,
        output_there,
    )
    input_grad, out_sum, gate_there, up_a_there, up_b_there, down_there = together(
        input_grad, out_sum, gate_there, up_a_there, up_b_there, down_there
    )
    (
        gate_total, up_total, down_total, query_total, key_total, value_total,
        layer_out, input_grad, output_total, first_gain, second_gain,
    ) = last_sums(
        (gate_low, up_a, up_b, down_low),
        (gate_there, up_a_there, up_b_there, down_there),
        qkv_packs,
        mixed,
        out_sum,
        input_grad,
        output_packs,
        gain_totals,
    )
    return (
        layer_out[None],
        input_grad[None],
        first_gain,
        query_total,
        key_total,
        value_total,
        output_total,
        second_gain,
        gate_total,
        up_total,
        down_total,
    )


def solution(mesh):
    return jax.shard_map(
        body,
        mesh=mesh,
        in_specs=(
            P("rep", "dp", None),
            P(),
            P("dp", None),
            P("dp", None),
            P("dp", None),
            P("dp", None),
            P(),
            P("dp", None),
            P("dp", None),
            P("dp", None),
            P("rep", None),
            P("rep", None),
            P("rep", "dp", None),
        ),
        out_specs=(
            P("rep", "dp", None),
            P("rep", "dp", None),
            P(),
            P("dp", None),
            P("dp", None),
            P("dp", None),
            P("dp", None),
            P(),
            P("dp", None),
            P("dp", None),
            P("dp", None),
        ),
        check_vma=False,
    )
```

```python
import functools
import math

import jax
import jax.numpy as jnp
from jax import lax
from jax.experimental import pallas as pl
from jax.experimental.pallas import tpu as pltpu
from jax.sharding import PartitionSpec as P

HEAD_DIM = 64
HALF = HEAD_DIM // 2
BLOCK = 128
CHUNK = 512
FF_TILE = 256
STRIPE = 128
EPSILON = 1e-05
ROPE_BASE = 130000.0
MASKED_SCORE = -1e30
MESH = pl.DeviceIdType.MESH
MIB = 2**20
LOW = jnp.bfloat16
F32 = jnp.float32


def dot_nn(a, b):
    return lax.dot_general(a, b, (((1,), (0,)), ((), ())), preferred_element_type=F32)


def dot_nt(a, b):
    return lax.dot_general(a, b, (((1,), (1,)), ((), ())), preferred_element_type=F32)


def dot_tn(a, b):
    return lax.dot_general(a, b, (((0,), (0,)), ((), ())), preferred_element_type=F32)


def grid_of(chips):
    depth = 4 if chips % 8 == 0 else 2
    return depth, chips // depth


def chip_at(place, chips):
    depth, width = grid_of(chips)
    place = lax.rem(place + chips, chips)
    later = place - depth
    row, column = later // (width - 1), later % (width - 1)
    odd = row % 2
    far = (depth - 1 - row) * width + 1 + column + odd * (width - 2 - 2 * column)
    return jnp.where(place < depth, place * width, far)


def place_of(chip, chips):
    depth, width = grid_of(chips)
    z, x = chip // width, chip % width
    row = depth - 1 - z
    odd = row % 2
    column = x - 1 + odd * (width - 2 * x)
    return jnp.where(x == 0, z, depth + row * (width - 1) + column)


def ring_order(chips):
    depth, width = grid_of(chips)
    order = [z * width for z in range(depth)]
    for row in range(depth):
        columns = list(range(1, width))
        order += [(depth - 1 - row) * width + x for x in (columns[::-1] if row % 2 else columns)]
    return order


class Ring:
    def __init__(self):
        self.chips = lax.axis_size("dp") // 2
        me = lax.axis_index("dp")
        self.core = me % 2
        self.chip = me // 2
        self.partner = self.chip * 2 + 1 - self.core
        self.place = place_of(self.chip, self.chips)
        self.next = (self.device(1), self.device(-1))
        self.back = (self.next[1], self.next[0])

    def chip_far(self, steps):
        return chip_at(self.place + steps, self.chips)

    def device(self, steps):
        return self.chip_far(steps) * 2 + self.core

    def greet(self, others):
        barrier = pltpu.get_barrier_semaphore()
        for other in others:
            pl.semaphore_signal(barrier, inc=1, device_id={"dp": other}, device_id_type=MESH)
        pl.semaphore_wait(barrier, len(others))


def remote(src, dst, send_sem, recv_sem, device):
    return pltpu.make_async_remote_copy(
        src_ref=src,
        dst_ref=dst,
        send_sem=send_sem,
        recv_sem=recv_sem,
        device_id={"dp": device},
        device_id_type=MESH,
    )


def half_rows(direction, rows):
    return pl.ds(direction * (rows // 2), rows // 2)


def turned(u):
    parts = []
    for at in range(0, u.shape[1], HEAD_DIM):
        parts += [-u[:, at + HALF : at + HEAD_DIM], u[:, at : at + HALF]]
    return jnp.concatenate(parts, 1)


def gather_project_kernel(
    tokens_in, gain, query_w, key_w, value_w, output_w, cos_t, sin_t, qkv, gathered, output_all,
    tokens, own_weights, normed, partner_weights, x_buf, staged,
    in_sem, ag_send, ag_recv, w_send, w_recv, q_send, q_recv, local_sem,
    o_send, o_recv, pair_send, pair_recv, rep_send, rep_recv, far_send, far_recv,
):
    ring = Ring()
    n = ring.chips
    packs, pack = lax.axis_size("rep"), lax.axis_index("rep")
    rows = normed.shape[0]
    half = rows // 2
    r = qkv.shape[2]
    sources = (query_w, key_w, value_w)
    load_tokens = pltpu.make_async_copy(tokens_in, tokens, in_sem.at[3])
    load_tokens.start()
    load_weights = [
        pltpu.make_async_copy(source, own_weights.at[i], in_sem.at[i]) for i, source in enumerate(sources)
    ]
    for load in load_weights:
        load.start()
    barrier = pltpu.get_barrier_semaphore()
    for k in range(1, packs):
        pl.semaphore_signal(
            barrier, inc=1, device_id={"rep": lax.rem(pack + k, packs)}, device_id_type=MESH
        )
    for other in (ring.next[0], ring.next[1], ring.partner):
        pl.semaphore_signal(barrier, inc=1, device_id={"dp": other}, device_id_type=MESH)
    pl.semaphore_wait(barrier, 3 + packs - 1)

    load_tokens.wait()

    def normalize(i, carry):
        span = pl.ds(pl.multiple_of(i * 32, 32), 32)
        value = tokens[span, :].astype(F32)
        scale = lax.rsqrt(jnp.mean(value * value, axis=1, keepdims=True) + EPSILON)
        normed[span, :] = (value * scale * gain[...]).astype(LOW)
        return carry

    lax.fori_loop(0, rows // 32, normalize, 0)

    def hop(t, d):
        chip = ring.chip_far((1 - t) if d == 0 else (t - 1))
        return chip, half_rows(d, rows)

    def send(t, d, first):
        chip, part = hop(t, d)
        src = normed.at[part] if first else gathered.at[chip, part]
        return remote(src, gathered.at[chip, part], ag_send.at[d, t - 1], ag_recv.at[d, t - 1], ring.next[d])

    out_rows, features = output_w.shape
    share = out_rows // packs
    spot = ring.place * 2 + ring.core

    def share_of(q, d):
        return pl.ds(pl.multiple_of(q * share, share), share), pl.ds(d * (features // 2), features // 2)

    def block_at(t, d, q, core):
        place = lax.rem(ring.place + (n - t if d == 0 else t), n)
        at_rows, columns = share_of(q, d)
        return output_all.at[place * 2 + core, at_rows, columns]

    def o_copy(t, d, first):
        at_rows, columns = share_of(pack, d)
        src = output_w.at[at_rows, columns] if first else block_at(t - 1, d, pack, ring.core)
        return remote(
            src, block_at(t - 1, d, pack, ring.core), o_send.at[d, t], o_recv.at[d, t], ring.next[d]
        )

    def pair_copy(t, d):
        block = block_at(t, d, pack, ring.core)
        return remote(block, block, pair_send.at[d, t], pair_recv.at[d, t], ring.partner)

    def rep_copy(t, d, k):
        block = block_at(t, d, pack, ring.core)
        return pltpu.make_async_remote_copy(
            src_ref=block,
            dst_ref=block,
            send_sem=rep_send.at[k - 1, d, t],
            recv_sem=rep_recv.at[k - 1, d, t],
            device_id={"rep": lax.rem(pack + k, packs)},
            device_id_type=MESH,
        )

    def far_copy(t, d, k):
        block = block_at(t, d, lax.rem(pack + packs - k, packs), ring.core)
        return remote(block, block, far_send.at[k - 1, d, t], far_recv.at[k - 1, d, t], ring.partner)

    def forward_far(t):
        for d in (0, 1):
            for k in range(1, packs):
                rep_copy(t, d, k).wait_recv()
                far_copy(t, d, k).start()

    for d in (0, 1):
        send(1, d, True).start()
    for d in (0, 1):
        o_copy(1, d, True).start()
    own_rows = remote(output_w, output_all.at[spot], local_sem.at[3], local_sem.at[4], ring.partner)
    own_rows.start()
    own_keep = pltpu.make_async_copy(output_w, output_all.at[spot], local_sem.at[5])
    own_keep.start()
    swaps = [
        remote(sources[i], partner_weights.at[i], w_send.at[i], w_recv.at[i], ring.partner)
        for i in range(3)
    ]
    for swap in swaps:
        swap.start()
    keep = pltpu.make_async_copy(normed, gathered.at[ring.chip], local_sem.at[2])
    keep.start()

    def project_block(t, from_input):
        x = normed[...] if from_input else x_buf[...]
        places = [ring.chip_far(-t), ring.chip_far(t)]
        starts = [
            pl.multiple_of((places[d] * 2 + ring.core) * rows + d * half, half) for d in (0, 1)
        ]

        def table(source):
            wide = [source[:, pl.ds(starts[d], half)] for d in (0, 1)]
            return jnp.concatenate(
                [jnp.concatenate([w] * (r // HALF), 0).T for w in wide], 0
            )

        cos, sin = table(cos_t), table(sin_t)

        def heads(w):
            query, key, value = [dot_nt(x, w[i][...]) for i in range(3)]
            return (
                (query * cos + turned(query) * sin).astype(LOW),
                (key * cos + turned(key) * sin).astype(LOW),
                value.astype(LOW),
            )

        for i, value in enumerate(heads([own_weights.at[i] for i in range(3)])):
            for d in (0, 1):
                qkv[i, pl.ds(starts[d], half), :] = value[d * half : (d + 1) * half]
        if from_input:
            for swap in swaps:
                swap.wait()
        for i, value in enumerate(heads([partner_weights.at[i] for i in range(3)])):
            staged[t, i] = value
        for d in (0, 1):
            remote(
                staged.at[t, :, half_rows(d, rows)],
                qkv.at[:, pl.ds(starts[d], half)],
                q_send.at[d, t],
                q_recv.at[d, t],
                ring.partner,
            ).start()

    for load in load_weights:
        load.wait()
    project_block(0, True)

    def step(t, carry):
        for d in (0, 1):
            send(t, d, False).wait_recv()

        @pl.when(t < n - 1)
        def _():
            for d in (0, 1):
                send(t + 1, d, False).start()

        for d in (0, 1):
            o_copy(t, d, False).wait_recv()

        @pl.when(t < n - 1)
        def _():
            for d in (0, 1):
                o_copy(t + 1, d, False).start()

        for d in (0, 1):
            for k in range(1, packs):
                rep_copy(t, d, k).start()
            pair_copy(t, d).start()

        @pl.when(t > 1)
        def _():
            forward_far(t - 1)

        loads = []
        for d in (0, 1):
            chip, part = hop(t + 1, d)
            loads.append(pltpu.make_async_copy(gathered.at[chip, part], x_buf.at[part], local_sem.at[d]))
        for load in loads:
            load.start()
        for load in loads:
            load.wait()
        project_block(t, False)
        return carry

    lax.fori_loop(1, n, step, 0)
    forward_far(n - 1)

    def finish(t, carry):
        for d in (0, 1):
            send(t, d, False).wait_send()
            o_copy(t, d, False).wait_send()
            pair_copy(t, d).wait()
            for k in range(1, packs):
                rep_copy(t, d, k).wait_send()
                far_copy(t, d, k).wait()
        return carry

    lax.fori_loop(1, n, finish, 0)
    own_rows.wait()
    own_keep.wait()

    def finish_heads(t, carry):
        for d in (0, 1):
            done = remote(
                staged.at[t, :, half_rows(d, rows)],
                qkv.at[:, half_rows(d, rows)],
                q_send.at[d, t],
                q_recv.at[d, t],
                ring.partner,
            )
            done.wait_send()
            done.wait_recv()
        return carry

    lax.fori_loop(0, n, finish_heads, 0)
    keep.wait()


def gather_project(tokens, gain, weights, output_weight, cos_t, sin_t):
    rows, features = tokens.shape
    r = weights[0].shape[0]
    devices = lax.axis_size("dp")
    packs = lax.axis_size("rep")
    n = devices // 2
    vmem = pl.BlockSpec(memory_space=pltpu.VMEM)
    dma = pltpu.SemaphoreType.DMA
    hbm = pl.BlockSpec(memory_space=pl.ANY)
    return pl.pallas_call(
        gather_project_kernel,
        out_shape=(
            jax.ShapeDtypeStruct((3, devices * rows, r), LOW),
            jax.ShapeDtypeStruct((n, rows, features), LOW),
            jax.ShapeDtypeStruct((devices,) + output_weight.shape, LOW),
        ),
        in_specs=[hbm, vmem] + [hbm] * 4 + [vmem] * 2,
        out_specs=(vmem, pl.BlockSpec(memory_space=pl.ANY), pl.BlockSpec(memory_space=pl.ANY)),
        scratch_shapes=[
            pltpu.VMEM((rows, features), LOW),
            pltpu.VMEM((3, r, features), LOW),
            pltpu.VMEM((rows, features), LOW),
            pltpu.VMEM((3, r, features), LOW),
            pltpu.VMEM((rows, features), LOW),
            pltpu.VMEM((n, 3, rows, r), LOW),
            dma((4,)),
            dma((2, n)), dma((2, n)), dma((3,)), dma((3,)), dma((2, n)), dma((2, n)), dma((6,)),
            dma((2, n)), dma((2, n)), dma((2, n)), dma((2, n)),
            dma((packs - 1, 2, n)), dma((packs - 1, 2, n)),
            dma((packs - 1, 2, n)), dma((packs - 1, 2, n)),
        ],
        compiler_params=pltpu.CompilerParams(
            collective_id=1, has_side_effects=True, vmem_limit_bytes=60 * MIB
        ),
        cost_estimate=pl.CostEstimate(
            flops=4 * n * rows * features * 3 * r, bytes_accessed=320 * MIB, transcendentals=0
        ),
        name="gather_project",
    )(tokens, gain, *weights, output_weight, cos_t, sin_t)


def split_heads(u):
    heads = u.shape[1] // HEAD_DIM
    if heads == 1:
        return u
    lane = lax.broadcasted_iota(jnp.int32, u.shape, 1) // HEAD_DIM
    zero = jnp.zeros_like(u)
    return jnp.concatenate([jnp.where(lane == h, u, zero) for h in range(heads)], 0)


def join_heads(u):
    heads = u.shape[0] // HEAD_DIM
    return jnp.concatenate(
        [u[h * HEAD_DIM : (h + 1) * HEAD_DIM, h * BLOCK : (h + 1) * BLOCK] for h in range(heads)], 0
    )


def transpose_blocks(source, target):
    def one(b, carry):
        at = pl.multiple_of(b * BLOCK, BLOCK)
        target[:, pl.ds(at, BLOCK)] = source[pl.ds(at, BLOCK), :].astype(F32).T.astype(LOW)
        return carry

    lax.fori_loop(0, source.shape[0] // BLOCK, one, 0)


def window_of(b, first, tail, columns):
    start = pl.multiple_of(jnp.maximum(b - (CHUNK // BLOCK - 1), 0) * BLOCK, BLOCK)
    whole = (b - first) // (CHUNK // BLOCK)
    lowest = (first + whole * (CHUNK // BLOCK)) * BLOCK
    key_index = start + lax.broadcasted_iota(jnp.int32, (CHUNK, columns), 0)
    query_index = b * BLOCK + lax.broadcasted_iota(jnp.int32, (CHUNK, columns), 1) % BLOCK
    allowed = (
        (key_index >= lowest)
        & (key_index <= query_index)
        & (key_index < b * BLOCK + tail)
    )
    return start, whole, allowed


def walk_rows(b, tok_dev, chips):
    device = b * BLOCK // tok_dev
    spot = place_of(device // 2, chips) * 2 + device % 2
    return pl.ds(pl.multiple_of(spot * tok_dev + b * BLOCK % tok_dev, BLOCK), BLOCK)


def attend_kernel(chips, first_ref, tail_ref, qkv, attended, log_total, value_t):
    tokens, r = qkv.shape[1:]
    tok_dev = tokens // (2 * chips)
    columns = (r // HEAD_DIM) * BLOCK
    scale = 1.0 / math.sqrt(HEAD_DIM)
    transpose_blocks(qkv.at[2], value_t)

    def block(b, carry):
        at = pl.multiple_of(b * BLOCK, BLOCK)
        query = split_heads(qkv[0, pl.ds(at, BLOCK), :])
        start, whole, allowed = window_of(b, first_ref[b], tail_ref[b], columns)
        scores = dot_nt(qkv[1, pl.ds(start, CHUNK), :], query) * scale
        scores = jnp.where(allowed, scores, MASKED_SCORE)
        top = jnp.max(scores, axis=0, keepdims=True)
        weights = jnp.exp(scores - top)
        total = jnp.sum(weights, axis=0, keepdims=True)
        out = dot_nn(value_t[:, pl.ds(start, CHUNK)], weights.astype(LOW))

        def more(i, state):
            top, total, out = state
            start = pl.multiple_of(first_ref[b] * BLOCK + i * CHUNK, BLOCK)
            scores = dot_nt(qkv[1, pl.ds(start, CHUNK), :], query) * scale
            higher = jnp.maximum(top, jnp.max(scores, axis=0, keepdims=True))
            shrink = jnp.exp(top - higher)
            weights = jnp.exp(scores - higher)
            total = total * shrink + jnp.sum(weights, axis=0, keepdims=True)
            out = out * shrink + dot_nn(value_t[:, pl.ds(start, CHUNK)], weights.astype(LOW))
            return higher, total, out

        top, total, out = lax.fori_loop(0, whole, more, (top, total, out))
        log_total[pl.ds(b, 1), :] = top + jnp.log(total)
        attended[walk_rows(b, tok_dev, chips), :] = join_heads(out / total).T.astype(LOW)
        return carry

    lax.fori_loop(0, tokens // BLOCK, block, 0)


def attend(first, tail, qkv):
    tokens, r = qkv.shape[1:]
    smem = pl.BlockSpec(memory_space=pltpu.SMEM)
    vmem = pl.BlockSpec(memory_space=pltpu.VMEM)
    return pl.pallas_call(
        functools.partial(attend_kernel, lax.axis_size("dp") // 2),
        out_shape=(
            jax.ShapeDtypeStruct((tokens, r), LOW),
            jax.ShapeDtypeStruct((tokens // BLOCK, (r // HEAD_DIM) * BLOCK), F32),
        ),
        in_specs=[smem, smem, vmem],
        out_specs=(vmem, vmem),
        scratch_shapes=[pltpu.VMEM((r, tokens), LOW)],
        compiler_params=pltpu.CompilerParams(vmem_limit_bytes=40 * MIB),
        cost_estimate=pl.CostEstimate(
            flops=4 * tokens * 1024 * r * 8, bytes_accessed=120 * MIB, transcendentals=tokens * 1024
        ),
        name="attend",
    )(first, tail, qkv)


def unrotate(g, cos, sin):
    parts = []
    for h in range(g.shape[0] // HEAD_DIM):
        one = g[h * HEAD_DIM : h * HEAD_DIM + HALF]
        two = g[h * HEAD_DIM + HALF : (h + 1) * HEAD_DIM]
        parts += [one * cos + two * sin, two * cos - one * sin]
    return jnp.concatenate(parts, 0)


def attend_back_kernel(
    chips, first_ref, tail_ref, qkv, grad_out, attended, log_total, cos_t, sin_t, grads,
    key_t, grad_key, grad_value, staged, store_sem,
):
    tokens, r = qkv.shape[1:]
    tok_dev = tokens // (2 * chips)
    heads = r // HEAD_DIM
    columns = heads * BLOCK
    scale = 1.0 / math.sqrt(HEAD_DIM)
    transpose_blocks(qkv.at[1], key_t)
    grad_key[...] = jnp.zeros_like(grad_key)
    grad_value[...] = jnp.zeros_like(grad_value)

    def block(b, carry):
        at = pl.multiple_of(b * BLOCK, BLOCK)
        here = pl.ds(at, BLOCK)
        query = split_heads(qkv[0, here, :])
        walk = walk_rows(b, tok_dev, chips)
        grad_rows = grad_out[walk, :]
        grad = split_heads(grad_rows)
        product = (grad_rows.astype(F32) * attended[walk, :].astype(F32)).T
        delta = jnp.concatenate(
            [
                jnp.sum(product[h * HEAD_DIM : (h + 1) * HEAD_DIM], axis=0, keepdims=True)
                for h in range(heads)
            ],
            1,
        )
        log_row = log_total[pl.ds(b, 1), :]

        def chunk(start, allowed, grad_query):
            span = pl.ds(start, CHUNK)
            scores = dot_nt(qkv[1, span, :], query) * scale
            weights = jnp.exp(scores - log_row)
            if allowed is not None:
                weights = jnp.where(allowed, weights, 0.0)
            grad_weights = dot_nt(qkv[2, span, :], grad)
            grad_scores = (weights * (grad_weights - delta)).astype(LOW)
            grad_value[span, :] += dot_nn(weights.astype(LOW), grad)
            grad_key[span, :] += dot_nn(grad_scores, query)
            return grad_query + dot_nn(key_t[:, span], grad_scores)

        start, whole, allowed = window_of(b, first_ref[b], tail_ref[b], columns)
        grad_query = chunk(start, allowed, jnp.zeros((r, columns), F32))
        grad_query = lax.fori_loop(
            0,
            whole,
            lambda i, g: chunk(pl.multiple_of(first_ref[b] * BLOCK + i * CHUNK, BLOCK), None, g),
            grad_query,
        )
        turned = unrotate(join_heads(grad_query) * scale, cos_t[:, here], sin_t[:, here])
        staged[0, here, :] = turned.T.astype(LOW)
        return carry

    lax.fori_loop(0, tokens // BLOCK, block, 0)
    query_store = pltpu.make_async_copy(staged.at[0], grads.at[0], store_sem.at[0])
    query_store.start()

    def close(b, carry):
        here = pl.ds(pl.multiple_of(b * BLOCK, BLOCK), BLOCK)
        turned = unrotate(grad_key[here, :].T * scale, cos_t[:, here], sin_t[:, here])
        staged[1, here, :] = turned.T.astype(LOW)
        staged[2, here, :] = grad_value[here, :].astype(LOW)
        return carry

    lax.fori_loop(0, tokens // BLOCK, close, 0)
    rest_store = pltpu.make_async_copy(staged.at[pl.ds(1, 2)], grads.at[pl.ds(1, 2)], store_sem.at[1])
    rest_store.start()
    query_store.wait()
    rest_store.wait()


def attend_back(first, tail, qkv, grad_out, attended, log_total, cos_t, sin_t):
    tokens, r = qkv.shape[1:]
    smem = pl.BlockSpec(memory_space=pltpu.SMEM)
    vmem = pl.BlockSpec(memory_space=pltpu.VMEM)
    return pl.pallas_call(
        functools.partial(attend_back_kernel, lax.axis_size("dp") // 2),
        out_shape=jax.ShapeDtypeStruct((3, tokens, r), LOW),
        in_specs=[smem, smem] + [vmem] * 6,
        out_specs=pl.BlockSpec(memory_space=pl.ANY),
        scratch_shapes=[
            pltpu.VMEM((r, tokens), LOW),
            pltpu.VMEM((tokens, r), F32),
            pltpu.VMEM((tokens, r), F32),
            pltpu.VMEM((3, tokens, r), LOW),
            pltpu.SemaphoreType.DMA((2,)),
        ],
        compiler_params=pltpu.CompilerParams(vmem_limit_bytes=40 * MIB),
        cost_estimate=pl.CostEstimate(
            flops=10 * tokens * 1024 * r * 8, bytes_accessed=240 * MIB, transcendentals=tokens * 1024
        ),
        name="attend_back",
    )(first, tail, qkv, grad_out, attended, log_total, cos_t, sin_t)


def mixed_kernel(
    attended, tokens_in, gain, output_all, mixed, normed, blocks,
    tokens, weights, sem, w_sem, send_sem, recv_sem,
):
    ring = Ring()
    n = ring.chips
    devices = 2 * n
    rows, features = mixed.shape
    r = attended.shape[1]
    spot = ring.place * 2 + ring.core
    load = pltpu.make_async_copy(tokens_in, tokens, sem)
    load.start()

    def place_at(j):
        return lax.rem(ring.place + (j % 2) * ((j + 1) // 2) + (1 - j % 2) * (n - j // 2), n)

    def chip_weights(j):
        place = place_at(j)
        return pltpu.make_async_copy(
            output_all.at[pl.ds(place * 2, 2)], weights.at[pl.ds(place * 2, 2)], w_sem.at[j]
        )

    def fetch(j, carry):
        chip_weights(j).start()
        return carry

    lax.fori_loop(0, n, fetch, 0)
    barrier = pltpu.get_barrier_semaphore()

    def to(k):
        other = lax.rem(spot + k, devices)
        return chip_at(other // 2, n) * 2 + other % 2

    def greet(k, carry):
        pl.semaphore_signal(barrier, inc=1, device_id={"dp": to(k)}, device_id_type=MESH)
        return carry

    lax.fori_loop(1, devices, greet, 0)
    pl.semaphore_wait(barrier, devices - 1)

    def rows_of(at):
        return pl.ds(pl.multiple_of(at * rows, rows), rows)

    def copy(k):
        return remote(
            attended.at[rows_of(lax.rem(spot + k, devices))],
            blocks.at[spot],
            send_sem.at[k],
            recv_sem.at[k],
            to(k),
        )

    def begin(k, carry):
        copy(k).start()
        return carry

    lax.fori_loop(1, devices, begin, 0)
    blocks[spot] = attended[rows_of(spot), :]
    load.wait()
    mixed[...] = tokens[...].astype(F32)

    def add(j, carry):
        chip_weights(j).wait()
        place = place_at(j)
        for core in (0, 1):
            k = lax.rem(spot + devices - place * 2 - core, devices)

            @pl.when(k > 0)
            def _():
                copy(k).wait_recv()

        both = jnp.concatenate([blocks[place * 2 + core] for core in (0, 1)], 1)
        mixed[...] += dot_nn(both, weights[pl.ds(place * 2, 2)].reshape(2 * r, features))
        return carry

    lax.fori_loop(0, n, add, 0)

    def normalize(i, carry):
        span = pl.ds(pl.multiple_of(i * 32, 32), 32)
        value = mixed[span, :]
        scale = lax.rsqrt(jnp.mean(value * value, axis=1, keepdims=True) + EPSILON)
        normed[span, :] = (value * scale * gain[...]).astype(LOW)
        return carry

    lax.fori_loop(0, rows // 32, normalize, 0)

    def finish(k, carry):
        copy(k).wait_send()
        return carry

    lax.fori_loop(1, devices, finish, 0)


def mix(attended, tokens, gain, output_all):
    rows, features = tokens.shape
    devices, r = output_all.shape[:2]
    vmem = pl.BlockSpec(memory_space=pltpu.VMEM)
    hbm = pl.BlockSpec(memory_space=pl.ANY)
    dma = pltpu.SemaphoreType.DMA
    return pl.pallas_call(
        mixed_kernel,
        out_shape=(
            jax.ShapeDtypeStruct((rows, features), F32),
            jax.ShapeDtypeStruct((rows, features), LOW),
            jax.ShapeDtypeStruct((devices, rows, r), LOW),
        ),
        in_specs=[vmem, hbm, vmem, hbm],
        out_specs=(vmem,) * 3,
        scratch_shapes=[
            pltpu.VMEM((rows, features), LOW),
            pltpu.VMEM((devices, r, features), LOW),
            dma, dma((devices // 2,)), dma((devices,)), dma((devices,)),
        ],
        compiler_params=pltpu.CompilerParams(
            collective_id=5, has_side_effects=True, vmem_limit_bytes=56 * MIB
        ),
        cost_estimate=pl.CostEstimate(
            flops=2 * rows * features * features, bytes_accessed=100 * MIB, transcendentals=0
        ),
        name="mix",
    )(attended, tokens, gain, output_all)


def dense_kernel(
    normed, cotangents, gate_w, up_w, down_w, gate_p, up_p, down_p,
    grad_sum, out_parts, gathered, gate_grad, up_a, up_b, down_grad,
    weights, totals, x_buf, g_buf, out_acc, grad_acc, sent, landed, cast_buf, pair_land,
    ag_send, ag_recv, rs_send, rs_recv, credit, local_sem, w_sem, cast_sem, pair_send, pair_recv,
):
    ring = Ring()
    n = ring.chips
    rows, features = normed.shape
    half = rows // 2
    own = gate_w.shape[0]
    tiles = 2 * own // FF_TILE
    loads = []
    for i, (mine, theirs) in enumerate(((gate_w, gate_p), (up_w, up_p), (down_w, down_p))):
        loads.append(pltpu.make_async_copy(mine, weights.at[i, pl.ds(0, own)], w_sem.at[2 * i]))
        loads.append(pltpu.make_async_copy(theirs, weights.at[i, pl.ds(own, own)], w_sem.at[2 * i + 1]))
    for load in loads:
        load.start()
    ring.greet((ring.next[0], ring.next[1], ring.partner))

    def source(t, d):
        return lax.rem(ring.place + (n - t if d == 0 else t), n)

    def send(t, d, first):
        place, part = source(t - 1, d), half_rows(d, rows)
        src = normed.at[part] if first else gathered.at[place, part]
        return remote(src, gathered.at[place, part], ag_send.at[d, t - 1], ag_recv.at[d, t - 1], ring.next[d])

    def reduce_copy(t, d):
        return remote(
            sent.at[d, t % 2], landed.at[d, t % 2], rs_send.at[d, t % 2], rs_recv.at[d, t % 2], ring.next[d]
        )

    def reduce_on(t):
        for d in (0, 1):
            @pl.when(t >= 2)
            def _():
                reduce_copy(t - 1, d).wait_recv()
                sent[d, t % 2] = (
                    sent[d, t % 2].astype(F32) + landed[d, (t - 1) % 2].astype(F32)
                ).astype(LOW)

                @pl.when(t <= n - 2)
                def _():
                    pl.semaphore_signal(
                        credit.at[d], inc=1, device_id={"dp": ring.back[d]}, device_id_type=MESH
                    )

            @pl.when(t >= 3)
            def _():
                pl.semaphore_wait(credit.at[d], 1)

            reduce_copy(t, d).start()

    for d in (0, 1):
        send(1, d, True).start()

    def clear(i, carry):
        span = pl.ds(pl.multiple_of(i * FF_TILE, FF_TILE), FF_TILE)
        for k in range(3):
            totals[k, span, :] = jnp.zeros((FF_TILE, features), F32)
        return carry

    lax.fori_loop(0, tiles, clear, 0)
    for load in loads:
        load.wait()

    def out_copy(t, d):
        part = half_rows(d, rows)
        return pltpu.make_async_copy(
            cast_buf.at[t % 2, part], out_parts.at[source(t, d), part], cast_sem.at[t % 2, d]
        )

    def pass_on(t):
        for d in (0, 1):
            send(t, d, False).wait_recv()

        @pl.when(t < n - 1)
        def _():
            for d in (0, 1):
                send(t + 1, d, False).start()

    def step(t, carry):
        copies = []
        for d in (0, 1):
            part = half_rows(d, rows)
            copies.append(
                pltpu.make_async_copy(cotangents.at[source(t, d), part], g_buf.at[part], local_sem.at[d])
            )
        for copy in copies:
            copy.start()

        @pl.when(t > 1)
        def _():
            pass_on(t)

        @pl.when(t > 0)
        def _():
            more = []
            for d in (0, 1):
                part = half_rows(d, rows)
                more.append(
                    pltpu.make_async_copy(gathered.at[source(t, d), part], x_buf.at[part], local_sem.at[2 + d])
                )
                more[-1].start()
            for copy in more:
                copy.wait()

        @pl.when(t == 0)
        def _():
            x_buf[...] = normed[...]

        for copy in copies:
            copy.wait()

        out_acc[...] = jnp.zeros_like(out_acc)
        grad_acc[...] = jnp.zeros_like(grad_acc)

        def tile(i, carry):
            @pl.when((t == 0) & (i == tiles - 1))
            def _():
                pass_on(1)

            @pl.when((t >= 2) & (i == tiles // 2))
            def _():
                reduce_on(t - 1)

            span = pl.ds(pl.multiple_of(i * FF_TILE, FF_TILE), FF_TILE)
            x = x_buf[...]
            g = g_buf[...]
            gate = dot_nt(x, weights[0, span, :])
            up = dot_nt(x, weights[1, span, :])
            grad_hidden = dot_nt(g, weights[2, span, :])
            sigma = 1.0 / (1.0 + jnp.exp(-gate))
            silu = gate * sigma
            hidden = (silu * up).astype(LOW)
            grad_gate = (grad_hidden * up * sigma * (1.0 + gate * (1.0 - sigma))).astype(LOW)
            grad_up = (grad_hidden * silu).astype(LOW)
            out_acc[...] += dot_nn(hidden, weights[2, span, :])
            grad_acc[...] += dot_nn(grad_gate, weights[0, span, :])
            grad_acc[...] += dot_nn(grad_up, weights[1, span, :])
            totals[0, span, :] += dot_tn(grad_gate, x)
            totals[1, span, :] += dot_tn(grad_up, x)
            totals[2, span, :] += dot_tn(hidden, g)
            return carry

        lax.fori_loop(0, tiles, tile, 0)

        @pl.when(t >= 2)
        def _():
            for d in (0, 1):
                out_copy(t - 2, d).wait()

        cast_buf[t % 2] = out_acc[...].astype(LOW)
        for d in (0, 1):
            out_copy(t, d).start()

        @pl.when(t == 0)
        def _():
            grad_sum[...] = grad_acc[...]

        @pl.when(t > 0)
        def _():
            for d in (0, 1):
                @pl.when(t >= 3)
                def _():
                    reduce_copy(t - 2, d).wait_send()

                sent[d, t % 2] = grad_acc[pl.ds(d * half, half), :].astype(LOW)

        return carry

    lax.fori_loop(0, n, step, 0)
    reduce_on(n - 1)
    for t in (n - 2, n - 1):
        for d in (0, 1):
            out_copy(t, d).wait()

    own_tiles = 3 * own // FF_TILE

    def tile_of(i, first):
        return i // (own // FF_TILE), pl.ds(
            pl.multiple_of(first + (i % (own // FF_TILE)) * FF_TILE, FF_TILE), FF_TILE
        )

    def pair_copy(i):
        return remote(cast_buf.at[i % 2], pair_land.at[i], pair_send.at[i % 2], pair_recv.at[i], ring.partner)

    def give(i, carry):
        @pl.when(i >= 2)
        def _():
            pair_copy(i - 2).wait_send()

        k, span = tile_of(i, own)
        cast_buf[i % 2] = totals[k, span, :].astype(LOW)
        pair_copy(i).start()
        return carry

    lax.fori_loop(0, own_tiles, give, 0)
    for i in (own_tiles - 2, own_tiles - 1):
        pair_copy(i).wait_send()

    def total_copies(i):
        matrix, low = i // (own // FF_TILE), (i % (own // FF_TILE)) * FF_TILE
        if matrix != 1:
            target = (gate_grad, None, down_grad)[matrix].at[pl.ds(low, FF_TILE)]
            return [pltpu.make_async_copy(cast_buf.at[i % 2], target, cast_sem.at[i % 2, 0])]
        copies = []
        for j in range(FF_TILE // STRIPE):
            for target, first, count in ((up_a, 0, STRIPE // 4), (up_b, STRIPE // 4, 3 * STRIPE // 4)):
                copies.append(
                    pltpu.make_async_copy(
                        cast_buf.at[i % 2, pl.ds(j * STRIPE + first, count)],
                        target.at[pl.ds((low // STRIPE + j) * count, count)],
                        cast_sem.at[i % 2, len(copies)],
                    )
                )
        return copies

    for i in range(own_tiles):
        if i >= 2:
            for copy in total_copies(i - 2):
                copy.wait()
        pair_copy(i).wait_recv()
        k, span = tile_of(i, 0)
        cast_buf[i % 2] = (totals[k, span, :] + pair_land[i].astype(F32)).astype(LOW)
        for copy in total_copies(i):
            copy.start()

    for d in (0, 1):
        part = pl.ds(d * half, half)
        reduce_copy(n - 1, d).wait_recv()
        grad_sum[part, :] += landed[d, (n - 1) % 2].astype(F32)
        reduce_copy(n - 2, d).wait_send()
        reduce_copy(n - 1, d).wait_send()

    for i in (own_tiles - 2, own_tiles - 1):
        for copy in total_copies(i):
            copy.wait()

    def finish(t, carry):
        for d in (0, 1):
            send(t, d, False).wait_send()
        return carry

    lax.fori_loop(1, n, finish, 0)


def dense(normed, cotangents, own_weights, partner_weights):
    rows, features = normed.shape
    n = lax.axis_size("dp") // 2
    own = own_weights[0].shape[0]
    half = rows // 2
    vmem = pl.BlockSpec(memory_space=pltpu.VMEM)
    hbm = pl.BlockSpec(memory_space=pl.ANY)
    dma = pltpu.SemaphoreType.DMA
    own_tiles = 3 * own // FF_TILE
    return pl.pallas_call(
        dense_kernel,
        out_shape=(
            jax.ShapeDtypeStruct((rows, features), F32),
            jax.ShapeDtypeStruct((n, rows, features), LOW),
            jax.ShapeDtypeStruct((n, rows, features), LOW),
            jax.ShapeDtypeStruct((own, features), LOW),
            jax.ShapeDtypeStruct((own // 4, features), LOW),
            jax.ShapeDtypeStruct((own - own // 4, features), LOW),
            jax.ShapeDtypeStruct((own, features), LOW),
        ),
        in_specs=[vmem] + [hbm] * 7,
        out_specs=(vmem,) + (hbm,) * 6,
        scratch_shapes=[
            pltpu.VMEM((3, 2 * own, features), LOW),
            pltpu.VMEM((3, 2 * own, features), F32),
            pltpu.VMEM((rows, features), LOW),
            pltpu.VMEM((rows, features), LOW),
            pltpu.VMEM((rows, features), F32),
            pltpu.VMEM((rows, features), F32),
            pltpu.VMEM((2, 2, half, features), LOW),
            pltpu.VMEM((2, 2, half, features), LOW),
            pltpu.VMEM((2, FF_TILE, features), LOW),
            pltpu.VMEM((own_tiles, FF_TILE, features), LOW),
            dma((2, n)), dma((2, n)), dma((2, 2)), dma((2, 2)),
            pltpu.SemaphoreType.REGULAR((2,)),
            dma((4,)), dma((6,)), dma((2, 2 * FF_TILE // STRIPE)), dma((2,)), dma((own_tiles,)),
        ],
        compiler_params=pltpu.CompilerParams(
            collective_id=2, has_side_effects=True, vmem_limit_bytes=62 * MIB
        ),
        cost_estimate=pl.CostEstimate(
            flops=2 * 9 * n * rows * features * 2 * own, bytes_accessed=500 * MIB, transcendentals=0
        ),
        name="dense",
    )(normed, cotangents, *own_weights, *partner_weights)


def output_split(r, packs):
    plain = r // 4 if (r - r // 4) // packs % 16 == 0 else 0
    return (r - plain) // packs, plain


def mixed_back_kernel(
    packs, mixed_in, grad_in, cotangent_in, gain, output_all, blocks, grad_mixed, gain_part, grad_heads, *rest
):
    sums = rest[:packs]
    given, taken = rest[packs : 2 * packs], rest[2 * packs : 3 * packs]
    (
        mixed, grad_two, cotangent, low, weights, staged, product,
        sem, w_sem, send_sem, recv_sem, g_sem, t_sem,
    ) = rest[3 * packs :]
    ring = Ring()
    n = ring.chips
    devices = 2 * n
    rows, features = mixed.shape
    r = grad_heads.shape[1]
    pack = lax.axis_index("rep")
    spot = ring.place * 2 + ring.core
    loads = [
        pltpu.make_async_copy(src, dst, sem.at[i])
        for i, (src, dst) in enumerate(((mixed_in, mixed), (grad_in, grad_two), (cotangent_in, cotangent)))
    ]
    for load in loads:
        load.start()

    def chip_weights(k):
        at = lax.rem(ring.place + k, n) * 2
        return pltpu.make_async_copy(output_all.at[pl.ds(at, 2)], weights.at[pl.ds(2 * k, 2)], w_sem.at[k])

    def fetch(k, carry):
        chip_weights(k).start()
        return carry

    lax.fori_loop(0, n, fetch, 0)
    barrier = pltpu.get_barrier_semaphore()

    def to(k):
        other = lax.rem(spot + k, devices)
        return {"dp": chip_at(other // 2, n) * 2 + other % 2}

    def greet(k, carry):
        pl.semaphore_signal(barrier, inc=1, device_id=to(k), device_id_type=MESH)
        return carry

    lax.fori_loop(1, devices, greet, 0)
    pl.semaphore_wait(barrier, devices - 1)
    for load in loads:
        load.wait()
    gain_part[...] = jnp.zeros_like(gain_part)

    def norm_back(i, carry):
        span = pl.ds(pl.multiple_of(i * 16, 16), 16)
        value, grad = mixed[span, :], grad_two[span, :]
        scale = lax.rsqrt(jnp.mean(value * value, axis=1, keepdims=True) + EPSILON)
        scaled = grad * gain[...]
        shift = jnp.mean(value * scaled, axis=1, keepdims=True)
        total = cotangent[span, :].astype(F32) + scale * scaled - value * (scale * scale * scale * shift)
        grad_mixed[span, :] = total
        low[span, :] = total.astype(LOW)
        gain_part[...] += jnp.sum(grad * value * scale, axis=0, keepdims=True)
        return carry

    lax.fori_loop(0, rows // 16, norm_back, 0)

    def copy(k):
        return remote(
            staged.at[k],
            grad_heads.at[pl.ds(pl.multiple_of(spot * rows, rows), rows)],
            send_sem.at[k],
            recv_sem.at[k],
            to(k)["dp"],
        )

    def project(k, carry):
        chip_weights(k).wait()
        both = dot_nt(low[...], weights[pl.ds(2 * k, 2)].reshape(2 * r, features))
        for core in (0, 1):
            step = lax.rem(2 * k + core - ring.core + devices, devices)
            staged[step] = both[:, core * r : (core + 1) * r].astype(LOW)

            @pl.when(step > 0)
            def _():
                copy(step).start()

        return carry

    lax.fori_loop(0, n, project, 0)
    grad_heads[pl.ds(pl.multiple_of(spot * rows, rows), rows), :] = staged[0]

    def give(k):
        return remote(given[k], taken[k], g_sem.at[k], t_sem.at[k], ring.partner)

    share, plain = output_split(r, packs)

    def spots(k, place, first, count):
        width = share + plain if k == 0 else share
        return pl.ds(pl.multiple_of(place * width + first, 16), count)

    def products(place, core, use):
        product[...] = dot_tn(blocks[place * 2 + core], low[...])
        for k in range(packs):
            at = pl.multiple_of(lax.rem(pack + k, packs) * share, share)
            use(k, spots(k, place, 0, share), product[pl.ds(at, share), :])
        if plain:
            use(0, spots(0, place, share, plain), product[pl.ds(r - plain, plain), :])

    def put(k, at, value):
        given[k][at, :] = value.astype(LOW)

    def total(k, at, value):
        sums[k][at, :] = (value + taken[k][at, :].astype(F32)).astype(LOW)

    def for_partner(place, carry):
        products(place, 1 - ring.core, put)
        return carry

    def for_self(place, carry):
        products(place, ring.core, total)
        return carry

    lax.fori_loop(0, n, for_partner, 0)
    for k in range(packs):
        give(k).start()
    for k in range(packs):
        give(k).wait_recv()
    lax.fori_loop(0, n, for_self, 0)

    def finish(k, carry):
        copy(k).wait_send()
        copy(k).wait_recv()
        return carry

    lax.fori_loop(1, devices, finish, 0)
    for k in range(packs):
        give(k).wait_send()


def mixed_back(mixed, grad_two, cotangent, gain, output_all, blocks):
    rows, features = mixed.shape
    devices, r = output_all.shape[:2]
    packs = lax.axis_size("rep")
    n = devices // 2
    share, plain = output_split(r, packs)
    sizes = [n * (share + plain)] + [n * share] * (packs - 1)
    vmem = pl.BlockSpec(memory_space=pltpu.VMEM)
    hbm = pl.BlockSpec(memory_space=pl.ANY)
    dma = pltpu.SemaphoreType.DMA
    return pl.pallas_call(
        functools.partial(mixed_back_kernel, packs),
        out_shape=(
            jax.ShapeDtypeStruct((rows, features), F32),
            jax.ShapeDtypeStruct((1, features), F32),
            jax.ShapeDtypeStruct((devices * rows, r), LOW),
        )
        + tuple(jax.ShapeDtypeStruct((size, features), LOW) for size in sizes),
        in_specs=[hbm] * 3 + [vmem, hbm, vmem],
        out_specs=(vmem,) * (3 + packs),
        scratch_shapes=[pltpu.VMEM((size, features), LOW) for size in sizes + sizes]
        + [
            pltpu.VMEM((rows, features), F32),
            pltpu.VMEM((rows, features), F32),
            pltpu.VMEM((rows, features), LOW),
            pltpu.VMEM((rows, features), LOW),
            pltpu.VMEM((devices, r, features), LOW),
            pltpu.VMEM((devices, rows, r), LOW),
            pltpu.VMEM((r, features), F32),
            dma((3,)), dma((n,)), dma((devices,)), dma((devices,)), dma((packs,)), dma((packs,)),
        ],
        compiler_params=pltpu.CompilerParams(
            collective_id=4, has_side_effects=True, vmem_limit_bytes=56 * MIB
        ),
        cost_estimate=pl.CostEstimate(
            flops=4 * rows * features * features, bytes_accessed=130 * MIB, transcendentals=0
        ),
        name="mixed_back",
    )(mixed, grad_two, cotangent, gain, output_all, blocks)


def normed_back_kernel(
    packs, grads_in, query_w, key_w, value_w, partner_w, tokens_in, gain, mixed_in, dense_gain_part, normed_all, output_mine, *rest
):
    outputs_in = (output_mine, *rest[: packs - 1])
    (
        out, gains, rep_land, o_packs,
        hidden_in, grad_mixed, output_mine, *output_there
    ) = rest[packs - 1 : 2 * packs + 5]
    (
        grads, joined, partner_grads, sent, landed, x_buf, parts, pair_out, pair_land,
        o_sent, o_landed, far_part, far_land, near_part, near_land,
        in_sem, w_sem, p_send, p_recv, rs_send, rs_recv, credit, x_sem, pair_sem, rep_send, rep_recv,
        o_send, o_recv, o_credit, swap_send, swap_recv, near_send, near_recv, far_send, far_recv,
    ) = rest[2 * packs + 5 :]
    ring = Ring()
    n = ring.chips
    rows, features = out.shape
    half = rows // 2
    r = grads.shape[2]
    share, plain = output_split(r, packs)
    pack = lax.axis_index("rep")
    mates = 2 * packs
    mate = pack * 2 + ring.core
    barrier = pltpu.get_barrier_semaphore()
    load_grads = pltpu.make_async_copy(grads_in, grads, in_sem)
    load_grads.start()
    load_weights = [
        pltpu.make_async_copy(src, joined.at[pl.ds(i * r, src.shape[0])], w_sem.at[i])
        for i, src in enumerate((query_w, key_w, value_w, partner_w))
    ]
    load_outputs = [
        pltpu.make_async_copy(src, dst, w_sem.at[4 + i])
        for i, (src, dst) in enumerate(zip(outputs_in, (output_mine, *output_there)))
    ]
    load_late = [
        pltpu.make_async_copy(tokens_in, hidden_in, w_sem.at[4 + packs]),
        pltpu.make_async_copy(mixed_in, grad_mixed, w_sem.at[5 + packs]),
    ]
    for load in load_weights + load_outputs + load_late:
        load.start()

    def near(k):
        to = lax.rem(mate + k, mates)
        return {"dp": ring.chip * 2 + to % 2, "rep": to // 2}

    def far(k):
        return {"dp": lax.rem(ring.chip + k, n) * 2 + ring.core}

    for k in range(1, mates):
        pl.semaphore_signal(barrier, inc=1, device_id=near(k), device_id_type=MESH)
    for k in range(1, n):
        pl.semaphore_signal(barrier, inc=1, device_id=far(k), device_id_type=MESH)
    pl.semaphore_wait(barrier, mates + n - 2)
    load_grads.wait()

    def place(t, d):
        return ring.chip_far(-t if d == 0 else t)

    def swap(t, d):
        start = (place(t, d) * 2 + 1 - ring.core) * rows + d * half
        return remote(
            grads.at[:, pl.ds(pl.multiple_of(start, half), half)],
            partner_grads.at[:, t % n, half_rows(d, rows)],
            p_send.at[d, t % n],
            p_recv.at[d, t % n],
            ring.partner,
        )

    def begin(t, carry):
        for d in (0, 1):
            swap(t, d).start()
        return carry

    lax.fori_loop(1, n + 1, begin, 0)

    def reduce_copy(t, d, u):
        return remote(
            sent.at[d, u, t % 2],
            landed.at[d, u, t % 2],
            rs_send.at[d, u, t % 2],
            rs_recv.at[d, u, t % 2],
            ring.next[d],
        )

    def output_copy(t, d):
        return remote(
            o_sent.at[d, t % 2],
            o_landed.at[d, t % 2],
            o_send.at[d, t % 2],
            o_recv.at[d, t % 2],
            ring.next[d],
        )

    def give_credit(sem, d):
        pl.semaphore_signal(sem, inc=1, device_id={"dp": ring.back[d]}, device_id_type=MESH)

    def mine(t, d):
        start = (place(t, d) * 2 + ring.core) * rows + d * half
        return pl.ds(pl.multiple_of(start, half), half)

    def load_rows(t, d):
        part = half_rows(d, rows)
        return pltpu.make_async_copy(normed_all.at[place(t, d), part], x_buf.at[t % 2, part], x_sem.at[t % 2, d])

    def block_grads(t):
        return jnp.concatenate(
            [jnp.concatenate([grads[i, mine(t, d), :] for d in (0, 1)], 0) for i in range(3)]
            + [partner_grads[i, t % n] for i in range(3)],
            1,
        )

    def weight_parts(t):
        for d in (0, 1):
            load_rows(t, d).wait()
        parts[...] += dot_tn(block_grads(t), x_buf[t % 2])

    def pair_copy():
        return remote(pair_out, pair_land, pair_sem.at[0], pair_sem.at[1], ring.partner)

    def rep_copy(k):
        return pltpu.make_async_remote_copy(
            src_ref=pair_out,
            dst_ref=rep_land.at[k - 1],
            send_sem=rep_send.at[k - 1],
            recv_sem=rep_recv.at[k - 1],
            device_id={"rep": lax.rem(pack + k, packs)},
            device_id_type=MESH,
        )

    middle = n // 2

    def output_step(t):
        for d in (0, 1):
            spot = lax.rem(ring.place + (n - t if d == 0 else t), n)
            columns = pl.ds(d * (features // 2), features // 2)
            own = pl.multiple_of(spot * (share + plain), 16)
            total = output_mine[pl.ds(own, share), columns].astype(F32)
            for there in output_there:
                total += there[pl.ds(pl.multiple_of(spot * share, share), share), columns].astype(F32)
            if plain:
                rest_rows = pl.ds(pl.multiple_of(own + share, 16), plain)
                total = jnp.concatenate([total, output_mine[rest_rows, columns].astype(F32)], 0)

            def pass_on(value):
                @pl.when(t >= 3)
                def _():
                    output_copy(t - 2, d).wait_send()
                    pl.semaphore_wait(o_credit.at[d], 1)

                o_sent[d, t % 2] = value.astype(LOW)
                output_copy(t, d).start()

            @pl.when(t == 1)
            def _():
                pass_on(total)

            @pl.when(t >= 2)
            def _():
                output_copy(t - 1, d).wait_recv()
                more = total + o_landed[d, (t - 1) % 2].astype(F32)

                @pl.when(t <= n - 2)
                def _():
                    give_credit(o_credit.at[d], d)

                @pl.when(t < n)
                def _():
                    pass_on(more)

                @pl.when(t == n)
                def _():
                    o_packs[packs - 1, :, columns] = more.astype(LOW)

    def output_swap(k):
        return pltpu.make_async_remote_copy(
            src_ref=o_packs.at[packs - 1],
            dst_ref=o_packs.at[k - 1],
            send_sem=swap_send.at[k - 1],
            recv_sem=swap_recv.at[k - 1],
            device_id={"rep": lax.rem(pack + k, packs)},
            device_id_type=MESH,
        )

    def copies_to(src, land, own, send_sem, recv_sem, device, count):
        return [
            pltpu.make_async_remote_copy(
                src_ref=src,
                dst_ref=land.at[own],
                send_sem=send_sem.at[k],
                recv_sem=recv_sem.at[k],
                device_id=device(k),
                device_id_type=MESH,
            )
            for k in range(1, count)
        ]

    def far_copies():
        return copies_to(far_part, far_land, ring.chip, far_send, far_recv, far, n)

    def near_copies():
        return copies_to(near_part, near_land, mate, near_send, near_recv, near, mates)

    def collect(copies, src, land, own, count):
        land[own] = src[...]
        for copy in copies:
            copy.wait()
        total = land[0]
        for k in range(1, count):
            total += land[k]
        return total

    def first_gain():
        def add(i, total):
            at = pl.ds(pl.multiple_of(i * 64, 64), 64)
            product = joined[at, :].astype(F32) * parts[at, :]
            return total + jnp.sum(product, axis=0, keepdims=True)

        return lax.fori_loop(0, 6 * r // 64, add, jnp.zeros((1, features), F32)) / gain[...]

    def step(t, carry):
        @pl.when(t <= middle)
        def _():
            for d in (0, 1):
                load_rows(2 * t - 1, d).start()
                load_rows(2 * t, d).start()

        for u in (0, 1):
            columns = pl.ds(u * (features // 2), features // 2)
            for d in (0, 1):
                part = pl.ds(d * half, half), columns

                @pl.when(t >= 2)
                def _():
                    reduce_copy(t - 1, d, u).wait_recv()
                    out[part] += landed[d, u, (t - 1) % 2].astype(F32)

                    @pl.when(t <= n - 2)
                    def _():
                        give_credit(credit.at[d, u], d)

                @pl.when(t < n)
                def _():
                    @pl.when(t >= 3)
                    def _():
                        reduce_copy(t - 2, d, u).wait_send()
                        pl.semaphore_wait(credit.at[d, u], 1)

                    sent[d, u, t % 2] = out[part].astype(LOW)
                    reduce_copy(t, d, u).start()

            @pl.when(2 * t - 1 + u <= n)
            def _():
                output_step(2 * t - 1 + u)

        @pl.when(2 * t == n)
        def _():
            for k in range(1, packs):
                output_swap(k).start()

        @pl.when(t == 1)
        def _():
            parts[...] = jnp.zeros_like(parts)

            def arrived(k, carry):
                for d in (0, 1):
                    swap(k, d).wait_recv()
                return carry

            lax.fori_loop(2, n + 1, arrived, 0)

        @pl.when(t <= middle)
        def _():
            weight_parts(2 * t - 1)
            weight_parts(2 * t)

        @pl.when(t == middle)
        def _():
            for i in range(3):
                pair_out[i] = parts[pl.ds((3 + i) * r, r), :].astype(LOW)
            pair_copy().start()
            far_part[0:1, :] = first_gain()
            far_part[1:2, :] = dense_gain_part[...]
            for copy in far_copies():
                copy.start()

        @pl.when(t == middle + 1)
        def _():
            pair_copy().wait()
            for i in range(3):
                pair_out[i] = (parts[pl.ds(i * r, r), :] + pair_land[i].astype(F32)).astype(LOW)
            for k in range(1, packs):
                rep_copy(k).start()
            rep_land[packs - 1] = pair_out[...]

        @pl.when(t == middle + 2)
        def _():
            near_part[...] = collect(far_copies(), far_part, far_land, ring.chip, n)
            for copy in near_copies():
                copy.start()

        @pl.when(t < n)
        def _():
            out[...] = dot_nn(block_grads(t + 1), joined[...])

        return carry

    for d in (0, 1):
        swap(1, d).wait_recv()
    for load in load_weights + load_outputs:
        load.wait()
    out[...] = dot_nn(block_grads(1), joined[...])
    lax.fori_loop(1, n + 1, step, 0)
    for t in (n - 2, n - 1):
        for d in (0, 1):
            output_copy(t, d).wait_send()
            for u in (0, 1):
                reduce_copy(t, d, u).wait_send()

    for load in load_late:
        load.wait()

    def close(i, carry):
        span = pl.ds(pl.multiple_of(i * 16, 16), 16)
        value = hidden_in[span, :].astype(F32)
        grad = out[span, :]
        scale = lax.rsqrt(jnp.mean(value * value, axis=1, keepdims=True) + EPSILON)
        scaled = grad * gain[...]
        shift = jnp.mean(value * scaled, axis=1, keepdims=True)
        out[span, :] = grad_mixed[span, :] + scale * scaled - value * (scale * scale * scale * shift)
        return carry

    lax.fori_loop(0, rows // 16, close, 0)

    def finish(t, carry):
        for d in (0, 1):
            swap(t, d).wait_send()
        return carry

    lax.fori_loop(1, n + 1, finish, 0)
    gains[...] = collect(near_copies(), near_part, near_land, mate, mates)
    for k in range(1, packs):
        rep_copy(k).wait()
        output_swap(k).wait()


def normed_back(
    grads, weights, partner_weights, hidden_in, gain, grad_mixed, dense_gain_part, normed_all, output_mine, output_there
):
    tokens, r = grads.shape[1:]
    features = partner_weights.shape[1]
    devices = lax.axis_size("dp")
    packs = lax.axis_size("rep")
    n = devices // 2
    rows = tokens // devices
    half = rows // 2
    share, plain = output_split(r, packs)
    carried = share + plain
    mates = 2 * packs
    vmem = pl.BlockSpec(memory_space=pltpu.VMEM)
    hbm = pl.BlockSpec(memory_space=pl.ANY)
    dma = pltpu.SemaphoreType.DMA
    return pl.pallas_call(
        functools.partial(normed_back_kernel, packs),
        out_shape=(
            jax.ShapeDtypeStruct((rows, features), F32),
            jax.ShapeDtypeStruct((2, features), F32),
        )
        + (
            jax.ShapeDtypeStruct((packs, 3, r, features), LOW),
            jax.ShapeDtypeStruct((packs, carried, features), LOW),
        ),
        in_specs=[hbm] * 6 + [vmem, hbm, vmem] + [hbm] * (1 + packs),
        out_specs=(vmem,) * 4,
        scratch_shapes=[pltpu.VMEM(a.shape, a.dtype) for a in (hidden_in, grad_mixed, output_mine, *output_there)]
        + [
            pltpu.VMEM(grads.shape, LOW),
            pltpu.VMEM((6 * r, features), LOW),
            pltpu.VMEM((3, n, rows, r), LOW),
            pltpu.VMEM((2, 2, 2, half, features // 2), LOW),
            pltpu.VMEM((2, 2, 2, half, features // 2), LOW),
            pltpu.VMEM((2, rows, features), LOW),
            pltpu.VMEM((6 * r, features), F32),
            pltpu.VMEM((3, r, features), LOW),
            pltpu.VMEM((3, r, features), LOW),
            pltpu.VMEM((2, 2, carried, features // 2), LOW),
            pltpu.VMEM((2, 2, carried, features // 2), LOW),
            pltpu.VMEM((2, features), F32),
            pltpu.VMEM((n, 2, features), F32),
            pltpu.VMEM((2, features), F32),
            pltpu.VMEM((mates, 2, features), F32),
            dma, dma((6 + packs,)), dma((2, n)), dma((2, n)), dma((2, 2, 2)), dma((2, 2, 2)),
            pltpu.SemaphoreType.REGULAR((2, 2)),
            dma((2, 2)), dma((2,)), dma((packs - 1,)), dma((packs - 1,)),
            dma((2, 2)), dma((2, 2)), pltpu.SemaphoreType.REGULAR((2,)),
            dma((packs - 1,)), dma((packs - 1,)), dma((mates,)), dma((mates,)), dma((n,)), dma((n,)),
        ],
        compiler_params=pltpu.CompilerParams(
            collective_id=3, has_side_effects=True, vmem_limit_bytes=56 * MIB
        ),
        cost_estimate=pl.CostEstimate(
            flops=2 * n * rows * features * 12 * r, bytes_accessed=320 * MIB, transcendentals=0
        ),
        name="normed_back",
    )(
        grads, *weights, partner_weights, hidden_in, gain, grad_mixed, dense_gain_part, normed_all,
        output_mine, *output_there,
    )


def last_sums_kernel(packs, *refs):
    gate, up_a, up_b, down, gate_o, up_a_o, up_b_o, down_o, qkv, mixed, out_sum, grad_in, output, gains = refs[:14]
    gate_t, up_t, down_t, query_t, key_t, value_t, layer, grad, output_t, first_gain, second_gain = refs[14:]

    def add(low, other):
        if packs == 2:
            return low[...].astype(F32) + other[...].astype(F32)
        return other[...].astype(F32)

    gate_t[...] = add(gate, gate_o)
    down_t[...] = add(down, down_o)
    up_t[...] = jnp.concatenate([add(up_a, up_a_o), add(up_b, up_b_o)], 0)
    pack = lax.axis_index("rep")
    slots = [lax.rem(pack + 2 * packs - q - 1, packs) for q in range(packs)]
    for i, target in enumerate((query_t, key_t, value_t)):
        total = qkv[slots[0], i].astype(F32)
        for slot in slots[1:]:
            total += qkv[slot, i].astype(F32)
        target[...] = total

    @pl.when(pl.program_id(0) == 0)
    def _():
        first_gain[...] = gains[0, :]
        second_gain[...] = gains[1, :]
        r = output_t.shape[0]
        share, plain = output_split(r, packs)
        for q, slot in enumerate(slots):
            output_t[q * share : (q + 1) * share, :] = output[slot, :share].astype(F32)
        if plain:
            total = output[slots[0], share:].astype(F32)
            for slot in slots[1:]:
                total += output[slot, share:].astype(F32)
            output_t[r - plain :, :] = total

    layer[...] = (mixed[...] + out_sum[...].astype(F32)).astype(LOW)
    grad[...] = grad_in[...]


def last_sums(lows, others, qkv, mixed, out_sum, grad_in, output, gains):
    own, features = lows[0].shape
    rows, r = mixed.shape[0], qkv.shape[2]
    packs = qkv.shape[0]
    steps = own // STRIPE

    def striped(array):
        return pl.BlockSpec((array.shape[0] // steps, features), lambda i: (i, 0))

    wide = jax.ShapeDtypeStruct((own, features), F32)
    narrow = jax.ShapeDtypeStruct((r, features), F32)
    layer = jax.ShapeDtypeStruct((rows, features), LOW)
    line = jax.ShapeDtypeStruct((features,), F32)
    out_shape = (wide,) * 3 + (narrow,) * 3 + (layer, grad_in, narrow, line, line)
    return pl.pallas_call(
        functools.partial(last_sums_kernel, packs),
        out_shape=tuple(jax.ShapeDtypeStruct(a.shape, a.dtype) for a in out_shape),
        grid=(steps,),
        in_specs=[striped(a) for a in (*lows, *others)]
        + [pl.BlockSpec((packs, 3, r // steps, features), lambda i: (0, 0, i, 0))]
        + [striped(a) for a in (mixed, out_sum, grad_in)]
        + [pl.BlockSpec(output.shape, lambda i: (0, 0, 0)), pl.BlockSpec(gains.shape, lambda i: (0, 0))],
        out_specs=tuple(striped(a) for a in out_shape[:-3])
        + (pl.BlockSpec((r, features), lambda i: (0, 0)),)
        + (pl.BlockSpec((features,), lambda i: (0,)),) * 2,
        compiler_params=pltpu.CompilerParams(vmem_limit_bytes=62 * MIB),
        cost_estimate=pl.CostEstimate(flops=8 * own * features, bytes_accessed=40 * MIB, transcendentals=0),
        name="last_sums",
    )(*lows, *others, qkv, mixed, out_sum, grad_in, output, gains)


def from_partner(value):
    devices = lax.axis_size("dp")
    return lax.ppermute(value, "dp", [(i, i ^ 1) for i in range(devices)])


def pack_swap(low):
    if lax.axis_size("rep") == 2:
        return lax.ppermute(low, "rep", [(0, 1), (1, 0)])
    return lax.psum(low, "rep")


def together(*values):
    return lax.optimization_barrier(values)


def body(
    tokens,
    attention_gain,
    query_weight,
    key_weight,
    value_weight,
    output_weight,
    dense_gain,
    gate_weight,
    up_weight,
    down_weight,
    block_document,
    document_tail,
    cotangent,
):
    devices = lax.axis_size("dp")
    chips = devices // 2
    tok_dev = tokens.shape[1]
    pack_tok = tok_dev * devices

    documents, tails = block_document[0], document_tail[0]
    first = jnp.sum((documents[None, :] < documents[:, None]).astype(jnp.int32), axis=1)
    last = jnp.concatenate([documents[1:] != documents[:-1], jnp.ones((1,), bool)])
    doc_ids = jnp.arange(tails.shape[0], dtype=jnp.int32)
    own_tail = jnp.sum((documents[:, None] == doc_ids[None, :]) * tails[None, :], axis=1)
    tail = jnp.where(last, own_tail, BLOCK).astype(jnp.int32)
    block_index = jnp.arange(documents.shape[0], dtype=jnp.int32)
    inside = jnp.arange(BLOCK, dtype=jnp.int32)
    frequency = ROPE_BASE ** (-(jnp.arange(HALF, dtype=F32) * (2.0 / HEAD_DIM)))
    start = ((block_index - first) * BLOCK).astype(F32)[None, :] * frequency[:, None]
    within = inside.astype(F32)[None, :] * frequency[:, None]
    cos_a, sin_a = jnp.cos(start)[:, :, None], jnp.sin(start)[:, :, None]
    cos_b, sin_b = jnp.cos(within)[:, None, :], jnp.sin(within)[:, None, :]
    cos_t = (cos_a * cos_b - sin_a * sin_b).reshape(HALF, -1)
    sin_t = (sin_a * cos_b + cos_a * sin_b).reshape(HALF, -1)
    r = query_weight.shape[0]

    qkv, normed_all, full_output = gather_project(
        tokens[0],
        attention_gain[None],
        (query_weight, key_weight, value_weight),
        output_weight,
        cos_t,
        sin_t,
    )

    order = ring_order(chips)
    lanes = [[2 * chip + k for chip in order] for k in (0, 1)]
    grad_low = cotangent[0]
    qkv, grad_late = together(qkv, grad_low)
    cotangents = lax.all_gather(grad_late, "dp", axis=0, axis_index_groups=lanes)
    gate_other, up_other, down_other = (
        from_partner(gate_weight),
        from_partner(up_weight),
        from_partner(down_weight),
    )
    qkv_weight = jnp.concatenate([query_weight, key_weight, value_weight], 0)

    attended, log_total = attend(first, tail, qkv)
    mixed, normed_two, attended_blocks = mix(attended, tokens[0], dense_gain[None], full_output)
    normed_two, qkv_weight = together(normed_two, qkv_weight)
    qkv_other = from_partner(qkv_weight)
    packs, pack = lax.axis_size("rep"), lax.axis_index("rep")

    grad_normed_two, out_parts, _, gate_low, up_a, up_b, down_low = dense(
        normed_two,
        cotangents,
        (gate_weight, up_weight, down_weight),
        (gate_other, up_other, down_other),
    )
    out_sum = lax.psum_scatter(
        out_parts.reshape(chips * tok_dev, -1),
        "dp",
        scatter_dimension=0,
        tiled=True,
        axis_index_groups=lanes,
    )
    gate_there = pack_swap(gate_low)

    grad_mixed, dense_gain_part, grad_heads, output_mine, *output_low = mixed_back(
        mixed, grad_normed_two, grad_low, dense_gain[None], full_output, attended_blocks
    )
    output_there = [
        lax.ppermute(low, "rep", [(i, (i + k) % packs) for i in range(packs)])
        for k, low in enumerate(output_low, 1)
    ]
    grad_heads, gate_there, output_mine = together(grad_heads, gate_there, output_mine)
    up_a, _ = together(up_a, grad_heads)
    up_a_there = pack_swap(up_a)
    grads = attend_back(first, tail, qkv, grad_heads, attended, log_total, cos_t, sin_t)
    grads, output_there, up_a_there, up_b, down_low = together(
        grads, output_there, up_a_there, up_b, down_low
    )
    up_b_there = pack_swap(up_b)
    down_there = pack_swap(down_low)
    input_grad, gain_totals, qkv_packs, output_packs = normed_back(
        grads,
        (query_weight, key_weight, value_weight),
        qkv_other,
        tokens[0],
        attention_gain[None],
        grad_mixed,
        dense_gain_part,
        normed_all,
        output_mine,
        output_there,
    )
    input_grad, out_sum, gate_there, up_a_there, up_b_there, down_there = together(
        input_grad, out_sum, gate_there, up_a_there, up_b_there, down_there
    )
    (
        gate_total, up_total, down_total, query_total, key_total, value_total,
        layer_out, input_grad, output_total, first_gain, second_gain,
    ) = last_sums(
        (gate_low, up_a, up_b, down_low),
        (gate_there, up_a_there, up_b_there, down_there),
        qkv_packs,
        mixed,
        out_sum,
        input_grad,
        output_packs,
        gain_totals,
    )
    return (
        layer_out[None],
        input_grad[None],
        first_gain,
        query_total,
        key_total,
        value_total,
        output_total,
        second_gain,
        gate_total,
        up_total,
        down_total,
    )


def solution(mesh):
    return jax.shard_map(
        body,
        mesh=mesh,
        in_specs=(
            P("rep", "dp", None),
            P(),
            P("dp", None),
            P("dp", None),
            P("dp", None),
            P("dp", None),
            P(),
            P("dp", None),
            P("dp", None),
            P("dp", None),
            P("rep", None),
            P("rep", None),
            P("rep", "dp", None),
        ),
        out_specs=(
            P("rep", "dp", None),
            P("rep", "dp", None),
            P(),
            P("dp", None),
            P("dp", None),
            P("dp", None),
            P("dp", None),
            P(),
            P("dp", None),
            P("dp", None),
            P("dp", None),
        ),
        check_vma=False,
    )
```

```python
import functools
import math

import jax
import jax.numpy as jnp
from jax import lax
from jax.experimental import pallas as pl
from jax.experimental.pallas import tpu as pltpu
from jax.sharding import PartitionSpec as P

HEAD_DIM = 64
HALF = HEAD_DIM // 2
BLOCK = 128
CHUNK = 512
FF_TILE = 256
STRIPE = 128
EPSILON = 1e-05
ROPE_BASE = 130000.0
MASKED_SCORE = -1e30
MESH = pl.DeviceIdType.MESH
MIB = 2**20
LOW = jnp.bfloat16
F32 = jnp.float32


def dot_nn(a, b):
    return lax.dot_general(a, b, (((1,), (0,)), ((), ())), preferred_element_type=F32)


def dot_nt(a, b):
    return lax.dot_general(a, b, (((1,), (1,)), ((), ())), preferred_element_type=F32)


def dot_tn(a, b):
    return lax.dot_general(a, b, (((0,), (0,)), ((), ())), preferred_element_type=F32)


def grid_of(chips):
    depth = 4 if chips % 8 == 0 else 2
    return depth, chips // depth


def chip_at(place, chips):
    depth, width = grid_of(chips)
    place = lax.rem(place + chips, chips)
    later = place - depth
    row, column = later // (width - 1), later % (width - 1)
    odd = row % 2
    far = (depth - 1 - row) * width + 1 + column + odd * (width - 2 - 2 * column)
    return jnp.where(place < depth, place * width, far)


def place_of(chip, chips):
    depth, width = grid_of(chips)
    z, x = chip // width, chip % width
    row = depth - 1 - z
    odd = row % 2
    column = x - 1 + odd * (width - 2 * x)
    return jnp.where(x == 0, z, depth + row * (width - 1) + column)


def ring_order(chips):
    depth, width = grid_of(chips)
    order = [z * width for z in range(depth)]
    for row in range(depth):
        columns = list(range(1, width))
        order += [(depth - 1 - row) * width + x for x in (columns[::-1] if row % 2 else columns)]
    return order


class Ring:
    def __init__(self):
        self.chips = lax.axis_size("dp") // 2
        me = lax.axis_index("dp")
        self.core = me % 2
        self.chip = me // 2
        self.partner = self.chip * 2 + 1 - self.core
        self.place = place_of(self.chip, self.chips)
        self.next = (self.device(1), self.device(-1))
        self.back = (self.next[1], self.next[0])

    def chip_far(self, steps):
        return chip_at(self.place + steps, self.chips)

    def device(self, steps):
        return self.chip_far(steps) * 2 + self.core

    def greet(self, others):
        barrier = pltpu.get_barrier_semaphore()
        for other in others:
            pl.semaphore_signal(barrier, inc=1, device_id={"dp": other}, device_id_type=MESH)
        pl.semaphore_wait(barrier, len(others))


def remote(src, dst, send_sem, recv_sem, device):
    return pltpu.make_async_remote_copy(
        src_ref=src,
        dst_ref=dst,
        send_sem=send_sem,
        recv_sem=recv_sem,
        device_id={"dp": device},
        device_id_type=MESH,
    )


def half_rows(direction, rows):
    return pl.ds(direction * (rows // 2), rows // 2)


def turned(u):
    parts = []
    for at in range(0, u.shape[1], HEAD_DIM):
        parts += [-u[:, at + HALF : at + HEAD_DIM], u[:, at : at + HALF]]
    return jnp.concatenate(parts, 1)


def gather_project_kernel(
    tokens_in, gain, query_w, key_w, value_w, output_w, cos_t, sin_t, qkv, gathered, output_all,
    tokens, own_weights, normed, partner_weights, x_buf, staged,
    in_sem, ag_send, ag_recv, w_send, w_recv, q_send, q_recv, local_sem,
    o_send, o_recv, pair_send, pair_recv, rep_send, rep_recv, far_send, far_recv,
):
    ring = Ring()
    n = ring.chips
    packs, pack = lax.axis_size("rep"), lax.axis_index("rep")
    rows = normed.shape[0]
    half = rows // 2
    r = qkv.shape[2]
    sources = (query_w, key_w, value_w)
    load_tokens = pltpu.make_async_copy(tokens_in, tokens, in_sem.at[3])
    load_tokens.start()
    load_weights = [
        pltpu.make_async_copy(source, own_weights.at[i], in_sem.at[i]) for i, source in enumerate(sources)
    ]
    for load in load_weights:
        load.start()
    barrier = pltpu.get_barrier_semaphore()
    for k in range(1, packs):
        pl.semaphore_signal(
            barrier, inc=1, device_id={"rep": lax.rem(pack + k, packs)}, device_id_type=MESH
        )
    for other in (ring.next[0], ring.next[1], ring.partner):
        pl.semaphore_signal(barrier, inc=1, device_id={"dp": other}, device_id_type=MESH)
    pl.semaphore_wait(barrier, 3 + packs - 1)

    load_tokens.wait()

    def normalize(i, carry):
        span = pl.ds(pl.multiple_of(i * 32, 32), 32)
        value = tokens[span, :].astype(F32)
        scale = lax.rsqrt(jnp.mean(value * value, axis=1, keepdims=True) + EPSILON)
        normed[span, :] = (value * scale * gain[...]).astype(LOW)
        return carry

    lax.fori_loop(0, rows // 32, normalize, 0)

    def hop(t, d):
        chip = ring.chip_far((1 - t) if d == 0 else (t - 1))
        return chip, half_rows(d, rows)

    def send(t, d, first):
        chip, part = hop(t, d)
        src = normed.at[part] if first else gathered.at[chip, part]
        return remote(src, gathered.at[chip, part], ag_send.at[d, t - 1], ag_recv.at[d, t - 1], ring.next[d])

    out_rows, features = output_w.shape
    share = out_rows // packs
    spot = ring.place * 2 + ring.core

    def share_of(q, d):
        return pl.ds(pl.multiple_of(q * share, share), share), pl.ds(d * (features // 2), features // 2)

    def block_at(t, d, q, core):
        place = lax.rem(ring.place + (n - t if d == 0 else t), n)
        at_rows, columns = share_of(q, d)
        return output_all.at[place * 2 + core, at_rows, columns]

    def o_copy(t, d, first):
        at_rows, columns = share_of(pack, d)
        src = output_w.at[at_rows, columns] if first else block_at(t - 1, d, pack, ring.core)
        return remote(
            src, block_at(t - 1, d, pack, ring.core), o_send.at[d, t], o_recv.at[d, t], ring.next[d]
        )

    def pair_copy(t, d):
        block = block_at(t, d, pack, ring.core)
        return remote(block, block, pair_send.at[d, t], pair_recv.at[d, t], ring.partner)

    def rep_copy(t, d, k):
        block = block_at(t, d, pack, ring.core)
        return pltpu.make_async_remote_copy(
            src_ref=block,
            dst_ref=block,
            send_sem=rep_send.at[k - 1, d, t],
            recv_sem=rep_recv.at[k - 1, d, t],
            device_id={"rep": lax.rem(pack + k, packs)},
            device_id_type=MESH,
        )

    def far_copy(t, d, k):
        block = block_at(t, d, lax.rem(pack + packs - k, packs), ring.core)
        return remote(block, block, far_send.at[k - 1, d, t], far_recv.at[k - 1, d, t], ring.partner)

    def forward_far(t):
        for d in (0, 1):
            for k in range(1, packs):
                rep_copy(t, d, k).wait_recv()
                far_copy(t, d, k).start()

    for d in (0, 1):
        send(1, d, True).start()
    for d in (0, 1):
        o_copy(1, d, True).start()
    own_rows = remote(output_w, output_all.at[spot], local_sem.at[3], local_sem.at[4], ring.partner)
    own_rows.start()
    own_keep = pltpu.make_async_copy(output_w, output_all.at[spot], local_sem.at[5])
    own_keep.start()
    swaps = [
        remote(sources[i], partner_weights.at[i], w_send.at[i], w_recv.at[i], ring.partner)
        for i in range(3)
    ]
    for swap in swaps:
        swap.start()
    keep = pltpu.make_async_copy(normed, gathered.at[ring.chip], local_sem.at[2])
    keep.start()

    def project_block(t, from_input):
        x = normed[...] if from_input else x_buf[...]
        places = [ring.chip_far(-t), ring.chip_far(t)]
        starts = [
            pl.multiple_of((places[d] * 2 + ring.core) * rows + d * half, half) for d in (0, 1)
        ]

        def table(source):
            wide = [source[:, pl.ds(starts[d], half)] for d in (0, 1)]
            return jnp.concatenate(
                [jnp.concatenate([w] * (r // HALF), 0).T for w in wide], 0
            )

        cos, sin = table(cos_t), table(sin_t)

        def heads(w):
            query, key, value = [dot_nt(x, w[i][...]) for i in range(3)]
            return (
                (query * cos + turned(query) * sin).astype(LOW),
                (key * cos + turned(key) * sin).astype(LOW),
                value.astype(LOW),
            )

        for i, value in enumerate(heads([own_weights.at[i] for i in range(3)])):
            for d in (0, 1):
                qkv[i, pl.ds(starts[d], half), :] = value[d * half : (d + 1) * half]
        if from_input:
            for swap in swaps:
                swap.wait()
        for i, value in enumerate(heads([partner_weights.at[i] for i in range(3)])):
            staged[t, i] = value
        for d in (0, 1):
            remote(
                staged.at[t, :, half_rows(d, rows)],
                qkv.at[:, pl.ds(starts[d], half)],
                q_send.at[d, t],
                q_recv.at[d, t],
                ring.partner,
            ).start()

    for load in load_weights:
        load.wait()
    project_block(0, True)

    def step(t, carry):
        for d in (0, 1):
            send(t, d, False).wait_recv()

        @pl.when(t < n - 1)
        def _():
            for d in (0, 1):
                send(t + 1, d, False).start()

        for d in (0, 1):
            o_copy(t, d, False).wait_recv()

        @pl.when(t < n - 1)
        def _():
            for d in (0, 1):
                o_copy(t + 1, d, False).start()

        for d in (0, 1):
            for k in range(1, packs):
                rep_copy(t, d, k).start()
            pair_copy(t, d).start()

        @pl.when(t > 1)
        def _():
            forward_far(t - 1)

        loads = []
        for d in (0, 1):
            chip, part = hop(t + 1, d)
            loads.append(pltpu.make_async_copy(gathered.at[chip, part], x_buf.at[part], local_sem.at[d]))
        for load in loads:
            load.start()
        for load in loads:
            load.wait()
        project_block(t, False)
        return carry

    lax.fori_loop(1, n, step, 0)
    forward_far(n - 1)

    def finish(t, carry):
        for d in (0, 1):
            send(t, d, False).wait_send()
            o_copy(t, d, False).wait_send()
            pair_copy(t, d).wait()
            for k in range(1, packs):
                rep_copy(t, d, k).wait_send()
                far_copy(t, d, k).wait()
        return carry

    lax.fori_loop(1, n, finish, 0)
    own_rows.wait()
    own_keep.wait()

    def finish_heads(t, carry):
        for d in (0, 1):
            done = remote(
                staged.at[t, :, half_rows(d, rows)],
                qkv.at[:, half_rows(d, rows)],
                q_send.at[d, t],
                q_recv.at[d, t],
                ring.partner,
            )
            done.wait_send()
            done.wait_recv()
        return carry

    lax.fori_loop(0, n, finish_heads, 0)
    keep.wait()


def gather_project(tokens, gain, weights, output_weight, cos_t, sin_t):
    rows, features = tokens.shape
    r = weights[0].shape[0]
    devices = lax.axis_size("dp")
    packs = lax.axis_size("rep")
    n = devices // 2
    vmem = pl.BlockSpec(memory_space=pltpu.VMEM)
    dma = pltpu.SemaphoreType.DMA
    hbm = pl.BlockSpec(memory_space=pl.ANY)
    return pl.pallas_call(
        gather_project_kernel,
        out_shape=(
            jax.ShapeDtypeStruct((3, devices * rows, r), LOW),
            jax.ShapeDtypeStruct((n, rows, features), LOW),
            jax.ShapeDtypeStruct((devices,) + output_weight.shape, LOW),
        ),
        in_specs=[hbm, vmem] + [hbm] * 4 + [vmem] * 2,
        out_specs=(vmem, pl.BlockSpec(memory_space=pl.ANY), pl.BlockSpec(memory_space=pl.ANY)),
        scratch_shapes=[
            pltpu.VMEM((rows, features), LOW),
            pltpu.VMEM((3, r, features), LOW),
            pltpu.VMEM((rows, features), LOW),
            pltpu.VMEM((3, r, features), LOW),
            pltpu.VMEM((rows, features), LOW),
            pltpu.VMEM((n, 3, rows, r), LOW),
            dma((4,)),
            dma((2, n)), dma((2, n)), dma((3,)), dma((3,)), dma((2, n)), dma((2, n)), dma((6,)),
            dma((2, n)), dma((2, n)), dma((2, n)), dma((2, n)),
            dma((packs - 1, 2, n)), dma((packs - 1, 2, n)),
            dma((packs - 1, 2, n)), dma((packs - 1, 2, n)),
        ],
        compiler_params=pltpu.CompilerParams(
            collective_id=1, has_side_effects=True, vmem_limit_bytes=60 * MIB
        ),
        cost_estimate=pl.CostEstimate(
            flops=4 * n * rows * features * 3 * r, bytes_accessed=320 * MIB, transcendentals=0
        ),
        name="gather_project",
    )(tokens, gain, *weights, output_weight, cos_t, sin_t)


def split_heads(u):
    heads = u.shape[1] // HEAD_DIM
    if heads == 1:
        return u
    lane = lax.broadcasted_iota(jnp.int32, u.shape, 1) // HEAD_DIM
    zero = jnp.zeros_like(u)
    return jnp.concatenate([jnp.where(lane == h, u, zero) for h in range(heads)], 0)


def join_heads(u):
    heads = u.shape[0] // HEAD_DIM
    return jnp.concatenate(
        [u[h * HEAD_DIM : (h + 1) * HEAD_DIM, h * BLOCK : (h + 1) * BLOCK] for h in range(heads)], 0
    )


def transpose_blocks(source, target):
    def one(b, carry):
        at = pl.multiple_of(b * BLOCK, BLOCK)
        target[:, pl.ds(at, BLOCK)] = source[pl.ds(at, BLOCK), :].astype(F32).T.astype(LOW)
        return carry

    lax.fori_loop(0, source.shape[0] // BLOCK, one, 0)


def window_of(b, first, tail, columns):
    start = pl.multiple_of(jnp.maximum(b - (CHUNK // BLOCK - 1), 0) * BLOCK, BLOCK)
    whole = (b - first) // (CHUNK // BLOCK)
    lowest = (first + whole * (CHUNK // BLOCK)) * BLOCK
    key_index = start + lax.broadcasted_iota(jnp.int32, (CHUNK, columns), 0)
    query_index = b * BLOCK + lax.broadcasted_iota(jnp.int32, (CHUNK, columns), 1) % BLOCK
    allowed = (
        (key_index >= lowest)
        & (key_index <= query_index)
        & (key_index < b * BLOCK + tail)
    )
    return start, whole, allowed


def walk_rows(b, tok_dev, chips):
    device = b * BLOCK // tok_dev
    spot = place_of(device // 2, chips) * 2 + device % 2
    return pl.ds(pl.multiple_of(spot * tok_dev + b * BLOCK % tok_dev, BLOCK), BLOCK)


def attend_kernel(chips, first_ref, tail_ref, qkv, attended, log_total, value_t):
    tokens, r = qkv.shape[1:]
    tok_dev = tokens // (2 * chips)
    columns = (r // HEAD_DIM) * BLOCK
    scale = 1.0 / math.sqrt(HEAD_DIM)
    transpose_blocks(qkv.at[2], value_t)

    def block(b, carry):
        at = pl.multiple_of(b * BLOCK, BLOCK)
        query = split_heads(qkv[0, pl.ds(at, BLOCK), :])
        start, whole, allowed = window_of(b, first_ref[b], tail_ref[b], columns)
        scores = dot_nt(qkv[1, pl.ds(start, CHUNK), :], query) * scale
        scores = jnp.where(allowed, scores, MASKED_SCORE)
        top = jnp.max(scores, axis=0, keepdims=True)
        weights = jnp.exp(scores - top)
        total = jnp.sum(weights, axis=0, keepdims=True)
        out = dot_nn(value_t[:, pl.ds(start, CHUNK)], weights.astype(LOW))

        def more(i, state):
            top, total, out = state
            start = pl.multiple_of(first_ref[b] * BLOCK + i * CHUNK, BLOCK)
            scores = dot_nt(qkv[1, pl.ds(start, CHUNK), :], query) * scale
            higher = jnp.maximum(top, jnp.max(scores, axis=0, keepdims=True))
            shrink = jnp.exp(top - higher)
            weights = jnp.exp(scores - higher)
            total = total * shrink + jnp.sum(weights, axis=0, keepdims=True)
            out = out * shrink + dot_nn(value_t[:, pl.ds(start, CHUNK)], weights.astype(LOW))
            return higher, total, out

        top, total, out = lax.fori_loop(0, whole, more, (top, total, out))
        log_total[pl.ds(b, 1), :] = top + jnp.log(total)
        attended[walk_rows(b, tok_dev, chips), :] = join_heads(out / total).T.astype(LOW)
        return carry

    lax.fori_loop(0, tokens // BLOCK, block, 0)


def attend(first, tail, qkv):
    tokens, r = qkv.shape[1:]
    smem = pl.BlockSpec(memory_space=pltpu.SMEM)
    vmem = pl.BlockSpec(memory_space=pltpu.VMEM)
    return pl.pallas_call(
        functools.partial(attend_kernel, lax.axis_size("dp") // 2),
        out_shape=(
            jax.ShapeDtypeStruct((tokens, r), LOW),
            jax.ShapeDtypeStruct((tokens // BLOCK, (r // HEAD_DIM) * BLOCK), F32),
        ),
        in_specs=[smem, smem, vmem],
        out_specs=(vmem, vmem),
        scratch_shapes=[pltpu.VMEM((r, tokens), LOW)],
        compiler_params=pltpu.CompilerParams(vmem_limit_bytes=40 * MIB),
        cost_estimate=pl.CostEstimate(
            flops=4 * tokens * 1024 * r * 8, bytes_accessed=120 * MIB, transcendentals=tokens * 1024
        ),
        name="attend",
    )(first, tail, qkv)


def unrotate(g, cos, sin):
    parts = []
    for h in range(g.shape[0] // HEAD_DIM):
        one = g[h * HEAD_DIM : h * HEAD_DIM + HALF]
        two = g[h * HEAD_DIM + HALF : (h + 1) * HEAD_DIM]
        parts += [one * cos + two * sin, two * cos - one * sin]
    return jnp.concatenate(parts, 0)


def attend_back_kernel(
    chips, first_ref, tail_ref, qkv, grad_out, attended, log_total, cos_t, sin_t, grads,
    key_t, grad_key, grad_value,
):
    tokens, r = qkv.shape[1:]
    tok_dev = tokens // (2 * chips)
    heads = r // HEAD_DIM
    columns = heads * BLOCK
    scale = 1.0 / math.sqrt(HEAD_DIM)
    transpose_blocks(qkv.at[1], key_t)
    grad_key[...] = jnp.zeros_like(grad_key)
    grad_value[...] = jnp.zeros_like(grad_value)

    def block(b, carry):
        at = pl.multiple_of(b * BLOCK, BLOCK)
        here = pl.ds(at, BLOCK)
        query = split_heads(qkv[0, here, :])
        walk = walk_rows(b, tok_dev, chips)
        grad_rows = grad_out[walk, :]
        grad = split_heads(grad_rows)
        product = (grad_rows.astype(F32) * attended[walk, :].astype(F32)).T
        delta = jnp.concatenate(
            [
                jnp.sum(product[h * HEAD_DIM : (h + 1) * HEAD_DIM], axis=0, keepdims=True)
                for h in range(heads)
            ],
            1,
        )
        log_row = log_total[pl.ds(b, 1), :]

        def chunk(start, allowed, grad_query):
            span = pl.ds(start, CHUNK)
            scores = dot_nt(qkv[1, span, :], query) * scale
            weights = jnp.exp(scores - log_row)
            if allowed is not None:
                weights = jnp.where(allowed, weights, 0.0)
            grad_weights = dot_nt(qkv[2, span, :], grad)
            grad_scores = (weights * (grad_weights - delta)).astype(LOW)
            grad_value[span, :] += dot_nn(weights.astype(LOW), grad)
            grad_key[span, :] += dot_nn(grad_scores, query)
            return grad_query + dot_nn(key_t[:, span], grad_scores)

        start, whole, allowed = window_of(b, first_ref[b], tail_ref[b], columns)
        grad_query = chunk(start, allowed, jnp.zeros((r, columns), F32))
        grad_query = lax.fori_loop(
            0,
            whole,
            lambda i, g: chunk(pl.multiple_of(first_ref[b] * BLOCK + i * CHUNK, BLOCK), None, g),
            grad_query,
        )
        turned = unrotate(join_heads(grad_query) * scale, cos_t[:, here], sin_t[:, here])
        grads[0, here, :] = turned.T.astype(LOW)
        return carry

    lax.fori_loop(0, tokens // BLOCK, block, 0)

    def close(b, carry):
        here = pl.ds(pl.multiple_of(b * BLOCK, BLOCK), BLOCK)
        turned = unrotate(grad_key[here, :].T * scale, cos_t[:, here], sin_t[:, here])
        grads[1, here, :] = turned.T.astype(LOW)
        grads[2, here, :] = grad_value[here, :].astype(LOW)
        return carry

    lax.fori_loop(0, tokens // BLOCK, close, 0)


def attend_back(first, tail, qkv, grad_out, attended, log_total, cos_t, sin_t):
    tokens, r = qkv.shape[1:]
    smem = pl.BlockSpec(memory_space=pltpu.SMEM)
    vmem = pl.BlockSpec(memory_space=pltpu.VMEM)
    return pl.pallas_call(
        functools.partial(attend_back_kernel, lax.axis_size("dp") // 2),
        out_shape=jax.ShapeDtypeStruct((3, tokens, r), LOW),
        in_specs=[smem, smem] + [vmem] * 6,
        out_specs=vmem,
        scratch_shapes=[
            pltpu.VMEM((r, tokens), LOW),
            pltpu.VMEM((tokens, r), F32),
            pltpu.VMEM((tokens, r), F32),
        ],
        compiler_params=pltpu.CompilerParams(vmem_limit_bytes=40 * MIB),
        cost_estimate=pl.CostEstimate(
            flops=10 * tokens * 1024 * r * 8, bytes_accessed=240 * MIB, transcendentals=tokens * 1024
        ),
        name="attend_back",
    )(first, tail, qkv, grad_out, attended, log_total, cos_t, sin_t)


def mixed_kernel(
    attended, tokens_in, gain, output_all, mixed, normed, blocks,
    tokens, weights, sem, w_sem, send_sem, recv_sem,
):
    ring = Ring()
    n = ring.chips
    devices = 2 * n
    rows, features = mixed.shape
    r = attended.shape[1]
    spot = ring.place * 2 + ring.core
    load = pltpu.make_async_copy(tokens_in, tokens, sem)
    load.start()

    def place_at(j):
        return lax.rem(ring.place + (j % 2) * ((j + 1) // 2) + (1 - j % 2) * (n - j // 2), n)

    def chip_weights(j):
        place = place_at(j)
        return pltpu.make_async_copy(
            output_all.at[pl.ds(place * 2, 2)], weights.at[pl.ds(place * 2, 2)], w_sem.at[j]
        )

    def fetch(j, carry):
        chip_weights(j).start()
        return carry

    lax.fori_loop(0, n, fetch, 0)
    barrier = pltpu.get_barrier_semaphore()

    def to(k):
        other = lax.rem(spot + k, devices)
        return chip_at(other // 2, n) * 2 + other % 2

    def greet(k, carry):
        pl.semaphore_signal(barrier, inc=1, device_id={"dp": to(k)}, device_id_type=MESH)
        return carry

    lax.fori_loop(1, devices, greet, 0)
    pl.semaphore_wait(barrier, devices - 1)

    def rows_of(at):
        return pl.ds(pl.multiple_of(at * rows, rows), rows)

    def copy(k):
        return remote(
            attended.at[rows_of(lax.rem(spot + k, devices))],
            blocks.at[spot],
            send_sem.at[k],
            recv_sem.at[k],
            to(k),
        )

    def begin(k, carry):
        copy(k).start()
        return carry

    lax.fori_loop(1, devices, begin, 0)
    blocks[spot] = attended[rows_of(spot), :]
    load.wait()
    mixed[...] = tokens[...].astype(F32)

    def add(j, carry):
        chip_weights(j).wait()
        place = place_at(j)
        for core in (0, 1):
            k = lax.rem(spot + devices - place * 2 - core, devices)

            @pl.when(k > 0)
            def _():
                copy(k).wait_recv()

        both = jnp.concatenate([blocks[place * 2 + core] for core in (0, 1)], 1)
        mixed[...] += dot_nn(both, weights[pl.ds(place * 2, 2)].reshape(2 * r, features))
        return carry

    lax.fori_loop(0, n, add, 0)

    def normalize(i, carry):
        span = pl.ds(pl.multiple_of(i * 32, 32), 32)
        value = mixed[span, :]
        scale = lax.rsqrt(jnp.mean(value * value, axis=1, keepdims=True) + EPSILON)
        normed[span, :] = (value * scale * gain[...]).astype(LOW)
        return carry

    lax.fori_loop(0, rows // 32, normalize, 0)

    def finish(k, carry):
        copy(k).wait_send()
        return carry

    lax.fori_loop(1, devices, finish, 0)


def mix(attended, tokens, gain, output_all):
    rows, features = tokens.shape
    devices, r = output_all.shape[:2]
    vmem = pl.BlockSpec(memory_space=pltpu.VMEM)
    hbm = pl.BlockSpec(memory_space=pl.ANY)
    dma = pltpu.SemaphoreType.DMA
    return pl.pallas_call(
        mixed_kernel,
        out_shape=(
            jax.ShapeDtypeStruct((rows, features), F32),
            jax.ShapeDtypeStruct((rows, features), LOW),
            jax.ShapeDtypeStruct((devices, rows, r), LOW),
        ),
        in_specs=[vmem, hbm, vmem, hbm],
        out_specs=(vmem,) * 3,
        scratch_shapes=[
            pltpu.VMEM((rows, features), LOW),
            pltpu.VMEM((devices, r, features), LOW),
            dma, dma((devices // 2,)), dma((devices,)), dma((devices,)),
        ],
        compiler_params=pltpu.CompilerParams(
            collective_id=5, has_side_effects=True, vmem_limit_bytes=56 * MIB
        ),
        cost_estimate=pl.CostEstimate(
            flops=2 * rows * features * features, bytes_accessed=100 * MIB, transcendentals=0
        ),
        name="mix",
    )(attended, tokens, gain, output_all)


def dense_kernel(
    normed, cotangents, gate_w, up_w, down_w, gate_p, up_p, down_p,
    grad_sum, out_parts, gathered, gate_grad, up_a, up_b, down_grad,
    weights, totals, x_buf, g_buf, out_acc, grad_acc, sent, landed, cast_buf, pair_land,
    ag_send, ag_recv, rs_send, rs_recv, credit, local_sem, w_sem, cast_sem, pair_send, pair_recv,
):
    ring = Ring()
    n = ring.chips
    rows, features = normed.shape
    half = rows // 2
    own = gate_w.shape[0]
    tiles = 2 * own // FF_TILE
    loads = []
    for i, (mine, theirs) in enumerate(((gate_w, gate_p), (up_w, up_p), (down_w, down_p))):
        loads.append(pltpu.make_async_copy(mine, weights.at[i, pl.ds(0, own)], w_sem.at[2 * i]))
        loads.append(pltpu.make_async_copy(theirs, weights.at[i, pl.ds(own, own)], w_sem.at[2 * i + 1]))
    for load in loads:
        load.start()
    ring.greet((ring.next[0], ring.next[1], ring.partner))

    def source(t, d):
        return lax.rem(ring.place + (n - t if d == 0 else t), n)

    def send(t, d, first):
        place, part = source(t - 1, d), half_rows(d, rows)
        src = normed.at[part] if first else gathered.at[place, part]
        return remote(src, gathered.at[place, part], ag_send.at[d, t - 1], ag_recv.at[d, t - 1], ring.next[d])

    def reduce_copy(t, d):
        return remote(
            sent.at[d, t % 2], landed.at[d, t % 2], rs_send.at[d, t % 2], rs_recv.at[d, t % 2], ring.next[d]
        )

    def reduce_on(t):
        for d in (0, 1):
            @pl.when(t >= 2)
            def _():
                reduce_copy(t - 1, d).wait_recv()
                sent[d, t % 2] = (
                    sent[d, t % 2].astype(F32) + landed[d, (t - 1) % 2].astype(F32)
                ).astype(LOW)

                @pl.when(t <= n - 2)
                def _():
                    pl.semaphore_signal(
                        credit.at[d], inc=1, device_id={"dp": ring.back[d]}, device_id_type=MESH
                    )

            @pl.when(t >= 3)
            def _():
                pl.semaphore_wait(credit.at[d], 1)

            reduce_copy(t, d).start()

    for d in (0, 1):
        send(1, d, True).start()

    def clear(i, carry):
        span = pl.ds(pl.multiple_of(i * FF_TILE, FF_TILE), FF_TILE)
        for k in range(3):
            totals[k, span, :] = jnp.zeros((FF_TILE, features), F32)
        return carry

    lax.fori_loop(0, tiles, clear, 0)
    for load in loads:
        load.wait()

    def out_copy(t, d):
        part = half_rows(d, rows)
        return pltpu.make_async_copy(
            cast_buf.at[t % 2, part], out_parts.at[source(t, d), part], cast_sem.at[t % 2, d]
        )

    def pass_on(t):
        for d in (0, 1):
            send(t, d, False).wait_recv()

        @pl.when(t < n - 1)
        def _():
            for d in (0, 1):
                send(t + 1, d, False).start()

    def step(t, carry):
        copies = []
        for d in (0, 1):
            part = half_rows(d, rows)
            copies.append(
                pltpu.make_async_copy(cotangents.at[source(t, d), part], g_buf.at[part], local_sem.at[d])
            )
        for copy in copies:
            copy.start()

        @pl.when(t > 1)
        def _():
            pass_on(t)

        @pl.when(t > 0)
        def _():
            more = []
            for d in (0, 1):
                part = half_rows(d, rows)
                more.append(
                    pltpu.make_async_copy(gathered.at[source(t, d), part], x_buf.at[part], local_sem.at[2 + d])
                )
                more[-1].start()
            for copy in more:
                copy.wait()

        @pl.when(t == 0)
        def _():
            x_buf[...] = normed[...]

        for copy in copies:
            copy.wait()

        out_acc[...] = jnp.zeros_like(out_acc)
        grad_acc[...] = jnp.zeros_like(grad_acc)

        def tile(i, carry):
            @pl.when((t == 0) & (i == tiles - 1))
            def _():
                pass_on(1)

            @pl.when((t >= 2) & (i == tiles // 2))
            def _():
                reduce_on(t - 1)

            span = pl.ds(pl.multiple_of(i * FF_TILE, FF_TILE), FF_TILE)
            x = x_buf[...]
            g = g_buf[...]
            gate = dot_nt(x, weights[0, span, :])
            up = dot_nt(x, weights[1, span, :])
            grad_hidden = dot_nt(g, weights[2, span, :])
            sigma = 1.0 / (1.0 + jnp.exp(-gate))
            silu = gate * sigma
            hidden = (silu * up).astype(LOW)
            grad_gate = (grad_hidden * up * sigma * (1.0 + gate * (1.0 - sigma))).astype(LOW)
            grad_up = (grad_hidden * silu).astype(LOW)
            out_acc[...] += dot_nn(hidden, weights[2, span, :])
            grad_acc[...] += dot_nn(grad_gate, weights[0, span, :])
            grad_acc[...] += dot_nn(grad_up, weights[1, span, :])
            totals[0, span, :] += dot_tn(grad_gate, x)
            totals[1, span, :] += dot_tn(grad_up, x)
            totals[2, span, :] += dot_tn(hidden, g)
            return carry

        lax.fori_loop(0, tiles, tile, 0)

        @pl.when(t >= 2)
        def _():
            for d in (0, 1):
                out_copy(t - 2, d).wait()

        cast_buf[t % 2] = out_acc[...].astype(LOW)
        for d in (0, 1):
            out_copy(t, d).start()

        @pl.when(t == 0)
        def _():
            grad_sum[...] = grad_acc[...]

        @pl.when(t > 0)
        def _():
            for d in (0, 1):
                @pl.when(t >= 3)
                def _():
                    reduce_copy(t - 2, d).wait_send()

                sent[d, t % 2] = grad_acc[pl.ds(d * half, half), :].astype(LOW)

        return carry

    lax.fori_loop(0, n, step, 0)
    reduce_on(n - 1)
    for t in (n - 2, n - 1):
        for d in (0, 1):
            out_copy(t, d).wait()

    own_tiles = 3 * own // FF_TILE

    def tile_of(i, first):
        return i // (own // FF_TILE), pl.ds(
            pl.multiple_of(first + (i % (own // FF_TILE)) * FF_TILE, FF_TILE), FF_TILE
        )

    def pair_copy(i):
        return remote(cast_buf.at[i % 2], pair_land.at[i], pair_send.at[i % 2], pair_recv.at[i], ring.partner)

    def give(i, carry):
        @pl.when(i >= 2)
        def _():
            pair_copy(i - 2).wait_send()

        k, span = tile_of(i, own)
        cast_buf[i % 2] = totals[k, span, :].astype(LOW)
        pair_copy(i).start()
        return carry

    lax.fori_loop(0, own_tiles, give, 0)
    for i in (own_tiles - 2, own_tiles - 1):
        pair_copy(i).wait_send()

    def total_copies(i):
        matrix, low = i // (own // FF_TILE), (i % (own // FF_TILE)) * FF_TILE
        if matrix != 1:
            target = (gate_grad, None, down_grad)[matrix].at[pl.ds(low, FF_TILE)]
            return [pltpu.make_async_copy(cast_buf.at[i % 2], target, cast_sem.at[i % 2, 0])]
        copies = []
        for j in range(FF_TILE // STRIPE):
            for target, first, count in ((up_a, 0, STRIPE // 4), (up_b, STRIPE // 4, 3 * STRIPE // 4)):
                copies.append(
                    pltpu.make_async_copy(
                        cast_buf.at[i % 2, pl.ds(j * STRIPE + first, count)],
                        target.at[pl.ds((low // STRIPE + j) * count, count)],
                        cast_sem.at[i % 2, len(copies)],
                    )
                )
        return copies

    for i in range(own_tiles):
        if i >= 2:
            for copy in total_copies(i - 2):
                copy.wait()
        pair_copy(i).wait_recv()
        k, span = tile_of(i, 0)
        cast_buf[i % 2] = (totals[k, span, :] + pair_land[i].astype(F32)).astype(LOW)
        for copy in total_copies(i):
            copy.start()

    for d in (0, 1):
        part = pl.ds(d * half, half)
        reduce_copy(n - 1, d).wait_recv()
        grad_sum[part, :] += landed[d, (n - 1) % 2].astype(F32)
        reduce_copy(n - 2, d).wait_send()
        reduce_copy(n - 1, d).wait_send()

    for i in (own_tiles - 2, own_tiles - 1):
        for copy in total_copies(i):
            copy.wait()

    def finish(t, carry):
        for d in (0, 1):
            send(t, d, False).wait_send()
        return carry

    lax.fori_loop(1, n, finish, 0)


def dense(normed, cotangents, own_weights, partner_weights):
    rows, features = normed.shape
    n = lax.axis_size("dp") // 2
    own = own_weights[0].shape[0]
    half = rows // 2
    vmem = pl.BlockSpec(memory_space=pltpu.VMEM)
    hbm = pl.BlockSpec(memory_space=pl.ANY)
    dma = pltpu.SemaphoreType.DMA
    own_tiles = 3 * own // FF_TILE
    return pl.pallas_call(
        dense_kernel,
        out_shape=(
            jax.ShapeDtypeStruct((rows, features), F32),
            jax.ShapeDtypeStruct((n, rows, features), LOW),
            jax.ShapeDtypeStruct((n, rows, features), LOW),
            jax.ShapeDtypeStruct((own, features), LOW),
            jax.ShapeDtypeStruct((own // 4, features), LOW),
            jax.ShapeDtypeStruct((own - own // 4, features), LOW),
            jax.ShapeDtypeStruct((own, features), LOW),
        ),
        in_specs=[vmem] + [hbm] * 7,
        out_specs=(vmem,) + (hbm,) * 6,
        scratch_shapes=[
            pltpu.VMEM((3, 2 * own, features), LOW),
            pltpu.VMEM((3, 2 * own, features), F32),
            pltpu.VMEM((rows, features), LOW),
            pltpu.VMEM((rows, features), LOW),
            pltpu.VMEM((rows, features), F32),
            pltpu.VMEM((rows, features), F32),
            pltpu.VMEM((2, 2, half, features), LOW),
            pltpu.VMEM((2, 2, half, features), LOW),
            pltpu.VMEM((2, FF_TILE, features), LOW),
            pltpu.VMEM((own_tiles, FF_TILE, features), LOW),
            dma((2, n)), dma((2, n)), dma((2, 2)), dma((2, 2)),
            pltpu.SemaphoreType.REGULAR((2,)),
            dma((4,)), dma((6,)), dma((2, 2 * FF_TILE // STRIPE)), dma((2,)), dma((own_tiles,)),
        ],
        compiler_params=pltpu.CompilerParams(
            collective_id=2, has_side_effects=True, vmem_limit_bytes=62 * MIB
        ),
        cost_estimate=pl.CostEstimate(
            flops=2 * 9 * n * rows * features * 2 * own, bytes_accessed=500 * MIB, transcendentals=0
        ),
        name="dense",
    )(normed, cotangents, *own_weights, *partner_weights)


def output_split(r, packs):
    plain = r // 4 if (r - r // 4) // packs % 16 == 0 else 0
    return (r - plain) // packs, plain


def mixed_back_kernel(
    packs, mixed_in, grad_in, cotangent_in, gain, output_all, blocks, grad_mixed, gain_part, grad_heads, *rest
):
    sums = rest[:packs]
    given, taken = rest[packs : 2 * packs], rest[2 * packs : 3 * packs]
    (
        mixed, grad_two, cotangent, low, weights, staged, product,
        sem, w_sem, send_sem, recv_sem, g_sem, t_sem,
    ) = rest[3 * packs :]
    ring = Ring()
    n = ring.chips
    devices = 2 * n
    rows, features = mixed.shape
    r = grad_heads.shape[1]
    pack = lax.axis_index("rep")
    spot = ring.place * 2 + ring.core
    loads = [
        pltpu.make_async_copy(src, dst, sem.at[i])
        for i, (src, dst) in enumerate(((mixed_in, mixed), (grad_in, grad_two), (cotangent_in, cotangent)))
    ]
    for load in loads:
        load.start()

    def chip_weights(k):
        at = lax.rem(ring.place + k, n) * 2
        return pltpu.make_async_copy(output_all.at[pl.ds(at, 2)], weights.at[pl.ds(2 * k, 2)], w_sem.at[k])

    def fetch(k, carry):
        chip_weights(k).start()
        return carry

    lax.fori_loop(0, n, fetch, 0)
    barrier = pltpu.get_barrier_semaphore()

    def to(k):
        other = lax.rem(spot + k, devices)
        return {"dp": chip_at(other // 2, n) * 2 + other % 2}

    def greet(k, carry):
        pl.semaphore_signal(barrier, inc=1, device_id=to(k), device_id_type=MESH)
        return carry

    lax.fori_loop(1, devices, greet, 0)
    pl.semaphore_wait(barrier, devices - 1)
    for load in loads:
        load.wait()
    gain_part[...] = jnp.zeros_like(gain_part)

    def norm_back(i, carry):
        span = pl.ds(pl.multiple_of(i * 16, 16), 16)
        value, grad = mixed[span, :], grad_two[span, :]
        scale = lax.rsqrt(jnp.mean(value * value, axis=1, keepdims=True) + EPSILON)
        scaled = grad * gain[...]
        shift = jnp.mean(value * scaled, axis=1, keepdims=True)
        total = cotangent[span, :].astype(F32) + scale * scaled - value * (scale * scale * scale * shift)
        grad_mixed[span, :] = total
        low[span, :] = total.astype(LOW)
        gain_part[...] += jnp.sum(grad * value * scale, axis=0, keepdims=True)
        return carry

    lax.fori_loop(0, rows // 16, norm_back, 0)

    def copy(k):
        return remote(
            staged.at[k],
            grad_heads.at[pl.ds(pl.multiple_of(spot * rows, rows), rows)],
            send_sem.at[k],
            recv_sem.at[k],
            to(k)["dp"],
        )

    def project(k, carry):
        chip_weights(k).wait()
        both = dot_nt(low[...], weights[pl.ds(2 * k, 2)].reshape(2 * r, features))
        for core in (0, 1):
            step = lax.rem(2 * k + core - ring.core + devices, devices)
            staged[step] = both[:, core * r : (core + 1) * r].astype(LOW)

            @pl.when(step > 0)
            def _():
                copy(step).start()

        return carry

    lax.fori_loop(0, n, project, 0)
    grad_heads[pl.ds(pl.multiple_of(spot * rows, rows), rows), :] = staged[0]

    def give(k):
        return remote(given[k], taken[k], g_sem.at[k], t_sem.at[k], ring.partner)

    share, plain = output_split(r, packs)

    def spots(k, place, first, count):
        width = share + plain if k == 0 else share
        return pl.ds(pl.multiple_of(place * width + first, 16), count)

    def products(place, core, use):
        product[...] = dot_tn(blocks[place * 2 + core], low[...])
        for k in range(packs):
            at = pl.multiple_of(lax.rem(pack + k, packs) * share, share)
            use(k, spots(k, place, 0, share), product[pl.ds(at, share), :])
        if plain:
            use(0, spots(0, place, share, plain), product[pl.ds(r - plain, plain), :])

    def put(k, at, value):
        given[k][at, :] = value.astype(LOW)

    def total(k, at, value):
        sums[k][at, :] = (value + taken[k][at, :].astype(F32)).astype(LOW)

    def for_partner(place, carry):
        products(place, 1 - ring.core, put)
        return carry

    def for_self(place, carry):
        products(place, ring.core, total)
        return carry

    lax.fori_loop(0, n, for_partner, 0)
    for k in range(packs):
        give(k).start()
    for k in range(packs):
        give(k).wait_recv()
    lax.fori_loop(0, n, for_self, 0)

    def finish(k, carry):
        copy(k).wait_send()
        copy(k).wait_recv()
        return carry

    lax.fori_loop(1, devices, finish, 0)
    for k in range(packs):
        give(k).wait_send()


def mixed_back(mixed, grad_two, cotangent, gain, output_all, blocks):
    rows, features = mixed.shape
    devices, r = output_all.shape[:2]
    packs = lax.axis_size("rep")
    n = devices // 2
    share, plain = output_split(r, packs)
    sizes = [n * (share + plain)] + [n * share] * (packs - 1)
    vmem = pl.BlockSpec(memory_space=pltpu.VMEM)
    hbm = pl.BlockSpec(memory_space=pl.ANY)
    dma = pltpu.SemaphoreType.DMA
    return pl.pallas_call(
        functools.partial(mixed_back_kernel, packs),
        out_shape=(
            jax.ShapeDtypeStruct((rows, features), F32),
            jax.ShapeDtypeStruct((1, features), F32),
            jax.ShapeDtypeStruct((devices * rows, r), LOW),
        )
        + tuple(jax.ShapeDtypeStruct((size, features), LOW) for size in sizes),
        in_specs=[hbm] * 3 + [vmem, hbm, vmem],
        out_specs=(vmem,) * (3 + packs),
        scratch_shapes=[pltpu.VMEM((size, features), LOW) for size in sizes + sizes]
        + [
            pltpu.VMEM((rows, features), F32),
            pltpu.VMEM((rows, features), F32),
            pltpu.VMEM((rows, features), LOW),
            pltpu.VMEM((rows, features), LOW),
            pltpu.VMEM((devices, r, features), LOW),
            pltpu.VMEM((devices, rows, r), LOW),
            pltpu.VMEM((r, features), F32),
            dma((3,)), dma((n,)), dma((devices,)), dma((devices,)), dma((packs,)), dma((packs,)),
        ],
        compiler_params=pltpu.CompilerParams(
            collective_id=4, has_side_effects=True, vmem_limit_bytes=56 * MIB
        ),
        cost_estimate=pl.CostEstimate(
            flops=4 * rows * features * features, bytes_accessed=130 * MIB, transcendentals=0
        ),
        name="mixed_back",
    )(mixed, grad_two, cotangent, gain, output_all, blocks)


def normed_back_kernel(
    packs, grads, query_w, key_w, value_w, partner_w, tokens_in, gain, mixed_in, dense_gain_part, normed_all, output_mine, *rest
):
    outputs_in = (output_mine, *rest[: packs - 1])
    (
        out, gains, rep_land, o_packs,
        hidden_in, grad_mixed, output_mine, *output_there
    ) = rest[packs - 1 : 2 * packs + 5]
    (
        joined, partner_grads, sent, landed, x_buf, parts, pair_out, pair_land,
        o_sent, o_landed, far_part, far_land, near_part, near_land,
        w_sem, p_send, p_recv, rs_send, rs_recv, credit, x_sem, pair_sem, rep_send, rep_recv,
        o_send, o_recv, o_credit, swap_send, swap_recv, near_send, near_recv, far_send, far_recv,
    ) = rest[2 * packs + 5 :]
    ring = Ring()
    n = ring.chips
    rows, features = out.shape
    half = rows // 2
    r = grads.shape[2]
    share, plain = output_split(r, packs)
    pack = lax.axis_index("rep")
    mates = 2 * packs
    mate = pack * 2 + ring.core
    barrier = pltpu.get_barrier_semaphore()
    load_weights = [
        pltpu.make_async_copy(src, joined.at[pl.ds(i * r, src.shape[0])], w_sem.at[i])
        for i, src in enumerate((query_w, key_w, value_w, partner_w))
    ]
    load_outputs = [
        pltpu.make_async_copy(src, dst, w_sem.at[4 + i])
        for i, (src, dst) in enumerate(zip(outputs_in, (output_mine, *output_there)))
    ]
    load_late = [
        pltpu.make_async_copy(tokens_in, hidden_in, w_sem.at[4 + packs]),
        pltpu.make_async_copy(mixed_in, grad_mixed, w_sem.at[5 + packs]),
    ]
    for load in load_weights + load_outputs + load_late:
        load.start()

    def near(k):
        to = lax.rem(mate + k, mates)
        return {"dp": ring.chip * 2 + to % 2, "rep": to // 2}

    def far(k):
        return {"dp": lax.rem(ring.chip + k, n) * 2 + ring.core}

    for k in range(1, mates):
        pl.semaphore_signal(barrier, inc=1, device_id=near(k), device_id_type=MESH)
    for k in range(1, n):
        pl.semaphore_signal(barrier, inc=1, device_id=far(k), device_id_type=MESH)
    pl.semaphore_wait(barrier, mates + n - 2)

    def place(t, d):
        return ring.chip_far(-t if d == 0 else t)

    def swap(t, d):
        start = (place(t, d) * 2 + 1 - ring.core) * rows + d * half
        return remote(
            grads.at[:, pl.ds(pl.multiple_of(start, half), half)],
            partner_grads.at[:, t % n, half_rows(d, rows)],
            p_send.at[d, t % n],
            p_recv.at[d, t % n],
            ring.partner,
        )

    def begin(t, carry):
        for d in (0, 1):
            swap(t, d).start()
        return carry

    lax.fori_loop(1, n + 1, begin, 0)

    def reduce_copy(t, d, u):
        return remote(
            sent.at[d, u, t % 2],
            landed.at[d, u, t % 2],
            rs_send.at[d, u, t % 2],
            rs_recv.at[d, u, t % 2],
            ring.next[d],
        )

    def output_copy(t, d):
        return remote(
            o_sent.at[d, t % 2],
            o_landed.at[d, t % 2],
            o_send.at[d, t % 2],
            o_recv.at[d, t % 2],
            ring.next[d],
        )

    def give_credit(sem, d):
        pl.semaphore_signal(sem, inc=1, device_id={"dp": ring.back[d]}, device_id_type=MESH)

    def mine(t, d):
        start = (place(t, d) * 2 + ring.core) * rows + d * half
        return pl.ds(pl.multiple_of(start, half), half)

    def load_rows(t, d):
        part = half_rows(d, rows)
        return pltpu.make_async_copy(normed_all.at[place(t, d), part], x_buf.at[t % 2, part], x_sem.at[t % 2, d])

    def block_grads(t):
        return jnp.concatenate(
            [jnp.concatenate([grads[i, mine(t, d), :] for d in (0, 1)], 0) for i in range(3)]
            + [partner_grads[i, t % n] for i in range(3)],
            1,
        )

    def weight_parts(t):
        for d in (0, 1):
            load_rows(t, d).wait()
        parts[...] += dot_tn(block_grads(t), x_buf[t % 2])

    def pair_copy():
        return remote(pair_out, pair_land, pair_sem.at[0], pair_sem.at[1], ring.partner)

    def rep_copy(k):
        return pltpu.make_async_remote_copy(
            src_ref=pair_out,
            dst_ref=rep_land.at[k - 1],
            send_sem=rep_send.at[k - 1],
            recv_sem=rep_recv.at[k - 1],
            device_id={"rep": lax.rem(pack + k, packs)},
            device_id_type=MESH,
        )

    middle = n // 2

    def output_step(t):
        for d in (0, 1):
            spot = lax.rem(ring.place + (n - t if d == 0 else t), n)
            columns = pl.ds(d * (features // 2), features // 2)
            own = pl.multiple_of(spot * (share + plain), 16)
            total = output_mine[pl.ds(own, share), columns].astype(F32)
            for there in output_there:
                total += there[pl.ds(pl.multiple_of(spot * share, share), share), columns].astype(F32)
            if plain:
                rest_rows = pl.ds(pl.multiple_of(own + share, 16), plain)
                total = jnp.concatenate([total, output_mine[rest_rows, columns].astype(F32)], 0)

            def pass_on(value):
                @pl.when(t >= 3)
                def _():
                    output_copy(t - 2, d).wait_send()
                    pl.semaphore_wait(o_credit.at[d], 1)

                o_sent[d, t % 2] = value.astype(LOW)
                output_copy(t, d).start()

            @pl.when(t == 1)
            def _():
                pass_on(total)

            @pl.when(t >= 2)
            def _():
                output_copy(t - 1, d).wait_recv()
                more = total + o_landed[d, (t - 1) % 2].astype(F32)

                @pl.when(t <= n - 2)
                def _():
                    give_credit(o_credit.at[d], d)

                @pl.when(t < n)
                def _():
                    pass_on(more)

                @pl.when(t == n)
                def _():
                    o_packs[packs - 1, :, columns] = more.astype(LOW)

    def output_swap(k):
        return pltpu.make_async_remote_copy(
            src_ref=o_packs.at[packs - 1],
            dst_ref=o_packs.at[k - 1],
            send_sem=swap_send.at[k - 1],
            recv_sem=swap_recv.at[k - 1],
            device_id={"rep": lax.rem(pack + k, packs)},
            device_id_type=MESH,
        )

    def copies_to(src, land, own, send_sem, recv_sem, device, count):
        return [
            pltpu.make_async_remote_copy(
                src_ref=src,
                dst_ref=land.at[own],
                send_sem=send_sem.at[k],
                recv_sem=recv_sem.at[k],
                device_id=device(k),
                device_id_type=MESH,
            )
            for k in range(1, count)
        ]

    def far_copies():
        return copies_to(far_part, far_land, ring.chip, far_send, far_recv, far, n)

    def near_copies():
        return copies_to(near_part, near_land, mate, near_send, near_recv, near, mates)

    def collect(copies, src, land, own, count):
        land[own] = src[...]
        for copy in copies:
            copy.wait()
        total = land[0]
        for k in range(1, count):
            total += land[k]
        return total

    def first_gain():
        def add(i, total):
            at = pl.ds(pl.multiple_of(i * 64, 64), 64)
            product = joined[at, :].astype(F32) * parts[at, :]
            return total + jnp.sum(product, axis=0, keepdims=True)

        return lax.fori_loop(0, 6 * r // 64, add, jnp.zeros((1, features), F32)) / gain[...]

    def step(t, carry):
        @pl.when(t <= middle)
        def _():
            for d in (0, 1):
                load_rows(2 * t - 1, d).start()
                load_rows(2 * t, d).start()

        for u in (0, 1):
            columns = pl.ds(u * (features // 2), features // 2)
            for d in (0, 1):
                part = pl.ds(d * half, half), columns

                @pl.when(t >= 2)
                def _():
                    reduce_copy(t - 1, d, u).wait_recv()
                    out[part] += landed[d, u, (t - 1) % 2].astype(F32)

                    @pl.when(t <= n - 2)
                    def _():
                        give_credit(credit.at[d, u], d)

                @pl.when(t < n)
                def _():
                    @pl.when(t >= 3)
                    def _():
                        reduce_copy(t - 2, d, u).wait_send()
                        pl.semaphore_wait(credit.at[d, u], 1)

                    sent[d, u, t % 2] = out[part].astype(LOW)
                    reduce_copy(t, d, u).start()

            @pl.when(2 * t - 1 + u <= n)
            def _():
                output_step(2 * t - 1 + u)

        @pl.when(2 * t == n)
        def _():
            for k in range(1, packs):
                output_swap(k).start()

        @pl.when(t == 1)
        def _():
            parts[...] = jnp.zeros_like(parts)

            def arrived(k, carry):
                for d in (0, 1):
                    swap(k, d).wait_recv()
                return carry

            lax.fori_loop(2, n + 1, arrived, 0)

        @pl.when(t <= middle)
        def _():
            weight_parts(2 * t - 1)
            weight_parts(2 * t)

        @pl.when(t == middle)
        def _():
            for i in range(3):
                pair_out[i] = parts[pl.ds((3 + i) * r, r), :].astype(LOW)
            pair_copy().start()
            far_part[0:1, :] = first_gain()
            far_part[1:2, :] = dense_gain_part[...]
            for copy in far_copies():
                copy.start()

        @pl.when(t == middle + 1)
        def _():
            pair_copy().wait()
            for i in range(3):
                pair_out[i] = (parts[pl.ds(i * r, r), :] + pair_land[i].astype(F32)).astype(LOW)
            for k in range(1, packs):
                rep_copy(k).start()
            rep_land[packs - 1] = pair_out[...]

        @pl.when(t == middle + 2)
        def _():
            near_part[...] = collect(far_copies(), far_part, far_land, ring.chip, n)
            for copy in near_copies():
                copy.start()

        @pl.when(t < n)
        def _():
            out[...] = dot_nn(block_grads(t + 1), joined[...])

        return carry

    for d in (0, 1):
        swap(1, d).wait_recv()
    for load in load_weights + load_outputs:
        load.wait()
    out[...] = dot_nn(block_grads(1), joined[...])
    lax.fori_loop(1, n + 1, step, 0)
    for t in (n - 2, n - 1):
        for d in (0, 1):
            output_copy(t, d).wait_send()
            for u in (0, 1):
                reduce_copy(t, d, u).wait_send()

    for load in load_late:
        load.wait()

    def close(i, carry):
        span = pl.ds(pl.multiple_of(i * 16, 16), 16)
        value = hidden_in[span, :].astype(F32)
        grad = out[span, :]
        scale = lax.rsqrt(jnp.mean(value * value, axis=1, keepdims=True) + EPSILON)
        scaled = grad * gain[...]
        shift = jnp.mean(value * scaled, axis=1, keepdims=True)
        out[span, :] = grad_mixed[span, :] + scale * scaled - value * (scale * scale * scale * shift)
        return carry

    lax.fori_loop(0, rows // 16, close, 0)

    def finish(t, carry):
        for d in (0, 1):
            swap(t, d).wait_send()
        return carry

    lax.fori_loop(1, n + 1, finish, 0)
    gains[...] = collect(near_copies(), near_part, near_land, mate, mates)
    for k in range(1, packs):
        rep_copy(k).wait()
        output_swap(k).wait()


def normed_back(
    grads, weights, partner_weights, hidden_in, gain, grad_mixed, dense_gain_part, normed_all, output_mine, output_there
):
    tokens, r = grads.shape[1:]
    features = partner_weights.shape[1]
    devices = lax.axis_size("dp")
    packs = lax.axis_size("rep")
    n = devices // 2
    rows = tokens // devices
    half = rows // 2
    share, plain = output_split(r, packs)
    carried = share + plain
    mates = 2 * packs
    vmem = pl.BlockSpec(memory_space=pltpu.VMEM)
    hbm = pl.BlockSpec(memory_space=pl.ANY)
    dma = pltpu.SemaphoreType.DMA
    return pl.pallas_call(
        functools.partial(normed_back_kernel, packs),
        out_shape=(
            jax.ShapeDtypeStruct((rows, features), F32),
            jax.ShapeDtypeStruct((2, features), F32),
        )
        + (
            jax.ShapeDtypeStruct((packs, 3, r, features), LOW),
            jax.ShapeDtypeStruct((packs, carried, features), LOW),
        ),
        in_specs=[vmem] + [hbm] * 5 + [vmem, hbm, vmem] + [hbm] * (1 + packs),
        out_specs=(vmem,) * 4,
        scratch_shapes=[pltpu.VMEM(a.shape, a.dtype) for a in (hidden_in, grad_mixed, output_mine, *output_there)]
        + [
            pltpu.VMEM((6 * r, features), LOW),
            pltpu.VMEM((3, n, rows, r), LOW),
            pltpu.VMEM((2, 2, 2, half, features // 2), LOW),
            pltpu.VMEM((2, 2, 2, half, features // 2), LOW),
            pltpu.VMEM((2, rows, features), LOW),
            pltpu.VMEM((6 * r, features), F32),
            pltpu.VMEM((3, r, features), LOW),
            pltpu.VMEM((3, r, features), LOW),
            pltpu.VMEM((2, 2, carried, features // 2), LOW),
            pltpu.VMEM((2, 2, carried, features // 2), LOW),
            pltpu.VMEM((2, features), F32),
            pltpu.VMEM((n, 2, features), F32),
            pltpu.VMEM((2, features), F32),
            pltpu.VMEM((mates, 2, features), F32),
            dma((6 + packs,)), dma((2, n)), dma((2, n)), dma((2, 2, 2)), dma((2, 2, 2)),
            pltpu.SemaphoreType.REGULAR((2, 2)),
            dma((2, 2)), dma((2,)), dma((packs - 1,)), dma((packs - 1,)),
            dma((2, 2)), dma((2, 2)), pltpu.SemaphoreType.REGULAR((2,)),
            dma((packs - 1,)), dma((packs - 1,)), dma((mates,)), dma((mates,)), dma((n,)), dma((n,)),
        ],
        compiler_params=pltpu.CompilerParams(
            collective_id=3, has_side_effects=True, vmem_limit_bytes=44 * MIB
        ),
        cost_estimate=pl.CostEstimate(
            flops=2 * n * rows * features * 12 * r, bytes_accessed=320 * MIB, transcendentals=0
        ),
        name="normed_back",
    )(
        grads, *weights, partner_weights, hidden_in, gain, grad_mixed, dense_gain_part, normed_all,
        output_mine, *output_there,
    )


def last_sums_kernel(packs, *refs):
    gate, up_a, up_b, down, gate_o, up_a_o, up_b_o, down_o, qkv, mixed, out_sum, grad_in, output, gains = refs[:14]
    gate_t, up_t, down_t, query_t, key_t, value_t, layer, grad, output_t, first_gain, second_gain = refs[14:]

    def add(low, other):
        if packs == 2:
            return low[...].astype(F32) + other[...].astype(F32)
        return other[...].astype(F32)

    gate_t[...] = add(gate, gate_o)
    down_t[...] = add(down, down_o)
    up_t[...] = jnp.concatenate([add(up_a, up_a_o), add(up_b, up_b_o)], 0)
    pack = lax.axis_index("rep")
    slots = [lax.rem(pack + 2 * packs - q - 1, packs) for q in range(packs)]
    for i, target in enumerate((query_t, key_t, value_t)):
        total = qkv[slots[0], i].astype(F32)
        for slot in slots[1:]:
            total += qkv[slot, i].astype(F32)
        target[...] = total

    @pl.when(pl.program_id(0) == 0)
    def _():
        first_gain[...] = gains[0, :]
        second_gain[...] = gains[1, :]
        r = output_t.shape[0]
        share, plain = output_split(r, packs)
        for q, slot in enumerate(slots):
            output_t[q * share : (q + 1) * share, :] = output[slot, :share].astype(F32)
        if plain:
            total = output[slots[0], share:].astype(F32)
            for slot in slots[1:]:
                total += output[slot, share:].astype(F32)
            output_t[r - plain :, :] = total

    layer[...] = (mixed[...] + out_sum[...].astype(F32)).astype(LOW)
    grad[...] = grad_in[...]


def last_sums(lows, others, qkv, mixed, out_sum, grad_in, output, gains):
    own, features = lows[0].shape
    rows, r = mixed.shape[0], qkv.shape[2]
    packs = qkv.shape[0]
    steps = own // STRIPE

    def striped(array):
        return pl.BlockSpec((array.shape[0] // steps, features), lambda i: (i, 0))

    wide = jax.ShapeDtypeStruct((own, features), F32)
    narrow = jax.ShapeDtypeStruct((r, features), F32)
    layer = jax.ShapeDtypeStruct((rows, features), LOW)
    line = jax.ShapeDtypeStruct((features,), F32)
    out_shape = (wide,) * 3 + (narrow,) * 3 + (layer, grad_in, narrow, line, line)
    return pl.pallas_call(
        functools.partial(last_sums_kernel, packs),
        out_shape=tuple(jax.ShapeDtypeStruct(a.shape, a.dtype) for a in out_shape),
        grid=(steps,),
        in_specs=[striped(a) for a in (*lows, *others)]
        + [pl.BlockSpec((packs, 3, r // steps, features), lambda i: (0, 0, i, 0))]
        + [striped(a) for a in (mixed, out_sum, grad_in)]
        + [pl.BlockSpec(output.shape, lambda i: (0, 0, 0)), pl.BlockSpec(gains.shape, lambda i: (0, 0))],
        out_specs=tuple(striped(a) for a in out_shape[:-3])
        + (pl.BlockSpec((r, features), lambda i: (0, 0)),)
        + (pl.BlockSpec((features,), lambda i: (0,)),) * 2,
        compiler_params=pltpu.CompilerParams(vmem_limit_bytes=62 * MIB),
        cost_estimate=pl.CostEstimate(flops=8 * own * features, bytes_accessed=40 * MIB, transcendentals=0),
        name="last_sums",
    )(*lows, *others, qkv, mixed, out_sum, grad_in, output, gains)


def from_partner(value):
    devices = lax.axis_size("dp")
    return lax.ppermute(value, "dp", [(i, i ^ 1) for i in range(devices)])


def pack_swap(low):
    if lax.axis_size("rep") == 2:
        return lax.ppermute(low, "rep", [(0, 1), (1, 0)])
    return lax.psum(low, "rep")


def together(*values):
    return lax.optimization_barrier(values)


def body(
    tokens,
    attention_gain,
    query_weight,
    key_weight,
    value_weight,
    output_weight,
    dense_gain,
    gate_weight,
    up_weight,
    down_weight,
    block_document,
    document_tail,
    cotangent,
):
    devices = lax.axis_size("dp")
    chips = devices // 2
    tok_dev = tokens.shape[1]
    pack_tok = tok_dev * devices

    documents, tails = block_document[0], document_tail[0]
    first = jnp.sum((documents[None, :] < documents[:, None]).astype(jnp.int32), axis=1)
    last = jnp.concatenate([documents[1:] != documents[:-1], jnp.ones((1,), bool)])
    doc_ids = jnp.arange(tails.shape[0], dtype=jnp.int32)
    own_tail = jnp.sum((documents[:, None] == doc_ids[None, :]) * tails[None, :], axis=1)
    tail = jnp.where(last, own_tail, BLOCK).astype(jnp.int32)
    block_index = jnp.arange(documents.shape[0], dtype=jnp.int32)
    inside = jnp.arange(BLOCK, dtype=jnp.int32)
    frequency = ROPE_BASE ** (-(jnp.arange(HALF, dtype=F32) * (2.0 / HEAD_DIM)))
    start = ((block_index - first) * BLOCK).astype(F32)[None, :] * frequency[:, None]
    within = inside.astype(F32)[None, :] * frequency[:, None]
    cos_a, sin_a = jnp.cos(start)[:, :, None], jnp.sin(start)[:, :, None]
    cos_b, sin_b = jnp.cos(within)[:, None, :], jnp.sin(within)[:, None, :]
    cos_t = (cos_a * cos_b - sin_a * sin_b).reshape(HALF, -1)
    sin_t = (sin_a * cos_b + cos_a * sin_b).reshape(HALF, -1)
    r = query_weight.shape[0]

    qkv, normed_all, full_output = gather_project(
        tokens[0],
        attention_gain[None],
        (query_weight, key_weight, value_weight),
        output_weight,
        cos_t,
        sin_t,
    )

    order = ring_order(chips)
    lanes = [[2 * chip + k for chip in order] for k in (0, 1)]
    grad_low = cotangent[0]
    qkv, grad_late = together(qkv, grad_low)
    cotangents = lax.all_gather(grad_late, "dp", axis=0, axis_index_groups=lanes)
    gate_other, up_other, down_other = (
        from_partner(gate_weight),
        from_partner(up_weight),
        from_partner(down_weight),
    )
    qkv_weight = jnp.concatenate([query_weight, key_weight, value_weight], 0)

    attended, log_total = attend(first, tail, qkv)
    mixed, normed_two, attended_blocks = mix(attended, tokens[0], dense_gain[None], full_output)
    normed_two, qkv_weight = together(normed_two, qkv_weight)
    qkv_other = from_partner(qkv_weight)
    packs, pack = lax.axis_size("rep"), lax.axis_index("rep")

    grad_normed_two, out_parts, _, gate_low, up_a, up_b, down_low = dense(
        normed_two,
        cotangents,
        (gate_weight, up_weight, down_weight),
        (gate_other, up_other, down_other),
    )
    out_sum = lax.psum_scatter(
        out_parts.reshape(chips * tok_dev, -1),
        "dp",
        scatter_dimension=0,
        tiled=True,
        axis_index_groups=lanes,
    )
    gate_there = pack_swap(gate_low)

    grad_mixed, dense_gain_part, grad_heads, output_mine, *output_low = mixed_back(
        mixed, grad_normed_two, grad_low, dense_gain[None], full_output, attended_blocks
    )
    output_there = [
        lax.ppermute(low, "rep", [(i, (i + k) % packs) for i in range(packs)])
        for k, low in enumerate(output_low, 1)
    ]
    grad_heads, gate_there, output_mine = together(grad_heads, gate_there, output_mine)
    up_a, _ = together(up_a, grad_heads)
    up_a_there = pack_swap(up_a)
    grads = attend_back(first, tail, qkv, grad_heads, attended, log_total, cos_t, sin_t)
    grads, output_there, up_a_there, up_b, down_low = together(
        grads, output_there, up_a_there, up_b, down_low
    )
    up_b_there = pack_swap(up_b)
    down_there = pack_swap(down_low)
    input_grad, gain_totals, qkv_packs, output_packs = normed_back(
        grads,
        (query_weight, key_weight, value_weight),
        qkv_other,
        tokens[0],
        attention_gain[None],
        grad_mixed,
        dense_gain_part,
        normed_all,
        output_mine,
        output_there,
    )
    input_grad, out_sum, gate_there, up_a_there, up_b_there, down_there = together(
        input_grad, out_sum, gate_there, up_a_there, up_b_there, down_there
    )
    (
        gate_total, up_total, down_total, query_total, key_total, value_total,
        layer_out, input_grad, output_total, first_gain, second_gain,
    ) = last_sums(
        (gate_low, up_a, up_b, down_low),
        (gate_there, up_a_there, up_b_there, down_there),
        qkv_packs,
        mixed,
        out_sum,
        input_grad,
        output_packs,
        gain_totals,
    )
    return (
        layer_out[None],
        input_grad[None],
        first_gain,
        query_total,
        key_total,
        value_total,
        output_total,
        second_gain,
        gate_total,
        up_total,
        down_total,
    )


def solution(mesh):
    return jax.shard_map(
        body,
        mesh=mesh,
        in_specs=(
            P("rep", "dp", None),
            P(),
            P("dp", None),
            P("dp", None),
            P("dp", None),
            P("dp", None),
            P(),
            P("dp", None),
            P("dp", None),
            P("dp", None),
            P("rep", None),
            P("rep", None),
            P("rep", "dp", None),
        ),
        out_specs=(
            P("rep", "dp", None),
            P("rep", "dp", None),
            P(),
            P("dp", None),
            P("dp", None),
            P("dp", None),
            P("dp", None),
            P(),
            P("dp", None),
            P("dp", None),
            P("dp", None),
        ),
        check_vma=False,
    )
```
